32 devices in a mesh: mem: 32 (over z, y, x, core).
Axes of the slice: x: 2, y: 2, z: 4, core: 2. Of those that a mesh axis runs over, the one named last changes fastest.
Arguments:
- query_feats: float32 [32768, 8], P('mem'), may hold values from -6 to 6
- feature_mask: int32 [32768, 8], P('mem'), may hold values from 0 to 1, as said below
- query_task: int32 [32768], P('mem'), may hold values from 0 to 3
- target_class: int32 [32768], P('mem'), may hold values from 0 to 15
- target_mask: int32 [32768], P('mem'), may hold values from 0 to 1, as said below
- memory_feats: float32 [2048, 8], P('mem'), may hold values from -6 to 6
- memory_task: int32 [2048], replicated, may hold values from 0 to 3, as said below
- memory_mask: int32 [2048], replicated, may hold values from 0 to 1, as said below
- anneal: float32 [1], replicated, may hold values from 0.3 to 0.7
- w_qkv: float32 [196608], P('mem'), may hold values from -0.375 to 0.375
- w_out: float32 [65536], P('mem'), may hold values from -6 to 6
- w_heads: float32 [6144], P('mem'), may hold values from -0.375 to 0.375
- w_small: float32 [1056], P('mem'), may hold values from 0.1 to 1.9
- m_qkv: float32 [196608], P('mem'), may hold values from -0.00015258789 to 0.00015258789
- m_out: float32 [65536], P('mem'), may hold values from -0.00015258789 to 0.00015258789
- m_heads: float32 [6144], P('mem'), may hold values from -0.00015258789 to 0.00015258789
- m_small: float32 [1056], P('mem'), may hold values from -0.00061035156 to 0.00061035156
- v_qkv: float32 [196608], P('mem'), may hold values from 9.536743e-12 to 3.814697e-11
- v_out: float32 [65536], P('mem'), may hold values from 9.536743e-13 to 3.8146973e-12
- v_heads: float32 [6144], P('mem'), may hold values from 9.536743e-12 to 3.814697e-11
- v_small: float32 [1056], P('mem'), may hold values from 1.5258789e-10 to 6.1035155e-10
Outputs:
- new_qkv: float32 [196608], P('mem')
- new_out: float32 [65536], P('mem')
- new_heads: float32 [6144], P('mem')
- new_small: float32 [1056], P('mem')
- first_qkv: float32 [196608], P('mem')
- first_out: float32 [65536], P('mem')
- first_heads: float32 [6144], P('mem')
- first_small: float32 [1056], P('mem')
- second_qkv: float32 [196608], P('mem')
- second_out: float32 [65536], P('mem')
- second_heads: float32 [6144], P('mem')
- second_small: float32 [1056], P('mem')
- copy_qkv: bfloat16 [196608], P('mem')
- copy_out: bfloat16 [65536], P('mem')
- copy_heads: bfloat16 [6144], P('mem')
- copy_small: bfloat16 [1056], P('mem')
- loss_value: float32 [1], replicated
- grad_norm: float32 [1], replicated
The draws below stay inside these ranges and needn't reach their ends.
Inputs may be any that keep to these rules, and one draw needn't show every extreme that they name: `memory_mask`: the live rows of each device's 64 memory rows are a prefix of a quarter of them or more; the first device's rows are all live. `memory_task`: the first 4 memory rows have the tasks 0 to 3 in order. `target_mask`: the share of labelled queries rises along the query rows from about a quarter to about three quarters. `feature_mask`: the share of hidden features rises along the query rows from about a quarter to about three quarters.
All inputs are finite; a program needn't handle non-finite values.
Results may differ from the reference program's by a relative error of at most 0.0087.
Values may be sent and summed in bfloat16 or wider, within the bound.
A program may use at most 128 MiB of HBM per device.

```python
import math
import jax
import jax.numpy as jnp
from jax import lax

F = 8
D = 256
H = 8
C = 16
TASKS = 4
STEP = 10
Q_DEV = 1024
MEM_DEV = 64
QUERIES = 32768
MEMORY = 2048
SMALLN = 1056


def draw_memory_mask(key, part):
    devices = MEMORY // MEM_DEV
    lengths = jax.random.randint(key, (devices,), max(1, MEM_DEV // 4), MEM_DEV + 1)
    lengths = lengths.at[0].set(MEM_DEV)
    position = jnp.arange(MEM_DEV, dtype=jnp.int32)
    return (position[None, :] < lengths[:, None]).astype(jnp.int32).reshape(MEMORY)


def draw_memory_task(key, part):
    values_drawn = jax.random.randint(key, (MEMORY,), 0, TASKS)
    return values_drawn.at[:TASKS].set(jnp.arange(TASKS, dtype=jnp.int32))


def rising_mask(key, row_count, col_count):
    last_dev = max(QUERIES // Q_DEV - 1, 1)
    device = jnp.arange(row_count, dtype=jnp.int32) // Q_DEV
    samples = jax.random.randint(key, (row_count, col_count), 0, 4 * last_dev)
    return (samples < last_dev + 2 * device[:, None]).astype(jnp.int32)


def draw_target_mask(key, part):
    return rising_mask(key, QUERIES, 1).reshape(QUERIES)


def draw_feature_mask(key, part):
    return rising_mask(jax.random.fold_in(key, 7), QUERIES, F)


def touch_ends(values, stream_key, smallest, largest):
    longest = values.shape.index(max(values.shape))
    spots = []
    for shift in (0, 1):
        where = [jax.random.randint(jax.random.fold_in(stream_key, axis), (), 0, length) for axis, length in enumerate(values.shape)]
        where[longest] = (where[longest] + shift) % values.shape[longest]
        spots.append(tuple(where))
    return values.at[spots[0]].set(smallest).at[spots[1]].set(largest)


def block_scale(stream_key, shape, pieces, smallest, largest):
    def one(dim, parts):
        steps = jax.random.uniform(jax.random.fold_in(jax.random.fold_in(stream_key, 6), dim), (parts,), jnp.float32, smallest / len(pieces), largest / len(pieces))
        return jnp.repeat(jnp.exp(steps), shape[dim] // parts).reshape((-1,) + (1,) * (len(shape) - dim - 1))

    gain = one(*pieces[0])
    for cut in pieces[1:]:
        gain = gain * one(*cut)
    return gain


def normal_values(key, shape, spread, bound, split=(), kind=jnp.bfloat16):
    entries = spread * jax.random.normal(key, shape, jnp.float32)
    if split:
        entries = entries * block_scale(key, shape, split, -0.22, 0.18)
    return jnp.clip(entries, -bound, bound).astype(kind)


def setup_inputs(seed: int = 0) -> dict:
    key_list = jax.random.split(jax.random.key(seed), 22)
    return {
        "query_feats": normal_values(key_list[0], (QUERIES, F), 1.0, 6.0, ((0, 32),), jnp.float32),
        "feature_mask": draw_feature_mask(jax.random.fold_in(key_list[21], 71), 0),
        "query_task": touch_ends(jax.random.randint(key_list[2], (QUERIES,), 0, TASKS), jax.random.fold_in(key_list[2], 1), 0, TASKS - 1).astype(jnp.int32),
        "target_class": touch_ends(jax.random.randint(key_list[3], (QUERIES,), 0, C), jax.random.fold_in(key_list[3], 1), 0, C - 1).astype(jnp.int32),
        "target_mask": draw_target_mask(jax.random.fold_in(key_list[21], 71), 0),
        "memory_feats": normal_values(key_list[5], (MEMORY, F), 1.0, 6.0, ((0, 32),), jnp.float32),
        "memory_task": draw_memory_task(jax.random.fold_in(key_list[21], 71), 0),
        "memory_mask": draw_memory_mask(jax.random.fold_in(key_list[21], 71), 0),
        "anneal": jnp.clip(jax.random.uniform(key_list[8], (1,), jnp.float32, 0.3, 0.7), 0.3, 0.7),
        "w_qkv": normal_values(key_list[9], (3 * D * D,), D ** -0.5, 0.375, ((0, 32),), jnp.float32),
        "w_out": normal_values(key_list[10], (D * D,), (max(1, 3 * TASKS * D // MEMORY)) ** -0.5, 6.0, ((0, 32),), jnp.float32),
        "w_heads": normal_values(key_list[11], (D * (C + F),), D ** -0.5, 0.375, ((0, 32),), jnp.float32),
        "w_small": jnp.clip(1.0 + 0.18 * jax.random.normal(key_list[12], (SMALLN,), jnp.float32), 0.1, 1.9),
        "m_qkv": normal_values(key_list[13], (3 * D * D,), (0.0055 * (4 * D * D) ** -0.5), 0.00015258789, ((0, 32),), jnp.float32),
        "m_out": normal_values(key_list[14], (D * D,), (0.0055 * (4 * D * D) ** -0.5), 0.00015258789, ((0, 32),), jnp.float32),
        "m_heads": normal_values(key_list[15], (D * (C + F),), (0.0055 * (4 * D * D) ** -0.5), 0.00015258789, ((0, 32),), jnp.float32),
        "m_small": normal_values(key_list[16], (SMALLN,), (0.022 * (4 * D * D) ** -0.5), 0.00061035156, ((0, 32),), jnp.float32),
        "v_qkv": jnp.clip(jnp.exp(math.log(3.8146971692576415e-11) - 1.3862944 * jax.random.uniform(key_list[17], (3 * D * D,), jnp.float32) ** block_scale(key_list[17], (3 * D * D,), ((0, 32),), -0.2, 0.2)), 9.536742923144104e-12, 3.8146971692576415e-11),
        "v_out": jnp.clip(jnp.exp(math.log(3.814697255993815e-12) - 1.3862944 * jax.random.uniform(key_list[18], (D * D,), jnp.float32) ** block_scale(key_list[18], (D * D,), ((0, 32),), -0.2, 0.2)), 9.536743139984538e-13, 3.814697255993815e-12),
        "v_heads": jnp.clip(jnp.exp(math.log(3.8146971692576415e-11) - 1.3862944 * jax.random.uniform(key_list[19], (D * (C + F),), jnp.float32) ** block_scale(key_list[19], (D * (C + F),), ((0, 32),), -0.2, 0.2)), 9.536742923144104e-12, 3.8146971692576415e-11),
        "v_small": jnp.clip(jnp.exp(math.log(6.103515470812226e-10) - 1.3862944 * jax.random.uniform(key_list[20], (SMALLN,), jnp.float32) ** block_scale(key_list[20], (SMALLN,), ((0, 32),), -0.2, 0.2)), 1.5258788677030566e-10, 6.103515470812226e-10),
    }


eps_norm = 1e-05
max_norm = 0.05
beta_one = 0.9
beta_two = 0.999
adam_eps = 1e-08
decay_rate = 0.01
learn_rates = (0.05, 1.0, 0.05, 0.5)
masked_score = -1e+30

@jax.custom_vjp
def low(v):
    return lax.optimization_barrier(v.astype(jnp.bfloat16)).astype(jnp.float32)

@jax.custom_vjp
def low_back(v):
    return v

def low_keep(v):
    return (low(v), None)

def low_pass(kept, grad):
    return (grad,)

def back_keep(v):
    return (v, None)

def back_low(kept, grad):
    return (low(grad),)
low.defvjp(low_keep, low_pass)
low_back.defvjp(back_keep, back_low)

def embed(feature_rows, table_flat, emb_bias):
    emb_table = table_flat.reshape(feature_rows.shape[1], -1)
    return (feature_rows[:, :, None] * emb_table[None]).reshape(feature_rows.shape[0], -1) + emb_bias

def standard(hidden):
    centred = hidden - lax.optimization_barrier(jnp.mean(hidden, -1, keepdims=True))
    inverse = lax.rsqrt(lax.optimization_barrier(jnp.mean(centred * centred, -1, keepdims=True)) + eps_norm)
    return (centred * inverse, inverse)

def adamw(weight, first_mom, second, grad_in, factor, step_num, step_rate):
    clipped = grad_in * factor
    first_new = beta_one * first_mom + (1 - beta_one) * clipped
    second_new = beta_two * second + (1 - beta_two) * clipped * clipped
    fix_one = 1 - beta_one ** step_num
    fix_two = 1 - beta_two ** step_num
    weight_new = weight - step_rate * (first_new / fix_one / (jnp.sqrt(second_new / fix_two) + adam_eps) + decay_rate * weight)
    return (first_new, second_new, weight_new)

def reference(query_feats, feature_mask, query_task, target_class, target_mask, memory_feats, memory_task, memory_mask, anneal, w_qkv, w_out, w_heads, w_small, m_qkv, m_out, m_heads, m_small, v_qkv, v_out, v_heads, v_small):
    high = lax.Precision.HIGHEST
    head_size = D // H
    kept_input = query_feats * (1 - feature_mask).astype(jnp.float32)
    feat_mask = feature_mask.astype(jnp.float32)
    label_mask = target_mask.astype(jnp.float32)
    count_target = jnp.maximum(jnp.sum(label_mask), 1.0)
    count_recon = jnp.maximum(jnp.sum(feat_mask), 1.0)
    weight_a = anneal[0]
    key_live = memory_mask > 0
    query_block = math.gcd(QUERIES, 1024)
    num_blocks = QUERIES // query_block

    def loss_fn(params):
        par_qkv, par_out, par_heads, par_small = params
        emb_table = par_small[:D]
        emb_bias = par_small[D:2 * D]
        gain_in = par_small[2 * D:3 * D]
        gain_out = par_small[3 * D:4 * D]
        score_coef = par_small[4 * D:4 * D + H] * head_size ** (-0.5)
        qkv_low = low(par_qkv).reshape(D, 3 * D)
        out_low = low(par_out).reshape(D, D)
        heads_low = low(par_heads).reshape(D, C + F)
        mem_hidden = embed(memory_feats, emb_table, emb_bias)
        mem_normed = low(standard(mem_hidden)[0] * gain_in)
        mem_kv = low(jnp.dot(mem_normed, qkv_low[:, D:], precision=high))
        key_rows = mem_kv[:, :D].reshape(-1, H, head_size)
        value_rows = mem_kv[:, D:].reshape(-1, H, head_size)

        def one_block(totals, row_data):
            x_kept, x_raw, feat_m, task_ids, class_ids, label_m = row_data
            hidden_in = embed(x_kept, emb_table, emb_bias)
            query_normed = low(standard(hidden_in)[0] * gain_in)
            queries = low_back(low(jnp.dot(query_normed, qkv_low[:, :D], precision=high))).reshape(-1, H, head_size)
            raw_scores = jnp.einsum('qhd,khd->hqk', queries, key_rows, precision=high)
            scores = low_back(score_coef[:, None, None] * raw_scores)
            allowed = ((task_ids[:, None] == memory_task[None, :]) & key_live[None, :])[None]
            scores = jnp.where(allowed, scores, masked_score)
            exp_vals = jnp.where(allowed, jnp.exp(scores - lax.optimization_barrier(jnp.max(scores, -1, keepdims=True))), 0.0)
            probs_low = low(exp_vals / lax.optimization_barrier(jnp.sum(exp_vals, -1, keepdims=True)))
            attended = jnp.einsum('hqk,khd->qhd', probs_low, value_rows, precision=high).reshape(-1, D)
            attended = low_back(low(attended))
            residual = hidden_in + low_back(jnp.dot(attended, out_low, precision=high))
            final_normed = low(standard(residual)[0] * gain_out)
            head_out = low_back(jnp.dot(final_normed, heads_low, precision=high))
            logits = head_out[:, :C]
            recon_out = head_out[:, C:]
            log_total = jax.nn.logsumexp(logits, -1)
            picked = lax.optimization_barrier(jnp.sum(logits * jax.nn.one_hot(class_ids, C, dtype=logits.dtype), -1))
            sum_target = jnp.sum(label_m * (log_total - picked))
            sum_recon = jnp.sum(feat_m * (recon_out - x_raw) ** 2)
            return ((totals[0] + sum_target, totals[1] + sum_recon), None)
        row_data = tuple((arr.reshape((num_blocks, query_block) + arr.shape[1:]) for arr in (kept_input, query_feats, feat_mask, query_task, target_class, label_mask)))
        zero_value = jnp.zeros((), kept_input.dtype)
        (sum_target, sum_recon), unused = lax.scan(jax.checkpoint(one_block), (zero_value, zero_value), row_data)
        return weight_a * sum_target / count_target + (1 - weight_a) * sum_recon / count_recon
    weights_all = (w_qkv, w_out, w_heads, w_small)
    loss_value, pull_back = jax.vjp(loss_fn, weights_all)
    gradients = pull_back(jnp.ones((), loss_value.dtype))[0]
    grad_total = jnp.sqrt(sum((jnp.sum(grad_in * grad_in) for grad_in in gradients)))
    factor = jnp.minimum(1.0, max_norm / (grad_total + 1e-06))
    step_num = float(STEP)
    firsts = (m_qkv, m_out, m_heads, m_small)
    seconds = (v_qkv, v_out, v_heads, v_small)
    results = [adamw(weight, first_mom, second, grad_in, factor, step_num, step_rate) for weight, first_mom, second, grad_in, step_rate in zip(weights_all, firsts, seconds, gradients, learn_rates)]
    new_w = [entry[2] for entry in results]
    return (new_w[0], new_w[1], new_w[2], new_w[3], results[0][0], results[1][0], results[2][0], results[3][0], results[0][1], results[1][1], results[2][1], results[3][1], new_w[0].astype(jnp.bfloat16), new_w[1].astype(jnp.bfloat16), new_w[2].astype(jnp.bfloat16), new_w[3].astype(jnp.bfloat16), loss_value.reshape(1), grad_total.reshape(1))
```

```python
import functools
import math

import jax
import jax.numpy as jnp
from jax import lax
from jax.experimental import pallas as pl
from jax.experimental.pallas import tpu as pltpu
from jax.sharding import PartitionSpec as P

F = 8
D = 256
H = 8
C = 16
TASKS = 4
STEP = 10


eps_norm = 1e-05
max_norm = 0.05
beta_one = 0.9
beta_two = 0.999
adam_eps = 1e-08
decay_rate = 0.01
learn_rates = (0.05, 1.0, 0.05, 0.5)
masked_score = -1e30


def embed(feature_rows, table_flat, emb_bias):
    emb_table = table_flat.reshape(feature_rows.shape[1], -1)
    return (feature_rows[:, :, None] * emb_table[None]).reshape(
        feature_rows.shape[0], -1
    ) + emb_bias


def standard(hidden):
    centred = hidden - jnp.mean(hidden, -1, keepdims=True)
    inverse = lax.rsqrt(jnp.mean(centred * centred, -1, keepdims=True) + eps_norm)
    return (centred * inverse, inverse)


def norm_back(grad_out, hidden, gain_vec):
    normed, inverse = standard(hidden)
    grad_gain = jnp.sum(grad_out * normed, 0)
    grad_scaled = grad_out * gain_vec
    grad_hidden = inverse * (
        grad_scaled
        - jnp.mean(grad_scaled, -1, keepdims=True)
        - normed * jnp.mean(grad_scaled * normed, -1, keepdims=True)
    )
    return (grad_hidden, grad_gain)


def split_pair(values):
    upper = values.astype(jnp.bfloat16)
    lower = (values - upper.astype(jnp.float32)).astype(jnp.bfloat16)
    return (upper, lower)


def adamw(weight, first_mom, second, grad_in, factor, step_num, step_rate):
    clipped = grad_in * factor
    first_new = beta_one * first_mom + (1 - beta_one) * clipped
    second_new = beta_two * second + (1 - beta_two) * clipped * clipped
    fix_one = 1 - beta_one**step_num
    fix_two = 1 - beta_two**step_num
    weight_new = weight - step_rate * (
        first_new / fix_one / (jnp.sqrt(second_new / fix_two) + adam_eps) + decay_rate * weight
    )
    return (first_new, second_new, weight_new)


def local(
    query_feats,
    feature_mask,
    query_task,
    target_class,
    target_mask,
    memory_feats,
    memory_task,
    memory_mask,
    anneal,
    w_qkv,
    w_out,
    w_heads,
    w_small,
    m_qkv,
    m_out,
    m_heads,
    m_small,
    v_qkv,
    v_out,
    v_heads,
    v_small,
):
    high = lax.Precision.HIGHEST
    head_size = D // H
    full_qkv, full_out, full_heads, full_small = (
        lax.all_gather(w_qkv, "mem", axis=0, tiled=True),
        lax.all_gather(w_out, "mem", axis=0, tiled=True),
        lax.all_gather(w_heads, "mem", axis=0, tiled=True),
        lax.all_gather(w_small, "mem", axis=0, tiled=True),
    )
    emb_table = full_small[:D]
    emb_bias = full_small[D : 2 * D]
    gain_in = full_small[2 * D : 3 * D]
    gain_out = full_small[3 * D : 4 * D]
    score_coef = full_small[4 * D : 4 * D + H] * head_size ** (-0.5)
    qkv_low = full_qkv.reshape(D, 3 * D).astype(jnp.bfloat16)
    out_low = full_out.reshape(D, D).astype(jnp.bfloat16)
    heads_low = full_heads.reshape(D, C + F).astype(jnp.bfloat16)
    mem_hidden = embed(memory_feats, emb_table, emb_bias)
    mem_normed = (standard(mem_hidden)[0] * gain_in).astype(jnp.bfloat16)
    mem_kv = jnp.dot(mem_normed, qkv_low[:, D:], preferred_element_type=jnp.float32).astype(
        jnp.bfloat16
    )
    all_kv = lax.all_gather(mem_kv, "mem", axis=0, tiled=True)
    memory_rows = all_kv.shape[0]
    block_keys = math.gcd(memory_rows, 512)
    num_blocks = memory_rows // block_keys
    key_rows = all_kv[:, :D].reshape(num_blocks, block_keys, H, head_size)
    value_rows = all_kv[:, D:].reshape(num_blocks, block_keys, H, head_size)
    task_blocks = memory_task.reshape(num_blocks, block_keys)
    live_blocks = memory_mask.reshape(num_blocks, block_keys)
    key_blocks = (key_rows, value_rows, task_blocks, live_blocks)
    kept_input = query_feats * (1 - feature_mask).astype(jnp.float32)
    hidden_in = embed(kept_input, emb_table, emb_bias)
    query_normed = (standard(hidden_in)[0] * gain_in).astype(jnp.bfloat16)
    queries = (
        jnp.dot(query_normed, qkv_low[:, :D], preferred_element_type=jnp.float32)
        .astype(jnp.bfloat16)
        .reshape(-1, H, head_size)
    )
    num_rows = queries.shape[0]

    def allowed_of(task_row, live_row):
        return ((query_task[:, None] == task_row[None, :]) & (live_row[None, :] > 0))[None]

    def scores_of(key_block, allowed):
        raw_scores = jnp.einsum(
            "qhd,khd->hqk", queries, key_block, preferred_element_type=jnp.float32
        )
        return (
            raw_scores,
            jnp.where(allowed, score_coef[:, None, None] * raw_scores, masked_score),
        )

    def stats_step(state_in, block_data):
        row_top, row_sum = state_in
        key_block, value_block, task_row, live_row = block_data
        allowed = allowed_of(task_row, live_row)
        scores = scores_of(key_block, allowed)[1]
        new_top = jnp.maximum(row_top, jnp.max(scores, -1))
        shifted = jnp.where(allowed, jnp.exp(scores - new_top[..., None]), 0.0)
        return ((new_top, row_sum * jnp.exp(row_top - new_top) + jnp.sum(shifted, -1)), None)

    start_state = (
        jnp.full((H, num_rows), masked_score, jnp.float32),
        jnp.zeros((H, num_rows), jnp.float32),
    )
    (row_top, row_sum), unused = lax.scan(stats_step, start_state, key_blocks)

    def probs_of(scores, allowed):
        return jnp.where(allowed, jnp.exp(scores - row_top[..., None]), 0.0) / row_sum[..., None]

    def value_step(accum, block_data):
        key_block, value_block, task_row, live_row = block_data
        allowed = allowed_of(task_row, live_row)
        probs_low = probs_of(scores_of(key_block, allowed)[1], allowed).astype(jnp.bfloat16)
        return (
            accum
            + jnp.einsum(
                "hqk,khd->qhd", probs_low, value_block, preferred_element_type=jnp.float32
            ),
            None,
        )

    attn_sum, unused = lax.scan(
        value_step, jnp.zeros((num_rows, H, head_size), jnp.float32), key_blocks
    )
    attended = attn_sum.reshape(num_rows, D).astype(jnp.bfloat16)
    residual = hidden_in + jnp.dot(attended, out_low, preferred_element_type=jnp.float32)
    final_normed = (standard(residual)[0] * gain_out).astype(jnp.bfloat16)
    head_out = jnp.dot(final_normed, heads_low, preferred_element_type=jnp.float32)
    logits = head_out[:, :C]
    recon_err = head_out[:, C:] - query_feats
    label_mask = target_mask.astype(jnp.float32)
    feat_mask = feature_mask.astype(jnp.float32)
    onehot_class = jax.nn.one_hot(target_class, C, dtype=jnp.float32)
    picked = jnp.sum(logits * onehot_class, -1)
    sum_target, sum_recon, count_target, count_recon = lax.psum(
        (
            jnp.sum(label_mask * (jax.nn.logsumexp(logits, -1) - picked)),
            jnp.sum(feat_mask * recon_err**2),
            jnp.sum(label_mask),
            jnp.sum(feat_mask),
        ),
        "mem",
    )
    count_target = jnp.maximum(count_target, 1.0)
    count_recon = jnp.maximum(count_recon, 1.0)
    weight_a = anneal[0]
    loss_value = weight_a * sum_target / count_target + (1 - weight_a) * sum_recon / count_recon
    grad_logits = (
        weight_a / count_target * label_mask[:, None] * (jax.nn.softmax(logits, -1) - onehot_class)
    )
    grad_recon = (1 - weight_a) / count_recon * feat_mask * 2.0 * recon_err
    grad_head_out = jnp.concatenate([grad_logits, grad_recon], 1).astype(jnp.bfloat16)
    grad_heads = jnp.dot(final_normed.T, grad_head_out, preferred_element_type=jnp.float32)
    grad_final = jnp.dot(grad_head_out, heads_low.T, preferred_element_type=jnp.float32)
    grad_resid, grad_gain_out = norm_back(grad_final, residual, gain_out)
    grad_branch = grad_resid.astype(jnp.bfloat16)
    grad_wout = jnp.dot(attended.T, grad_branch, preferred_element_type=jnp.float32)
    grad_attn = (
        jnp.dot(grad_branch, out_low.T, preferred_element_type=jnp.float32)
        .astype(jnp.bfloat16)
        .reshape(num_rows, H, head_size)
    )
    row_delta = jnp.sum(
        grad_attn.astype(jnp.float32)
        * attended.reshape(num_rows, H, head_size).astype(jnp.float32),
        -1,
    ).T

    def back_step(state_in, block_data):
        key_block, value_block, task_row, live_row = block_data
        allowed = allowed_of(task_row, live_row)
        raw_scores, scores = scores_of(key_block, allowed)
        soft_probs = probs_of(scores, allowed)
        grad_probs = jnp.einsum(
            "qhd,khd->hqk", grad_attn, value_block, preferred_element_type=jnp.float32
        )
        grad_scores = (soft_probs * (grad_probs - row_delta[..., None])).astype(jnp.bfloat16)
        grad_beta = jnp.sum(grad_scores.astype(jnp.float32) * raw_scores, (1, 2))
        grad_query = jnp.einsum(
            "hqk,khd->qhd", grad_scores, key_block, preferred_element_type=jnp.float32
        )
        grad_key = (
            jnp.einsum("hqk,qhd->khd", grad_scores, queries, preferred_element_type=jnp.float32)
            * score_coef[None, :, None]
        )
        grad_value = jnp.einsum(
            "hqk,qhd->khd",
            soft_probs.astype(jnp.bfloat16),
            grad_attn,
            preferred_element_type=jnp.float32,
        )
        block_rows = key_block.shape[0]
        grad_kv = jnp.concatenate(
            [grad_key.reshape(block_rows, D), grad_value.reshape(block_rows, D)], 1
        )
        return ((state_in[0] + grad_query, state_in[1] + grad_beta), grad_kv)

    init_state = (jnp.zeros((num_rows, H, head_size), jnp.float32), jnp.zeros((H,), jnp.float32))
    (grad_q_sum, grad_beta_sum), kv_parts = lax.scan(back_step, init_state, key_blocks)
    kv_grad = lax.psum_scatter(
        kv_parts.reshape(memory_rows, 2 * D), "mem", scatter_dimension=0, tiled=True
    )
    grad_q_low = (grad_q_sum * score_coef[None, :, None]).reshape(num_rows, D).astype(jnp.bfloat16)
    grad_wq = jnp.dot(query_normed.T, grad_q_low, preferred_element_type=jnp.float32)
    grad_qn = jnp.dot(grad_q_low, qkv_low[:, :D].T, preferred_element_type=jnp.float32)
    grad_in_q, gain_in_q = norm_back(grad_qn, hidden_in, gain_in)
    grad_hidden = grad_resid + grad_in_q
    kv_upper, kv_lower = split_pair(kv_grad)
    grad_wkv = jnp.dot(mem_normed.T, kv_upper, preferred_element_type=jnp.float32) + jnp.dot(
        mem_normed.T, kv_lower, preferred_element_type=jnp.float32
    )
    grad_mn = jnp.dot(kv_upper, qkv_low[:, D:].T, preferred_element_type=jnp.float32) + jnp.dot(
        kv_lower, qkv_low[:, D:].T, preferred_element_type=jnp.float32
    )
    grad_mem, gain_in_m = norm_back(grad_mn, mem_hidden, gain_in)
    grad_table = jnp.einsum(
        "qf,qfe->fe", kept_input, grad_hidden.reshape(num_rows, F, -1), precision=high
    )
    grad_table = grad_table + jnp.einsum(
        "qf,qfe->fe", memory_feats, grad_mem.reshape(memory_feats.shape[0], F, -1), precision=high
    )
    grad_bias = jnp.sum(grad_hidden, 0) + jnp.sum(grad_mem, 0)
    small_size = full_small.shape[0]
    grad_small = jnp.concatenate(
        [
            grad_table.reshape(-1),
            grad_bias,
            gain_in_q + gain_in_m,
            grad_gain_out,
            grad_beta_sum * head_size ** (-0.5),
            jnp.zeros((small_size - 4 * D - H,), jnp.float32),
        ]
    )
    grad_qkv = jnp.concatenate([grad_wq, grad_wkv], 1).reshape(-1)
    shards = (
        lax.psum_scatter(grad_qkv, "mem", scatter_dimension=0, tiled=True),
        lax.psum_scatter(grad_wout.reshape(-1), "mem", scatter_dimension=0, tiled=True),
        lax.psum_scatter(grad_heads.reshape(-1), "mem", scatter_dimension=0, tiled=True),
        lax.psum_scatter(grad_small, "mem", scatter_dimension=0, tiled=True),
    )
    local_squares = sum((jnp.sum(piece_grad * piece_grad) for piece_grad in shards))
    grad_total = jnp.sqrt(lax.psum(local_squares, "mem"))
    factor = jnp.minimum(1.0, max_norm / (grad_total + 1e-06))
    step_num = float(STEP)
    weights_all = (w_qkv, w_out, w_heads, w_small)
    firsts = (m_qkv, m_out, m_heads, m_small)
    seconds = (v_qkv, v_out, v_heads, v_small)
    results = [
        adamw(weight, first_mom, second, grad_in, factor, step_num, step_rate)
        for weight, first_mom, second, grad_in, step_rate in zip(
            weights_all, firsts, seconds, shards, learn_rates
        )
    ]
    new_w = [entry[2] for entry in results]
    return (
        new_w[0],
        new_w[1],
        new_w[2],
        new_w[3],
        results[0][0],
        results[1][0],
        results[2][0],
        results[3][0],
        results[0][1],
        results[1][1],
        results[2][1],
        results[3][1],
        new_w[0].astype(jnp.bfloat16),
        new_w[1].astype(jnp.bfloat16),
        new_w[2].astype(jnp.bfloat16),
        new_w[3].astype(jnp.bfloat16),
        loss_value.reshape(1),
        grad_total.reshape(1),
    )


f32 = jnp.float32
bf16 = jnp.bfloat16
LOG2E = math.log2(math.e)
QB = 128
KC = 384
VROWS = 80
E_CAP = 16
SMALL_LANE = 88
COUNT_LANE = 122


def place_of(dev, planes):
    return (dev % 2) * (4 * planes) + ((dev // 2) % 4) * planes + dev // 8


def nt(a, b):
    return lax.dot_general(a, b, (((1,), (1,)), ((), ())), preferred_element_type=f32)


def tn(a, b):
    return lax.dot_general(a, b, (((0,), (0,)), ((), ())), preferred_element_type=f32)


def nn(a, b):
    return jnp.dot(a, b, preferred_element_type=f32)


def iota(shape, dim):
    return lax.broadcasted_iota(jnp.int32, shape, dim)


def split3(v):
    hi = v.astype(bf16).astype(f32)
    rest = v - hi
    mid = rest.astype(bf16).astype(f32)
    return hi, mid, rest - mid


def wide(v, lanes):
    return jnp.concatenate([v] * (lanes // v.shape[1]), axis=1) if lanes > v.shape[1] else v


def embed_t(kept, table, bias):
    parts = []
    for f in range(F):
        rows = slice(32 * f, 32 * f + 32)
        parts.append(kept[f : f + 1] * table[rows] + bias[rows])
    return jnp.concatenate(parts, axis=0)


def norm_t(v):
    centred = v - jnp.mean(v, axis=0, keepdims=True)
    inverse = lax.rsqrt(jnp.mean(centred * centred, axis=0, keepdims=True) + eps_norm)
    return centred * inverse, inverse


def norm_back_t(grad, normed, inverse, gain):
    scaled = grad * gain
    return inverse * (
        scaled
        - jnp.mean(scaled, axis=0, keepdims=True)
        - normed * jnp.mean(scaled * normed, axis=0, keepdims=True)
    )


def sizes(n, num_q, num_mem):
    q_blocks = (num_q + TASKS * (QB - 1)) // QB
    q_blocks += q_blocks % 2
    k_chunks = (num_mem + TASKS * (KC - 1)) // KC
    return q_blocks, k_chunks


def step_kernel(
    n, num_q, num_mem, small_size,
    qf, fm, qt, tc, tm, mt, mm, an, gw, gf,
    out_s, out_l,
    w_s, wt_s, wh_s, wht_s, kdup_s, vaug_w,
    cols, coefb,
    posq, posm, xs, fs, ct, f3_s, mfeat,
    kaug, vaug, kt_s, vt_s, mnt, gk, gv,
    qn_s, q_s, qhi, qlo, att, il_s, gres, fn_s, gho_s, gb_s, dap, dneg, dq_s, stat_q,
    ebuf, sbuf, ecur, acc, m_s,
    acc_gain, gqkv, gout, ghead,
    blk_c0, blk_nc, blk_tile, ch_base, ch_end,
):
    planes = n // 8
    rows_dev = D // n
    per_small = small_size // n
    q_blocks, k_chunks = sizes(n, num_q, num_mem)
    qs = q_blocks * QB

    pieces = [gw[place_of(d, planes)].astype(f32) for d in range(n)]
    for col in range(8):
        block = jnp.concatenate([piece[8 * col : 8 * col + 8] for piece in pieces], axis=0)
        w_s[:, 128 * col : 128 * col + 128] = block.astype(bf16)
        wt_s[128 * col : 128 * col + 128, :] = block.T.astype(bf16)
    lane = iota((8, 128), 1)
    tiles = [gf[8 * place_of(d, planes) : 8 * place_of(d, planes) + 8, :] for d in range(n)]
    lane_w = iota((D, 128), 1)
    heads = pltpu.roll(jnp.concatenate(tiles, axis=0), 64, 1)
    heads = jnp.where(lane_w < C + F, heads, 0.0)
    wh_s[...] = heads.astype(bf16)
    wht_s[...] = heads.T[:32].astype(bf16)
    feats = []
    for b in range(n // 2):
        feats.append(jnp.where(lane < 64, tiles[2 * b], pltpu.roll(tiles[2 * b + 1], 64, 1)))
    feats = jnp.concatenate(feats, axis=1)
    f3_s[...] = jnp.concatenate(list(split3(feats)) + [jnp.zeros_like(feats)], axis=0).astype(bf16)
    dup_r = iota((D, 4 * 128), 0)
    dup_l = iota((D, 4 * 128), 1)
    low6 = dup_l & 127
    dup = (dup_r == 64 * (dup_l >> 7) + (low6 & 63)).astype(f32).astype(bf16)
    once = ((dup_r == 64 * (dup_l >> 7) + low6) & (low6 < 64)).astype(f32).astype(bf16)
    kdup_s[...] = nn(w_s[:, D : 2 * D], dup).astype(bf16)
    vaug_w[...] = nn(w_s[:, 2 * D : 3 * D], once).astype(bf16)

    small_rows = gf[pl.ds(0, n, stride=8), :]
    lane_n = iota((n, 128), 1)
    count_t = jnp.maximum(jnp.sum(jnp.where(lane_n == COUNT_LANE, small_rows, 0.0)), 1.0)
    count_r = jnp.maximum(jnp.sum(jnp.where(lane_n == COUNT_LANE + 1, small_rows, 0.0)), 1.0)
    used = 4 * D + 2 * H
    s3 = jnp.concatenate(
        list(split3(small_rows)) + [jnp.zeros((128 - 3 * n, 128), f32)], axis=0
    ).astype(bf16)
    row = iota((used, 128), 0)
    lan = iota((used, 128), 1)
    slot = lan & (n - 1)
    core_of = slot // (4 * planes)
    dev_of = (slot % planes) * 8 + ((slot // planes) % 4) * 2 + core_of
    pick = (row >= per_small * dev_of) & (row < per_small * dev_of + per_small) & (lan < 3 * n)
    spread = nn(pick.astype(f32).astype(bf16), s3)
    row_dev = jnp.floor((row.astype(f32) + 0.5) * (1.0 / per_small)).astype(jnp.int32)
    here = (lan - SMALL_LANE) == (row - per_small * row_dev)
    column = jnp.sum(jnp.where(here, spread, 0.0), axis=1, keepdims=True)
    cols[...] = jnp.broadcast_to(column[: 4 * D], (4 * D, 128))
    for h in range(H):
        coefb[32 * h : 32 * h + 32, :] = jnp.broadcast_to(
            column[4 * D + h : 4 * D + h + 1] * (32 ** (-0.5)), (32, 128)
        )

    task_row = iota((8, 256), 0)
    marks = []
    for b in range(num_q // 256):
        marks.append((qt[:, 256 * b : 256 * b + 256] == task_row).astype(f32))
    for b in range(num_mem // 256):
        cut = slice(256 * b, 256 * b + 256)
        marks.append(((mt[:, cut] == task_row) & (mm[:, cut] > 0)).astype(f32))
    marks_all = jnp.concatenate(marks, axis=0)
    tri = (iota((256, 256), 0) < iota((256, 256), 1)).astype(f32).astype(bf16)
    ranks = nn(marks_all.astype(bf16), tri)
    totals = jnp.sum(marks_all, axis=1, keepdims=True)
    task_col = iota((8, 1), 0)

    def lay_out(first, count, unit):
        carry = jnp.zeros((8, 1), f32)
        before = []
        for b in range(count):
            before.append(carry)
            at = 8 * (first + b)
            carry = carry + totals[at : at + 8]
        base = jnp.int32(0)
        bases, counts, units = [], [], []
        base_vec = jnp.zeros((8, 1), f32)
        for t in range(TASKS):
            num = jnp.sum(jnp.where(task_col == t, carry, 0.0)).astype(jnp.int32)
            bases.append(base)
            counts.append(num)
            used_units = lax.div(num + (unit - 1), jnp.int32(unit))
            units.append(used_units)
            base_vec = base_vec + jnp.where(task_col == t, base.astype(f32), 0.0)
            base = base + used_units * unit
        places = []
        for b in range(count):
            at = 8 * (first + b)
            places.append(
                jnp.sum(
                    marks[first + b] * (base_vec + before[b] + ranks[at : at + 8]),
                    axis=0,
                    keepdims=True,
                )
                - (1.0 - jnp.sum(marks[first + b], axis=0, keepdims=True))
            )
        return jnp.concatenate(places, axis=1), bases, counts, units

    place_q, q_base, q_count, q_units = lay_out(0, num_q // 256, QB)
    place_m, m_base, m_count, m_units = lay_out(num_q // 256, num_mem // 256, KC)
    posq[...] = place_q
    posm[...] = place_m

    tile = jnp.int32(0)
    for t in range(TASKS):
        first_chunk = lax.div(m_base[t], jnp.int32(KC))
        first_block = lax.div(q_base[t], jnp.int32(QB))

        def fill_chunk(i, carry, t=t, first_chunk=first_chunk):
            ch_base[first_chunk + i] = m_base[t]
            ch_end[first_chunk + i] = m_base[t] + m_count[t]
            return carry

        lax.fori_loop(0, m_units[t], fill_chunk, 0)

        def fill_block(i, tile_in, t=t, first_chunk=first_chunk, first_block=first_block):
            blk_c0[first_block + i] = first_chunk
            blk_nc[first_block + i] = m_units[t]
            blk_tile[first_block + i] = tile_in
            return tile_in + m_units[t]

        tile = lax.fori_loop(0, q_units[t], fill_block, tile)
    num_blocks = q_units[0] + q_units[1] + q_units[2] + q_units[3]
    num_chunks = m_units[0] + m_units[1] + m_units[2] + m_units[3]

    xq = qf[...]
    fmq = fm[...].astype(f32)
    row8 = iota((8, num_q), 0)
    label_rows = jnp.where(
        row8 == 0, tc[...].astype(f32), jnp.where(row8 == 1, tm[...].astype(f32), 0.0)
    )
    q_rows = jnp.concatenate(
        list(split3(xq)) + [fmq, label_rows, jnp.zeros((8, num_q), f32)], axis=0
    ).astype(bf16)
    for b in range(qs // 256):
        chosen = (
            (place_q == (iota((256, 1), 0) + 256 * b).astype(f32)).astype(f32).astype(bf16)
        )
        got = nt(q_rows, chosen)
        cut = slice(256 * b, 256 * b + 256)
        xs[:, cut] = got[0:8] + got[8:16] + got[16:24]
        fs[:, cut] = got[24:32]
        ct[:, cut] = got[32:40]

    emb_w = lambda lanes: wide(cols[0:D, :], lanes)
    emb_b = lambda lanes: wide(cols[D : 2 * D, :], lanes)
    gain_in = lambda lanes: wide(cols[2 * D : 3 * D, :], lanes)
    gain_out = lambda lanes: wide(cols[3 * D : 4 * D, :], lanes)

    def mem_chunk(c, carry):
        at = pl.ds(pl.multiple_of(c * KC, KC), KC)
        base, end = ch_base[c], ch_end[c]
        s_col = iota((KC, 1), 0) + c * KC
        source = jnp.where(s_col < end, s_col, base).astype(f32)
        chosen = (posm[...] == source).astype(f32).astype(bf16)
        got = nt(f3_s[...], chosen)
        feats_c = got[0:8] + got[8:16] + got[16:24]
        mfeat[:, at] = feats_c
        hidden = embed_t(feats_c, emb_w(KC), emb_b(KC))
        normed, unused = norm_t(hidden)
        mn = (normed * gain_in(KC)).astype(bf16)
        mnt[:, at] = mn
        kt_s[:, at] = nn(wt_s[D : 2 * D, :], mn).astype(bf16)
        live_row = ((iota((1, KC), 1) + c * KC) < end).astype(f32)
        vt = nn(wt_s[2 * D : 3 * D, :], mn) * live_row
        tail = jnp.where(iota((16, KC), 0) == 0, live_row, 0.0)
        vt_s[:, at] = jnp.concatenate(
            [part for p in range(4) for part in (vt[64 * p : 64 * p + 64], tail)], axis=0
        ).astype(bf16)
        kaug[at, :] = tn(mn, kdup_s[...]).astype(bf16)
        live_col = (s_col < end).astype(f32)
        low = iota((KC, 512), 1) & 127
        vn = jnp.where((low == 64) | (low == 65), 1.0, tn(mn, vaug_w[...]))
        vaug[at, :] = (vn * live_col).astype(bf16)
        gk[at, :] = jnp.zeros((KC, D), f32)
        gv[at, :] = jnp.zeros((KC, D), f32)
        return carry

    lax.fori_loop(0, num_chunks, mem_chunk, 0)

    coef2 = wide(coefb[...], 256)

    def pre_block(j, carry):
        at = pl.ds(pl.multiple_of(j * 256, 256), 256)
        kept = xs[:, at] * (1.0 - fs[:, at])
        hidden = embed_t(kept, emb_w(256), emb_b(256))
        normed, unused = norm_t(hidden)
        qn = (normed * gain_in(256)).astype(bf16)
        qn_s[:, at] = qn
        q = nn(wt_s[0:D, :], qn).astype(bf16)
        q_s[:, at] = q
        scaled = q.astype(f32) * (coef2 * LOG2E)
        upper = scaled.astype(bf16)
        qhi[:, at] = upper
        qlo[:, at] = (scaled - upper.astype(f32)).astype(bf16)
        att[:, at] = jnp.zeros((D, 256), bf16)
        il_s[:, at] = jnp.zeros((H, 256), f32)
        dq_s[:, at] = jnp.zeros((D, 256), f32)
        return carry

    lax.fori_loop(0, qs // 256, pre_block, 0)

    zero_h = jnp.zeros((32, 128), bf16)

    def diagonal(ref, at, p):
        return [
            jnp.concatenate([ref[64 * p : 64 * p + 32, at], zero_h], axis=1),
            jnp.concatenate([zero_h, ref[64 * p + 32 : 64 * p + 64, at]], axis=1),
        ]

    def score_operand(at, p):
        return jnp.concatenate(diagonal(qhi, at, p) + diagonal(qlo, at, p), axis=0)

    def finish_forward(at, p, got):
        inverse = 1.0 / got[64:65, :]
        il_s[2 * p : 2 * p + 1, at] = inverse[:, :128]
        il_s[2 * p + 1 : 2 * p + 2, at] = inverse[:, 128:]
        att[64 * p : 64 * p + 32, at] = (got[0:32, :128] * inverse[:, :128]).astype(bf16)
        att[64 * p + 32 : 64 * p + 64, at] = (got[32:64, 128:] * inverse[:, 128:]).astype(bf16)

    def pair(p, width):
        return slice(width * p, width * p + width)

    def forward_block(i, carry):
        at = pl.ds(pl.multiple_of(i * QB, QB), QB)
        c0, nc, tile0 = blk_c0[i], blk_nc[i], blk_tile[i]

        @pl.when(nc == 1)
        def one():
            keys = pl.ds(pl.multiple_of(c0 * KC, KC), KC)
            keep = jnp.minimum(tile0, E_CAP)
            for p in range(4):
                s = nn(kaug[keys, pair(p, 128)], score_operand(at, p))
                top = jnp.max(s, axis=0, keepdims=True)
                m_s[i, :, pair(p, 256)] = top
                e = jnp.exp2(s - top).astype(bf16)
                ebuf[keep, :, pair(p, 256)] = e
                finish_forward(at, p, nn(vt_s[pair(p, VROWS), keys], e))

        @pl.when(nc > 1)
        def many():
            m_s[i] = jnp.full((1, 1024), -3e38, f32)
            acc[...] = jnp.zeros_like(acc)

            def tops(c, inner):
                keys = pl.ds(pl.multiple_of((c0 + c) * KC, KC), KC)
                for p in range(4):
                    s = nn(kaug[keys, pair(p, 128)], score_operand(at, p))
                    m_s[i, :, pair(p, 256)] = jnp.maximum(
                        m_s[i, :, pair(p, 256)], jnp.max(s, axis=0, keepdims=True)
                    )
                return inner

            lax.fori_loop(0, nc, tops, 0)

            def sums(c, inner):
                keys = pl.ds(pl.multiple_of((c0 + c) * KC, KC), KC)
                keep = jnp.minimum(tile0 + c, E_CAP)
                for p in range(4):
                    s = nn(kaug[keys, pair(p, 128)], score_operand(at, p))
                    e = jnp.exp2(s - m_s[i, :, pair(p, 256)]).astype(bf16)
                    ebuf[keep, :, pair(p, 256)] = e
                    acc[pair(p, VROWS), :] += nn(vt_s[pair(p, VROWS), keys], e)
                return inner

            lax.fori_loop(0, nc, sums, 0)
            for p in range(4):
                finish_forward(at, p, acc[pair(p, VROWS), :])

        return carry

    lax.fori_loop(0, num_blocks, forward_block, 0)

    weight_a = an[0]
    scale_t = weight_a / count_t
    scale_r = (1.0 - weight_a) / count_r
    acc_gain[...] = jnp.zeros_like(acc_gain)
    out_l[...] = jnp.zeros_like(out_l)

    def fold(v):
        return v[:, :128] + v[:, 128:256]

    def mid_block(j, carry):
        at = pl.ds(pl.multiple_of(j * 256, 256), 256)
        x = xs[:, at]
        fmask = fs[:, at]
        kept = x * (1.0 - fmask)
        hidden = embed_t(kept, emb_w(256), emb_b(256))
        attended = att[:, at]
        residual = hidden + nn(wt_s[3 * D : 4 * D, :], attended)
        normed, inverse = norm_t(residual)
        fn = (normed * gain_out(256)).astype(bf16)
        fn_s[:, at] = fn
        head = nn(wht_s[...], fn)
        logits = head[0:C]
        err = head[C : C + F] - x
        label = ct[1:2, at]
        hot = (iota((C, 256), 0).astype(f32) == ct[0:1, at]).astype(f32)
        top = jnp.max(logits, axis=0, keepdims=True)
        e = jnp.exp(logits - top)
        total = jnp.sum(e, axis=0, keepdims=True)
        picked = jnp.sum(logits * hot, axis=0, keepdims=True)
        out_l[0:1, :] += fold(
            scale_t * label * (jnp.log(total) + top - picked)
            + scale_r * jnp.sum(fmask * err * err, axis=0, keepdims=True)
        )
        g_log = scale_t * label * (e / total - hot)
        g_rec = scale_r * fmask * 2.0 * err
        gho = jnp.concatenate([g_log, g_rec, jnp.zeros((8, 256), f32)], axis=0).astype(bf16)
        gho_s[:, at] = gho
        g_final = nn(wh_s[:, :32], gho)
        acc_gain[D : 2 * D, :] += fold(g_final * normed)
        g_res = norm_back_t(g_final, normed, inverse, gain_out(256))
        gres[:, at] = g_res
        gb = g_res.astype(bf16)
        gb_s[:, at] = gb
        ga = nn(w_s[:, 3 * D : 4 * D], gb).astype(bf16).astype(f32)
        attf = attended.astype(f32)
        for h in range(H):
            rows = slice(32 * h, 32 * h + 32)
            da = (ga[rows] * il_s[h : h + 1, at]).astype(bf16)
            dap[rows, at] = da
            dneg[h : h + 1, at] = -jnp.sum(da.astype(f32) * attf[rows], axis=0, keepdims=True)
        return carry

    lax.fori_loop(0, qs // 256, mid_block, 0)

    zero_p = jnp.zeros((64, 256), bf16)

    def backward_chunk(at, c, e_of):
        keys = pl.ds(pl.multiple_of(c * KC, KC), KC)
        dks, dvs, dqs = [], [], []
        ds_all, e_all, qd_all, da_all = [], [], [], []
        for p in range(4):
            e = e_of(p)
            da = jnp.concatenate(diagonal(dap, at, p), axis=0)
            qd = jnp.concatenate(diagonal(q_s, at, p), axis=0)
            neg = jnp.concatenate(
                [dneg[2 * p : 2 * p + 1, at], dneg[2 * p + 1 : 2 * p + 2, at]], axis=1
            )
            neg_hi = neg.astype(bf16).astype(f32)
            r16 = iota((16, 256), 0)
            tail = jnp.where(r16 == 0, neg_hi, jnp.where(r16 == 1, neg - neg_hi, 0.0)).astype(bf16)
            operand = jnp.concatenate([da, tail, jnp.zeros((48, 256), bf16)], axis=0)
            dp = nn(vaug[keys, pair(p, 128)], operand)
            ds = (e.astype(f32) * dp).astype(bf16)
            dq = nn(kt_s[64 * p : 64 * p + 64, keys], ds)
            dq_s[64 * p : 64 * p + 32, at] += dq[0:32, :128]
            dq_s[64 * p + 32 : 64 * p + 64, at] += dq[32:64, 128:]
            order = (lambda v: [v, zero_p]) if p % 2 == 0 else (lambda v: [zero_p, v])
            dvs.append(nt(e, jnp.concatenate(order(da), axis=0)))
            dks.append(nt(ds, jnp.concatenate(order(qd), axis=0)))
        for half in range(2):
            lanes = slice(128 * half, 128 * half + 128)
            gk[keys, lanes] += dks[2 * half] + dks[2 * half + 1]
            gv[keys, lanes] += dvs[2 * half] + dvs[2 * half + 1]

    def backward_block(i, carry):
        at = pl.ds(pl.multiple_of(i * QB, QB), QB)
        c0, nc, tile0 = blk_c0[i], blk_nc[i], blk_tile[i]
        simple = (nc == 1) & (tile0 < E_CAP)

        @pl.when(simple)
        def one():
            backward_chunk(at, c0, lambda p: ebuf[tile0, :, pair(p, 256)])

        @pl.when(jnp.logical_not(simple))
        def many():
            def one_chunk(c, inner):
                @pl.when(tile0 + c < E_CAP)
                def kept():
                    ecur[...] = ebuf[tile0 + c]

                @pl.when(tile0 + c >= E_CAP)
                def again():
                    keys = pl.ds(pl.multiple_of((c0 + c) * KC, KC), KC)
                    for p in range(4):
                        s = nn(kaug[keys, pair(p, 128)], score_operand(at, p))
                        ecur[:, pair(p, 256)] = jnp.exp2(
                            s - m_s[i, :, pair(p, 256)]
                        ).astype(bf16)

                backward_chunk(at, c0 + c, lambda p: ecur[:, pair(p, 256)])
                return inner

            lax.fori_loop(0, nc, one_chunk, 0)

        return carry

    lax.fori_loop(0, num_blocks, backward_block, 0)

    def sum_in(grad, normed, kept, lanes):
        by_feature = jnp.concatenate(
            [kept[f : f + 1] * grad[32 * f : 32 * f + 32] for f in range(F)], axis=0
        )
        outs = []
        for v in (by_feature, grad):
            total = v[:, :128]
            for k in range(1, lanes // 128):
                total = total + v[:, 128 * k : 128 * k + 128]
            outs.append(total)
        return outs

    def post_block(j, carry):
        at = pl.ds(pl.multiple_of(j * 256, 256), 256)
        kept = xs[:, at] * (1.0 - fs[:, at])
        hidden = embed_t(kept, emb_w(256), emb_b(256))
        normed, inverse = norm_t(hidden)
        dq = dq_s[:, at]
        gq = (dq * coef2).astype(bf16)
        prod = fold(dq * q_s[:, at].astype(f32))
        for h in range(H):
            acc_gain[4 * D + h : 4 * D + h + 1, :] += jnp.sum(
                prod[32 * h : 32 * h + 32], axis=0, keepdims=True
            )
        gqkv[:, 0:D] += nt(qn_s[:, at], gq)
        gqn = nn(w_s[:, 0:D], gq)
        acc_gain[0:D, :] += fold(gqn * normed)
        gh = gres[:, at] + norm_back_t(gqn, normed, inverse, gain_in(256))
        by_f, plain = sum_in(gh, normed, kept, 256)
        acc_gain[2 * D : 3 * D, :] += by_f
        acc_gain[3 * D : 4 * D, :] += plain
        return carry

    gqkv[...] = jnp.zeros_like(gqkv)
    lax.fori_loop(0, qs // 256, post_block, 0)
    gout[...] = nt(att[...], gb_s[...])
    ghead[...] = nt(fn_s[...], gho_s[...])

    def mem_back(c, carry):
        at = pl.ds(pl.multiple_of(c * KC, KC), KC)
        live = ((iota((KC, 1), 0) + c * KC) < ch_end[c]).astype(f32)
        coef_lane = carry
        gk_c = (gk[at, :] * coef_lane * live).astype(bf16)
        gv_c = (gv[at, :] * live).astype(bf16)
        mn = mnt[:, at]
        gqkv[:, D : 2 * D] += nn(mn, gk_c)
        gqkv[:, 2 * D : 3 * D] += nn(mn, gv_c)
        gmn = nt(w_s[:, D : 2 * D], gk_c) + nt(w_s[:, 2 * D : 3 * D], gv_c)
        feats_c = mfeat[:, at]
        hidden = embed_t(feats_c, emb_w(KC), emb_b(KC))
        normed, inverse = norm_t(hidden)
        dgain = gmn * normed
        acc_gain[0:D, :] += dgain[:, :128] + dgain[:, 128:256] + dgain[:, 256:384]
        gm = norm_back_t(gmn, normed, inverse, gain_in(KC))
        by_f, plain = sum_in(gm, normed, feats_c, KC)
        acc_gain[2 * D : 3 * D, :] += by_f
        acc_gain[3 * D : 4 * D, :] += plain
        return carry

    coef_lane = jnp.concatenate([coefb[0:128, :].T[0:1], coefb[128:256, :].T[0:1]], axis=1)
    lax.fori_loop(0, num_chunks, mem_back, coef_lane)

    sums = jnp.sum(acc_gain[...], axis=1, keepdims=True)
    small = jnp.concatenate(
        [
            sums[2 * D : 3 * D],
            sums[3 * D : 4 * D],
            sums[0:D],
            sums[D : 2 * D],
            sums[4 * D : 4 * D + H] * (32 ** (-0.5)),
            jnp.zeros((H, 1), f32),
        ],
        axis=0,
    )
    placed = jnp.where(lan == (row - per_small * row_dev), small, 0.0).astype(bf16)
    r_dev = iota((n, used), 0)
    r_row = iota((n, used), 1)
    mine = (r_row >= per_small * r_dev) & (r_row < per_small * r_dev + per_small)
    small_rows_out = nn(mine.astype(f32).astype(bf16), placed)
    to_flat_r = iota((32, 256), 0)
    to_flat_l = iota((32, 256), 1)
    lane_row = jnp.floor((to_flat_l.astype(f32) + 0.5) * (1.0 / (C + F))).astype(jnp.int32)
    to_flat = ((to_flat_l - (C + F) * lane_row == to_flat_r) & (to_flat_r < C + F)).astype(f32)
    spread_h = nn(ghead[...].astype(bf16), to_flat.astype(bf16))
    lr = iota((D, 256), 1)
    lr_row = jnp.floor((lr.astype(f32) + 0.5) * (1.0 / (C + F))).astype(jnp.int32)
    spread_h = jnp.where(lr_row == (iota((D, 256), 0) & (rows_dev - 1)), spread_h, 0.0)
    r8 = iota((8, 128), 0)
    for d in range(n):
        rows = slice(rows_dev * d, rows_dev * d + rows_dev)
        head_flat = jnp.sum(spread_h[rows], axis=0, keepdims=True)
        extra = jnp.where(
            r8 == 0,
            head_flat[:, :128],
            jnp.where(r8 == 1, head_flat[:, 128:], jnp.where(r8 == 2, small_rows_out[d : d + 1], 0.0)),
        )
        block = [gqkv[rows, 128 * k : 128 * k + 128] for k in range(6)]
        block += [gout[rows, 128 * k : 128 * k + 128] for k in range(2)]
        block += [extra, jnp.zeros((8, 128), f32)]
        out_s[place_of(d, planes)] = jnp.concatenate(block, axis=0).astype(bf16)


def step_call(n, small_size, qf, fm, qt, tc, tm, mt, mm, an, gw, gf):
    num_q, num_mem = qf.shape[1], mt.shape[1]
    q_blocks, k_chunks = sizes(n, num_q, num_mem)
    qs, ks = q_blocks * QB, k_chunks * KC
    V = pltpu.VMEM
    S = pltpu.SMEM
    vm = pl.BlockSpec(memory_space=pltpu.VMEM)
    scratch = [
        V((D, 4 * D), bf16), V((4 * D, D), bf16), V((D, 128), bf16), V((32, D), bf16),
        V((D, 512), bf16), V((D, 512), bf16),
        V((4 * D, 128), f32), V((D, 128), f32),
        V((1, num_q), f32), V((1, num_mem), f32), V((8, qs), f32), V((8, qs), f32), V((8, qs), f32),
        V((32, num_mem), bf16), V((8, ks), f32),
        V((ks, 512), bf16), V((ks, 512), bf16), V((D, ks), bf16), V((4 * VROWS, ks), bf16),
        V((D, ks), bf16), V((ks, D), f32), V((ks, D), f32),
        V((D, qs), bf16), V((D, qs), bf16), V((D, qs), bf16), V((D, qs), bf16), V((D, qs), bf16),
        V((H, qs), f32), V((D, qs), f32), V((D, qs), bf16), V((32, qs), bf16), V((D, qs), bf16),
        V((D, qs), bf16), V((H, qs), f32), V((D, qs), f32), V((8, qs), f32),
        V((E_CAP + 1, KC, 1024), bf16), V((8, 128), f32), V((KC, 1024), bf16),
        V((4 * VROWS, 256), f32), V((q_blocks, 1, 1024), f32),
        V((4 * D + H, 128), f32), V((D, 3 * D), f32), V((D, D), f32), V((D, 32), f32),
        S((q_blocks,), jnp.int32), S((q_blocks,), jnp.int32), S((q_blocks,), jnp.int32),
        S((k_chunks,), jnp.int32), S((k_chunks,), jnp.int32),
    ]
    return pl.pallas_call(
        functools.partial(step_kernel, n, num_q, num_mem, small_size),
        out_shape=(
            jax.ShapeDtypeStruct((n, 80, 128), bf16),
            jax.ShapeDtypeStruct((8, 128), f32),
        ),
        in_specs=[vm] * 7 + [pl.BlockSpec(memory_space=pltpu.SMEM)] + [vm] * 2,
        out_specs=(vm, vm),
        scratch_shapes=scratch,
        compiler_params=pltpu.CompilerParams(vmem_limit_bytes=58 * 1024 * 1024),
    )(qf, fm, qt, tc, tm, mt, mm, an, gw, gf)


MESH = pl.DeviceIdType.MESH


def greet(targets):
    barrier = pltpu.get_barrier_semaphore()
    for target in targets:
        pl.semaphore_signal(barrier, inc=1, device_id=(target,), device_id_type=MESH)
    return barrier


def send(src, dst, send_sem, recv_sem, target):
    copy = pltpu.make_async_remote_copy(
        src_ref=src,
        dst_ref=dst,
        send_sem=send_sem,
        recv_sem=recv_sem,
        device_id=(target,),
        device_id_type=MESH,
    )
    copy.start()
    return copy


def where_am_i(planes):
    me = lax.axis_index("mem")
    core = lax.rem(me, 2)
    square = lax.rem(lax.div(me, 2), 4)
    plane = lax.div(me, 8)
    return me, core, square, plane


def gather_kernel(
    n, w_qkv, w_out, w_heads, w_small, mfeat, fm, tm, gw, gf,
    send_z, recv_z, send_s, recv_s, send_c, recv_c,
):
    planes = n // 8
    me, core, square, plane = where_am_i(planes)
    in_plane = core + 2 * square
    z_of = [lax.rem(plane + k, planes) * 8 + in_plane for k in range(1, planes)]
    s_of = [plane * 8 + lax.rem(square + k, 4) * 2 + core for k in range(1, 4)]
    c_of = plane * 8 + square * 2 + (1 - core)
    barrier = greet(z_of + s_of + [c_of])

    place = core * (4 * planes) + square * planes + plane
    rows = []
    for c in range(6):
        rows.append(w_qkv[pl.ds(c, 8, stride=6), :])
    for c in range(2):
        rows.append(w_out[pl.ds(c, 8, stride=2), :])
    gw[place] = jnp.concatenate(rows, axis=0).astype(bf16)
    per_head = w_heads.shape[1]
    lane = iota((8, 256), 1)
    head_row = jnp.concatenate([w_heads[...], jnp.zeros((1, 256 - per_head), f32)], axis=1)
    owner = jnp.floor((lane.astype(f32) + 0.5) * (1.0 / (C + F))).astype(jnp.int32)
    kept_heads = jnp.where(owner == iota((8, 256), 0), head_row, 0.0).astype(bf16)
    fold_r = iota((256, 128), 0)
    fold_row = jnp.floor((fold_r.astype(f32) + 0.5) * (1.0 / (C + F))).astype(jnp.int32)
    fold_m = (fold_r - (C + F) * fold_row == iota((256, 128), 1) - 64).astype(f32).astype(bf16)
    heads = nn(kept_heads, fold_m)
    per_small = w_small.shape[1]
    small = jnp.concatenate([w_small[...], jnp.zeros((1, 128 - per_small), f32)], axis=1)
    small = pltpu.roll(jnp.broadcast_to(small, (8, 128)), SMALL_LANE, 1)
    feats = jnp.concatenate([mfeat[...], jnp.zeros((8, 64), f32)], axis=1)
    lane8 = iota((8, 128), 1)
    row8 = iota((8, 128), 0)
    num_t = jnp.sum(tm[...].astype(f32), axis=1, keepdims=True)
    num_r = jnp.sum(jnp.sum(fm[...].astype(f32), axis=0, keepdims=True), axis=1, keepdims=True)
    block = feats + heads
    first = (row8 == 0) & (lane8 >= SMALL_LANE) & (lane8 < SMALL_LANE + per_small)
    block = jnp.where(first, small, block)
    block = jnp.where((row8 == 0) & (lane8 == COUNT_LANE), num_t, block)
    block = jnp.where((row8 == 0) & (lane8 == COUNT_LANE + 1), num_r, block)
    gf[place] = block

    pl.semaphore_wait(barrier, planes - 1 + 4)
    copies = []
    for k in range(planes - 1):
        for i, ref in enumerate((gf, gw)):
            copies.append(
                send(ref.at[place], ref.at[place], send_z.at[i, k], recv_z.at[i, k], z_of[k])
            )
    for copy in copies:
        copy.wait_recv()
    done = list(copies)
    line = pl.ds(core * (4 * planes) + square * planes, planes)
    copies = []
    for k in range(3):
        for i, ref in enumerate((gf, gw)):
            copies.append(
                send(ref.at[line], ref.at[line], send_s.at[i, k], recv_s.at[i, k], s_of[k])
            )
    for copy in copies:
        copy.wait_recv()
    done += copies
    half = pl.ds(core * (4 * planes), 4 * planes)
    copies = []
    for i, ref in enumerate((gf, gw)):
        copies.append(send(ref.at[half], ref.at[half], send_c.at[i], recv_c.at[i], c_of))
    for copy in copies:
        copy.wait_recv()
    done += copies
    for copy in done:
        copy.wait_send()


def gather_call(n, w_qkv, w_out, w_heads, w_small, mfeat, fm, tm):
    planes = n // 8
    vm = pl.BlockSpec(memory_space=pltpu.VMEM)
    dma = pltpu.SemaphoreType.DMA
    return pl.pallas_call(
        functools.partial(gather_kernel, n),
        out_shape=(
            jax.ShapeDtypeStruct((n, 64, 128), bf16),
            jax.ShapeDtypeStruct((n, 8, 128), f32),
        ),
        in_specs=[vm] * 7,
        out_specs=(vm, vm),
        scratch_shapes=[
            dma((2, planes - 1)), dma((2, planes - 1)), dma((2, 3)), dma((2, 3)), dma((2,)), dma((2,)),
        ],
        compiler_params=pltpu.CompilerParams(collective_id=0, has_side_effects=True),
    )(w_qkv, w_out, w_heads, w_small, mfeat, fm, tm)


def reduce_kernel(
    n, s_in, l_in, g_out, t_out,
    r_core, r_square, r_plane, t_square, t_plane, own, n_mine, n_square, n_sum, n_plane,
    send_c, recv_c, send_s, recv_s, send_z, recv_z, send_n, recv_n, send_m, recv_m,
):
    planes = n // 8
    me, core, square, plane = where_am_i(planes)
    in_plane = core + 2 * square
    p_of = [plane * 8 + lax.rem(in_plane + k, 8) for k in range(1, 8)]
    z_of = [lax.rem(plane + k, planes) * 8 + in_plane for k in range(1, planes)]
    s_of = [plane * 8 + lax.rem(square + k, 4) * 2 + core for k in range(1, 4)]
    c_of = plane * 8 + square * 2 + (1 - core)
    barrier = greet(p_of + z_of)
    pl.semaphore_wait(barrier, planes - 1 + 7)

    lines = 4 * planes
    done = []
    copy = send(s_in.at[pl.ds((1 - core) * lines, lines)], r_core, send_c, recv_c, c_of)
    done.append(copy)
    copy.wait_recv()
    copies = []
    for k in range(1, 4):
        line = lax.rem(square + k, 4) * planes
        for z in range(planes):
            t_square[k - 1, z] = (
                s_in[core * lines + line + z].astype(f32) + r_core[line + z].astype(f32)
            ).astype(bf16)
        copies.append(
            send(t_square.at[k - 1], r_square.at[k - 1], send_s.at[k - 1], recv_s.at[k - 1], s_of[k - 1])
        )
    line = square * planes
    for z in range(planes):
        own[z] = s_in[core * lines + line + z].astype(f32) + r_core[line + z].astype(f32)
    for copy in copies:
        copy.wait_recv()
    done += copies
    copies = []
    for k in range(1, planes):
        z = lax.rem(plane + k, planes)
        total = own[z]
        for j in range(3):
            total = total + r_square[j, z].astype(f32)
        t_plane[k - 1] = total.astype(bf16)
        copies.append(
            send(t_plane.at[k - 1], r_plane.at[k - 1], send_z.at[k - 1], recv_z.at[k - 1], z_of[k - 1])
        )
    total = own[plane]
    for j in range(3):
        total = total + r_square[j, plane].astype(f32)
    for copy in copies:
        copy.wait_recv()
    done += copies
    for k in range(planes - 1):
        total = total + r_plane[k].astype(f32)
    g_out[...] = total
    squares = jnp.sum(total * total, axis=0, keepdims=True)
    row8 = iota((8, 128), 0)
    n_mine[...] = jnp.where(row8 == 0, squares, jnp.where(row8 == 1, l_in[0:1, :], 0.0))
    copies = []
    for k in range(7):
        copies.append(send(n_mine, n_square.at[k], send_n.at[k], recv_n.at[k], p_of[k]))
    for copy in copies:
        copy.wait_recv()
    done += copies
    total = n_mine[...]
    for k in range(7):
        total = total + n_square[k]
    n_sum[...] = total
    copies = []
    for k in range(planes - 1):
        copies.append(send(n_sum, n_plane.at[k], send_m.at[k], recv_m.at[k], z_of[k]))
    for copy in copies:
        copy.wait_recv()
    done += copies
    parts = jnp.zeros((8, 128), f32)
    total = n_sum[...]
    for k in range(planes - 1):
        total = total + n_plane[k]
    t_out[...] = total
    for copy in done:
        copy.wait_send()


def reduce_call(n, s_in, l_in):
    planes = n // 8
    rows = s_in.shape[1]
    vm = pl.BlockSpec(memory_space=pltpu.VMEM)
    dma = pltpu.SemaphoreType.DMA
    V = pltpu.VMEM
    z = planes - 1
    return pl.pallas_call(
        functools.partial(reduce_kernel, n),
        out_shape=(
            jax.ShapeDtypeStruct((rows, 128), f32),
            jax.ShapeDtypeStruct((8, 128), f32),
        ),
        in_specs=[vm] * 2,
        out_specs=(vm, vm),
        scratch_shapes=[
            V((4 * planes, rows, 128), bf16), V((3, planes, rows, 128), bf16), V((z, rows, 128), bf16),
            V((3, planes, rows, 128), bf16), V((z, rows, 128), bf16), V((planes, rows, 128), f32),
            V((8, 128), f32), V((7, 8, 128), f32), V((8, 128), f32), V((z, 8, 128), f32),
            dma, dma, dma((3,)), dma((3,)), dma((z,)), dma((z,)), dma((7,)), dma((7,)), dma((z,)), dma((z,)),
        ],
        compiler_params=pltpu.CompilerParams(collective_id=1, has_side_effects=True),
    )(s_in, l_in)


def update_kernel(g, tot, *refs):
    weights, firsts, seconds = refs[0:4], refs[4:8], refs[8:12]
    new, first_o, second_o, copy_o = refs[12:16], refs[16:20], refs[20:24], refs[24:28]
    loss_o, norm_o, gq_s, go_s = refs[28:32]
    for c in range(6):
        gq_s[pl.ds(c, 8, stride=6), :] = g[8 * c : 8 * c + 8, :]
    for c in range(2):
        go_s[pl.ds(c, 8, stride=2), :] = g[48 + 8 * c : 56 + 8 * c, :]
    norm = jnp.sqrt(jnp.sum(tot[0:1, :], axis=1, keepdims=True))
    loss_o[...] = jnp.sum(tot[1:2, :], axis=1, keepdims=True)
    norm_o[...] = norm
    factor = jnp.minimum(1.0, max_norm / (norm + 1e-06))
    per_head, per_small = weights[2].shape[1], weights[3].shape[1]
    grads = (
        gq_s[...],
        go_s[...],
        jnp.concatenate([g[64:65, :], g[65:66, : per_head - 128]], axis=1),
        g[66:67, :per_small],
    )
    for i in range(4):
        first_new, second_new, weight_new = adamw(
            weights[i][...], firsts[i][...], seconds[i][...], grads[i], factor, float(STEP), learn_rates[i]
        )
        new[i][...] = weight_new
        first_o[i][...] = first_new
        second_o[i][...] = second_new
        copy_o[i][...] = weight_new.astype(bf16)


def update_call(g, tot, weights, firsts, seconds):
    vm = pl.BlockSpec(memory_space=pltpu.VMEM)
    shapes = [w.shape for w in weights]
    outs = [jax.ShapeDtypeStruct(s, f32) for s in shapes] * 3
    outs += [jax.ShapeDtypeStruct(s, bf16) for s in shapes]
    outs += [jax.ShapeDtypeStruct((1, 1), f32)] * 2
    return pl.pallas_call(
        update_kernel,
        out_shape=tuple(outs),
        in_specs=[vm] * 14,
        out_specs=(vm,) * 18,
        scratch_shapes=[pltpu.VMEM((48, 128), f32), pltpu.VMEM((16, 128), f32)],
    )(g, tot, *weights, *firsts, *seconds)


def local_fast(
    n, query_feats, feature_mask, query_task, target_class, target_mask, memory_feats, memory_task,
    memory_mask, anneal, w_qkv, w_out, w_heads, w_small, m_qkv, m_out, m_heads, m_small,
    v_qkv, v_out, v_heads, v_small,
):
    def row(v):
        return v.reshape(1, -1)

    def tiles(v):
        return v.reshape(-1, 128)

    fm = feature_mask.T
    tm = row(target_mask)
    weights = (tiles(w_qkv), tiles(w_out), row(w_heads), row(w_small))
    firsts = (tiles(m_qkv), tiles(m_out), row(m_heads), row(m_small))
    seconds = (tiles(v_qkv), tiles(v_out), row(v_heads), row(v_small))
    gw, gf = gather_call(n, *weights, memory_feats.T, fm, tm)
    pieces, losses = step_call(
        n, w_small.shape[0] * n, query_feats.T, fm, row(query_task), row(target_class), tm,
        row(memory_task), row(memory_mask), anneal, gw, gf.reshape(n * 8, 128),
    )
    grads, totals = reduce_call(n, pieces, losses)
    outs = update_call(grads, totals, weights, firsts, seconds)
    return tuple(out.reshape(-1) for out in outs)


def solution(mesh):
    placed = (
        P("mem", None),
        P("mem", None),
        P("mem"),
        P("mem"),
        P("mem"),
        P("mem", None),
        P(),
        P(),
        P(),
        P("mem"),
        P("mem"),
        P("mem"),
        P("mem"),
        P("mem"),
        P("mem"),
        P("mem"),
        P("mem"),
        P("mem"),
        P("mem"),
        P("mem"),
        P("mem"),
    )
    n = mesh.shape["mem"]

    def choose(*args):
        if D // n == 8 and args[6].shape[0] <= 4096:
            return local_fast(n, *args)
        return local(*args)

    return jax.shard_map(
        choose,
        mesh=mesh,
        in_specs=placed,
        out_specs=(
            P("mem"),
            P("mem"),
            P("mem"),
            P("mem"),
            P("mem"),
            P("mem"),
            P("mem"),
            P("mem"),
            P("mem"),
            P("mem"),
            P("mem"),
            P("mem"),
            P("mem"),
            P("mem"),
            P("mem"),
            P("mem"),
            P(),
            P(),
        ),
        check_vma=False,
    )
```

```python
import functools
import math

import jax
import jax.numpy as jnp
from jax import lax
from jax.experimental import pallas as pl
from jax.experimental.pallas import tpu as pltpu
from jax.sharding import PartitionSpec as P

F = 8
D = 256
H = 8
C = 16
TASKS = 4
STEP = 10


eps_norm = 1e-05
max_norm = 0.05
beta_one = 0.9
beta_two = 0.999
adam_eps = 1e-08
decay_rate = 0.01
learn_rates = (0.05, 1.0, 0.05, 0.5)
masked_score = -1e30


def embed(feature_rows, table_flat, emb_bias):
    emb_table = table_flat.reshape(feature_rows.shape[1], -1)
    return (feature_rows[:, :, None] * emb_table[None]).reshape(
        feature_rows.shape[0], -1
    ) + emb_bias


def standard(hidden):
    centred = hidden - jnp.mean(hidden, -1, keepdims=True)
    inverse = lax.rsqrt(jnp.mean(centred * centred, -1, keepdims=True) + eps_norm)
    return (centred * inverse, inverse)


def norm_back(grad_out, hidden, gain_vec):
    normed, inverse = standard(hidden)
    grad_gain = jnp.sum(grad_out * normed, 0)
    grad_scaled = grad_out * gain_vec
    grad_hidden = inverse * (
        grad_scaled
        - jnp.mean(grad_scaled, -1, keepdims=True)
        - normed * jnp.mean(grad_scaled * normed, -1, keepdims=True)
    )
    return (grad_hidden, grad_gain)


def split_pair(values):
    upper = values.astype(jnp.bfloat16)
    lower = (values - upper.astype(jnp.float32)).astype(jnp.bfloat16)
    return (upper, lower)


def adamw(weight, first_mom, second, grad_in, factor, step_num, step_rate):
    clipped = grad_in * factor
    first_new = beta_one * first_mom + (1 - beta_one) * clipped
    second_new = beta_two * second + (1 - beta_two) * clipped * clipped
    fix_one = 1 - beta_one**step_num
    fix_two = 1 - beta_two**step_num
    weight_new = weight - step_rate * (
        first_new / fix_one / (jnp.sqrt(second_new / fix_two) + adam_eps) + decay_rate * weight
    )
    return (first_new, second_new, weight_new)


def local(
    query_feats,
    feature_mask,
    query_task,
    target_class,
    target_mask,
    memory_feats,
    memory_task,
    memory_mask,
    anneal,
    w_qkv,
    w_out,
    w_heads,
    w_small,
    m_qkv,
    m_out,
    m_heads,
    m_small,
    v_qkv,
    v_out,
    v_heads,
    v_small,
):
    high = lax.Precision.HIGHEST
    head_size = D // H
    full_qkv, full_out, full_heads, full_small = (
        lax.all_gather(w_qkv, "mem", axis=0, tiled=True),
        lax.all_gather(w_out, "mem", axis=0, tiled=True),
        lax.all_gather(w_heads, "mem", axis=0, tiled=True),
        lax.all_gather(w_small, "mem", axis=0, tiled=True),
    )
    emb_table = full_small[:D]
    emb_bias = full_small[D : 2 * D]
    gain_in = full_small[2 * D : 3 * D]
    gain_out = full_small[3 * D : 4 * D]
    score_coef = full_small[4 * D : 4 * D + H] * head_size ** (-0.5)
    qkv_low = full_qkv.reshape(D, 3 * D).astype(jnp.bfloat16)
    out_low = full_out.reshape(D, D).astype(jnp.bfloat16)
    heads_low = full_heads.reshape(D, C + F).astype(jnp.bfloat16)
    mem_hidden = embed(memory_feats, emb_table, emb_bias)
    mem_normed = (standard(mem_hidden)[0] * gain_in).astype(jnp.bfloat16)
    mem_kv = jnp.dot(mem_normed, qkv_low[:, D:], preferred_element_type=jnp.float32).astype(
        jnp.bfloat16
    )
    all_kv = lax.all_gather(mem_kv, "mem", axis=0, tiled=True)
    memory_rows = all_kv.shape[0]
    block_keys = math.gcd(memory_rows, 512)
    num_blocks = memory_rows // block_keys
    key_rows = all_kv[:, :D].reshape(num_blocks, block_keys, H, head_size)
    value_rows = all_kv[:, D:].reshape(num_blocks, block_keys, H, head_size)
    task_blocks = memory_task.reshape(num_blocks, block_keys)
    live_blocks = memory_mask.reshape(num_blocks, block_keys)
    key_blocks = (key_rows, value_rows, task_blocks, live_blocks)
    kept_input = query_feats * (1 - feature_mask).astype(jnp.float32)
    hidden_in = embed(kept_input, emb_table, emb_bias)
    query_normed = (standard(hidden_in)[0] * gain_in).astype(jnp.bfloat16)
    queries = (
        jnp.dot(query_normed, qkv_low[:, :D], preferred_element_type=jnp.float32)
        .astype(jnp.bfloat16)
        .reshape(-1, H, head_size)
    )
    num_rows = queries.shape[0]

    def allowed_of(task_row, live_row):
        return ((query_task[:, None] == task_row[None, :]) & (live_row[None, :] > 0))[None]

    def scores_of(key_block, allowed):
        raw_scores = jnp.einsum(
            "qhd,khd->hqk", queries, key_block, preferred_element_type=jnp.float32
        )
        return (
            raw_scores,
            jnp.where(allowed, score_coef[:, None, None] * raw_scores, masked_score),
        )

    def stats_step(state_in, block_data):
        row_top, row_sum = state_in
        key_block, value_block, task_row, live_row = block_data
        allowed = allowed_of(task_row, live_row)
        scores = scores_of(key_block, allowed)[1]
        new_top = jnp.maximum(row_top, jnp.max(scores, -1))
        shifted = jnp.where(allowed, jnp.exp(scores - new_top[..., None]), 0.0)
        return ((new_top, row_sum * jnp.exp(row_top - new_top) + jnp.sum(shifted, -1)), None)

    start_state = (
        jnp.full((H, num_rows), masked_score, jnp.float32),
        jnp.zeros((H, num_rows), jnp.float32),
    )
    (row_top, row_sum), unused = lax.scan(stats_step, start_state, key_blocks)

    def probs_of(scores, allowed):
        return jnp.where(allowed, jnp.exp(scores - row_top[..., None]), 0.0) / row_sum[..., None]

    def value_step(accum, block_data):
        key_block, value_block, task_row, live_row = block_data
        allowed = allowed_of(task_row, live_row)
        probs_low = probs_of(scores_of(key_block, allowed)[1], allowed).astype(jnp.bfloat16)
        return (
            accum
            + jnp.einsum(
                "hqk,khd->qhd", probs_low, value_block, preferred_element_type=jnp.float32
            ),
            None,
        )

    attn_sum, unused = lax.scan(
        value_step, jnp.zeros((num_rows, H, head_size), jnp.float32), key_blocks
    )
    attended = attn_sum.reshape(num_rows, D).astype(jnp.bfloat16)
    residual = hidden_in + jnp.dot(attended, out_low, preferred_element_type=jnp.float32)
    final_normed = (standard(residual)[0] * gain_out).astype(jnp.bfloat16)
    head_out = jnp.dot(final_normed, heads_low, preferred_element_type=jnp.float32)
    logits = head_out[:, :C]
    recon_err = head_out[:, C:] - query_feats
    label_mask = target_mask.astype(jnp.float32)
    feat_mask = feature_mask.astype(jnp.float32)
    onehot_class = jax.nn.one_hot(target_class, C, dtype=jnp.float32)
    picked = jnp.sum(logits * onehot_class, -1)
    sum_target, sum_recon, count_target, count_recon = lax.psum(
        (
            jnp.sum(label_mask * (jax.nn.logsumexp(logits, -1) - picked)),
            jnp.sum(feat_mask * recon_err**2),
            jnp.sum(label_mask),
            jnp.sum(feat_mask),
        ),
        "mem",
    )
    count_target = jnp.maximum(count_target, 1.0)
    count_recon = jnp.maximum(count_recon, 1.0)
    weight_a = anneal[0]
    loss_value = weight_a * sum_target / count_target + (1 - weight_a) * sum_recon / count_recon
    grad_logits = (
        weight_a / count_target * label_mask[:, None] * (jax.nn.softmax(logits, -1) - onehot_class)
    )
    grad_recon = (1 - weight_a) / count_recon * feat_mask * 2.0 * recon_err
    grad_head_out = jnp.concatenate([grad_logits, grad_recon], 1).astype(jnp.bfloat16)
    grad_heads = jnp.dot(final_normed.T, grad_head_out, preferred_element_type=jnp.float32)
    grad_final = jnp.dot(grad_head_out, heads_low.T, preferred_element_type=jnp.float32)
    grad_resid, grad_gain_out = norm_back(grad_final, residual, gain_out)
    grad_branch = grad_resid.astype(jnp.bfloat16)
    grad_wout = jnp.dot(attended.T, grad_branch, preferred_element_type=jnp.float32)
    grad_attn = (
        jnp.dot(grad_branch, out_low.T, preferred_element_type=jnp.float32)
        .astype(jnp.bfloat16)
        .reshape(num_rows, H, head_size)
    )
    row_delta = jnp.sum(
        grad_attn.astype(jnp.float32)
        * attended.reshape(num_rows, H, head_size).astype(jnp.float32),
        -1,
    ).T

    def back_step(state_in, block_data):
        key_block, value_block, task_row, live_row = block_data
        allowed = allowed_of(task_row, live_row)
        raw_scores, scores = scores_of(key_block, allowed)
        soft_probs = probs_of(scores, allowed)
        grad_probs = jnp.einsum(
            "qhd,khd->hqk", grad_attn, value_block, preferred_element_type=jnp.float32
        )
        grad_scores = (soft_probs * (grad_probs - row_delta[..., None])).astype(jnp.bfloat16)
        grad_beta = jnp.sum(grad_scores.astype(jnp.float32) * raw_scores, (1, 2))
        grad_query = jnp.einsum(
            "hqk,khd->qhd", grad_scores, key_block, preferred_element_type=jnp.float32
        )
        grad_key = (
            jnp.einsum("hqk,qhd->khd", grad_scores, queries, preferred_element_type=jnp.float32)
            * score_coef[None, :, None]
        )
        grad_value = jnp.einsum(
            "hqk,qhd->khd",
            soft_probs.astype(jnp.bfloat16),
            grad_attn,
            preferred_element_type=jnp.float32,
        )
        block_rows = key_block.shape[0]
        grad_kv = jnp.concatenate(
            [grad_key.reshape(block_rows, D), grad_value.reshape(block_rows, D)], 1
        )
        return ((state_in[0] + grad_query, state_in[1] + grad_beta), grad_kv)

    init_state = (jnp.zeros((num_rows, H, head_size), jnp.float32), jnp.zeros((H,), jnp.float32))
    (grad_q_sum, grad_beta_sum), kv_parts = lax.scan(back_step, init_state, key_blocks)
    kv_grad = lax.psum_scatter(
        kv_parts.reshape(memory_rows, 2 * D), "mem", scatter_dimension=0, tiled=True
    )
    grad_q_low = (grad_q_sum * score_coef[None, :, None]).reshape(num_rows, D).astype(jnp.bfloat16)
    grad_wq = jnp.dot(query_normed.T, grad_q_low, preferred_element_type=jnp.float32)
    grad_qn = jnp.dot(grad_q_low, qkv_low[:, :D].T, preferred_element_type=jnp.float32)
    grad_in_q, gain_in_q = norm_back(grad_qn, hidden_in, gain_in)
    grad_hidden = grad_resid + grad_in_q
    kv_upper, kv_lower = split_pair(kv_grad)
    grad_wkv = jnp.dot(mem_normed.T, kv_upper, preferred_element_type=jnp.float32) + jnp.dot(
        mem_normed.T, kv_lower, preferred_element_type=jnp.float32
    )
    grad_mn = jnp.dot(kv_upper, qkv_low[:, D:].T, preferred_element_type=jnp.float32) + jnp.dot(
        kv_lower, qkv_low[:, D:].T, preferred_element_type=jnp.float32
    )
    grad_mem, gain_in_m = norm_back(grad_mn, mem_hidden, gain_in)
    grad_table = jnp.einsum(
        "qf,qfe->fe", kept_input, grad_hidden.reshape(num_rows, F, -1), precision=high
    )
    grad_table = grad_table + jnp.einsum(
        "qf,qfe->fe", memory_feats, grad_mem.reshape(memory_feats.shape[0], F, -1), precision=high
    )
    grad_bias = jnp.sum(grad_hidden, 0) + jnp.sum(grad_mem, 0)
    small_size = full_small.shape[0]
    grad_small = jnp.concatenate(
        [
            grad_table.reshape(-1),
            grad_bias,
            gain_in_q + gain_in_m,
            grad_gain_out,
            grad_beta_sum * head_size ** (-0.5),
            jnp.zeros((small_size - 4 * D - H,), jnp.float32),
        ]
    )
    grad_qkv = jnp.concatenate([grad_wq, grad_wkv], 1).reshape(-1)
    shards = (
        lax.psum_scatter(grad_qkv, "mem", scatter_dimension=0, tiled=True),
        lax.psum_scatter(grad_wout.reshape(-1), "mem", scatter_dimension=0, tiled=True),
        lax.psum_scatter(grad_heads.reshape(-1), "mem", scatter_dimension=0, tiled=True),
        lax.psum_scatter(grad_small, "mem", scatter_dimension=0, tiled=True),
    )
    local_squares = sum((jnp.sum(piece_grad * piece_grad) for piece_grad in shards))
    grad_total = jnp.sqrt(lax.psum(local_squares, "mem"))
    factor = jnp.minimum(1.0, max_norm / (grad_total + 1e-06))
    step_num = float(STEP)
    weights_all = (w_qkv, w_out, w_heads, w_small)
    firsts = (m_qkv, m_out, m_heads, m_small)
    seconds = (v_qkv, v_out, v_heads, v_small)
    results = [
        adamw(weight, first_mom, second, grad_in, factor, step_num, step_rate)
        for weight, first_mom, second, grad_in, step_rate in zip(
            weights_all, firsts, seconds, shards, learn_rates
        )
    ]
    new_w = [entry[2] for entry in results]
    return (
        new_w[0],
        new_w[1],
        new_w[2],
        new_w[3],
        results[0][0],
        results[1][0],
        results[2][0],
        results[3][0],
        results[0][1],
        results[1][1],
        results[2][1],
        results[3][1],
        new_w[0].astype(jnp.bfloat16),
        new_w[1].astype(jnp.bfloat16),
        new_w[2].astype(jnp.bfloat16),
        new_w[3].astype(jnp.bfloat16),
        loss_value.reshape(1),
        grad_total.reshape(1),
    )


f32 = jnp.float32
bf16 = jnp.bfloat16
LOG2E = math.log2(math.e)
QB = 128
KC = 384
VROWS = 80
E_CAP = 16
SMALL_LANE = 88
COUNT_LANE = 122


def place_of(dev, planes):
    return (dev % 2) * (4 * planes) + ((dev // 2) % 4) * planes + dev // 8


def nt(a, b):
    return lax.dot_general(a, b, (((1,), (1,)), ((), ())), preferred_element_type=f32)


def tn(a, b):
    return lax.dot_general(a, b, (((0,), (0,)), ((), ())), preferred_element_type=f32)


def nn(a, b):
    return jnp.dot(a, b, preferred_element_type=f32)


def iota(shape, dim):
    return lax.broadcasted_iota(jnp.int32, shape, dim)


def split2(v):
    hi = v.astype(bf16).astype(f32)
    return hi, v - hi


def split3(v):
    hi, rest = split2(v)
    mid = rest.astype(bf16).astype(f32)
    return hi, mid, rest - mid


def wide(v, lanes):
    return jnp.concatenate([v] * (lanes // v.shape[1]), axis=1) if lanes > v.shape[1] else v


def embed_t(kept, table, bias):
    parts = []
    for f in range(F):
        rows = slice(32 * f, 32 * f + 32)
        parts.append(kept[f : f + 1] * table[rows] + bias[rows])
    return jnp.concatenate(parts, axis=0)


def norm_t(v):
    centred = v - jnp.mean(v, axis=0, keepdims=True)
    inverse = lax.rsqrt(jnp.mean(centred * centred, axis=0, keepdims=True) + eps_norm)
    return centred * inverse, inverse


def norm_back_t(grad, normed, inverse, gain):
    scaled = grad * gain
    return inverse * (
        scaled
        - jnp.mean(scaled, axis=0, keepdims=True)
        - normed * jnp.mean(scaled * normed, axis=0, keepdims=True)
    )


def sizes(n, num_q, num_mem):
    q_blocks = (num_q + TASKS * (QB - 1)) // QB
    q_blocks += q_blocks % 2
    k_chunks = (num_mem + TASKS * (KC - 1)) // KC
    return q_blocks, k_chunks


def step_kernel(
    n, num_q, num_mem, small_size,
    xs, fs, ct, posm, units, an, gw,
    gqkv, gout, ghead, out_sums, out_l,
    w_s, wt_s, wh_s, wht_s, kdup_s, vaug_w,
    cols, coefb,
    f2_s, mfeat,
    kaug, vaug, kt_s, vt_s, mnt, gk, gv,
    qn_s, q_s, qhi, qlo, att, il_s, gres, fn_s, gho_s, gb_s, dap, dneg, dq_s, stat_q,
    ebuf, sbuf, ecur, acc, m_s,
    acc_gain,
    blk_c0, blk_nc, blk_tile, ch_base, ch_end,
):
    planes = n // 8
    rows_dev = D // n
    per_small = small_size // n
    qs = num_q

    pieces = [gw[place_of(d, planes)].astype(f32) for d in range(n)]
    for col in range(8):
        block = jnp.concatenate([piece[8 * col : 8 * col + 8] for piece in pieces], axis=0)
        w_s[:, 128 * col : 128 * col + 128] = block.astype(bf16)
        wt_s[128 * col : 128 * col + 128, :] = block.T.astype(bf16)
    lane = iota((8, 128), 1)
    tiles = [piece[64:72] + piece[72:80] for piece in pieces]
    lane_w = iota((D, 128), 1)
    heads = pltpu.roll(jnp.concatenate(tiles, axis=0), 64, 1)
    heads = jnp.where(lane_w < C + F, heads, 0.0)
    wh_s[...] = heads.astype(bf16)
    wht_s[...] = heads.T[:32].astype(bf16)
    feats = []
    for b in range(n // 2):
        feats.append(jnp.where(lane < 64, tiles[2 * b], pltpu.roll(tiles[2 * b + 1], 64, 1)))
    feats = jnp.concatenate(feats, axis=1)
    f2_s[...] = jnp.concatenate(split2(feats), axis=0).astype(bf16)
    dup_r = iota((D, 4 * 128), 0)
    dup_l = iota((D, 4 * 128), 1)
    low6 = dup_l & 127
    dup = (dup_r == 64 * (dup_l >> 7) + (low6 & 63)).astype(f32).astype(bf16)
    once = ((dup_r == 64 * (dup_l >> 7) + low6) & (low6 < 64)).astype(f32).astype(bf16)
    kdup_s[...] = nn(w_s[:, D : 2 * D], dup).astype(bf16)
    vaug_w[...] = nn(w_s[:, 2 * D : 3 * D], once).astype(bf16)

    small_rows = jnp.concatenate([tile[0:1] for tile in tiles], axis=0)
    lane_n = iota((n, 128), 1)
    count_t = jnp.maximum(jnp.sum(jnp.where(lane_n == COUNT_LANE, small_rows, 0.0)), 1.0)
    count_r = jnp.maximum(jnp.sum(jnp.where(lane_n == COUNT_LANE + 1, small_rows, 0.0)), 1.0)
    used = 4 * D + 2 * H
    s2 = jnp.concatenate(
        list(split2(small_rows)) + [jnp.zeros((128 - 2 * n, 128), f32)], axis=0
    ).astype(bf16)
    row = iota((used, 128), 0)
    lan = iota((used, 128), 1)
    dev_of = lan & (n - 1)
    pick = (row >= per_small * dev_of) & (row < per_small * dev_of + per_small) & (lan < 2 * n)
    spread = nn(pick.astype(f32).astype(bf16), s2)
    row_dev = jnp.floor((row.astype(f32) + 0.5) * (1.0 / per_small)).astype(jnp.int32)
    here = (lan - SMALL_LANE) == (row - per_small * row_dev)
    column = jnp.sum(jnp.where(here, spread, 0.0), axis=1, keepdims=True)
    cols[...] = jnp.broadcast_to(column[: 4 * D], (4 * D, 128))
    for h in range(H):
        coefb[32 * h : 32 * h + 32, :] = jnp.broadcast_to(
            column[4 * D + h : 4 * D + h + 1] * (32 ** (-0.5)), (32, 128)
        )

    m_base = [units[t] for t in range(TASKS)]
    m_count = [units[TASKS + t] for t in range(TASKS)]
    m_units = [units[2 * TASKS + t] for t in range(TASKS)]
    q_base = [units[3 * TASKS + t] for t in range(TASKS)]
    q_units = [units[4 * TASKS + t] for t in range(TASKS)]
    tile = jnp.int32(0)
    for t in range(TASKS):
        first_chunk = lax.div(m_base[t], jnp.int32(KC))
        first_block = lax.div(q_base[t], jnp.int32(QB))

        def fill_chunk(i, carry, t=t, first_chunk=first_chunk):
            ch_base[first_chunk + i] = m_base[t]
            ch_end[first_chunk + i] = m_base[t] + m_count[t]
            return carry

        lax.fori_loop(0, m_units[t], fill_chunk, 0)

        def fill_block(i, tile_in, t=t, first_chunk=first_chunk, first_block=first_block):
            blk_c0[first_block + i] = first_chunk
            blk_nc[first_block + i] = m_units[t]
            blk_tile[first_block + i] = tile_in
            return tile_in + m_units[t]

        tile = lax.fori_loop(0, q_units[t], fill_block, tile)
    num_blocks = q_units[0] + q_units[1] + q_units[2] + q_units[3]
    num_chunks = m_units[0] + m_units[1] + m_units[2] + m_units[3]

    emb_w = lambda lanes: wide(cols[0:D, :], lanes)
    emb_b = lambda lanes: wide(cols[D : 2 * D, :], lanes)
    gain_in = lambda lanes: wide(cols[2 * D : 3 * D, :], lanes)
    gain_out = lambda lanes: wide(cols[3 * D : 4 * D, :], lanes)

    def mem_chunk(c, carry):
        at = pl.ds(pl.multiple_of(c * KC, KC), KC)
        base, end = ch_base[c], ch_end[c]
        s_col = iota((KC, 1), 0) + c * KC
        source = jnp.where(s_col < end, s_col, base).astype(f32)
        chosen = (posm[...] == source).astype(f32).astype(bf16)
        got = nt(f2_s[...], chosen)
        feats_c = got[0:8] + got[8:16]
        mfeat[:, at] = feats_c
        hidden = embed_t(feats_c, emb_w(KC), emb_b(KC))
        normed, unused = norm_t(hidden)
        mn = (normed * gain_in(KC)).astype(bf16)
        mnt[:, at] = mn
        kt_s[:, at] = nn(wt_s[D : 2 * D, :], mn).astype(bf16)
        live_row = ((iota((1, KC), 1) + c * KC) < end).astype(f32)
        vt = nn(wt_s[2 * D : 3 * D, :], mn) * live_row
        tail = jnp.where(iota((16, KC), 0) == 0, live_row, 0.0)
        vt_s[:, at] = jnp.concatenate(
            [part for p in range(4) for part in (vt[64 * p : 64 * p + 64], tail)], axis=0
        ).astype(bf16)
        kaug[at, :] = tn(mn, kdup_s[...]).astype(bf16)
        live_col = (s_col < end).astype(f32)
        low = iota((KC, 512), 1) & 127
        vn = jnp.where((low == 64) | (low == 65), 1.0, tn(mn, vaug_w[...]))
        vaug[at, :] = (vn * live_col).astype(bf16)
        gk[at, :] = jnp.zeros((KC, D), f32)
        gv[at, :] = jnp.zeros((KC, D), f32)
        return carry

    lax.fori_loop(0, num_chunks, mem_chunk, 0)

    coef2 = wide(coefb[...], 256)

    def pre_block(j, carry):
        at = pl.ds(pl.multiple_of(j * 256, 256), 256)
        kept = xs[:, at] * (1.0 - fs[:, at])
        hidden = embed_t(kept, emb_w(256), emb_b(256))
        normed, unused = norm_t(hidden)
        qn = (normed * gain_in(256)).astype(bf16)
        qn_s[:, at] = qn
        q = nn(wt_s[0:D, :], qn).astype(bf16)
        q_s[:, at] = q
        scaled = q.astype(f32) * (coef2 * LOG2E)
        upper = scaled.astype(bf16)
        qhi[:, at] = upper
        qlo[:, at] = (scaled - upper.astype(f32)).astype(bf16)
        att[:, at] = jnp.zeros((D, 256), bf16)
        il_s[:, at] = jnp.zeros((H, 256), f32)
        dq_s[:, at] = jnp.zeros((D, 256), f32)
        return carry

    lax.fori_loop(0, qs // 256, pre_block, 0)

    zero_h = jnp.zeros((32, 128), bf16)

    def diagonal(ref, at, p):
        return [
            jnp.concatenate([ref[64 * p : 64 * p + 32, at], zero_h], axis=1),
            jnp.concatenate([zero_h, ref[64 * p + 32 : 64 * p + 64, at]], axis=1),
        ]

    def score_operand(at, p):
        return jnp.concatenate(diagonal(qhi, at, p) + diagonal(qlo, at, p), axis=0)

    def finish_forward(at, p, got):
        inverse = 1.0 / got[64:65, :]
        il_s[2 * p : 2 * p + 1, at] = inverse[:, :128]
        il_s[2 * p + 1 : 2 * p + 2, at] = inverse[:, 128:]
        att[64 * p : 64 * p + 32, at] = (got[0:32, :128] * inverse[:, :128]).astype(bf16)
        att[64 * p + 32 : 64 * p + 64, at] = (got[32:64, 128:] * inverse[:, 128:]).astype(bf16)

    def pair(p, width):
        return slice(width * p, width * p + width)

    def forward_block(i, carry):
        at = pl.ds(pl.multiple_of(i * QB, QB), QB)
        c0, nc, tile0 = blk_c0[i], blk_nc[i], blk_tile[i]

        @pl.when(nc == 1)
        def one():
            keys = pl.ds(pl.multiple_of(c0 * KC, KC), KC)
            keep = jnp.minimum(tile0, E_CAP)
            operands = [score_operand(at, p) for p in range(4)]
            values = [vt_s[pair(p, VROWS), keys] for p in range(4)]
            scores = [nn(kaug[keys, pair(p, 128)], operands[p]) for p in range(4)]
            tops = [jnp.max(s, axis=0, keepdims=True) for s in scores]
            es = [jnp.exp2(scores[p] - tops[p]).astype(bf16) for p in range(4)]
            sums = [nn(values[p], es[p]) for p in range(4)]
            for p in range(4):
                m_s[i, :, pair(p, 256)] = tops[p]
                ebuf[keep, :, pair(p, 256)] = es[p]
                finish_forward(at, p, sums[p])

        @pl.when(nc > 1)
        def many():
            m_s[i] = jnp.full((1, 1024), -3e38, f32)
            acc[...] = jnp.zeros_like(acc)

            def tops(c, inner):
                keys = pl.ds(pl.multiple_of((c0 + c) * KC, KC), KC)
                for p in range(4):
                    s = nn(kaug[keys, pair(p, 128)], score_operand(at, p))
                    m_s[i, :, pair(p, 256)] = jnp.maximum(
                        m_s[i, :, pair(p, 256)], jnp.max(s, axis=0, keepdims=True)
                    )
                return inner

            lax.fori_loop(0, nc, tops, 0)

            def sums(c, inner):
                keys = pl.ds(pl.multiple_of((c0 + c) * KC, KC), KC)
                keep = jnp.minimum(tile0 + c, E_CAP)
                for p in range(4):
                    s = nn(kaug[keys, pair(p, 128)], score_operand(at, p))
                    e = jnp.exp2(s - m_s[i, :, pair(p, 256)]).astype(bf16)
                    ebuf[keep, :, pair(p, 256)] = e
                    acc[pair(p, VROWS), :] += nn(vt_s[pair(p, VROWS), keys], e)
                return inner

            lax.fori_loop(0, nc, sums, 0)
            for p in range(4):
                finish_forward(at, p, acc[pair(p, VROWS), :])

        return carry

    lax.fori_loop(0, num_blocks, forward_block, 0)

    weight_a = an[0]
    scale_t = weight_a / count_t
    scale_r = (1.0 - weight_a) / count_r
    acc_gain[...] = jnp.zeros_like(acc_gain)
    out_l[...] = jnp.zeros_like(out_l)

    def fold(v):
        return v[:, :128] + v[:, 128:256]

    def mid_block(j, carry):
        at = pl.ds(pl.multiple_of(j * 256, 256), 256)
        x = xs[:, at]
        fmask = fs[:, at]
        kept = x * (1.0 - fmask)
        hidden = embed_t(kept, emb_w(256), emb_b(256))
        attended = att[:, at]
        residual = hidden + nn(wt_s[3 * D : 4 * D, :], attended)
        normed, inverse = norm_t(residual)
        fn = (normed * gain_out(256)).astype(bf16)
        fn_s[:, at] = fn
        head = nn(wht_s[...], fn)
        logits = head[0:C]
        err = head[C : C + F] - x
        label = ct[1:2, at]
        hot = (iota((C, 256), 0).astype(f32) == ct[0:1, at]).astype(f32)
        top = jnp.max(logits, axis=0, keepdims=True)
        e = jnp.exp(logits - top)
        total = jnp.sum(e, axis=0, keepdims=True)
        picked = jnp.sum(logits * hot, axis=0, keepdims=True)
        out_l[0:1, :] += fold(
            scale_t * label * (jnp.log(total) + top - picked)
            + scale_r * jnp.sum(fmask * err * err, axis=0, keepdims=True)
        )
        g_log = scale_t * label * (e / total - hot)
        g_rec = scale_r * fmask * 2.0 * err
        gho = jnp.concatenate([g_log, g_rec, jnp.zeros((8, 256), f32)], axis=0).astype(bf16)
        gho_s[:, at] = gho
        g_final = nn(wh_s[:, :32], gho)
        acc_gain[D : 2 * D, :] += fold(g_final * normed)
        g_res = norm_back_t(g_final, normed, inverse, gain_out(256))
        gres[:, at] = g_res
        gb = g_res.astype(bf16)
        gb_s[:, at] = gb
        ga = nn(w_s[:, 3 * D : 4 * D], gb).astype(bf16).astype(f32)
        attf = attended.astype(f32)
        for h in range(H):
            rows = slice(32 * h, 32 * h + 32)
            da = (ga[rows] * il_s[h : h + 1, at]).astype(bf16)
            dap[rows, at] = da
            dneg[h : h + 1, at] = -jnp.sum(da.astype(f32) * attf[rows], axis=0, keepdims=True)
        return carry

    lax.fori_loop(0, qs // 256, mid_block, 0)

    zero_p = jnp.zeros((64, 256), bf16)
    zero_t = jnp.zeros((48, 256), bf16)
    r16 = iota((16, 256), 0)

    def backward_chunk(at, c, e_of):
        keys = pl.ds(pl.multiple_of(c * KC, KC), KC)
        es = [e_of(p) for p in range(4)]
        das = [jnp.concatenate(diagonal(dap, at, p), axis=0) for p in range(4)]
        qds = [jnp.concatenate(diagonal(q_s, at, p), axis=0) for p in range(4)]
        negs = dneg[:, at]
        vals = [vaug[keys, pair(p, 128)] for p in range(4)]
        kts = [kt_s[64 * p : 64 * p + 64, keys] for p in range(4)]
        old_dq = dq_s[:, at]
        old_gk = gk[keys, :]
        old_gv = gv[keys, :]
        operands = []
        for p in range(4):
            neg = jnp.concatenate([negs[2 * p : 2 * p + 1], negs[2 * p + 1 : 2 * p + 2]], axis=1)
            neg_hi = neg.astype(bf16).astype(f32)
            tail = jnp.where(r16 == 0, neg_hi, jnp.where(r16 == 1, neg - neg_hi, 0.0)).astype(bf16)
            operands.append(jnp.concatenate([das[p], tail, zero_t], axis=0))
        dps = [nn(vals[p], operands[p]) for p in range(4)]
        dss = [(es[p].astype(f32) * dps[p]).astype(bf16) for p in range(4)]
        dqs = [nn(kts[p], dss[p]) for p in range(4)]

        def by_key(grads, others):
            halves = []
            for a in (0, 2):
                left = jnp.concatenate([grads[a], grads[a + 1]], axis=1)
                upper = jnp.concatenate([others[a], zero_p], axis=1)
                lower = jnp.concatenate([zero_p, others[a + 1]], axis=1)
                halves.append(nt(left, jnp.concatenate([upper, lower], axis=0)))
            return jnp.concatenate(halves, axis=1)

        new_gv = old_gv + by_key(es, das)
        new_gk = old_gk + by_key(dss, qds)
        parts = []
        for p in range(4):
            parts += [dqs[p][0:32, :128], dqs[p][32:64, 128:]]
        dq_s[:, at] = old_dq + jnp.concatenate(parts, axis=0)
        gk[keys, :] = new_gk
        gv[keys, :] = new_gv

    def backward_block(i, carry):
        at = pl.ds(pl.multiple_of(i * QB, QB), QB)
        c0, nc, tile0 = blk_c0[i], blk_nc[i], blk_tile[i]
        simple = (nc == 1) & (tile0 < E_CAP)

        @pl.when(simple)
        def one():
            backward_chunk(at, c0, lambda p: ebuf[tile0, :, pair(p, 256)])

        @pl.when(jnp.logical_not(simple))
        def many():
            def one_chunk(c, inner):
                @pl.when(tile0 + c < E_CAP)
                def kept():
                    ecur[...] = ebuf[tile0 + c]

                @pl.when(tile0 + c >= E_CAP)
                def again():
                    keys = pl.ds(pl.multiple_of((c0 + c) * KC, KC), KC)
                    for p in range(4):
                        s = nn(kaug[keys, pair(p, 128)], score_operand(at, p))
                        ecur[:, pair(p, 256)] = jnp.exp2(
                            s - m_s[i, :, pair(p, 256)]
                        ).astype(bf16)

                backward_chunk(at, c0 + c, lambda p: ecur[:, pair(p, 256)])
                return inner

            lax.fori_loop(0, nc, one_chunk, 0)

        return carry

    lax.fori_loop(0, num_blocks, backward_block, 0)

    def sum_in(grad, normed, kept, lanes):
        by_feature = jnp.concatenate(
            [kept[f : f + 1] * grad[32 * f : 32 * f + 32] for f in range(F)], axis=0
        )
        outs = []
        for v in (by_feature, grad):
            total = v[:, :128]
            for k in range(1, lanes // 128):
                total = total + v[:, 128 * k : 128 * k + 128]
            outs.append(total)
        return outs

    def post_block(j, carry):
        at = pl.ds(pl.multiple_of(j * 256, 256), 256)
        kept = xs[:, at] * (1.0 - fs[:, at])
        hidden = embed_t(kept, emb_w(256), emb_b(256))
        normed, inverse = norm_t(hidden)
        dq = dq_s[:, at]
        gq = (dq * coef2).astype(bf16)
        prod = fold(dq * q_s[:, at].astype(f32))
        for h in range(H):
            acc_gain[4 * D + h : 4 * D + h + 1, :] += jnp.sum(
                prod[32 * h : 32 * h + 32], axis=0, keepdims=True
            )
        gqkv[:, 0:D] += nt(qn_s[:, at], gq)
        gqn = nn(w_s[:, 0:D], gq)
        acc_gain[0:D, :] += fold(gqn * normed)
        gh = gres[:, at] + norm_back_t(gqn, normed, inverse, gain_in(256))
        by_f, plain = sum_in(gh, normed, kept, 256)
        acc_gain[2 * D : 3 * D, :] += by_f
        acc_gain[3 * D : 4 * D, :] += plain
        return carry

    gqkv[...] = jnp.zeros_like(gqkv)
    lax.fori_loop(0, qs // 256, post_block, 0)
    gout[...] = nt(att[...], gb_s[...])
    ghead[...] = nt(fn_s[...], gho_s[...])

    def mem_back(c, carry):
        at = pl.ds(pl.multiple_of(c * KC, KC), KC)
        live = ((iota((KC, 1), 0) + c * KC) < ch_end[c]).astype(f32)
        coef_lane = carry
        gk_c = (gk[at, :] * coef_lane * live).astype(bf16)
        gv_c = (gv[at, :] * live).astype(bf16)
        mn = mnt[:, at]
        gqkv[:, D : 2 * D] += nn(mn, gk_c)
        gqkv[:, 2 * D : 3 * D] += nn(mn, gv_c)
        gmn = nt(w_s[:, D : 2 * D], gk_c) + nt(w_s[:, 2 * D : 3 * D], gv_c)
        feats_c = mfeat[:, at]
        hidden = embed_t(feats_c, emb_w(KC), emb_b(KC))
        normed, inverse = norm_t(hidden)
        dgain = gmn * normed
        acc_gain[0:D, :] += dgain[:, :128] + dgain[:, 128:256] + dgain[:, 256:384]
        gm = norm_back_t(gmn, normed, inverse, gain_in(KC))
        by_f, plain = sum_in(gm, normed, feats_c, KC)
        acc_gain[2 * D : 3 * D, :] += by_f
        acc_gain[3 * D : 4 * D, :] += plain
        return carry

    coef_lane = jnp.concatenate([coefb[0:128, :].T[0:1], coefb[128:256, :].T[0:1]], axis=1)
    lax.fori_loop(0, num_chunks, mem_back, coef_lane)

    out_sums[...] = jnp.broadcast_to(
        jnp.sum(acc_gain[...], axis=1, keepdims=True), (4 * D + H, 128)
    )


def step_call(n, num_mem, small_size, xs, fs, ct, posm, units, an, gw):
    num_q = xs.shape[1]
    q_blocks, k_chunks = xs.shape[1] // QB, (num_mem + TASKS * (KC - 1)) // KC
    qs, ks = q_blocks * QB, k_chunks * KC
    V = pltpu.VMEM
    S = pltpu.SMEM
    vm = pl.BlockSpec(memory_space=pltpu.VMEM)
    sm = pl.BlockSpec(memory_space=pltpu.SMEM)
    scratch = [
        V((D, 4 * D), bf16), V((4 * D, D), bf16), V((D, 128), bf16), V((32, D), bf16),
        V((D, 512), bf16), V((D, 512), bf16),
        V((4 * D, 128), f32), V((D, 128), f32),
        V((16, num_mem), bf16), V((8, ks), f32),
        V((ks, 512), bf16), V((ks, 512), bf16), V((D, ks), bf16), V((4 * VROWS, ks), bf16),
        V((D, ks), bf16), V((ks, D), f32), V((ks, D), f32),
        V((D, qs), bf16), V((D, qs), bf16), V((D, qs), bf16), V((D, qs), bf16), V((D, qs), bf16),
        V((H, qs), f32), V((D, qs), f32), V((D, qs), bf16), V((32, qs), bf16), V((D, qs), bf16),
        V((D, qs), bf16), V((H, qs), f32), V((D, qs), f32), V((8, qs), f32),
        V((E_CAP + 1, KC, 1024), bf16), V((8, 128), f32), V((KC, 1024), bf16),
        V((4 * VROWS, 256), f32), V((q_blocks, 1, 1024), f32),
        V((4 * D + H, 128), f32),
        S((q_blocks,), jnp.int32), S((q_blocks,), jnp.int32), S((q_blocks,), jnp.int32),
        S((k_chunks,), jnp.int32), S((k_chunks,), jnp.int32),
    ]
    return pl.pallas_call(
        functools.partial(step_kernel, n, qs, num_mem, small_size),
        out_shape=(
            jax.ShapeDtypeStruct((D, 3 * D), f32),
            jax.ShapeDtypeStruct((D, D), f32),
            jax.ShapeDtypeStruct((D, 32), f32),
            jax.ShapeDtypeStruct((4 * D + H, 128), f32),
            jax.ShapeDtypeStruct((8, 128), f32),
        ),
        in_specs=[vm] * 4 + [sm] * 2 + [vm],
        out_specs=(vm,) * 5,
        scratch_shapes=scratch,
        compiler_params=pltpu.CompilerParams(vmem_limit_bytes=58 * 1024 * 1024),
    )(xs, fs, ct, posm, units, an, gw)


MESH = pl.DeviceIdType.MESH


def greet(targets):
    barrier = pltpu.get_barrier_semaphore()
    for target in targets:
        pl.semaphore_signal(barrier, inc=1, device_id=(target,), device_id_type=MESH)
    return barrier


def send(src, dst, send_sem, recv_sem, target):
    copy = pltpu.make_async_remote_copy(
        src_ref=src,
        dst_ref=dst,
        send_sem=send_sem,
        recv_sem=recv_sem,
        device_id=(target,),
        device_id_type=MESH,
    )
    copy.start()
    return copy


def where_am_i(planes):
    me = lax.axis_index("mem")
    core = lax.rem(me, 2)
    square = lax.rem(lax.div(me, 2), 4)
    plane = lax.div(me, 8)
    return me, core, square, plane


def gather_kernel(
    n, num_q, num_mem, w_qkv, w_out, w_heads, w_small, mfeat, qf, fm, qt, tc, tm, mt, mm,
    gw, xs, fs, ct, posm, units_out,
    send_z, recv_z, send_s, recv_s, send_c, recv_c,
):
    planes = n // 8
    me, core, square, plane = where_am_i(planes)
    in_plane = core + 2 * square
    z_of = [lax.rem(plane + k, planes) * 8 + in_plane for k in range(1, planes)]
    s_of = [plane * 8 + lax.rem(square + k, 4) * 2 + core for k in range(1, 4)]
    c_of = plane * 8 + square * 2 + (1 - core)
    barrier = greet(z_of + s_of + [c_of])

    rows = []
    for c in range(6):
        rows.append(w_qkv[pl.ds(c, 8, stride=6), :])
    for c in range(2):
        rows.append(w_out[pl.ds(c, 8, stride=2), :])
    per_head = w_heads.shape[1]
    lane = iota((8, 256), 1)
    head_row = jnp.concatenate([w_heads[...], jnp.zeros((1, 256 - per_head), f32)], axis=1)
    owner = jnp.floor((lane.astype(f32) + 0.5) * (1.0 / (C + F))).astype(jnp.int32)
    kept_heads = jnp.where(owner == iota((8, 256), 0), head_row, 0.0).astype(bf16)
    fold_r = iota((256, 128), 0)
    fold_row = jnp.floor((fold_r.astype(f32) + 0.5) * (1.0 / (C + F))).astype(jnp.int32)
    fold_m = (fold_r - (C + F) * fold_row == iota((256, 128), 1) - 64).astype(f32).astype(bf16)
    heads = nn(kept_heads, fold_m)
    per_small = w_small.shape[1]
    small = jnp.concatenate([w_small[...], jnp.zeros((1, 128 - per_small), f32)], axis=1)
    small = pltpu.roll(jnp.broadcast_to(small, (8, 128)), SMALL_LANE, 1)
    feats = jnp.concatenate([mfeat[...], jnp.zeros((8, 64), f32)], axis=1)
    lane8 = iota((8, 128), 1)
    row8 = iota((8, 128), 0)
    num_t = jnp.sum(tm[...].astype(f32), axis=1, keepdims=True)
    num_r = jnp.sum(jnp.sum(fm[...].astype(f32), axis=0, keepdims=True), axis=1, keepdims=True)
    block = feats + heads
    first = (row8 == 0) & (lane8 >= SMALL_LANE) & (lane8 < SMALL_LANE + per_small)
    block = jnp.where(first, small, block)
    block = jnp.where((row8 == 0) & (lane8 == COUNT_LANE), num_t, block)
    block = jnp.where((row8 == 0) & (lane8 == COUNT_LANE + 1), num_r, block)

    def slot_of(k, j, c):
        back = lax.rem(plane + planes - k, planes)
        return c * (4 * planes) + lax.rem(square + 4 - j, 4) * planes + back

    gw[slot_of(0, 0, core)] = jnp.concatenate(rows + list(split2(block)), axis=0).astype(bf16)

    pl.semaphore_wait(barrier, planes - 1 + 4)

    def spread(k, done):
        at = gw.at[slot_of(k, 0, core)]
        for j in range(1, 4):
            done[k, j] = send(at, at, send_s.at[k, j - 1], recv_s.at[k, j - 1], s_of[j - 1])
        done[k, 0, "c"] = send(at, at, send_c.at[k, 0], recv_c.at[k, 0], c_of)

    at = gw.at[slot_of(0, 0, core)]
    done = {}
    for k in range(1, planes):
        done[k] = send(at, at, send_z.at[k - 1], recv_z.at[k - 1], z_of[k - 1])
    spread(0, done)

    task_row = iota((8, 256), 0)
    marks = []
    for b in range(num_q // 256):
        marks.append((qt[:, 256 * b : 256 * b + 256] == task_row).astype(f32))
    for b in range(num_mem // 256):
        cut = slice(256 * b, 256 * b + 256)
        marks.append(((mt[:, cut] == task_row) & (mm[:, cut] > 0)).astype(f32))
    marks_all = jnp.concatenate(marks, axis=0)
    tri = (iota((256, 256), 0) < iota((256, 256), 1)).astype(f32).astype(bf16)
    ranks = nn(marks_all.astype(bf16), tri)
    totals = jnp.sum(marks_all, axis=1, keepdims=True)
    task_col = iota((8, 1), 0)

    def lay_out(first, count, unit):
        carry = jnp.zeros((8, 1), f32)
        before = []
        for b in range(count):
            before.append(carry)
            at = 8 * (first + b)
            carry = carry + totals[at : at + 8]
        base = jnp.int32(0)
        bases, counts, units = [], [], []
        base_vec = jnp.zeros((8, 1), f32)
        for t in range(TASKS):
            num = jnp.sum(jnp.where(task_col == t, carry, 0.0)).astype(jnp.int32)
            bases.append(base)
            counts.append(num)
            used_units = lax.div(num + (unit - 1), jnp.int32(unit))
            units.append(used_units)
            base_vec = base_vec + jnp.where(task_col == t, base.astype(f32), 0.0)
            base = base + used_units * unit
        places = []
        for b in range(count):
            at = 8 * (first + b)
            places.append(
                jnp.sum(
                    marks[first + b] * (base_vec + before[b] + ranks[at : at + 8]),
                    axis=0,
                    keepdims=True,
                )
                - (1.0 - jnp.sum(marks[first + b], axis=0, keepdims=True))
            )
        return jnp.concatenate(places, axis=1), bases, counts, units

    place_q, q_base, q_count, q_units = lay_out(0, num_q // 256, QB)
    place_m, m_base, m_count, m_units = lay_out(num_q // 256, num_mem // 256, KC)

    posm[...] = place_m
    for t in range(TASKS):
        units_out[t] = m_base[t]
        units_out[TASKS + t] = m_count[t]
        units_out[2 * TASKS + t] = m_units[t]
        units_out[3 * TASKS + t] = q_base[t]
        units_out[4 * TASKS + t] = q_units[t]
    qs = xs.shape[1]
    xq = qf[...]
    fmq = fm[...].astype(f32)
    row8 = iota((8, num_q), 0)
    label_rows = jnp.where(
        row8 == 0, tc[...].astype(f32), jnp.where(row8 == 1, tm[...].astype(f32), 0.0)
    )
    q_rows = jnp.concatenate(
        list(split3(xq)) + [fmq, label_rows, jnp.zeros((8, num_q), f32)], axis=0
    ).astype(bf16)
    for b in range(qs // 256):
        chosen = (
            (place_q == (iota((256, 1), 0) + 256 * b).astype(f32)).astype(f32).astype(bf16)
        )
        got = nt(q_rows, chosen)
        cut = slice(256 * b, 256 * b + 256)
        xs[:, cut] = got[0:8] + got[8:16] + got[16:24]
        fs[:, cut] = got[24:32]
        ct[:, cut] = got[32:40]


    for k in range(1, planes):
        done[k].wait_recv()
        spread(k, done)
    for k in range(planes):
        for j in range(1, 4):
            done[k, j].wait_recv()
            at = gw.at[slot_of(k, j, core)]
            done[k, j, "c"] = send(at, at, send_c.at[k, j], recv_c.at[k, j], c_of)
    for k in range(planes):
        for j in range(4):
            done[k, j, "c"].wait_recv()
    for copy in done.values():
        copy.wait_send()


def gather_call(n, w_qkv, w_out, w_heads, w_small, mfeat, qf, fm, qt, tc, tm, mt, mm):
    planes = n // 8
    num_q, num_mem = qf.shape[1], mt.shape[1]
    qs = sizes(n, num_q, num_mem)[0] * QB
    vm = pl.BlockSpec(memory_space=pltpu.VMEM)
    dma = pltpu.SemaphoreType.DMA
    return pl.pallas_call(
        functools.partial(gather_kernel, n, num_q, num_mem),
        out_shape=(
            jax.ShapeDtypeStruct((n, 80, 128), bf16),
            jax.ShapeDtypeStruct((8, qs), f32),
            jax.ShapeDtypeStruct((8, qs), f32),
            jax.ShapeDtypeStruct((8, qs), f32),
            jax.ShapeDtypeStruct((1, num_mem), f32),
            jax.ShapeDtypeStruct((5 * TASKS,), jnp.int32),
        ),
        in_specs=[vm] * 12,
        out_specs=(vm,) * 5 + (pl.BlockSpec(memory_space=pltpu.SMEM),),
        scratch_shapes=[
            dma((planes - 1,)), dma((planes - 1,)), dma((planes, 3)), dma((planes, 3)),
            dma((planes, 4)), dma((planes, 4)),
        ],
        compiler_params=pltpu.CompilerParams(collective_id=0, has_side_effects=True),
    )(w_qkv, w_out, w_heads, w_small, mfeat, qf, fm, qt, tc, tm, mt, mm)


def reduce_kernel(
    n, per_small, gqkv, gout, ghead, sums_in, l_in, g_out, t_out,
    s_s, r_core, t_square, r_square, t_plane, r_plane, own, n_mine, n_all,
    send_c, recv_c, send_s, recv_s, send_z, recv_z, send_n, recv_n,
):
    planes = n // 8
    rows_dev = D // n
    me, core, square, plane = where_am_i(planes)
    in_plane = core + 2 * square
    a_of = [lax.rem(me + k, n) for k in range(1, n)]
    z_of = [lax.rem(plane + k, planes) * 8 + in_plane for k in range(1, planes)]
    s_of = [plane * 8 + lax.rem(square + k, 4) * 2 + core for k in range(1, 4)]
    c_of = plane * 8 + square * 2 + (1 - core)
    barrier = greet(a_of)

    used = 4 * D + 2 * H
    row = iota((used, 128), 0)
    lan = iota((used, 128), 1)
    row_dev = jnp.floor((row.astype(f32) + 0.5) * (1.0 / per_small)).astype(jnp.int32)
    sums = sums_in[...]
    small = jnp.concatenate(
        [
            sums[2 * D : 3 * D],
            sums[3 * D : 4 * D],
            sums[0:D],
            sums[D : 2 * D],
            sums[4 * D : 4 * D + H] * (32 ** (-0.5)),
            jnp.zeros((H, 128), f32),
        ],
        axis=0,
    )
    placed = jnp.where(lan == (row - per_small * row_dev), small, 0.0).astype(bf16)
    r_dev = iota((n, used), 0)
    r_row = iota((n, used), 1)
    mine = (r_row >= per_small * r_dev) & (r_row < per_small * r_dev + per_small)
    small_rows_out = nn(mine.astype(f32).astype(bf16), placed)
    to_flat_r = iota((32, 256), 0)
    to_flat_l = iota((32, 256), 1)
    lane_row = jnp.floor((to_flat_l.astype(f32) + 0.5) * (1.0 / (C + F))).astype(jnp.int32)
    to_flat = ((to_flat_l - (C + F) * lane_row == to_flat_r) & (to_flat_r < C + F)).astype(f32)
    spread_h = nn(ghead[...].astype(bf16), to_flat.astype(bf16))
    lr = iota((D, 256), 1)
    lr_row = jnp.floor((lr.astype(f32) + 0.5) * (1.0 / (C + F))).astype(jnp.int32)
    spread_h = jnp.where(lr_row == (iota((D, 256), 0) & (rows_dev - 1)), spread_h, 0.0)
    r8 = iota((8, 128), 0)
    for d in range(n):
        rows = slice(rows_dev * d, rows_dev * d + rows_dev)
        head_flat = jnp.sum(spread_h[rows], axis=0, keepdims=True)
        extra = jnp.where(
            r8 == 0,
            head_flat[:, :128],
            jnp.where(r8 == 1, head_flat[:, 128:], jnp.where(r8 == 2, small_rows_out[d : d + 1], 0.0)),
        )
        block = [gqkv[rows, 128 * k : 128 * k + 128] for k in range(6)]
        block += [gout[rows, 128 * k : 128 * k + 128] for k in range(2)]
        block += [extra, jnp.zeros((8, 128), f32)]
        s_s[place_of(d, planes)] = jnp.concatenate(block, axis=0).astype(bf16)

    pl.semaphore_wait(barrier, n - 1)

    def part(c, j, k):
        z = lax.rem(plane + k, planes)
        return c * (4 * planes) + lax.rem(square + j, 4) * planes + z

    done = []
    pieces = {}
    for j in (1, 2, 3, 0):
        line = pl.ds((1 - core) * (4 * planes) + lax.rem(square + j, 4) * planes, planes)
        pieces[j] = send(s_s.at[line], r_core.at[j], send_c.at[j], recv_c.at[j], c_of)
    for j in (1, 2, 3):
        pieces[j].wait_recv()
    order = [2, 1, 3, 0] if planes == 4 else list(range(1, planes)) + [0]
    crossing = {}
    for k in order:
        z = lax.rem(plane + k, planes)
        for j in range(1, 4):
            t_square[j - 1, k] = (
                s_s[part(core, j, k)].astype(f32) + r_core[j, z].astype(f32)
            ).astype(bf16)
            crossing[k, j] = send(
                t_square.at[j - 1, k], r_square.at[j - 1, k],
                send_s.at[j - 1, k], recv_s.at[j - 1, k], s_of[j - 1],
            )
    pieces[0].wait_recv()
    for k in order:
        z = lax.rem(plane + k, planes)
        own[k] = s_s[part(core, 0, k)].astype(f32) + r_core[0, z].astype(f32)
    along = {}
    for k in order:
        total = own[k]
        for j in range(1, 4):
            crossing[k, j].wait_recv()
            total = total + r_square[j - 1, k].astype(f32)
        if k:
            t_plane[k - 1] = total.astype(bf16)
            along[k] = send(
                t_plane.at[k - 1], r_plane.at[k - 1], send_z.at[k - 1], recv_z.at[k - 1], z_of[k - 1]
            )
    for k in range(1, planes):
        along[k].wait_recv()
        total = total + r_plane[k - 1].astype(f32)
    g_out[...] = total
    squares = jnp.sum(total * total, axis=0, keepdims=True)
    squares = squares + pltpu.roll(squares, 64, 1)
    losses = l_in[0:1, :]
    losses = losses + pltpu.roll(losses, 64, 1)
    n_mine[...] = jnp.where(iota((1, 128), 1) < 64, squares, losses)
    last = []
    for k in range(1, n):
        last.append(send(n_mine, n_all.at[k - 1], send_n.at[k - 1], recv_n.at[k - 1], a_of[k - 1]))
    total = n_mine[...]
    for k in range(1, n):
        last[k - 1].wait_recv()
        total = total + n_all[k - 1]
    t_out[...] = total
    for copies in (pieces, crossing, along):
        for copy in copies.values():
            copy.wait_send()
    for copy in last:
        copy.wait_send()


def reduce_call(n, per_small, *grads):
    planes = n // 8
    rows = 80
    vm = pl.BlockSpec(memory_space=pltpu.VMEM)
    dma = pltpu.SemaphoreType.DMA
    V = pltpu.VMEM
    z = planes - 1
    return pl.pallas_call(
        functools.partial(reduce_kernel, n, per_small),
        out_shape=(
            jax.ShapeDtypeStruct((rows, 128), f32),
            jax.ShapeDtypeStruct((1, 128), f32),
        ),
        in_specs=[vm] * 5,
        out_specs=(vm, vm),
        scratch_shapes=[
            V((n, rows, 128), bf16), V((4, planes, rows, 128), bf16), V((3, planes, rows, 128), bf16),
            V((3, planes, rows, 128), bf16), V((z, rows, 128), bf16), V((z, rows, 128), bf16),
            V((planes, rows, 128), f32), V((1, 128), f32), V((n - 1, 1, 128), f32),
            dma((4,)), dma((4,)), dma((3, planes)), dma((3, planes)), dma((z,)), dma((z,)),
            dma((n - 1,)), dma((n - 1,)),
        ],
        compiler_params=pltpu.CompilerParams(collective_id=1, has_side_effects=True),
    )(*grads)


def update_kernel(g, tot, *refs):
    weights, firsts, seconds = refs[0:4], refs[4:8], refs[8:12]
    new, first_o, second_o, copy_o = refs[12:16], refs[16:20], refs[20:24], refs[24:28]
    loss_o, norm_o, gq_s, go_s = refs[28:32]
    for c in range(6):
        gq_s[pl.ds(c, 8, stride=6), :] = g[8 * c : 8 * c + 8, :]
    for c in range(2):
        go_s[pl.ds(c, 8, stride=2), :] = g[48 + 8 * c : 56 + 8 * c, :]
    first_half = iota((1, 128), 1) < 64
    norm = jnp.sqrt(jnp.sum(jnp.where(first_half, tot[...], 0.0), axis=1, keepdims=True))
    loss_o[...] = jnp.sum(jnp.where(first_half, 0.0, tot[...]), axis=1, keepdims=True)
    norm_o[...] = norm
    factor = jnp.minimum(1.0, max_norm / (norm + 1e-06))
    per_head, per_small = weights[2].shape[1], weights[3].shape[1]
    grads = (
        gq_s[...],
        go_s[...],
        jnp.concatenate([g[64:65, :], g[65:66, : per_head - 128]], axis=1),
        g[66:67, :per_small],
    )
    for i in range(4):
        first_new, second_new, weight_new = adamw(
            weights[i][...], firsts[i][...], seconds[i][...], grads[i], factor, float(STEP), learn_rates[i]
        )
        new[i][...] = weight_new
        first_o[i][...] = first_new
        second_o[i][...] = second_new
        copy_o[i][...] = weight_new.astype(bf16)


def update_call(g, tot, weights, firsts, seconds):
    vm = pl.BlockSpec(memory_space=pltpu.VMEM)
    shapes = [w.shape for w in weights]
    outs = [jax.ShapeDtypeStruct(s, f32) for s in shapes] * 3
    outs += [jax.ShapeDtypeStruct(s, bf16) for s in shapes]
    outs += [jax.ShapeDtypeStruct((1, 1), f32)] * 2
    return pl.pallas_call(
        update_kernel,
        out_shape=tuple(outs),
        in_specs=[vm] * 14,
        out_specs=(vm,) * 18,
        scratch_shapes=[pltpu.VMEM((48, 128), f32), pltpu.VMEM((16, 128), f32)],
    )(g, tot, *weights, *firsts, *seconds)


def local_fast(
    n, query_feats, feature_mask, query_task, target_class, target_mask, memory_feats, memory_task,
    memory_mask, anneal, w_qkv, w_out, w_heads, w_small, m_qkv, m_out, m_heads, m_small,
    v_qkv, v_out, v_heads, v_small,
):
    def row(v):
        return v.reshape(1, -1)

    def tiles(v):
        return v.reshape(-1, 128)

    weights = (tiles(w_qkv), tiles(w_out), row(w_heads), row(w_small))
    firsts = (tiles(m_qkv), tiles(m_out), row(m_heads), row(m_small))
    seconds = (tiles(v_qkv), tiles(v_out), row(v_heads), row(v_small))
    tm, mt = row(target_mask), row(memory_task)
    gw, xs, fs, ct, posm, units = gather_call(
        n, *weights, memory_feats.T, query_feats.T, feature_mask.T, row(query_task),
        row(target_class), tm, mt, row(memory_mask),
    )
    found = step_call(n, mt.shape[1], w_small.shape[0] * n, xs, fs, ct, posm, units, anneal, gw)
    grads, totals = reduce_call(n, w_small.shape[0], *found)
    outs = update_call(grads, totals, weights, firsts, seconds)
    return tuple(out.reshape(-1) for out in outs)


def solution(mesh):
    placed = (
        P("mem", None),
        P("mem", None),
        P("mem"),
        P("mem"),
        P("mem"),
        P("mem", None),
        P(),
        P(),
        P(),
        P("mem"),
        P("mem"),
        P("mem"),
        P("mem"),
        P("mem"),
        P("mem"),
        P("mem"),
        P("mem"),
        P("mem"),
        P("mem"),
        P("mem"),
        P("mem"),
    )
    n = mesh.shape["mem"]

    def choose(*args):
        if D // n == 8 and args[6].shape[0] <= 4096:
            return local_fast(n, *args)
        return local(*args)

    return jax.shard_map(
        choose,
        mesh=mesh,
        in_specs=placed,
        out_specs=(
            P("mem"),
            P("mem"),
            P("mem"),
            P("mem"),
            P("mem"),
            P("mem"),
            P("mem"),
            P("mem"),
            P("mem"),
            P("mem"),
            P("mem"),
            P("mem"),
            P("mem"),
            P("mem"),
            P("mem"),
            P("mem"),
            P(),
            P(),
        ),
        check_vma=False,
    )
```

```python
import functools
import math

import jax
import jax.numpy as jnp
from jax import lax
from jax.experimental import pallas as pl
from jax.experimental.pallas import tpu as pltpu
from jax.sharding import PartitionSpec as P

F = 8
D = 256
H = 8
C = 16
TASKS = 4
STEP = 10


eps_norm = 1e-05
max_norm = 0.05
beta_one = 0.9
beta_two = 0.999
adam_eps = 1e-08
decay_rate = 0.01
learn_rates = (0.05, 1.0, 0.05, 0.5)
masked_score = -1e30


def embed(feature_rows, table_flat, emb_bias):
    emb_table = table_flat.reshape(feature_rows.shape[1], -1)
    return (feature_rows[:, :, None] * emb_table[None]).reshape(
        feature_rows.shape[0], -1
    ) + emb_bias


def standard(hidden):
    centred = hidden - jnp.mean(hidden, -1, keepdims=True)
    inverse = lax.rsqrt(jnp.mean(centred * centred, -1, keepdims=True) + eps_norm)
    return (centred * inverse, inverse)


def norm_back(grad_out, hidden, gain_vec):
    normed, inverse = standard(hidden)
    grad_gain = jnp.sum(grad_out * normed, 0)
    grad_scaled = grad_out * gain_vec
    grad_hidden = inverse * (
        grad_scaled
        - jnp.mean(grad_scaled, -1, keepdims=True)
        - normed * jnp.mean(grad_scaled * normed, -1, keepdims=True)
    )
    return (grad_hidden, grad_gain)


def split_pair(values):
    upper = values.astype(jnp.bfloat16)
    lower = (values - upper.astype(jnp.float32)).astype(jnp.bfloat16)
    return (upper, lower)


def adamw(weight, first_mom, second, grad_in, factor, step_num, step_rate):
    clipped = grad_in * factor
    first_new = beta_one * first_mom + (1 - beta_one) * clipped
    second_new = beta_two * second + (1 - beta_two) * clipped * clipped
    fix_one = 1 - beta_one**step_num
    fix_two = 1 - beta_two**step_num
    weight_new = weight - step_rate * (
        first_new / fix_one / (jnp.sqrt(second_new / fix_two) + adam_eps) + decay_rate * weight
    )
    return (first_new, second_new, weight_new)


def local(
    query_feats,
    feature_mask,
    query_task,
    target_class,
    target_mask,
    memory_feats,
    memory_task,
    memory_mask,
    anneal,
    w_qkv,
    w_out,
    w_heads,
    w_small,
    m_qkv,
    m_out,
    m_heads,
    m_small,
    v_qkv,
    v_out,
    v_heads,
    v_small,
):
    high = lax.Precision.HIGHEST
    head_size = D // H
    full_qkv, full_out, full_heads, full_small = (
        lax.all_gather(w_qkv, "mem", axis=0, tiled=True),
        lax.all_gather(w_out, "mem", axis=0, tiled=True),
        lax.all_gather(w_heads, "mem", axis=0, tiled=True),
        lax.all_gather(w_small, "mem", axis=0, tiled=True),
    )
    emb_table = full_small[:D]
    emb_bias = full_small[D : 2 * D]
    gain_in = full_small[2 * D : 3 * D]
    gain_out = full_small[3 * D : 4 * D]
    score_coef = full_small[4 * D : 4 * D + H] * head_size ** (-0.5)
    qkv_low = full_qkv.reshape(D, 3 * D).astype(jnp.bfloat16)
    out_low = full_out.reshape(D, D).astype(jnp.bfloat16)
    heads_low = full_heads.reshape(D, C + F).astype(jnp.bfloat16)
    mem_hidden = embed(memory_feats, emb_table, emb_bias)
    mem_normed = (standard(mem_hidden)[0] * gain_in).astype(jnp.bfloat16)
    mem_kv = jnp.dot(mem_normed, qkv_low[:, D:], preferred_element_type=jnp.float32).astype(
        jnp.bfloat16
    )
    all_kv = lax.all_gather(mem_kv, "mem", axis=0, tiled=True)
    memory_rows = all_kv.shape[0]
    block_keys = math.gcd(memory_rows, 512)
    num_blocks = memory_rows // block_keys
    key_rows = all_kv[:, :D].reshape(num_blocks, block_keys, H, head_size)
    value_rows = all_kv[:, D:].reshape(num_blocks, block_keys, H, head_size)
    task_blocks = memory_task.reshape(num_blocks, block_keys)
    live_blocks = memory_mask.reshape(num_blocks, block_keys)
    key_blocks = (key_rows, value_rows, task_blocks, live_blocks)
    kept_input = query_feats * (1 - feature_mask).astype(jnp.float32)
    hidden_in = embed(kept_input, emb_table, emb_bias)
    query_normed = (standard(hidden_in)[0] * gain_in).astype(jnp.bfloat16)
    queries = (
        jnp.dot(query_normed, qkv_low[:, :D], preferred_element_type=jnp.float32)
        .astype(jnp.bfloat16)
        .reshape(-1, H, head_size)
    )
    num_rows = queries.shape[0]

    def allowed_of(task_row, live_row):
        return ((query_task[:, None] == task_row[None, :]) & (live_row[None, :] > 0))[None]

    def scores_of(key_block, allowed):
        raw_scores = jnp.einsum(
            "qhd,khd->hqk", queries, key_block, preferred_element_type=jnp.float32
        )
        return (
            raw_scores,
            jnp.where(allowed, score_coef[:, None, None] * raw_scores, masked_score),
        )

    def stats_step(state_in, block_data):
        row_top, row_sum = state_in
        key_block, value_block, task_row, live_row = block_data
        allowed = allowed_of(task_row, live_row)
        scores = scores_of(key_block, allowed)[1]
        new_top = jnp.maximum(row_top, jnp.max(scores, -1))
        shifted = jnp.where(allowed, jnp.exp(scores - new_top[..., None]), 0.0)
        return ((new_top, row_sum * jnp.exp(row_top - new_top) + jnp.sum(shifted, -1)), None)

    start_state = (
        jnp.full((H, num_rows), masked_score, jnp.float32),
        jnp.zeros((H, num_rows), jnp.float32),
    )
    (row_top, row_sum), unused = lax.scan(stats_step, start_state, key_blocks)

    def probs_of(scores, allowed):
        return jnp.where(allowed, jnp.exp(scores - row_top[..., None]), 0.0) / row_sum[..., None]

    def value_step(accum, block_data):
        key_block, value_block, task_row, live_row = block_data
        allowed = allowed_of(task_row, live_row)
        probs_low = probs_of(scores_of(key_block, allowed)[1], allowed).astype(jnp.bfloat16)
        return (
            accum
            + jnp.einsum(
                "hqk,khd->qhd", probs_low, value_block, preferred_element_type=jnp.float32
            ),
            None,
        )

    attn_sum, unused = lax.scan(
        value_step, jnp.zeros((num_rows, H, head_size), jnp.float32), key_blocks
    )
    attended = attn_sum.reshape(num_rows, D).astype(jnp.bfloat16)
    residual = hidden_in + jnp.dot(attended, out_low, preferred_element_type=jnp.float32)
    final_normed = (standard(residual)[0] * gain_out).astype(jnp.bfloat16)
    head_out = jnp.dot(final_normed, heads_low, preferred_element_type=jnp.float32)
    logits = head_out[:, :C]
    recon_err = head_out[:, C:] - query_feats
    label_mask = target_mask.astype(jnp.float32)
    feat_mask = feature_mask.astype(jnp.float32)
    onehot_class = jax.nn.one_hot(target_class, C, dtype=jnp.float32)
    picked = jnp.sum(logits * onehot_class, -1)
    sum_target, sum_recon, count_target, count_recon = lax.psum(
        (
            jnp.sum(label_mask * (jax.nn.logsumexp(logits, -1) - picked)),
            jnp.sum(feat_mask * recon_err**2),
            jnp.sum(label_mask),
            jnp.sum(feat_mask),
        ),
        "mem",
    )
    count_target = jnp.maximum(count_target, 1.0)
    count_recon = jnp.maximum(count_recon, 1.0)
    weight_a = anneal[0]
    loss_value = weight_a * sum_target / count_target + (1 - weight_a) * sum_recon / count_recon
    grad_logits = (
        weight_a / count_target * label_mask[:, None] * (jax.nn.softmax(logits, -1) - onehot_class)
    )
    grad_recon = (1 - weight_a) / count_recon * feat_mask * 2.0 * recon_err
    grad_head_out = jnp.concatenate([grad_logits, grad_recon], 1).astype(jnp.bfloat16)
    grad_heads = jnp.dot(final_normed.T, grad_head_out, preferred_element_type=jnp.float32)
    grad_final = jnp.dot(grad_head_out, heads_low.T, preferred_element_type=jnp.float32)
    grad_resid, grad_gain_out = norm_back(grad_final, residual, gain_out)
    grad_branch = grad_resid.astype(jnp.bfloat16)
    grad_wout = jnp.dot(attended.T, grad_branch, preferred_element_type=jnp.float32)
    grad_attn = (
        jnp.dot(grad_branch, out_low.T, preferred_element_type=jnp.float32)
        .astype(jnp.bfloat16)
        .reshape(num_rows, H, head_size)
    )
    row_delta = jnp.sum(
        grad_attn.astype(jnp.float32)
        * attended.reshape(num_rows, H, head_size).astype(jnp.float32),
        -1,
    ).T

    def back_step(state_in, block_data):
        key_block, value_block, task_row, live_row = block_data
        allowed = allowed_of(task_row, live_row)
        raw_scores, scores = scores_of(key_block, allowed)
        soft_probs = probs_of(scores, allowed)
        grad_probs = jnp.einsum(
            "qhd,khd->hqk", grad_attn, value_block, preferred_element_type=jnp.float32
        )
        grad_scores = (soft_probs * (grad_probs - row_delta[..., None])).astype(jnp.bfloat16)
        grad_beta = jnp.sum(grad_scores.astype(jnp.float32) * raw_scores, (1, 2))
        grad_query = jnp.einsum(
            "hqk,khd->qhd", grad_scores, key_block, preferred_element_type=jnp.float32
        )
        grad_key = (
            jnp.einsum("hqk,qhd->khd", grad_scores, queries, preferred_element_type=jnp.float32)
            * score_coef[None, :, None]
        )
        grad_value = jnp.einsum(
            "hqk,qhd->khd",
            soft_probs.astype(jnp.bfloat16),
            grad_attn,
            preferred_element_type=jnp.float32,
        )
        block_rows = key_block.shape[0]
        grad_kv = jnp.concatenate(
            [grad_key.reshape(block_rows, D), grad_value.reshape(block_rows, D)], 1
        )
        return ((state_in[0] + grad_query, state_in[1] + grad_beta), grad_kv)

    init_state = (jnp.zeros((num_rows, H, head_size), jnp.float32), jnp.zeros((H,), jnp.float32))
    (grad_q_sum, grad_beta_sum), kv_parts = lax.scan(back_step, init_state, key_blocks)
    kv_grad = lax.psum_scatter(
        kv_parts.reshape(memory_rows, 2 * D), "mem", scatter_dimension=0, tiled=True
    )
    grad_q_low = (grad_q_sum * score_coef[None, :, None]).reshape(num_rows, D).astype(jnp.bfloat16)
    grad_wq = jnp.dot(query_normed.T, grad_q_low, preferred_element_type=jnp.float32)
    grad_qn = jnp.dot(grad_q_low, qkv_low[:, :D].T, preferred_element_type=jnp.float32)
    grad_in_q, gain_in_q = norm_back(grad_qn, hidden_in, gain_in)
    grad_hidden = grad_resid + grad_in_q
    kv_upper, kv_lower = split_pair(kv_grad)
    grad_wkv = jnp.dot(mem_normed.T, kv_upper, preferred_element_type=jnp.float32) + jnp.dot(
        mem_normed.T, kv_lower, preferred_element_type=jnp.float32
    )
    grad_mn = jnp.dot(kv_upper, qkv_low[:, D:].T, preferred_element_type=jnp.float32) + jnp.dot(
        kv_lower, qkv_low[:, D:].T, preferred_element_type=jnp.float32
    )
    grad_mem, gain_in_m = norm_back(grad_mn, mem_hidden, gain_in)
    grad_table = jnp.einsum(
        "qf,qfe->fe", kept_input, grad_hidden.reshape(num_rows, F, -1), precision=high
    )
    grad_table = grad_table + jnp.einsum(
        "qf,qfe->fe", memory_feats, grad_mem.reshape(memory_feats.shape[0], F, -1), precision=high
    )
    grad_bias = jnp.sum(grad_hidden, 0) + jnp.sum(grad_mem, 0)
    small_size = full_small.shape[0]
    grad_small = jnp.concatenate(
        [
            grad_table.reshape(-1),
            grad_bias,
            gain_in_q + gain_in_m,
            grad_gain_out,
            grad_beta_sum * head_size ** (-0.5),
            jnp.zeros((small_size - 4 * D - H,), jnp.float32),
        ]
    )
    grad_qkv = jnp.concatenate([grad_wq, grad_wkv], 1).reshape(-1)
    shards = (
        lax.psum_scatter(grad_qkv, "mem", scatter_dimension=0, tiled=True),
        lax.psum_scatter(grad_wout.reshape(-1), "mem", scatter_dimension=0, tiled=True),
        lax.psum_scatter(grad_heads.reshape(-1), "mem", scatter_dimension=0, tiled=True),
        lax.psum_scatter(grad_small, "mem", scatter_dimension=0, tiled=True),
    )
    local_squares = sum((jnp.sum(piece_grad * piece_grad) for piece_grad in shards))
    grad_total = jnp.sqrt(lax.psum(local_squares, "mem"))
    factor = jnp.minimum(1.0, max_norm / (grad_total + 1e-06))
    step_num = float(STEP)
    weights_all = (w_qkv, w_out, w_heads, w_small)
    firsts = (m_qkv, m_out, m_heads, m_small)
    seconds = (v_qkv, v_out, v_heads, v_small)
    results = [
        adamw(weight, first_mom, second, grad_in, factor, step_num, step_rate)
        for weight, first_mom, second, grad_in, step_rate in zip(
            weights_all, firsts, seconds, shards, learn_rates
        )
    ]
    new_w = [entry[2] for entry in results]
    return (
        new_w[0],
        new_w[1],
        new_w[2],
        new_w[3],
        results[0][0],
        results[1][0],
        results[2][0],
        results[3][0],
        results[0][1],
        results[1][1],
        results[2][1],
        results[3][1],
        new_w[0].astype(jnp.bfloat16),
        new_w[1].astype(jnp.bfloat16),
        new_w[2].astype(jnp.bfloat16),
        new_w[3].astype(jnp.bfloat16),
        loss_value.reshape(1),
        grad_total.reshape(1),
    )


f32 = jnp.float32
bf16 = jnp.bfloat16
LOG2E = math.log2(math.e)
QB = 128
KC = 384
KC_LOW = 320
VROWS = 80
E_CAP = 16
SMALL_LANE = 88
COUNT_LANE = 122


def place_of(dev, planes):
    return (dev % 2) * (4 * planes) + ((dev // 2) % 4) * planes + dev // 8


def nt(a, b):
    return lax.dot_general(a, b, (((1,), (1,)), ((), ())), preferred_element_type=f32)


def tn(a, b):
    return lax.dot_general(a, b, (((0,), (0,)), ((), ())), preferred_element_type=f32)


def nn(a, b):
    return jnp.dot(a, b, preferred_element_type=f32)


def iota(shape, dim):
    return lax.broadcasted_iota(jnp.int32, shape, dim)


def split2(v):
    hi = v.astype(bf16).astype(f32)
    return hi, v - hi


def split3(v):
    hi, rest = split2(v)
    mid = rest.astype(bf16).astype(f32)
    return hi, mid, rest - mid


def wide(v, lanes):
    return jnp.concatenate([v] * (lanes // v.shape[1]), axis=1) if lanes > v.shape[1] else v


def embed_t(kept, table, bias):
    parts = []
    for f in range(F):
        rows = slice(32 * f, 32 * f + 32)
        parts.append(kept[f : f + 1] * table[rows] + bias[rows])
    return jnp.concatenate(parts, axis=0)


def norm_t(v):
    centred = v - jnp.mean(v, axis=0, keepdims=True)
    inverse = lax.rsqrt(jnp.mean(centred * centred, axis=0, keepdims=True) + eps_norm)
    return centred * inverse, inverse


def norm_back_t(grad, normed, inverse, gain):
    scaled = grad * gain
    return inverse * (
        scaled
        - jnp.mean(scaled, axis=0, keepdims=True)
        - normed * jnp.mean(scaled * normed, axis=0, keepdims=True)
    )


def blocks_of(num_q):
    blocks = (num_q + TASKS * (QB - 1)) // QB
    return -(-blocks // 4) * 4


def chunks_of(num_mem):
    chunks = (num_mem + TASKS * (KC - 1)) // KC
    return chunks + chunks % 2


def step_kernel(
    n, qs, num_mem, small_size,
    xs, fs, ct, posb, table, units, an, gw,
    gqkv, gout, ghead, out_sums, out_l,
    w_s, wt_s, wh_s, wht_s,
    cols, coefb,
    mfeat, kn, vn, kt_s, vt_s, mnt, gk, gv,
    qn_s, q_s, att, il_s, gres, fn_s, gho_s, gb_s, dap, delta, dq_s,
    ebuf, ecur, acc, m_s, acc_gain,
    blk_c0, blk_nc, blk_tile, blk_rows, ch_base, ch_end,
):
    planes = n // 8
    per_small = small_size // n
    k_chunks = ch_base.shape[0]

    m_base = [units[t] for t in range(TASKS)]
    m_count = [units[TASKS + t] for t in range(TASKS)]
    m_units = [units[2 * TASKS + t] for t in range(TASKS)]
    q_base = [units[3 * TASKS + t] for t in range(TASKS)]
    q_units = [units[4 * TASKS + t] for t in range(TASKS)]
    num_blocks = q_units[0] + q_units[1] + q_units[2] + q_units[3]
    num_chunks = m_units[0] + m_units[1] + m_units[2] + m_units[3]
    for c in range(k_chunks):
        ch_base[c] = jnp.int32(c * KC)
        ch_end[c] = jnp.int32(c * KC)
    tile = jnp.int32(0)
    for t in range(TASKS):
        first_chunk = lax.div(m_base[t], jnp.int32(KC))
        first_block = lax.div(q_base[t], jnp.int32(QB))

        def fill_chunk(i, carry, t=t, first_chunk=first_chunk):
            ch_base[first_chunk + i] = m_base[t]
            ch_end[first_chunk + i] = m_base[t] + m_count[t]
            return carry

        lax.fori_loop(0, m_units[t], fill_chunk, 0)

        def fill_block(i, tile_in, t=t, first_chunk=first_chunk, first_block=first_block):
            blk_c0[first_block + i] = first_chunk
            blk_nc[first_block + i] = m_units[t]
            blk_rows[first_block + i] = m_count[t]
            blk_tile[first_block + i] = tile_in
            return tile_in + m_units[t]

        tile = lax.fori_loop(0, q_units[t], fill_block, tile)

    pieces = [gw[place_of(d, planes)].astype(f32) for d in range(n)]
    for col in range(8):
        block = jnp.concatenate([piece[8 * col : 8 * col + 8] for piece in pieces], axis=0)
        w_s[:, 128 * col : 128 * col + 128] = block.astype(bf16)
        wt_s[128 * col : 128 * col + 128, :] = block.T.astype(bf16)
    lane = iota((8, 128), 1)
    tiles = [piece[64:72] + piece[72:80] for piece in pieces]
    lane_w = iota((D, 128), 1)
    heads = pltpu.roll(jnp.concatenate(tiles, axis=0), 64, 1)
    heads = jnp.where(lane_w < C + F, heads, 0.0)
    wh_s[...] = heads.astype(bf16)
    wht_s[...] = heads.T[:32].astype(bf16)

    small_rows = jnp.concatenate([tile[0:1] for tile in tiles], axis=0)
    lane_n = iota((n, 128), 1)
    count_t = jnp.maximum(jnp.sum(jnp.where(lane_n == COUNT_LANE, small_rows, 0.0)), 1.0)
    count_r = jnp.maximum(jnp.sum(jnp.where(lane_n == COUNT_LANE + 1, small_rows, 0.0)), 1.0)
    used = 4 * D + 2 * H
    s2 = jnp.concatenate(
        list(split2(small_rows)) + [jnp.zeros((128 - 2 * n, 128), f32)], axis=0
    ).astype(bf16)
    row = iota((used, 128), 0)
    lan = iota((used, 128), 1)
    dev_of = lan & (n - 1)
    pick = (row >= per_small * dev_of) & (row < per_small * dev_of + per_small) & (lan < 2 * n)
    spread = nn(pick.astype(f32).astype(bf16), s2)
    row_dev = jnp.floor((row.astype(f32) + 0.5) * (1.0 / per_small)).astype(jnp.int32)
    here = (lan - SMALL_LANE) == (row - per_small * row_dev)
    column = jnp.sum(jnp.where(here, spread, 0.0), axis=1, keepdims=True)
    cols[...] = jnp.broadcast_to(column[: 4 * D], (4 * D, 128))
    for h in range(H):
        coefb[32 * h : 32 * h + 32, :] = jnp.broadcast_to(
            column[4 * D + h : 4 * D + h + 1] * (32 ** (-0.5)), (32, 128)
        )

    emb_w = lambda lanes: wide(cols[0:D, :], lanes)
    emb_b = lambda lanes: wide(cols[D : 2 * D, :], lanes)
    gain_in = lambda lanes: wide(cols[2 * D : 3 * D, :], lanes)
    gain_out = lambda lanes: wide(cols[3 * D : 4 * D, :], lanes)

    for b in range(n // 2):
        raw = jnp.where(lane < 64, tiles[2 * b], pltpu.roll(tiles[2 * b + 1], 64, 1))
        chosen = (posb[:, 128 * b : 128 * b + 128] == iota((128, 1), 0).astype(f32)).astype(f32)
        got = nt(jnp.concatenate(split2(raw), axis=0).astype(bf16), chosen.astype(bf16))
        run = got[0:8] + got[8:16]
        for t in range(TASKS):
            i = 8 * b + t
            start, count, slot = table[0, i], table[1, i], table[2, i]
            first = slot & 127
            shift = (first - start) & 127
            moved = pltpu.roll(run, shift, 1)
            at = pl.multiple_of(slot - first, 128)
            pltpu.store(
                mfeat.at[:, pl.ds(at, 128)], moved, mask=(lane >= first) & (lane < first + count)
            )
            pltpu.store(mfeat.at[:, pl.ds(at + 128, 128)], moved, mask=lane < first + count - 128)

    def mem_feats(c):
        base, end = ch_base[c], ch_end[c]
        at = pl.ds(pl.multiple_of(c * KC, KC), KC)
        slot = iota((8, KC), 1) + c * KC
        head = mfeat[:, pl.ds(pl.multiple_of(base, KC), 128)][:, 0:1]
        live = (slot < end).astype(f32)[0:1]
        return jnp.where(slot < end, mfeat[:, at], jnp.where(end > base, head, 0.0)), live

    def mem_pair(i, carry):
        found = []
        for k in range(2):
            c = 2 * i + k
            feats_c, live = mem_feats(c)
            normed, unused = norm_t(embed_t(feats_c, emb_w(KC), emb_b(KC)))
            mnf = normed * gain_in(KC)
            mn = mnf.astype(bf16)
            keys_t = (nn(wt_s[D : 2 * D, :], mn) * live).astype(bf16)
            vals_t = nn(wt_s[2 * D : 3 * D, :], mn) * live
            tail = jnp.where(iota((16, KC), 0) == 0, live, 0.0)
            vals_t = jnp.concatenate(
                [part for p in range(4) for part in (vals_t[64 * p : 64 * p + 64], tail)], axis=0
            ).astype(bf16)
            both = nn(mnf.T.astype(bf16), w_s[:, D : 3 * D])
            live_col = ((iota((KC, 1), 0) + c * KC) < ch_end[c]).astype(f32)
            found.append((mn, keys_t, vals_t, both[:, :D], both[:, D:] * live_col))
        for k in range(2):
            at = pl.ds(pl.multiple_of((2 * i + k) * KC, KC), KC)
            mnt[:, at], kt_s[:, at], vt_s[:, at] = found[k][0:3]
            kn[at, :] = found[k][3].astype(bf16)
            vn[at, :] = found[k][4].astype(bf16)
            gk[at, :] = jnp.zeros((KC, D), f32)
            gv[at, :] = jnp.zeros((KC, D), f32)
        return carry

    lax.fori_loop(0, lax.div(num_chunks + 1, jnp.int32(2)), mem_pair, 0)

    def spots(j):
        return [pl.ds(pl.multiple_of(j * 512 + 256 * k, 256), 256) for k in range(2)]

    def pre_block(j, carry):
        found = []
        for at in spots(j):
            kept = xs[:, at] * (1.0 - fs[:, at])
            normed, unused = norm_t(embed_t(kept, emb_w(256), emb_b(256)))
            qn = (normed * gain_in(256)).astype(bf16)
            found.append((qn, nn(wt_s[0:D, :], qn).astype(bf16)))
        for k, at in enumerate(spots(j)):
            qn_s[:, at], q_s[:, at] = found[k]
            att[:, at] = jnp.zeros((D, 256), bf16)
            il_s[:, at] = jnp.zeros((H, 256), f32)
            dq_s[:, at] = jnp.zeros((D, 256), f32)
        return carry

    lax.fori_loop(0, qs // 512, pre_block, 0)

    zero_h = jnp.zeros((32, 128), bf16)
    zero_p = jnp.zeros((64, 256), bf16)

    def pair(p, width):
        return slice(width * p, width * p + width)

    def half(p):
        return slice(128 * (p // 2), 128 * (p // 2) + 128)

    def two_heads(ref, at, p):
        diag = jnp.concatenate(
            [
                jnp.concatenate([ref[64 * p : 64 * p + 32, at], zero_h], axis=1),
                jnp.concatenate([zero_h, ref[64 * p + 32 : 64 * p + 64, at]], axis=1),
            ],
            axis=0,
        )
        return jnp.concatenate([zero_p, diag] if p % 2 else [diag, zero_p], axis=0)

    def coef_row(p):
        return LOG2E * jnp.concatenate(
            [coefb[64 * p : 64 * p + 1, :], coefb[64 * p + 32 : 64 * p + 33, :]], axis=1
        )

    def finish_forward(at, p, got):
        inverse = 1.0 / got[64:65, :]
        il_s[2 * p : 2 * p + 1, at] = inverse[:, :128]
        il_s[2 * p + 1 : 2 * p + 2, at] = inverse[:, 128:]
        att[64 * p : 64 * p + 32, at] = (got[0:32, :128] * inverse[:, :128]).astype(bf16)
        att[64 * p + 32 : 64 * p + 64, at] = (got[32:64, 128:] * inverse[:, 128:]).astype(bf16)

    def forward_block(i, carry):
        at = pl.ds(pl.multiple_of(i * QB, QB), QB)
        c0, nc, tile0, count = blk_c0[i], blk_nc[i], blk_tile[i], blk_rows[i]

        def one(rows):
            keys = pl.ds(pl.multiple_of(c0 * KC, KC), rows)
            keep = jnp.minimum(tile0, E_CAP)
            operands = [two_heads(q_s, at, p) for p in range(4)]
            values = [vt_s[pair(p, VROWS), pl.ds(pl.multiple_of(c0 * KC, KC), KC)][:, :rows] for p in range(4)]
            scores = [nn(kn[keys, half(p)], operands[p]) * coef_row(p) for p in range(4)]
            tops = [jnp.max(s, axis=0, keepdims=True) for s in scores]
            es = [jnp.exp2(scores[p] - tops[p]).astype(bf16) for p in range(4)]
            sums = [nn(values[p], es[p]) for p in range(4)]
            for p in range(4):
                m_s[i, :, pair(p, 256)] = tops[p]
                ebuf[keep, :rows, pair(p, 256)] = es[p]
                finish_forward(at, p, sums[p])

        @pl.when(count <= KC_LOW)
        def few():
            one(KC_LOW)

        @pl.when((count > KC_LOW) & (nc == 1))
        def full():
            one(KC)

        @pl.when(nc > 1)
        def many():
            m_s[i] = jnp.full((1, 1024), -3e38, f32)
            acc[...] = jnp.zeros_like(acc)

            def tops(c, inner):
                keys = pl.ds(pl.multiple_of((c0 + c) * KC, KC), KC)
                for p in range(4):
                    s = nn(kn[keys, half(p)], two_heads(q_s, at, p)) * coef_row(p)
                    m_s[i, :, pair(p, 256)] = jnp.maximum(
                        m_s[i, :, pair(p, 256)], jnp.max(s, axis=0, keepdims=True)
                    )
                return inner

            lax.fori_loop(0, nc, tops, 0)

            def sums(c, inner):
                keys = pl.ds(pl.multiple_of((c0 + c) * KC, KC), KC)
                keep = jnp.minimum(tile0 + c, E_CAP)
                for p in range(4):
                    s = nn(kn[keys, half(p)], two_heads(q_s, at, p)) * coef_row(p)
                    e = jnp.exp2(s - m_s[i, :, pair(p, 256)]).astype(bf16)
                    ebuf[keep, :, pair(p, 256)] = e
                    acc[pair(p, VROWS), :] += nn(vt_s[pair(p, VROWS), keys], e)
                return inner

            lax.fori_loop(0, nc, sums, 0)
            for p in range(4):
                finish_forward(at, p, acc[pair(p, VROWS), :])

        return carry

    lax.fori_loop(0, num_blocks, forward_block, 0)

    weight_a = an[0]
    scale_t = weight_a / count_t
    scale_r = (1.0 - weight_a) / count_r
    acc_gain[...] = jnp.zeros_like(acc_gain)
    out_l[...] = jnp.zeros_like(out_l)

    def fold(v):
        total = v[:, :128]
        for k in range(1, v.shape[1] // 128):
            total = total + v[:, 128 * k : 128 * k + 128]
        return total

    def mid_values(at):
        x = xs[:, at]
        fmask = fs[:, at]
        hidden = embed_t(x * (1.0 - fmask), emb_w(256), emb_b(256))
        attended = att[:, at]
        residual = hidden + nn(wt_s[3 * D : 4 * D, :], attended)
        normed, inverse = norm_t(residual)
        fn = (normed * gain_out(256)).astype(bf16)
        head = nn(wht_s[...], fn)
        logits = head[0:C]
        err = head[C : C + F] - x
        label = ct[1:2, at]
        hot = (iota((C, 256), 0).astype(f32) == ct[0:1, at]).astype(f32)
        top = jnp.max(logits, axis=0, keepdims=True)
        e = jnp.exp(logits - top)
        total = jnp.sum(e, axis=0, keepdims=True)
        picked = jnp.sum(logits * hot, axis=0, keepdims=True)
        loss = scale_t * label * (jnp.log(total) + top - picked) + scale_r * jnp.sum(
            fmask * err * err, axis=0, keepdims=True
        )
        g_log = scale_t * label * (e / total - hot)
        g_rec = scale_r * fmask * 2.0 * err
        gho = jnp.concatenate([g_log, g_rec, jnp.zeros((8, 256), f32)], axis=0).astype(bf16)
        g_final = nn(wh_s[:, :32], gho)
        g_res = norm_back_t(g_final, normed, inverse, gain_out(256))
        gb = g_res.astype(bf16)
        ga = nn(w_s[:, 3 * D : 4 * D], gb).astype(bf16).astype(f32)
        attf = attended.astype(f32)
        das, deltas = [], []
        for h in range(H):
            rows = slice(32 * h, 32 * h + 32)
            da = (ga[rows] * il_s[h : h + 1, at]).astype(bf16)
            das.append(da)
            deltas.append(jnp.sum(da.astype(f32) * attf[rows], axis=0, keepdims=True))
        return (
            fold(loss), fold(g_final * normed),
            fn, gho, g_res, gb, jnp.concatenate(das, axis=0), jnp.concatenate(deltas, axis=0),
        )

    def mid_block(j, carry):
        found = [mid_values(at) for at in spots(j)]
        out_l[0:1, :] += found[0][0] + found[1][0]
        acc_gain[D : 2 * D, :] += found[0][1] + found[1][1]
        for k, at in enumerate(spots(j)):
            for ref, value in zip((fn_s, gho_s, gres, gb_s, dap, delta), found[k][2:]):
                ref[:, at] = value
        return carry

    lax.fori_loop(0, qs // 512, mid_block, 0)

    def backward_chunk(at, c, rows, e_of):
        keys = pl.ds(pl.multiple_of(c * KC, KC), rows)
        lanes = pl.ds(pl.multiple_of(c * KC, KC), KC)
        es = [e_of(p) for p in range(4)]
        das = [two_heads(dap, at, p) for p in range(4)]
        qds = [two_heads(q_s, at, p) for p in range(4)]
        deltas = delta[:, at]
        kts = [kt_s[64 * p : 64 * p + 64, lanes][:, :rows] for p in range(4)]
        old_dq = dq_s[:, at]
        old_gk = gk[keys, :]
        old_gv = gv[keys, :]
        dps = [nn(vn[keys, half(p)], das[p]) for p in range(4)]
        dss = []
        for p in range(4):
            take = jnp.concatenate([deltas[2 * p : 2 * p + 1], deltas[2 * p + 1 : 2 * p + 2]], axis=1)
            dss.append((es[p].astype(f32) * (dps[p] - take)).astype(bf16))
        dqs = [nn(kts[p], dss[p]) for p in range(4)]

        def by_key(grads, others):
            return jnp.concatenate(
                [
                    nt(
                        jnp.concatenate([grads[a], grads[a + 1]], axis=1),
                        jnp.concatenate([others[a], others[a + 1]], axis=1),
                    )
                    for a in (0, 2)
                ],
                axis=1,
            )

        new_gv = old_gv + by_key(es, das)
        new_gk = old_gk + by_key(dss, qds)
        parts = []
        for p in range(4):
            parts += [dqs[p][0:32, :128], dqs[p][32:64, 128:]]
        dq_s[:, at] = old_dq + jnp.concatenate(parts, axis=0)
        gk[keys, :] = new_gk
        gv[keys, :] = new_gv

    def backward_block(i, carry):
        at = pl.ds(pl.multiple_of(i * QB, QB), QB)
        c0, nc, tile0, count = blk_c0[i], blk_nc[i], blk_tile[i], blk_rows[i]
        simple = (nc == 1) & (tile0 < E_CAP)

        @pl.when(simple & (count <= KC_LOW))
        def few():
            backward_chunk(at, c0, KC_LOW, lambda p: ebuf[tile0, :KC_LOW, pair(p, 256)])

        @pl.when(simple & (count > KC_LOW))
        def full():
            backward_chunk(at, c0, KC, lambda p: ebuf[tile0, :, pair(p, 256)])

        @pl.when(jnp.logical_not(simple))
        def many():
            def one_chunk(c, inner):
                keys = pl.ds(pl.multiple_of((c0 + c) * KC, KC), KC)

                @pl.when((tile0 + c < E_CAP) & (nc > 1))
                def kept():
                    ecur[...] = ebuf[tile0 + c]

                @pl.when((tile0 + c >= E_CAP) | (nc == 1))
                def again():
                    for p in range(4):
                        s = nn(kn[keys, half(p)], two_heads(q_s, at, p)) * coef_row(p)
                        ecur[:, pair(p, 256)] = jnp.exp2(
                            s - m_s[i, :, pair(p, 256)]
                        ).astype(bf16)

                backward_chunk(at, c0 + c, KC, lambda p: ecur[:, pair(p, 256)])
                return inner

            lax.fori_loop(0, nc, one_chunk, 0)

        return carry

    lax.fori_loop(0, num_blocks, backward_block, 0)

    def by_feature(grad, kept):
        return jnp.concatenate(
            [kept[f : f + 1] * grad[32 * f : 32 * f + 32] for f in range(F)], axis=0
        )

    coef2 = wide(coefb[...], 256)

    def post_values(at):
        kept = xs[:, at] * (1.0 - fs[:, at])
        normed, inverse = norm_t(embed_t(kept, emb_w(256), emb_b(256)))
        dq = dq_s[:, at]
        gq = (dq * coef2).astype(bf16)
        prod = fold(dq * q_s[:, at].astype(f32))
        betas = jnp.concatenate(
            [jnp.sum(prod[32 * h : 32 * h + 32], axis=0, keepdims=True) for h in range(H)], axis=0
        )
        gqn = nn(w_s[:, 0:D], gq)
        gh = gres[:, at] + norm_back_t(gqn, normed, inverse, gain_in(256))
        return gq, betas, fold(gqn * normed), fold(by_feature(gh, kept)), fold(gh)

    def post_block(j, carry):
        cuts = spots(j)
        found = [post_values(at) for at in cuts]
        qn = jnp.concatenate([qn_s[:, at] for at in cuts], axis=1)
        gq = jnp.concatenate([found[0][0], found[1][0]], axis=1)
        gqkv[:, 0:D] += nt(qn, gq)
        for k, rows in ((1, slice(4 * D, 4 * D + H)), (2, slice(0, D)), (3, slice(2 * D, 3 * D)), (4, slice(3 * D, 4 * D))):
            acc_gain[rows, :] += found[0][k] + found[1][k]
        return carry

    gqkv[...] = jnp.zeros_like(gqkv)
    lax.fori_loop(0, qs // 512, post_block, 0)
    gout[...] = nt(att[...], gb_s[...])
    ghead[...] = nt(fn_s[...], gho_s[...])

    def mem_back(i, coef_lane):
        found = []
        for k in range(2):
            c = 2 * i + k
            at = pl.ds(pl.multiple_of(c * KC, KC), KC)
            feats_c, unused = mem_feats(c)
            live = ((iota((KC, 1), 0) + c * KC) < ch_end[c]).astype(f32)
            gk_c = (gk[at, :] * coef_lane * live).astype(bf16)
            gv_c = (gv[at, :] * live).astype(bf16)
            gmn = nt(w_s[:, D : 2 * D], gk_c) + nt(w_s[:, 2 * D : 3 * D], gv_c)
            normed, inverse = norm_t(embed_t(feats_c, emb_w(KC), emb_b(KC)))
            gm = norm_back_t(gmn, normed, inverse, gain_in(KC))
            found.append((gk_c, gv_c, fold(gmn * normed), fold(by_feature(gm, feats_c)), fold(gm)))
        mn = mnt[:, pl.ds(pl.multiple_of(2 * i * KC, KC), 2 * KC)]
        gqkv[:, D : 2 * D] += nn(mn, jnp.concatenate([found[0][0], found[1][0]], axis=0))
        gqkv[:, 2 * D : 3 * D] += nn(mn, jnp.concatenate([found[0][1], found[1][1]], axis=0))
        for k, rows in ((2, slice(0, D)), (3, slice(2 * D, 3 * D)), (4, slice(3 * D, 4 * D))):
            acc_gain[rows, :] += found[0][k] + found[1][k]
        return coef_lane

    coef_lane = jnp.concatenate([coefb[0:128, :].T[0:1], coefb[128:256, :].T[0:1]], axis=1)
    lax.fori_loop(0, lax.div(num_chunks + 1, jnp.int32(2)), mem_back, coef_lane)

    out_sums[...] = jnp.broadcast_to(
        jnp.sum(acc_gain[...], axis=1, keepdims=True), (4 * D + H, 128)
    )


def step_call(n, num_mem, small_size, xs, fs, ct, posb, table, units, an, gw):
    qs = xs.shape[1]
    q_blocks, k_chunks = qs // QB, chunks_of(num_mem)
    ks = k_chunks * KC
    V = pltpu.VMEM
    S = pltpu.SMEM
    vm = pl.BlockSpec(memory_space=pltpu.VMEM)
    sm = pl.BlockSpec(memory_space=pltpu.SMEM)
    scratch = [
        V((D, 4 * D), bf16), V((4 * D, D), bf16), V((D, 128), bf16), V((32, D), bf16),
        V((4 * D, 128), f32), V((D, 128), f32),
        V((8, ks + 128), f32), V((ks, D), bf16), V((ks, D), bf16), V((D, ks), bf16),
        V((4 * VROWS, ks), bf16), V((D, ks), bf16), V((ks, D), f32), V((ks, D), f32),
        V((D, qs), bf16), V((D, qs), bf16), V((D, qs), bf16), V((H, qs), f32), V((D, qs), f32),
        V((D, qs), bf16), V((32, qs), bf16), V((D, qs), bf16), V((D, qs), bf16), V((H, qs), f32),
        V((D, qs), f32),
        V((E_CAP + 1, KC, 1024), bf16), V((KC, 1024), bf16), V((4 * VROWS, 256), f32),
        V((q_blocks, 1, 1024), f32), V((4 * D + H, 128), f32),
        S((q_blocks,), jnp.int32), S((q_blocks,), jnp.int32), S((q_blocks,), jnp.int32),
        S((q_blocks,), jnp.int32), S((k_chunks,), jnp.int32), S((k_chunks,), jnp.int32),
    ]
    return pl.pallas_call(
        functools.partial(step_kernel, n, qs, num_mem, small_size),
        out_shape=(
            jax.ShapeDtypeStruct((D, 3 * D), f32),
            jax.ShapeDtypeStruct((D, D), f32),
            jax.ShapeDtypeStruct((D, 32), f32),
            jax.ShapeDtypeStruct((4 * D + H, 128), f32),
            jax.ShapeDtypeStruct((8, 128), f32),
        ),
        in_specs=[vm] * 4 + [sm] * 3 + [vm],
        out_specs=(vm,) * 5,
        scratch_shapes=scratch,
        compiler_params=pltpu.CompilerParams(vmem_limit_bytes=58 * 1024 * 1024),
    )(xs, fs, ct, posb, table, units, an, gw)


MESH = pl.DeviceIdType.MESH


def greet(targets):
    barrier = pltpu.get_barrier_semaphore()
    for target in targets:
        pl.semaphore_signal(barrier, inc=1, device_id=(target,), device_id_type=MESH)
    return barrier


def send(src, dst, send_sem, recv_sem, target):
    copy = pltpu.make_async_remote_copy(
        src_ref=src,
        dst_ref=dst,
        send_sem=send_sem,
        recv_sem=recv_sem,
        device_id=(target,),
        device_id_type=MESH,
    )
    copy.start()
    return copy


def where_am_i(planes):
    me = lax.axis_index("mem")
    core = lax.rem(me, 2)
    square = lax.rem(lax.div(me, 2), 4)
    plane = lax.div(me, 8)
    return me, core, square, plane


def gather_kernel(
    n, num_q, num_mem, w_qkv, w_out, w_heads, w_small, mfeat, qf, fm, qt, tc, tm, mt, mm,
    gw, xs, fs, ct, posb, table, units_out,
    send_z, recv_z, send_s, recv_s, send_c, recv_c,
):
    planes = n // 8
    me, core, square, plane = where_am_i(planes)
    in_plane = core + 2 * square
    z_of = [lax.rem(plane + k, planes) * 8 + in_plane for k in range(1, planes)]
    s_of = [plane * 8 + lax.rem(square + k, 4) * 2 + core for k in range(1, 4)]
    c_of = plane * 8 + square * 2 + (1 - core)
    barrier = greet(z_of + s_of + [c_of])

    rows = []
    for c in range(6):
        rows.append(w_qkv[pl.ds(c, 8, stride=6), :])
    for c in range(2):
        rows.append(w_out[pl.ds(c, 8, stride=2), :])
    per_head = w_heads.shape[1]
    lane = iota((8, 256), 1)
    head_row = jnp.concatenate([w_heads[...], jnp.zeros((1, 256 - per_head), f32)], axis=1)
    owner = jnp.floor((lane.astype(f32) + 0.5) * (1.0 / (C + F))).astype(jnp.int32)
    kept_heads = jnp.where(owner == iota((8, 256), 0), head_row, 0.0).astype(bf16)
    fold_r = iota((256, 128), 0)
    fold_row = jnp.floor((fold_r.astype(f32) + 0.5) * (1.0 / (C + F))).astype(jnp.int32)
    fold_m = (fold_r - (C + F) * fold_row == iota((256, 128), 1) - 64).astype(f32).astype(bf16)
    heads = nn(kept_heads, fold_m)
    per_small = w_small.shape[1]
    small = jnp.concatenate([w_small[...], jnp.zeros((1, 128 - per_small), f32)], axis=1)
    small = pltpu.roll(jnp.broadcast_to(small, (8, 128)), SMALL_LANE, 1)
    feats = jnp.concatenate([mfeat[...], jnp.zeros((8, 64), f32)], axis=1)
    lane8 = iota((8, 128), 1)
    row8 = iota((8, 128), 0)
    num_t = jnp.sum(tm[...].astype(f32), axis=1, keepdims=True)
    num_r = jnp.sum(jnp.sum(fm[...].astype(f32), axis=0, keepdims=True), axis=1, keepdims=True)
    block = feats + heads
    first = (row8 == 0) & (lane8 >= SMALL_LANE) & (lane8 < SMALL_LANE + per_small)
    block = jnp.where(first, small, block)
    block = jnp.where((row8 == 0) & (lane8 == COUNT_LANE), num_t, block)
    block = jnp.where((row8 == 0) & (lane8 == COUNT_LANE + 1), num_r, block)

    def slot_of(k, j, c):
        back = lax.rem(plane + planes - k, planes)
        return c * (4 * planes) + lax.rem(square + 4 - j, 4) * planes + back

    gw[slot_of(0, 0, core)] = jnp.concatenate(rows + list(split2(block)), axis=0).astype(bf16)

    pl.semaphore_wait(barrier, planes - 1 + 4)

    def spread(k, done):
        at = gw.at[slot_of(k, 0, core)]
        for j in range(1, 4):
            done[k, j] = send(at, at, send_s.at[k, j - 1], recv_s.at[k, j - 1], s_of[j - 1])
        done[k, 0, "c"] = send(at, at, send_c.at[k, 0], recv_c.at[k, 0], c_of)

    at = gw.at[slot_of(0, 0, core)]
    done = {}
    for k in range(1, planes):
        done[k] = send(at, at, send_z.at[k - 1], recv_z.at[k - 1], z_of[k - 1])
    spread(0, done)

    task_row = iota((8, 256), 0)
    marks = [(qt[:, 256 * b : 256 * b + 256] == task_row).astype(f32) for b in range(num_q // 256)]
    marks_q = jnp.concatenate(marks, axis=0)
    before = (iota((256, 256), 0) < iota((256, 256), 1)).astype(f32).astype(bf16)
    ranks = nn(marks_q.astype(bf16), before)
    totals = jnp.sum(marks_q, axis=1, keepdims=True)
    task_col = iota((8, 1), 0)

    def bases_of(sums, unit):
        base = jnp.int32(0)
        bases, counts, used = [], [], []
        base_vec = jnp.zeros((8, 1), f32)
        for t in range(TASKS):
            count = jnp.sum(jnp.where(task_col == t, sums, 0.0)).astype(jnp.int32)
            bases.append(base)
            counts.append(count)
            used.append(lax.div(count + (unit - 1), jnp.int32(unit)))
            base_vec = base_vec + jnp.where(task_col == t, base.astype(f32), 0.0)
            base = base + used[t] * unit
        return bases, counts, used, base_vec

    carry = jnp.zeros((8, 1), f32)
    carries = []
    for b in range(num_q // 256):
        carries.append(carry)
        carry = carry + totals[8 * b : 8 * b + 8]
    q_base, q_count, q_units, base_vec = bases_of(carry, QB)
    place_q = jnp.concatenate(
        [
            jnp.sum(marks[b] * (base_vec + carries[b] + ranks[8 * b : 8 * b + 8]), axis=0, keepdims=True)
            for b in range(num_q // 256)
        ],
        axis=1,
    )

    cuts = num_mem // 128
    task_row = iota((8, 128), 0)
    marks = []
    for b in range(cuts):
        cut = slice(128 * b, 128 * b + 128)
        marks.append(((mt[:, cut] == task_row) & (mm[:, cut] > 0)).astype(f32))
    marks_m = jnp.concatenate(marks, axis=0)
    ranks = nn(marks_m.astype(bf16), before[:128, :128])
    totals = jnp.broadcast_to(jnp.sum(marks_m, axis=1, keepdims=True), (8 * cuts, 128))
    r_to = iota((8 * cuts, 8 * cuts), 0)
    r_from = iota((8 * cuts, 8 * cuts), 1)
    same_cut = (r_to // 8 == r_from // 8) & (r_from < r_to)
    same_task = (r_to % 8 == r_from % 8) & (r_from < r_to)
    low_totals = totals.astype(bf16)
    starts = nn(same_cut.astype(f32).astype(bf16), low_totals)
    earlier = nn(same_task.astype(f32).astype(bf16), low_totals)
    last = slice(8 * cuts - 8, 8 * cuts)
    m_base, m_count, m_units, base_vec = bases_of((earlier + totals)[last, 0:1], KC)
    slots = earlier + jnp.concatenate([base_vec] * cuts, axis=0)
    posb[...] = jnp.concatenate(
        [
            jnp.sum(marks[b] * (starts[8 * b : 8 * b + 8] + ranks[8 * b : 8 * b + 8] + 1.0), axis=0, keepdims=True)
            - 1.0
            for b in range(cuts)
        ],
        axis=1,
    )
    eye = r_to == r_from

    def as_row(column):
        return jnp.sum(jnp.where(eye, wide(column, 8 * cuts), 0.0), axis=0, keepdims=True)

    row_t = iota((8, 8 * cuts), 0)
    table[...] = jnp.where(
        row_t == 0, as_row(starts), jnp.where(row_t == 1, as_row(totals), as_row(slots))
    ).astype(jnp.int32)
    for t in range(TASKS):
        units_out[t] = m_base[t]
        units_out[TASKS + t] = m_count[t]
        units_out[2 * TASKS + t] = m_units[t]
        units_out[3 * TASKS + t] = q_base[t]
        units_out[4 * TASKS + t] = q_units[t]
    qs = xs.shape[1]
    xq = qf[...]
    fmq = fm[...].astype(f32)
    row8 = iota((8, num_q), 0)
    label_rows = jnp.where(
        row8 == 0, tc[...].astype(f32), jnp.where(row8 == 1, tm[...].astype(f32), 0.0)
    )
    q_rows = jnp.concatenate(
        list(split3(xq)) + [fmq, label_rows, jnp.zeros((8, num_q), f32)], axis=0
    ).astype(bf16)
    for b in range(qs // 256):
        chosen = (
            (place_q == (iota((256, 1), 0) + 256 * b).astype(f32)).astype(f32).astype(bf16)
        )
        got = nt(q_rows, chosen)
        cut = slice(256 * b, 256 * b + 256)
        xs[:, cut] = got[0:8] + got[8:16] + got[16:24]
        fs[:, cut] = got[24:32]
        ct[:, cut] = got[32:40]


    for k in range(1, planes):
        done[k].wait_recv()
        spread(k, done)
    for k in range(planes):
        for j in range(1, 4):
            done[k, j].wait_recv()
            at = gw.at[slot_of(k, j, core)]
            done[k, j, "c"] = send(at, at, send_c.at[k, j], recv_c.at[k, j], c_of)
    for k in range(planes):
        for j in range(4):
            done[k, j, "c"].wait_recv()
    for copy in done.values():
        copy.wait_send()


def gather_call(n, w_qkv, w_out, w_heads, w_small, mfeat, qf, fm, qt, tc, tm, mt, mm):
    planes = n // 8
    num_q, num_mem = qf.shape[1], mt.shape[1]
    qs = blocks_of(num_q) * QB
    vm = pl.BlockSpec(memory_space=pltpu.VMEM)
    dma = pltpu.SemaphoreType.DMA
    return pl.pallas_call(
        functools.partial(gather_kernel, n, num_q, num_mem),
        out_shape=(
            jax.ShapeDtypeStruct((n, 80, 128), bf16),
            jax.ShapeDtypeStruct((8, qs), f32),
            jax.ShapeDtypeStruct((8, qs), f32),
            jax.ShapeDtypeStruct((8, qs), f32),
            jax.ShapeDtypeStruct((1, num_mem), f32),
            jax.ShapeDtypeStruct((8, num_mem // 16), jnp.int32),
            jax.ShapeDtypeStruct((5 * TASKS,), jnp.int32),
        ),
        in_specs=[vm] * 12,
        out_specs=(vm,) * 6 + (pl.BlockSpec(memory_space=pltpu.SMEM),),
        scratch_shapes=[
            dma((planes - 1,)), dma((planes - 1,)), dma((planes, 3)), dma((planes, 3)),
            dma((planes, 4)), dma((planes, 4)),
        ],
        compiler_params=pltpu.CompilerParams(collective_id=0, has_side_effects=True),
    )(w_qkv, w_out, w_heads, w_small, mfeat, qf, fm, qt, tc, tm, mt, mm)


def reduce_kernel(
    n, per_small, gqkv, gout, ghead, sums_in, l_in, g_out, t_out,
    s_s, r_core, t_square, r_square, t_plane, r_plane, own, n_mine, n_all,
    send_c, recv_c, send_s, recv_s, send_z, recv_z, send_n, recv_n,
):
    planes = n // 8
    rows_dev = D // n
    me, core, square, plane = where_am_i(planes)
    in_plane = core + 2 * square
    a_of = [lax.rem(me + k, n) for k in range(1, n)]
    z_of = [lax.rem(plane + k, planes) * 8 + in_plane for k in range(1, planes)]
    s_of = [plane * 8 + lax.rem(square + k, 4) * 2 + core for k in range(1, 4)]
    c_of = plane * 8 + square * 2 + (1 - core)
    barrier = greet(a_of)

    used = 4 * D + 2 * H
    row = iota((used, 128), 0)
    lan = iota((used, 128), 1)
    row_dev = jnp.floor((row.astype(f32) + 0.5) * (1.0 / per_small)).astype(jnp.int32)
    sums = sums_in[...]
    small = jnp.concatenate(
        [
            sums[2 * D : 3 * D],
            sums[3 * D : 4 * D],
            sums[0:D],
            sums[D : 2 * D],
            sums[4 * D : 4 * D + H] * (32 ** (-0.5)),
            jnp.zeros((H, 128), f32),
        ],
        axis=0,
    )
    placed = jnp.where(lan == (row - per_small * row_dev), small, 0.0).astype(bf16)
    r_dev = iota((n, used), 0)
    r_row = iota((n, used), 1)
    mine = (r_row >= per_small * r_dev) & (r_row < per_small * r_dev + per_small)
    small_rows_out = nn(mine.astype(f32).astype(bf16), placed)
    to_flat_r = iota((32, 256), 0)
    to_flat_l = iota((32, 256), 1)
    lane_row = jnp.floor((to_flat_l.astype(f32) + 0.5) * (1.0 / (C + F))).astype(jnp.int32)
    to_flat = ((to_flat_l - (C + F) * lane_row == to_flat_r) & (to_flat_r < C + F)).astype(f32)
    spread_h = nn(ghead[...].astype(bf16), to_flat.astype(bf16))
    lr = iota((D, 256), 1)
    lr_row = jnp.floor((lr.astype(f32) + 0.5) * (1.0 / (C + F))).astype(jnp.int32)
    spread_h = jnp.where(lr_row == (iota((D, 256), 0) & (rows_dev - 1)), spread_h, 0.0)
    r8 = iota((8, 128), 0)
    for d in range(n):
        rows = slice(rows_dev * d, rows_dev * d + rows_dev)
        head_flat = jnp.sum(spread_h[rows], axis=0, keepdims=True)
        extra = jnp.where(
            r8 == 0,
            head_flat[:, :128],
            jnp.where(r8 == 1, head_flat[:, 128:], jnp.where(r8 == 2, small_rows_out[d : d + 1], 0.0)),
        )
        block = [gqkv[rows, 128 * k : 128 * k + 128] for k in range(6)]
        block += [gout[rows, 128 * k : 128 * k + 128] for k in range(2)]
        block += [extra, jnp.zeros((8, 128), f32)]
        s_s[place_of(d, planes)] = jnp.concatenate(block, axis=0).astype(bf16)

    pl.semaphore_wait(barrier, n - 1)

    def part(c, j, k):
        z = lax.rem(plane + k, planes)
        return c * (4 * planes) + lax.rem(square + j, 4) * planes + z

    done = []
    pieces = {}
    for j in (1, 2, 3, 0):
        line = pl.ds((1 - core) * (4 * planes) + lax.rem(square + j, 4) * planes, planes)
        pieces[j] = send(s_s.at[line], r_core.at[j], send_c.at[j], recv_c.at[j], c_of)
    for j in (1, 2, 3):
        pieces[j].wait_recv()
    order = [2, 1, 3, 0] if planes == 4 else list(range(1, planes)) + [0]
    crossing = {}
    for k in order:
        z = lax.rem(plane + k, planes)
        for j in range(1, 4):
            t_square[j - 1, k] = (
                s_s[part(core, j, k)].astype(f32) + r_core[j, z].astype(f32)
            ).astype(bf16)
            crossing[k, j] = send(
                t_square.at[j - 1, k], r_square.at[j - 1, k],
                send_s.at[j - 1, k], recv_s.at[j - 1, k], s_of[j - 1],
            )
    pieces[0].wait_recv()
    for k in order:
        z = lax.rem(plane + k, planes)
        own[k] = s_s[part(core, 0, k)].astype(f32) + r_core[0, z].astype(f32)
    along = {}
    for k in order:
        total = own[k]
        for j in range(1, 4):
            crossing[k, j].wait_recv()
            total = total + r_square[j - 1, k].astype(f32)
        if k:
            t_plane[k - 1] = total.astype(bf16)
            along[k] = send(
                t_plane.at[k - 1], r_plane.at[k - 1], send_z.at[k - 1], recv_z.at[k - 1], z_of[k - 1]
            )
    for k in range(1, planes):
        along[k].wait_recv()
        total = total + r_plane[k - 1].astype(f32)
    g_out[...] = total
    squares = jnp.sum(total * total, axis=0, keepdims=True)
    squares = squares + pltpu.roll(squares, 64, 1)
    losses = l_in[0:1, :]
    losses = losses + pltpu.roll(losses, 64, 1)
    n_mine[...] = jnp.where(iota((1, 128), 1) < 64, squares, losses)
    last = []
    for k in range(1, n):
        last.append(send(n_mine, n_all.at[k - 1], send_n.at[k - 1], recv_n.at[k - 1], a_of[k - 1]))
    total = n_mine[...]
    for k in range(1, n):
        last[k - 1].wait_recv()
        total = total + n_all[k - 1]
    t_out[...] = total
    for copies in (pieces, crossing, along):
        for copy in copies.values():
            copy.wait_send()
    for copy in last:
        copy.wait_send()


def reduce_call(n, per_small, *grads):
    planes = n // 8
    rows = 80
    vm = pl.BlockSpec(memory_space=pltpu.VMEM)
    dma = pltpu.SemaphoreType.DMA
    V = pltpu.VMEM
    z = planes - 1
    return pl.pallas_call(
        functools.partial(reduce_kernel, n, per_small),
        out_shape=(
            jax.ShapeDtypeStruct((rows, 128), f32),
            jax.ShapeDtypeStruct((1, 128), f32),
        ),
        in_specs=[vm] * 5,
        out_specs=(vm, vm),
        scratch_shapes=[
            V((n, rows, 128), bf16), V((4, planes, rows, 128), bf16), V((3, planes, rows, 128), bf16),
            V((3, planes, rows, 128), bf16), V((z, rows, 128), bf16), V((z, rows, 128), bf16),
            V((planes, rows, 128), f32), V((1, 128), f32), V((n - 1, 1, 128), f32),
            dma((4,)), dma((4,)), dma((3, planes)), dma((3, planes)), dma((z,)), dma((z,)),
            dma((n - 1,)), dma((n - 1,)),
        ],
        compiler_params=pltpu.CompilerParams(collective_id=1, has_side_effects=True),
    )(*grads)


def update_kernel(g, tot, *refs):
    weights, firsts, seconds = refs[0:4], refs[4:8], refs[8:12]
    new, first_o, second_o = refs[12:16], refs[16:20], refs[20:24]
    copy_o = (refs[24], refs[25], None, refs[26])
    loss_o, norm_o, gq_s, go_s = refs[27:31]
    for c in range(6):
        gq_s[pl.ds(c, 8, stride=6), :] = g[8 * c : 8 * c + 8, :]
    for c in range(2):
        go_s[pl.ds(c, 8, stride=2), :] = g[48 + 8 * c : 56 + 8 * c, :]
    first_half = iota((1, 128), 1) < 64
    norm = jnp.sqrt(jnp.sum(jnp.where(first_half, tot[...], 0.0), axis=1, keepdims=True))
    loss_o[...] = jnp.sum(jnp.where(first_half, 0.0, tot[...]), axis=1, keepdims=True)
    norm_o[...] = norm
    factor = jnp.minimum(1.0, max_norm / (norm + 1e-06))
    per_head, per_small = weights[2].shape[1], weights[3].shape[1]
    grads = (
        gq_s[...],
        go_s[...],
        jnp.concatenate([g[64:65, :], g[65:66, : per_head - 128]], axis=1),
        g[66:67, :per_small],
    )
    for i in range(4):
        first_new, second_new, weight_new = adamw(
            weights[i][...], firsts[i][...], seconds[i][...], grads[i], factor, float(STEP), learn_rates[i]
        )
        new[i][...] = weight_new
        first_o[i][...] = first_new
        second_o[i][...] = second_new
        if copy_o[i] is not None:
            copy_o[i][...] = weight_new.astype(bf16)


def update_call(g, tot, weights, firsts, seconds):
    vm = pl.BlockSpec(memory_space=pltpu.VMEM)
    shapes = [w.shape for w in weights]
    outs = [jax.ShapeDtypeStruct(s, f32) for s in shapes] * 3
    outs += [jax.ShapeDtypeStruct(s, bf16) for s in shapes[:2] + shapes[3:]]
    outs += [jax.ShapeDtypeStruct((1, 1), f32)] * 2
    return pl.pallas_call(
        update_kernel,
        out_shape=tuple(outs),
        in_specs=[vm] * 14,
        out_specs=(vm,) * 17,
        scratch_shapes=[pltpu.VMEM((48, 128), f32), pltpu.VMEM((16, 128), f32)],
    )(g, tot, *weights, *firsts, *seconds)


def local_fast(
    n, query_feats, feature_mask, query_task, target_class, target_mask, memory_feats, memory_task,
    memory_mask, anneal, w_qkv, w_out, w_heads, w_small, m_qkv, m_out, m_heads, m_small,
    v_qkv, v_out, v_heads, v_small,
):
    def row(v):
        return v.reshape(1, -1)

    def tiles(v):
        return v.reshape(-1, 128)

    weights = (tiles(w_qkv), tiles(w_out), row(w_heads), row(w_small))
    firsts = (tiles(m_qkv), tiles(m_out), row(m_heads), row(m_small))
    seconds = (tiles(v_qkv), tiles(v_out), row(v_heads), row(v_small))
    tm, mt = row(target_mask), row(memory_task)
    gw, xs, fs, ct, posb, table, units = gather_call(
        n, *weights, memory_feats.T, query_feats.T, feature_mask.T, row(query_task),
        row(target_class), tm, mt, row(memory_mask),
    )
    found = step_call(n, mt.shape[1], w_small.shape[0] * n, xs, fs, ct, posb, table, units, anneal, gw)
    grads, totals = reduce_call(n, w_small.shape[0], *found)
    outs = update_call(grads, totals, weights, firsts, seconds)
    outs = [out.reshape(-1) for out in outs]
    return tuple(outs[:14] + [outs[2].astype(bf16)] + outs[14:])


def solution(mesh):
    placed = (
        P("mem", None),
        P("mem", None),
        P("mem"),
        P("mem"),
        P("mem"),
        P("mem", None),
        P(),
        P(),
        P(),
        P("mem"),
        P("mem"),
        P("mem"),
        P("mem"),
        P("mem"),
        P("mem"),
        P("mem"),
        P("mem"),
        P("mem"),
        P("mem"),
        P("mem"),
        P("mem"),
    )
    n = mesh.shape["mem"]

    def choose(*args):
        if D // n == 8 and args[6].shape[0] <= 4096:
            return local_fast(n, *args)
        return local(*args)

    return jax.shard_map(
        choose,
        mesh=mesh,
        in_specs=placed,
        out_specs=(
            P("mem"),
            P("mem"),
            P("mem"),
            P("mem"),
            P("mem"),
            P("mem"),
            P("mem"),
            P("mem"),
            P("mem"),
            P("mem"),
            P("mem"),
            P("mem"),
            P("mem"),
            P("mem"),
            P("mem"),
            P("mem"),
            P(),
            P(),
        ),
        check_vma=False,
    )
```

```python
import functools
import math

import jax
import jax.numpy as jnp
from jax import lax
from jax.experimental import pallas as pl
from jax.experimental.pallas import tpu as pltpu
from jax.sharding import PartitionSpec as P

F = 8
D = 256
H = 8
C = 16
TASKS = 4
STEP = 10


eps_norm = 1e-05
max_norm = 0.05
beta_one = 0.9
beta_two = 0.999
adam_eps = 1e-08
decay_rate = 0.01
learn_rates = (0.05, 1.0, 0.05, 0.5)
masked_score = -1e30


def embed(feature_rows, table_flat, emb_bias):
    emb_table = table_flat.reshape(feature_rows.shape[1], -1)
    return (feature_rows[:, :, None] * emb_table[None]).reshape(
        feature_rows.shape[0], -1
    ) + emb_bias


def standard(hidden):
    centred = hidden - jnp.mean(hidden, -1, keepdims=True)
    inverse = lax.rsqrt(jnp.mean(centred * centred, -1, keepdims=True) + eps_norm)
    return (centred * inverse, inverse)


def norm_back(grad_out, hidden, gain_vec):
    normed, inverse = standard(hidden)
    grad_gain = jnp.sum(grad_out * normed, 0)
    grad_scaled = grad_out * gain_vec
    grad_hidden = inverse * (
        grad_scaled
        - jnp.mean(grad_scaled, -1, keepdims=True)
        - normed * jnp.mean(grad_scaled * normed, -1, keepdims=True)
    )
    return (grad_hidden, grad_gain)


def split_pair(values):
    upper = values.astype(jnp.bfloat16)
    lower = (values - upper.astype(jnp.float32)).astype(jnp.bfloat16)
    return (upper, lower)


def adamw(weight, first_mom, second, grad_in, factor, step_num, step_rate):
    clipped = grad_in * factor
    first_new = beta_one * first_mom + (1 - beta_one) * clipped
    second_new = beta_two * second + (1 - beta_two) * clipped * clipped
    fix_one = 1 - beta_one**step_num
    fix_two = 1 - beta_two**step_num
    weight_new = weight - step_rate * (
        first_new / fix_one / (jnp.sqrt(second_new / fix_two) + adam_eps) + decay_rate * weight
    )
    return (first_new, second_new, weight_new)


def local(
    query_feats,
    feature_mask,
    query_task,
    target_class,
    target_mask,
    memory_feats,
    memory_task,
    memory_mask,
    anneal,
    w_qkv,
    w_out,
    w_heads,
    w_small,
    m_qkv,
    m_out,
    m_heads,
    m_small,
    v_qkv,
    v_out,
    v_heads,
    v_small,
):
    high = lax.Precision.HIGHEST
    head_size = D // H
    full_qkv, full_out, full_heads, full_small = (
        lax.all_gather(w_qkv, "mem", axis=0, tiled=True),
        lax.all_gather(w_out, "mem", axis=0, tiled=True),
        lax.all_gather(w_heads, "mem", axis=0, tiled=True),
        lax.all_gather(w_small, "mem", axis=0, tiled=True),
    )
    emb_table = full_small[:D]
    emb_bias = full_small[D : 2 * D]
    gain_in = full_small[2 * D : 3 * D]
    gain_out = full_small[3 * D : 4 * D]
    score_coef = full_small[4 * D : 4 * D + H] * head_size ** (-0.5)
    qkv_low = full_qkv.reshape(D, 3 * D).astype(jnp.bfloat16)
    out_low = full_out.reshape(D, D).astype(jnp.bfloat16)
    heads_low = full_heads.reshape(D, C + F).astype(jnp.bfloat16)
    mem_hidden = embed(memory_feats, emb_table, emb_bias)
    mem_normed = (standard(mem_hidden)[0] * gain_in).astype(jnp.bfloat16)
    mem_kv = jnp.dot(mem_normed, qkv_low[:, D:], preferred_element_type=jnp.float32).astype(
        jnp.bfloat16
    )
    all_kv = lax.all_gather(mem_kv, "mem", axis=0, tiled=True)
    memory_rows = all_kv.shape[0]
    block_keys = math.gcd(memory_rows, 512)
    num_blocks = memory_rows // block_keys
    key_rows = all_kv[:, :D].reshape(num_blocks, block_keys, H, head_size)
    value_rows = all_kv[:, D:].reshape(num_blocks, block_keys, H, head_size)
    task_blocks = memory_task.reshape(num_blocks, block_keys)
    live_blocks = memory_mask.reshape(num_blocks, block_keys)
    key_blocks = (key_rows, value_rows, task_blocks, live_blocks)
    kept_input = query_feats * (1 - feature_mask).astype(jnp.float32)
    hidden_in = embed(kept_input, emb_table, emb_bias)
    query_normed = (standard(hidden_in)[0] * gain_in).astype(jnp.bfloat16)
    queries = (
        jnp.dot(query_normed, qkv_low[:, :D], preferred_element_type=jnp.float32)
        .astype(jnp.bfloat16)
        .reshape(-1, H, head_size)
    )
    num_rows = queries.shape[0]

    def allowed_of(task_row, live_row):
        return ((query_task[:, None] == task_row[None, :]) & (live_row[None, :] > 0))[None]

    def scores_of(key_block, allowed):
        raw_scores = jnp.einsum(
            "qhd,khd->hqk", queries, key_block, preferred_element_type=jnp.float32
        )
        return (
            raw_scores,
            jnp.where(allowed, score_coef[:, None, None] * raw_scores, masked_score),
        )

    def stats_step(state_in, block_data):
        row_top, row_sum = state_in
        key_block, value_block, task_row, live_row = block_data
        allowed = allowed_of(task_row, live_row)
        scores = scores_of(key_block, allowed)[1]
        new_top = jnp.maximum(row_top, jnp.max(scores, -1))
        shifted = jnp.where(allowed, jnp.exp(scores - new_top[..., None]), 0.0)
        return ((new_top, row_sum * jnp.exp(row_top - new_top) + jnp.sum(shifted, -1)), None)

    start_state = (
        jnp.full((H, num_rows), masked_score, jnp.float32),
        jnp.zeros((H, num_rows), jnp.float32),
    )
    (row_top, row_sum), unused = lax.scan(stats_step, start_state, key_blocks)

    def probs_of(scores, allowed):
        return jnp.where(allowed, jnp.exp(scores - row_top[..., None]), 0.0) / row_sum[..., None]

    def value_step(accum, block_data):
        key_block, value_block, task_row, live_row = block_data
        allowed = allowed_of(task_row, live_row)
        probs_low = probs_of(scores_of(key_block, allowed)[1], allowed).astype(jnp.bfloat16)
        return (
            accum
            + jnp.einsum(
                "hqk,khd->qhd", probs_low, value_block, preferred_element_type=jnp.float32
            ),
            None,
        )

    attn_sum, unused = lax.scan(
        value_step, jnp.zeros((num_rows, H, head_size), jnp.float32), key_blocks
    )
    attended = attn_sum.reshape(num_rows, D).astype(jnp.bfloat16)
    residual = hidden_in + jnp.dot(attended, out_low, preferred_element_type=jnp.float32)
    final_normed = (standard(residual)[0] * gain_out).astype(jnp.bfloat16)
    head_out = jnp.dot(final_normed, heads_low, preferred_element_type=jnp.float32)
    logits = head_out[:, :C]
    recon_err = head_out[:, C:] - query_feats
    label_mask = target_mask.astype(jnp.float32)
    feat_mask = feature_mask.astype(jnp.float32)
    onehot_class = jax.nn.one_hot(target_class, C, dtype=jnp.float32)
    picked = jnp.sum(logits * onehot_class, -1)
    sum_target, sum_recon, count_target, count_recon = lax.psum(
        (
            jnp.sum(label_mask * (jax.nn.logsumexp(logits, -1) - picked)),
            jnp.sum(feat_mask * recon_err**2),
            jnp.sum(label_mask),
            jnp.sum(feat_mask),
        ),
        "mem",
    )
    count_target = jnp.maximum(count_target, 1.0)
    count_recon = jnp.maximum(count_recon, 1.0)
    weight_a = anneal[0]
    loss_value = weight_a * sum_target / count_target + (1 - weight_a) * sum_recon / count_recon
    grad_logits = (
        weight_a / count_target * label_mask[:, None] * (jax.nn.softmax(logits, -1) - onehot_class)
    )
    grad_recon = (1 - weight_a) / count_recon * feat_mask * 2.0 * recon_err
    grad_head_out = jnp.concatenate([grad_logits, grad_recon], 1).astype(jnp.bfloat16)
    grad_heads = jnp.dot(final_normed.T, grad_head_out, preferred_element_type=jnp.float32)
    grad_final = jnp.dot(grad_head_out, heads_low.T, preferred_element_type=jnp.float32)
    grad_resid, grad_gain_out = norm_back(grad_final, residual, gain_out)
    grad_branch = grad_resid.astype(jnp.bfloat16)
    grad_wout = jnp.dot(attended.T, grad_branch, preferred_element_type=jnp.float32)
    grad_attn = (
        jnp.dot(grad_branch, out_low.T, preferred_element_type=jnp.float32)
        .astype(jnp.bfloat16)
        .reshape(num_rows, H, head_size)
    )
    row_delta = jnp.sum(
        grad_attn.astype(jnp.float32)
        * attended.reshape(num_rows, H, head_size).astype(jnp.float32),
        -1,
    ).T

    def back_step(state_in, block_data):
        key_block, value_block, task_row, live_row = block_data
        allowed = allowed_of(task_row, live_row)
        raw_scores, scores = scores_of(key_block, allowed)
        soft_probs = probs_of(scores, allowed)
        grad_probs = jnp.einsum(
            "qhd,khd->hqk", grad_attn, value_block, preferred_element_type=jnp.float32
        )
        grad_scores = (soft_probs * (grad_probs - row_delta[..., None])).astype(jnp.bfloat16)
        grad_beta = jnp.sum(grad_scores.astype(jnp.float32) * raw_scores, (1, 2))
        grad_query = jnp.einsum(
            "hqk,khd->qhd", grad_scores, key_block, preferred_element_type=jnp.float32
        )
        grad_key = (
            jnp.einsum("hqk,qhd->khd", grad_scores, queries, preferred_element_type=jnp.float32)
            * score_coef[None, :, None]
        )
        grad_value = jnp.einsum(
            "hqk,qhd->khd",
            soft_probs.astype(jnp.bfloat16),
            grad_attn,
            preferred_element_type=jnp.float32,
        )
        block_rows = key_block.shape[0]
        grad_kv = jnp.concatenate(
            [grad_key.reshape(block_rows, D), grad_value.reshape(block_rows, D)], 1
        )
        return ((state_in[0] + grad_query, state_in[1] + grad_beta), grad_kv)

    init_state = (jnp.zeros((num_rows, H, head_size), jnp.float32), jnp.zeros((H,), jnp.float32))
    (grad_q_sum, grad_beta_sum), kv_parts = lax.scan(back_step, init_state, key_blocks)
    kv_grad = lax.psum_scatter(
        kv_parts.reshape(memory_rows, 2 * D), "mem", scatter_dimension=0, tiled=True
    )
    grad_q_low = (grad_q_sum * score_coef[None, :, None]).reshape(num_rows, D).astype(jnp.bfloat16)
    grad_wq = jnp.dot(query_normed.T, grad_q_low, preferred_element_type=jnp.float32)
    grad_qn = jnp.dot(grad_q_low, qkv_low[:, :D].T, preferred_element_type=jnp.float32)
    grad_in_q, gain_in_q = norm_back(grad_qn, hidden_in, gain_in)
    grad_hidden = grad_resid + grad_in_q
    kv_upper, kv_lower = split_pair(kv_grad)
    grad_wkv = jnp.dot(mem_normed.T, kv_upper, preferred_element_type=jnp.float32) + jnp.dot(
        mem_normed.T, kv_lower, preferred_element_type=jnp.float32
    )
    grad_mn = jnp.dot(kv_upper, qkv_low[:, D:].T, preferred_element_type=jnp.float32) + jnp.dot(
        kv_lower, qkv_low[:, D:].T, preferred_element_type=jnp.float32
    )
    grad_mem, gain_in_m = norm_back(grad_mn, mem_hidden, gain_in)
    grad_table = jnp.einsum(
        "qf,qfe->fe", kept_input, grad_hidden.reshape(num_rows, F, -1), precision=high
    )
    grad_table = grad_table + jnp.einsum(
        "qf,qfe->fe", memory_feats, grad_mem.reshape(memory_feats.shape[0], F, -1), precision=high
    )
    grad_bias = jnp.sum(grad_hidden, 0) + jnp.sum(grad_mem, 0)
    small_size = full_small.shape[0]
    grad_small = jnp.concatenate(
        [
            grad_table.reshape(-1),
            grad_bias,
            gain_in_q + gain_in_m,
            grad_gain_out,
            grad_beta_sum * head_size ** (-0.5),
            jnp.zeros((small_size - 4 * D - H,), jnp.float32),
        ]
    )
    grad_qkv = jnp.concatenate([grad_wq, grad_wkv], 1).reshape(-1)
    shards = (
        lax.psum_scatter(grad_qkv, "mem", scatter_dimension=0, tiled=True),
        lax.psum_scatter(grad_wout.reshape(-1), "mem", scatter_dimension=0, tiled=True),
        lax.psum_scatter(grad_heads.reshape(-1), "mem", scatter_dimension=0, tiled=True),
        lax.psum_scatter(grad_small, "mem", scatter_dimension=0, tiled=True),
    )
    local_squares = sum((jnp.sum(piece_grad * piece_grad) for piece_grad in shards))
    grad_total = jnp.sqrt(lax.psum(local_squares, "mem"))
    factor = jnp.minimum(1.0, max_norm / (grad_total + 1e-06))
    step_num = float(STEP)
    weights_all = (w_qkv, w_out, w_heads, w_small)
    firsts = (m_qkv, m_out, m_heads, m_small)
    seconds = (v_qkv, v_out, v_heads, v_small)
    results = [
        adamw(weight, first_mom, second, grad_in, factor, step_num, step_rate)
        for weight, first_mom, second, grad_in, step_rate in zip(
            weights_all, firsts, seconds, shards, learn_rates
        )
    ]
    new_w = [entry[2] for entry in results]
    return (
        new_w[0],
        new_w[1],
        new_w[2],
        new_w[3],
        results[0][0],
        results[1][0],
        results[2][0],
        results[3][0],
        results[0][1],
        results[1][1],
        results[2][1],
        results[3][1],
        new_w[0].astype(jnp.bfloat16),
        new_w[1].astype(jnp.bfloat16),
        new_w[2].astype(jnp.bfloat16),
        new_w[3].astype(jnp.bfloat16),
        loss_value.reshape(1),
        grad_total.reshape(1),
    )


f32 = jnp.float32
bf16 = jnp.bfloat16
LOG2E = math.log2(math.e)
QB = 128
KC = 384
KC_LOW = 320
VROWS = 80
E_CAP = 12
STEP_VMEM = 40 * 1024 * 1024
SMALL_LANE = 88
COUNT_LANE = 122


def place_of(dev, planes):
    return (dev % 2) * (4 * planes) + ((dev // 2) % 4) * planes + dev // 8


def nt(a, b):
    return lax.dot_general(a, b, (((1,), (1,)), ((), ())), preferred_element_type=f32)


def tn(a, b):
    return lax.dot_general(a, b, (((0,), (0,)), ((), ())), preferred_element_type=f32)


def nn(a, b):
    return jnp.dot(a, b, preferred_element_type=f32)


def iota(shape, dim):
    return lax.broadcasted_iota(jnp.int32, shape, dim)


def split2(v):
    hi = v.astype(bf16).astype(f32)
    return hi, v - hi


def split3(v):
    hi, rest = split2(v)
    mid = rest.astype(bf16).astype(f32)
    return hi, mid, rest - mid


def wide(v, lanes):
    return jnp.concatenate([v] * (lanes // v.shape[1]), axis=1) if lanes > v.shape[1] else v


def embed_t(kept, table, bias):
    parts = []
    for f in range(F):
        rows = slice(32 * f, 32 * f + 32)
        parts.append(kept[f : f + 1] * table[rows] + bias[rows])
    return jnp.concatenate(parts, axis=0)


def fold(v):
    total = v[:, :128]
    for k in range(1, v.shape[1] // 128):
        total = total + v[:, 128 * k : 128 * k + 128]
    return total


def by_feature(grad, kept):
    return jnp.concatenate(
        [kept[f : f + 1] * grad[32 * f : 32 * f + 32] for f in range(F)], axis=0
    )


def norm_t(v):
    centred = v - jnp.mean(v, axis=0, keepdims=True)
    inverse = lax.rsqrt(jnp.mean(centred * centred, axis=0, keepdims=True) + eps_norm)
    return centred * inverse, inverse


def norm_back_t(grad, normed, inverse, gain):
    scaled = grad * gain
    return inverse * (
        scaled
        - jnp.mean(scaled, axis=0, keepdims=True)
        - normed * jnp.mean(scaled * normed, axis=0, keepdims=True)
    )


def blocks_of(num_q):
    blocks = (num_q + TASKS * (QB - 1)) // QB
    return -(-blocks // 4) * 4


def chunks_of(num_mem):
    chunks = (num_mem + TASKS * (KC - 1)) // KC
    return chunks + chunks % 2


def step_kernel(
    n, qs, num_mem, small_size,
    table, an, gw,
    xs, fs, qn_s, q_s, att, gb_s, fn_s, gho_s, gres, dq_s, gkv, w_q, cols, coefb, acc_gain, out_l,
    ct, w_s, wt_s, wh_s, wht_s,
    mfeat, kn, vn, kt_s, vt_s, mnt, gk, gv,
    il_s, dap, delta, ebuf, ecur, acc, m_s,
    blk_c0, blk_nc, blk_tile, blk_rows, ch_base, ch_end,
):
    planes = n // 8
    per_small = small_size // n
    k_chunks = ch_base.shape[0]

    m_base, m_count, m_units, q_base, q_units = (
        [table[3, TASKS * k + t] for t in range(TASKS)] for k in range(5)
    )
    num_blocks = q_units[0] + q_units[1] + q_units[2] + q_units[3]
    num_chunks = m_units[0] + m_units[1] + m_units[2] + m_units[3]
    for c in range(k_chunks):
        ch_base[c] = jnp.int32(c * KC)
        ch_end[c] = jnp.int32(c * KC)
    tile = jnp.int32(0)
    for t in range(TASKS):
        first_chunk = lax.div(m_base[t], jnp.int32(KC))
        first_block = lax.div(q_base[t], jnp.int32(QB))

        def fill_chunk(i, carry, t=t, first_chunk=first_chunk):
            ch_base[first_chunk + i] = m_base[t]
            ch_end[first_chunk + i] = m_base[t] + m_count[t]
            return carry

        lax.fori_loop(0, m_units[t], fill_chunk, 0)

        def fill_block(i, tile_in, t=t, first_chunk=first_chunk, first_block=first_block):
            blk_c0[first_block + i] = first_chunk
            blk_nc[first_block + i] = m_units[t]
            blk_rows[first_block + i] = m_count[t]
            blk_tile[first_block + i] = tile_in
            return tile_in + m_units[t]

        tile = lax.fori_loop(0, q_units[t], fill_block, tile)

    pieces = [gw[place_of(d, planes)].astype(f32) for d in range(n)]
    for col in range(8):
        block = jnp.concatenate([piece[8 * col : 8 * col + 8] for piece in pieces], axis=0)
        w_s[:, 128 * col : 128 * col + 128] = block.astype(bf16)
        wt_s[128 * col : 128 * col + 128, :] = block.T.astype(bf16)
    lane = iota((8, 128), 1)
    tiles = [piece[64:72] + piece[72:80] for piece in pieces]
    lane_w = iota((D, 128), 1)
    heads = pltpu.roll(jnp.concatenate(tiles, axis=0), 64, 1)
    heads = jnp.where(lane_w < C + F, heads, 0.0)
    wh_s[...] = heads.astype(bf16)
    wht_s[...] = heads.T[:32].astype(bf16)

    for b in range(qs // 128):
        block = gw[n + b, 0:48, :].astype(f32)
        cut = slice(128 * b, 128 * b + 128)
        xs[:, cut] = block[0:8] + block[8:16] + block[16:24]
        fs[:, cut] = block[24:32]
        ct[:, cut] = block[32:40]

    small_rows = jnp.concatenate([tile[0:1] for tile in tiles], axis=0)
    lane_n = iota((n, 128), 1)
    count_t = jnp.maximum(jnp.sum(jnp.where(lane_n == COUNT_LANE, small_rows, 0.0)), 1.0)
    count_r = jnp.maximum(jnp.sum(jnp.where(lane_n == COUNT_LANE + 1, small_rows, 0.0)), 1.0)
    used = 4 * D + 2 * H
    s2 = jnp.concatenate(
        list(split2(small_rows)) + [jnp.zeros((128 - 2 * n, 128), f32)], axis=0
    ).astype(bf16)
    row = iota((used, 128), 0)
    lan = iota((used, 128), 1)
    dev_of = lan & (n - 1)
    pick = (row >= per_small * dev_of) & (row < per_small * dev_of + per_small) & (lan < 2 * n)
    spread = nn(pick.astype(f32).astype(bf16), s2)
    row_dev = jnp.floor((row.astype(f32) + 0.5) * (1.0 / per_small)).astype(jnp.int32)
    here = (lan - SMALL_LANE) == (row - per_small * row_dev)
    column = jnp.sum(jnp.where(here, spread, 0.0), axis=1, keepdims=True)
    cols[...] = jnp.broadcast_to(column[: 4 * D], (4 * D, 128))
    for h in range(H):
        coefb[32 * h : 32 * h + 32, :] = jnp.broadcast_to(
            column[4 * D + h : 4 * D + h + 1] * (32 ** (-0.5)), (32, 128)
        )

    emb_w = lambda lanes: wide(cols[0:D, :], lanes)
    emb_b = lambda lanes: wide(cols[D : 2 * D, :], lanes)
    gain_in = lambda lanes: wide(cols[2 * D : 3 * D, :], lanes)
    gain_out = lambda lanes: wide(cols[3 * D : 4 * D, :], lanes)

    places = gw[n, 48 : 48 + n // 2, :].astype(f32)
    for b in range(n // 2):
        raw = jnp.where(lane < 64, tiles[2 * b], pltpu.roll(tiles[2 * b + 1], 64, 1))
        chosen = (places[b : b + 1] == iota((128, 1), 0).astype(f32)).astype(f32)
        got = nt(jnp.concatenate(split2(raw), axis=0).astype(bf16), chosen.astype(bf16))
        run = got[0:8] + got[8:16]
        for t in range(TASKS):
            i = 8 * b + t
            start, count, slot = table[0, i], table[1, i], table[2, i]
            first = slot & 127
            shift = (first - start) & 127
            moved = pltpu.roll(run, shift, 1)
            at = pl.multiple_of(slot - first, 128)
            pltpu.store(
                mfeat.at[:, pl.ds(at, 128)], moved, mask=(lane >= first) & (lane < first + count)
            )
            pltpu.store(mfeat.at[:, pl.ds(at + 128, 128)], moved, mask=lane < first + count - 128)

    def mem_feats(c):
        base, end = ch_base[c], ch_end[c]
        at = pl.ds(pl.multiple_of(c * KC, KC), KC)
        slot = iota((8, KC), 1) + c * KC
        head = mfeat[:, pl.ds(pl.multiple_of(base, KC), 128)][:, 0:1]
        live = (slot < end).astype(f32)[0:1]
        return jnp.where(slot < end, mfeat[:, at], jnp.where(end > base, head, 0.0)), live

    def mem_pair(i, carry):
        found = []
        for k in range(2):
            c = 2 * i + k
            feats_c, live = mem_feats(c)
            normed, unused = norm_t(embed_t(feats_c, emb_w(KC), emb_b(KC)))
            mnf = normed * gain_in(KC)
            mn = mnf.astype(bf16)
            keys_t = (nn(wt_s[D : 2 * D, :], mn) * live).astype(bf16)
            vals_t = nn(wt_s[2 * D : 3 * D, :], mn) * live
            tail = jnp.where(iota((16, KC), 0) == 0, live, 0.0)
            vals_t = jnp.concatenate(
                [part for p in range(4) for part in (vals_t[64 * p : 64 * p + 64], tail)], axis=0
            ).astype(bf16)
            both = nn(mnf.T.astype(bf16), w_s[:, D : 3 * D])
            live_col = ((iota((KC, 1), 0) + c * KC) < ch_end[c]).astype(f32)
            found.append((mn, keys_t, vals_t, both[:, :D], both[:, D:] * live_col))
        for k in range(2):
            at = pl.ds(pl.multiple_of((2 * i + k) * KC, KC), KC)
            mnt[:, at], kt_s[:, at], vt_s[:, at] = found[k][0:3]
            kn[at, :] = found[k][3].astype(bf16)
            vn[at, :] = found[k][4].astype(bf16)
            gk[at, :] = jnp.zeros((KC, D), f32)
            gv[at, :] = jnp.zeros((KC, D), f32)
        return carry

    lax.fori_loop(0, lax.div(num_chunks + 1, jnp.int32(2)), mem_pair, 0)

    def spots(j):
        return [pl.ds(pl.multiple_of(j * 512 + 256 * k, 256), 256) for k in range(2)]

    def pre_block(j, carry):
        found = []
        for at in spots(j):
            kept = xs[:, at] * (1.0 - fs[:, at])
            normed, unused = norm_t(embed_t(kept, emb_w(256), emb_b(256)))
            qn = (normed * gain_in(256)).astype(bf16)
            found.append((qn, nn(wt_s[0:D, :], qn).astype(bf16)))
        for k, at in enumerate(spots(j)):
            qn_s[:, at], q_s[:, at] = found[k]
            att[:, at] = jnp.zeros((D, 256), bf16)
            il_s[:, at] = jnp.zeros((H, 256), f32)
            dq_s[:, at] = jnp.zeros((D, 256), f32)
        return carry

    lax.fori_loop(0, qs // 512, pre_block, 0)

    zero_h = jnp.zeros((32, 128), bf16)
    zero_p = jnp.zeros((64, 256), bf16)

    def pair(p, width):
        return slice(width * p, width * p + width)

    def half(p):
        return slice(128 * (p // 2), 128 * (p // 2) + 128)

    def two_heads(ref, at, p):
        diag = jnp.concatenate(
            [
                jnp.concatenate([ref[64 * p : 64 * p + 32, at], zero_h], axis=1),
                jnp.concatenate([zero_h, ref[64 * p + 32 : 64 * p + 64, at]], axis=1),
            ],
            axis=0,
        )
        return jnp.concatenate([zero_p, diag] if p % 2 else [diag, zero_p], axis=0)

    def coef_row(p):
        return LOG2E * jnp.concatenate(
            [coefb[64 * p : 64 * p + 1, :], coefb[64 * p + 32 : 64 * p + 33, :]], axis=1
        )

    def finish_forward(at, p, got):
        inverse = 1.0 / got[64:65, :]
        il_s[2 * p : 2 * p + 1, at] = inverse[:, :128]
        il_s[2 * p + 1 : 2 * p + 2, at] = inverse[:, 128:]
        att[64 * p : 64 * p + 32, at] = (got[0:32, :128] * inverse[:, :128]).astype(bf16)
        att[64 * p + 32 : 64 * p + 64, at] = (got[32:64, 128:] * inverse[:, 128:]).astype(bf16)

    def forward_block(i, carry):
        at = pl.ds(pl.multiple_of(i * QB, QB), QB)
        c0, nc, tile0, count = blk_c0[i], blk_nc[i], blk_tile[i], blk_rows[i]

        def one(rows):
            keys = pl.ds(pl.multiple_of(c0 * KC, KC), rows)
            keep = jnp.minimum(tile0, E_CAP)
            operands = [two_heads(q_s, at, p) for p in range(4)]
            values = [vt_s[pair(p, VROWS), pl.ds(pl.multiple_of(c0 * KC, KC), KC)][:, :rows] for p in range(4)]
            scores = [nn(kn[keys, half(p)], operands[p]) * coef_row(p) for p in range(4)]
            tops = [jnp.max(s, axis=0, keepdims=True) for s in scores]
            es = [jnp.exp2(scores[p] - tops[p]).astype(bf16) for p in range(4)]
            sums = [nn(values[p], es[p]) for p in range(4)]
            for p in range(4):
                m_s[i, :, pair(p, 256)] = tops[p]
                ebuf[keep, :rows, pair(p, 256)] = es[p]
                finish_forward(at, p, sums[p])

        @pl.when(count <= KC_LOW)
        def few():
            one(KC_LOW)

        @pl.when((count > KC_LOW) & (nc == 1))
        def full():
            one(KC)

        @pl.when(nc > 1)
        def many():
            m_s[i] = jnp.full((1, 1024), -3e38, f32)
            acc[...] = jnp.zeros_like(acc)

            def tops(c, inner):
                keys = pl.ds(pl.multiple_of((c0 + c) * KC, KC), KC)
                for p in range(4):
                    s = nn(kn[keys, half(p)], two_heads(q_s, at, p)) * coef_row(p)
                    m_s[i, :, pair(p, 256)] = jnp.maximum(
                        m_s[i, :, pair(p, 256)], jnp.max(s, axis=0, keepdims=True)
                    )
                return inner

            lax.fori_loop(0, nc, tops, 0)

            def sums(c, inner):
                keys = pl.ds(pl.multiple_of((c0 + c) * KC, KC), KC)
                keep = jnp.minimum(tile0 + c, E_CAP)
                for p in range(4):
                    s = nn(kn[keys, half(p)], two_heads(q_s, at, p)) * coef_row(p)
                    e = jnp.exp2(s - m_s[i, :, pair(p, 256)]).astype(bf16)
                    ebuf[keep, :, pair(p, 256)] = e
                    acc[pair(p, VROWS), :] += nn(vt_s[pair(p, VROWS), keys], e)
                return inner

            lax.fori_loop(0, nc, sums, 0)
            for p in range(4):
                finish_forward(at, p, acc[pair(p, VROWS), :])

        return carry

    lax.fori_loop(0, num_blocks, forward_block, 0)

    weight_a = an[0]
    scale_t = weight_a / count_t
    scale_r = (1.0 - weight_a) / count_r
    acc_gain[...] = jnp.zeros_like(acc_gain)
    out_l[...] = jnp.zeros_like(out_l)

    def mid_values(at):
        x = xs[:, at]
        fmask = fs[:, at]
        hidden = embed_t(x * (1.0 - fmask), emb_w(256), emb_b(256))
        attended = att[:, at]
        residual = hidden + nn(wt_s[3 * D : 4 * D, :], attended)
        normed, inverse = norm_t(residual)
        fn = (normed * gain_out(256)).astype(bf16)
        head = nn(wht_s[...], fn)
        logits = head[0:C]
        err = head[C : C + F] - x
        label = ct[1:2, at]
        hot = (iota((C, 256), 0).astype(f32) == ct[0:1, at]).astype(f32)
        top = jnp.max(logits, axis=0, keepdims=True)
        e = jnp.exp(logits - top)
        total = jnp.sum(e, axis=0, keepdims=True)
        picked = jnp.sum(logits * hot, axis=0, keepdims=True)
        loss = scale_t * label * (jnp.log(total) + top - picked) + scale_r * jnp.sum(
            fmask * err * err, axis=0, keepdims=True
        )
        g_log = scale_t * label * (e / total - hot)
        g_rec = scale_r * fmask * 2.0 * err
        gho = jnp.concatenate([g_log, g_rec, jnp.zeros((8, 256), f32)], axis=0).astype(bf16)
        g_final = nn(wh_s[:, :32], gho)
        g_res = norm_back_t(g_final, normed, inverse, gain_out(256))
        gb = g_res.astype(bf16)
        ga = nn(w_s[:, 3 * D : 4 * D], gb).astype(bf16).astype(f32)
        attf = attended.astype(f32)
        das, deltas = [], []
        for h in range(H):
            rows = slice(32 * h, 32 * h + 32)
            da = (ga[rows] * il_s[h : h + 1, at]).astype(bf16)
            das.append(da)
            deltas.append(jnp.sum(da.astype(f32) * attf[rows], axis=0, keepdims=True))
        return (
            fold(loss), fold(g_final * normed),
            fn, gho, g_res, gb, jnp.concatenate(das, axis=0), jnp.concatenate(deltas, axis=0),
        )

    def mid_block(j, carry):
        found = [mid_values(at) for at in spots(j)]
        out_l[0:1, :] += found[0][0] + found[1][0]
        acc_gain[D : 2 * D, :] += found[0][1] + found[1][1]
        for k, at in enumerate(spots(j)):
            for ref, value in zip((fn_s, gho_s, gres, gb_s, dap, delta), found[k][2:]):
                ref[:, at] = value
        return carry

    lax.fori_loop(0, qs // 512, mid_block, 0)

    def backward_chunk(at, c, rows, e_of):
        keys = pl.ds(pl.multiple_of(c * KC, KC), rows)
        lanes = pl.ds(pl.multiple_of(c * KC, KC), KC)
        es = [e_of(p) for p in range(4)]
        das = [two_heads(dap, at, p) for p in range(4)]
        qds = [two_heads(q_s, at, p) for p in range(4)]
        deltas = delta[:, at]
        kts = [kt_s[64 * p : 64 * p + 64, lanes][:, :rows] for p in range(4)]
        old_dq = dq_s[:, at]
        old_gk = gk[keys, :]
        old_gv = gv[keys, :]
        dps = [nn(vn[keys, half(p)], das[p]) for p in range(4)]
        dss = []
        for p in range(4):
            take = jnp.concatenate([deltas[2 * p : 2 * p + 1], deltas[2 * p + 1 : 2 * p + 2]], axis=1)
            dss.append((es[p].astype(f32) * (dps[p] - take)).astype(bf16))
        dqs = [nn(kts[p], dss[p]) for p in range(4)]

        def by_key(grads, others):
            return jnp.concatenate(
                [
                    nt(
                        jnp.concatenate([grads[a], grads[a + 1]], axis=1),
                        jnp.concatenate([others[a], others[a + 1]], axis=1),
                    )
                    for a in (0, 2)
                ],
                axis=1,
            )

        new_gv = old_gv + by_key(es, das)
        new_gk = old_gk + by_key(dss, qds)
        parts = []
        for p in range(4):
            parts += [dqs[p][0:32, :128], dqs[p][32:64, 128:]]
        dq_s[:, at] = old_dq + jnp.concatenate(parts, axis=0)
        gk[keys, :] = new_gk
        gv[keys, :] = new_gv

    def backward_block(i, carry):
        at = pl.ds(pl.multiple_of(i * QB, QB), QB)
        c0, nc, tile0, count = blk_c0[i], blk_nc[i], blk_tile[i], blk_rows[i]
        simple = (nc == 1) & (tile0 < E_CAP)

        @pl.when(simple & (count <= KC_LOW))
        def few():
            backward_chunk(at, c0, KC_LOW, lambda p: ebuf[tile0, :KC_LOW, pair(p, 256)])

        @pl.when(simple & (count > KC_LOW))
        def full():
            backward_chunk(at, c0, KC, lambda p: ebuf[tile0, :, pair(p, 256)])

        @pl.when(jnp.logical_not(simple))
        def many():
            def one_chunk(c, inner):
                keys = pl.ds(pl.multiple_of((c0 + c) * KC, KC), KC)

                @pl.when((tile0 + c < E_CAP) & (nc > 1))
                def kept():
                    ecur[...] = ebuf[tile0 + c]

                @pl.when((tile0 + c >= E_CAP) | (nc == 1))
                def again():
                    for p in range(4):
                        s = nn(kn[keys, half(p)], two_heads(q_s, at, p)) * coef_row(p)
                        ecur[:, pair(p, 256)] = jnp.exp2(
                            s - m_s[i, :, pair(p, 256)]
                        ).astype(bf16)

                backward_chunk(at, c0 + c, KC, lambda p: ecur[:, pair(p, 256)])
                return inner

            lax.fori_loop(0, nc, one_chunk, 0)

        return carry

    lax.fori_loop(0, num_blocks, backward_block, 0)

    gkv[...] = jnp.zeros_like(gkv)
    w_q[...] = w_s[:, 0:D]

    def mem_back(i, coef_lane):
        found = []
        for k in range(2):
            c = 2 * i + k
            at = pl.ds(pl.multiple_of(c * KC, KC), KC)
            feats_c, unused = mem_feats(c)
            live = ((iota((KC, 1), 0) + c * KC) < ch_end[c]).astype(f32)
            gk_c = (gk[at, :] * coef_lane * live).astype(bf16)
            gv_c = (gv[at, :] * live).astype(bf16)
            gmn = nt(w_s[:, D : 2 * D], gk_c) + nt(w_s[:, 2 * D : 3 * D], gv_c)
            normed, inverse = norm_t(embed_t(feats_c, emb_w(KC), emb_b(KC)))
            gm = norm_back_t(gmn, normed, inverse, gain_in(KC))
            found.append((gk_c, gv_c, fold(gmn * normed), fold(by_feature(gm, feats_c)), fold(gm)))
        mn = mnt[:, pl.ds(pl.multiple_of(2 * i * KC, KC), 2 * KC)]
        gkv[:, 0:D] += nn(mn, jnp.concatenate([found[0][0], found[1][0]], axis=0))
        gkv[:, D : 2 * D] += nn(mn, jnp.concatenate([found[0][1], found[1][1]], axis=0))
        for k, rows in ((2, slice(0, D)), (3, slice(2 * D, 3 * D)), (4, slice(3 * D, 4 * D))):
            acc_gain[rows, :] += found[0][k] + found[1][k]
        return coef_lane

    coef_lane = jnp.concatenate([coefb[0:128, :].T[0:1], coefb[128:256, :].T[0:1]], axis=1)
    lax.fori_loop(0, lax.div(num_chunks + 1, jnp.int32(2)), mem_back, coef_lane)


def step_call(n, num_mem, small_size, table, an, gw):
    q_blocks, k_chunks = gw.shape[0] - n, chunks_of(num_mem)
    qs, ks = q_blocks * QB, k_chunks * KC
    V = pltpu.VMEM
    S = pltpu.SMEM
    A = jax.ShapeDtypeStruct
    vm = pl.BlockSpec(memory_space=pltpu.VMEM)
    sm = pl.BlockSpec(memory_space=pltpu.SMEM)
    outs = (
        A((8, qs), f32), A((8, qs), f32), A((D, qs), bf16), A((D, qs), bf16), A((D, qs), bf16),
        A((D, qs), bf16), A((D, qs), bf16), A((32, qs), bf16), A((D, qs), f32), A((D, qs), f32),
        A((D, 2 * D), f32), A((D, D), bf16), A((4 * D, 128), f32), A((D, 128), f32),
        A((4 * D + H, 128), f32), A((8, 128), f32),
    )
    scratch = [
        V((8, qs), f32), V((D, 4 * D), bf16), V((4 * D, D), bf16), V((D, 128), bf16), V((32, D), bf16),
        V((8, ks + 128), f32), V((ks, D), bf16), V((ks, D), bf16), V((D, ks), bf16),
        V((4 * VROWS, ks), bf16), V((D, ks), bf16), V((ks, D), f32), V((ks, D), f32),
        V((H, qs), f32), V((D, qs), bf16), V((H, qs), f32),
        V((E_CAP + 1, KC, 1024), bf16), V((KC, 1024), bf16), V((4 * VROWS, 256), f32),
        V((q_blocks, 1, 1024), f32),
        S((q_blocks,), jnp.int32), S((q_blocks,), jnp.int32), S((q_blocks,), jnp.int32),
        S((q_blocks,), jnp.int32), S((k_chunks,), jnp.int32), S((k_chunks,), jnp.int32),
    ]
    return pl.pallas_call(
        functools.partial(step_kernel, n, qs, num_mem, small_size),
        out_shape=outs,
        in_specs=[sm, sm, vm],
        out_specs=(vm,) * len(outs),
        scratch_shapes=scratch,
        compiler_params=pltpu.CompilerParams(vmem_limit_bytes=STEP_VMEM),
    )(table, an, gw)


MESH = pl.DeviceIdType.MESH


def greet(targets):
    barrier = pltpu.get_barrier_semaphore()
    for target in targets:
        pl.semaphore_signal(barrier, inc=1, device_id=(target,), device_id_type=MESH)
    return barrier


def send(src, dst, send_sem, recv_sem, target):
    copy = pltpu.make_async_remote_copy(
        src_ref=src,
        dst_ref=dst,
        send_sem=send_sem,
        recv_sem=recv_sem,
        device_id=(target,),
        device_id_type=MESH,
    )
    copy.start()
    return copy


def where_am_i(planes):
    me = lax.axis_index("mem")
    core = lax.rem(me, 2)
    square = lax.rem(lax.div(me, 2), 4)
    plane = lax.div(me, 8)
    return me, core, square, plane


def gather_kernel(
    n, num_q, num_mem, *refs,
):
    sources, refs = refs[:12], refs[12:]
    gw, table, keep = refs[:3]
    copied, refs = refs[3:15], refs[15:]
    send_z, recv_z, send_s, recv_s, send_c, recv_c, load = refs
    loads = [
        pltpu.make_async_copy(sources[i], copied[i], load.at[i]) for i in range(len(sources))
    ]
    for copy in loads:
        copy.start()
    w_qkv, w_out, w_heads, w_small, mfeat, qf, fm, qt, tc, tm, mt, mm = copied
    planes = n // 8
    me, core, square, plane = where_am_i(planes)
    in_plane = core + 2 * square
    z_of = [lax.rem(plane + k, planes) * 8 + in_plane for k in range(1, planes)]
    s_of = [plane * 8 + lax.rem(square + k, 4) * 2 + core for k in range(1, 4)]
    c_of = plane * 8 + square * 2 + (1 - core)
    barrier = greet(z_of + s_of + [c_of])
    for copy in loads:
        copy.wait()

    rows = []
    for c in range(6):
        rows.append(w_qkv[pl.ds(c, 8, stride=6), :])
    for c in range(2):
        rows.append(w_out[pl.ds(c, 8, stride=2), :])
    per_head = w_heads.shape[1]
    lane = iota((8, 256), 1)
    head_row = jnp.concatenate([w_heads[...], jnp.zeros((1, 256 - per_head), f32)], axis=1)
    owner = jnp.floor((lane.astype(f32) + 0.5) * (1.0 / (C + F))).astype(jnp.int32)
    kept_heads = jnp.where(owner == iota((8, 256), 0), head_row, 0.0).astype(bf16)
    fold_r = iota((256, 128), 0)
    fold_row = jnp.floor((fold_r.astype(f32) + 0.5) * (1.0 / (C + F))).astype(jnp.int32)
    fold_m = (fold_r - (C + F) * fold_row == iota((256, 128), 1) - 64).astype(f32).astype(bf16)
    heads = nn(kept_heads, fold_m)
    per_small = w_small.shape[1]
    small = jnp.concatenate([w_small[...], jnp.zeros((1, 128 - per_small), f32)], axis=1)
    small = pltpu.roll(jnp.broadcast_to(small, (8, 128)), SMALL_LANE, 1)
    feats = jnp.concatenate([mfeat[...], jnp.zeros((8, 64), f32)], axis=1)
    lane8 = iota((8, 128), 1)
    row8 = iota((8, 128), 0)
    num_t = jnp.sum(tm[...].astype(f32), axis=1, keepdims=True)
    num_r = jnp.sum(jnp.sum(fm[...].astype(f32), axis=0, keepdims=True), axis=1, keepdims=True)
    block = feats + heads
    first = (row8 == 0) & (lane8 >= SMALL_LANE) & (lane8 < SMALL_LANE + per_small)
    block = jnp.where(first, small, block)
    block = jnp.where((row8 == 0) & (lane8 == COUNT_LANE), num_t, block)
    block = jnp.where((row8 == 0) & (lane8 == COUNT_LANE + 1), num_r, block)

    def slot_of(k, j, c):
        back = lax.rem(plane + planes - k, planes)
        return c * (4 * planes) + lax.rem(square + 4 - j, 4) * planes + back

    gw[slot_of(0, 0, core)] = jnp.concatenate(rows + list(split2(block)), axis=0).astype(bf16)

    pl.semaphore_wait(barrier, planes - 1 + 4)

    def spread(k, done):
        at = gw.at[slot_of(k, 0, core)]
        for j in range(1, 4):
            done[k, j] = send(at, at, send_s.at[k, j - 1], recv_s.at[k, j - 1], s_of[j - 1])
        done[k, 0, "c"] = send(at, at, send_c.at[k, 0], recv_c.at[k, 0], c_of)

    at = gw.at[slot_of(0, 0, core)]
    done = {}
    for k in range(1, planes):
        done[k] = send(at, at, send_z.at[k - 1], recv_z.at[k - 1], z_of[k - 1])
    spread(0, done)

    task_row = iota((8, 256), 0)
    marks = [(qt[:, 256 * b : 256 * b + 256] == task_row).astype(f32) for b in range(num_q // 256)]
    marks_q = jnp.concatenate(marks, axis=0)
    before = (iota((256, 256), 0) < iota((256, 256), 1)).astype(f32).astype(bf16)
    ranks = nn(marks_q.astype(bf16), before)
    totals = jnp.sum(marks_q, axis=1, keepdims=True)
    task_col = iota((8, 1), 0)

    def bases_of(sums, unit):
        base = jnp.int32(0)
        bases, counts, used = [], [], []
        base_vec = jnp.zeros((8, 1), f32)
        for t in range(TASKS):
            count = jnp.sum(jnp.where(task_col == t, sums, 0.0)).astype(jnp.int32)
            bases.append(base)
            counts.append(count)
            used.append(lax.div(count + (unit - 1), jnp.int32(unit)))
            base_vec = base_vec + jnp.where(task_col == t, base.astype(f32), 0.0)
            base = base + used[t] * unit
        return bases, counts, used, base_vec

    carry = jnp.zeros((8, 1), f32)
    carries = []
    for b in range(num_q // 256):
        carries.append(carry)
        carry = carry + totals[8 * b : 8 * b + 8]
    q_base, q_count, q_units, base_vec = bases_of(carry, QB)
    place_q = jnp.concatenate(
        [
            jnp.sum(marks[b] * (base_vec + carries[b] + ranks[8 * b : 8 * b + 8]), axis=0, keepdims=True)
            for b in range(num_q // 256)
        ],
        axis=1,
    )

    cuts = num_mem // 128
    task_row = iota((8, 128), 0)
    marks = []
    for b in range(cuts):
        cut = slice(128 * b, 128 * b + 128)
        marks.append(((mt[:, cut] == task_row) & (mm[:, cut] > 0)).astype(f32))
    marks_m = jnp.concatenate(marks, axis=0)
    ranks = nn(marks_m.astype(bf16), before[:128, :128])
    totals = jnp.broadcast_to(jnp.sum(marks_m, axis=1, keepdims=True), (8 * cuts, 128))
    r_to = iota((8 * cuts, 8 * cuts), 0)
    r_from = iota((8 * cuts, 8 * cuts), 1)
    same_cut = (r_to // 8 == r_from // 8) & (r_from < r_to)
    same_task = (r_to % 8 == r_from % 8) & (r_from < r_to)
    low_totals = totals.astype(bf16)
    starts = nn(same_cut.astype(f32).astype(bf16), low_totals)
    earlier = nn(same_task.astype(f32).astype(bf16), low_totals)
    last = slice(8 * cuts - 8, 8 * cuts)
    m_base, m_count, m_units, base_vec = bases_of((earlier + totals)[last, 0:1], KC)
    slots = earlier + jnp.concatenate([base_vec] * cuts, axis=0)
    places_m = jnp.concatenate(
        [
            jnp.sum(marks[b] * (starts[8 * b : 8 * b + 8] + ranks[8 * b : 8 * b + 8] + 1.0), axis=0, keepdims=True)
            - 1.0
            for b in range(cuts)
        ],
        axis=0,
    )
    eye = r_to == r_from

    def as_row(column):
        return jnp.sum(jnp.where(eye, wide(column, 8 * cuts), 0.0), axis=0, keepdims=True)

    row_t = iota((8, 8 * cuts), 0)
    lane_t = iota((8, 8 * cuts), 1)
    numbers = jnp.where(
        row_t == 0, as_row(starts), jnp.where(row_t == 1, as_row(totals), as_row(slots))
    ).astype(jnp.int32)
    for i, number in enumerate(m_base + m_count + m_units + q_base + q_units):
        numbers = jnp.where((row_t == 3) & (lane_t == i), number, numbers)
    table[...] = numbers
    gw[n, 48 : 48 + cuts, :] = places_m.astype(bf16)
    heads_low = jnp.concatenate([w_heads[:, 128:], jnp.zeros((1, 256 - per_head), f32)], axis=1)
    small_row = jnp.concatenate([w_small[...], jnp.zeros((1, 128 - per_small), f32)], axis=1)
    keep[...] = jnp.where(
        row8 == 0, w_heads[:, :128], jnp.where(row8 == 1, heads_low, small_row)
    )
    xq = qf[...]
    fmq = fm[...].astype(f32)
    row8 = iota((8, num_q), 0)
    label_rows = jnp.where(
        row8 == 0, tc[...].astype(f32), jnp.where(row8 == 1, tm[...].astype(f32), 0.0)
    )
    q_rows = jnp.concatenate(
        list(split3(xq)) + [fmq, label_rows, jnp.zeros((8, num_q), f32)], axis=0
    ).astype(bf16)
    for b in range((gw.shape[0] - n) // 2):
        chosen = (
            (place_q == (iota((256, 1), 0) + 256 * b).astype(f32)).astype(f32).astype(bf16)
        )
        got = nt(q_rows, chosen).astype(bf16)
        gw[n + 2 * b, 0:48, :] = got[:, :128]
        gw[n + 2 * b + 1, 0:48, :] = got[:, 128:]


    for k in range(1, planes):
        done[k].wait_recv()
        spread(k, done)
    for k in range(planes):
        for j in range(1, 4):
            done[k, j].wait_recv()
            at = gw.at[slot_of(k, j, core)]
            done[k, j, "c"] = send(at, at, send_c.at[k, j], recv_c.at[k, j], c_of)
    for k in range(planes):
        for j in range(4):
            done[k, j, "c"].wait_recv()
    for copy in done.values():
        copy.wait_send()


def gather_call(n, w_qkv, w_out, w_heads, w_small, mfeat, qf, fm, qt, tc, tm, mt, mm):
    planes = n // 8
    operands = (w_qkv, w_out, w_heads, w_small, mfeat, qf, fm, qt, tc, tm, mt, mm)
    num_q, num_mem = qf.shape[1], mt.shape[1]
    qs = blocks_of(num_q) * QB
    vm = pl.BlockSpec(memory_space=pltpu.VMEM)
    dma = pltpu.SemaphoreType.DMA
    return pl.pallas_call(
        functools.partial(gather_kernel, n, num_q, num_mem),
        out_shape=(
            jax.ShapeDtypeStruct((n + qs // 128, 80, 128), bf16),
            jax.ShapeDtypeStruct((8, num_mem // 16), jnp.int32),
            jax.ShapeDtypeStruct((8, 128), f32),
        ),
        in_specs=[pl.BlockSpec(memory_space=pltpu.HBM)] * 12,
        out_specs=(vm,) * 3,
        scratch_shapes=[pltpu.VMEM(v.shape, v.dtype) for v in operands]
        + [
            dma((planes - 1,)), dma((planes - 1,)), dma((planes, 3)), dma((planes, 3)),
            dma((planes, 4)), dma((planes, 4)), dma((12,)),
        ],
        compiler_params=pltpu.CompilerParams(collective_id=0, has_side_effects=True),
    )(*operands)


def reduce_kernel(
    n, per_small,
    xs, fs, qn_s, q_s, att, gb_s, fn_s, gho_s, gres, dq_s, gkv, w_q, cols, coefb, sums_in, l_in,
    g_out, t_out, gq, acc_gain, s_s, r_core, t_square, r_square, t_plane, r_plane, own, n_mine, n_all,
    send_c, recv_c, send_s, recv_s, send_z, recv_z, send_n, recv_n,
):
    planes = n // 8
    rows_dev = D // n
    me, core, square, plane = where_am_i(planes)
    in_plane = core + 2 * square
    a_of = [lax.rem(me + k, n) for k in range(1, n)]
    z_of = [lax.rem(plane + k, planes) * 8 + in_plane for k in range(1, planes)]
    s_of = [plane * 8 + lax.rem(square + k, 4) * 2 + core for k in range(1, 4)]
    c_of = plane * 8 + square * 2 + (1 - core)
    barrier = greet(a_of)

    def over(rows, lanes):
        return wide(cols[rows, :], lanes)

    def spots(j):
        return [pl.ds(pl.multiple_of(j * 512 + 256 * k, 256), 256) for k in range(2)]

    coef2 = wide(coefb[...], 256)

    def post_values(at):
        kept = xs[:, at] * (1.0 - fs[:, at])
        normed, inverse = norm_t(embed_t(kept, over(slice(0, D), 256), over(slice(D, 2 * D), 256)))
        dq = dq_s[:, at]
        low = (dq * coef2).astype(bf16)
        prod = fold(dq * q_s[:, at].astype(f32))
        betas = jnp.concatenate(
            [jnp.sum(prod[32 * h : 32 * h + 32], axis=0, keepdims=True) for h in range(H)], axis=0
        )
        gqn = nn(w_q[...], low)
        gh = gres[:, at] + norm_back_t(gqn, normed, inverse, over(slice(2 * D, 3 * D), 256))
        return low, betas, fold(gqn * normed), fold(by_feature(gh, kept)), fold(gh)

    def post_block(j, carry):
        cuts = spots(j)
        found = [post_values(at) for at in cuts]
        qn = jnp.concatenate([qn_s[:, at] for at in cuts], axis=1)
        gq_c = jnp.concatenate([found[0][0], found[1][0]], axis=1)
        gq[...] += nt(qn, gq_c)
        for k, rows in ((1, slice(4 * D, 4 * D + H)), (2, slice(0, D)), (3, slice(2 * D, 3 * D)), (4, slice(3 * D, 4 * D))):
            acc_gain[rows, :] += found[0][k] + found[1][k]
        return carry

    gq[...] = jnp.zeros_like(gq)
    acc_gain[...] = sums_in[...]
    lax.fori_loop(0, xs.shape[1] // 512, post_block, 0)
    gout = nt(att[...], gb_s[...])
    ghead = nt(fn_s[...], gho_s[...])

    used = 4 * D + 2 * H
    row = iota((used, 128), 0)
    lan = iota((used, 128), 1)
    row_dev = jnp.floor((row.astype(f32) + 0.5) * (1.0 / per_small)).astype(jnp.int32)
    sums = jnp.sum(acc_gain[...], axis=1, keepdims=True)
    small = jnp.concatenate(
        [
            sums[2 * D : 3 * D],
            sums[3 * D : 4 * D],
            sums[0:D],
            sums[D : 2 * D],
            sums[4 * D : 4 * D + H] * (32 ** (-0.5)),
            jnp.zeros((H, 1), f32),
        ],
        axis=0,
    )
    placed = jnp.where(lan == (row - per_small * row_dev), small, 0.0).astype(bf16)
    r_dev = iota((n, used), 0)
    r_row = iota((n, used), 1)
    mine = (r_row >= per_small * r_dev) & (r_row < per_small * r_dev + per_small)
    small_rows_out = nn(mine.astype(f32).astype(bf16), placed)
    to_flat_r = iota((32, 256), 0)
    to_flat_l = iota((32, 256), 1)
    lane_row = jnp.floor((to_flat_l.astype(f32) + 0.5) * (1.0 / (C + F))).astype(jnp.int32)
    to_flat = ((to_flat_l - (C + F) * lane_row == to_flat_r) & (to_flat_r < C + F)).astype(f32)
    spread_h = nn(ghead.astype(bf16), to_flat.astype(bf16))
    lr = iota((D, 256), 1)
    lr_row = jnp.floor((lr.astype(f32) + 0.5) * (1.0 / (C + F))).astype(jnp.int32)
    spread_h = jnp.where(lr_row == (iota((D, 256), 0) & (rows_dev - 1)), spread_h, 0.0)
    r8 = iota((8, 128), 0)
    for d in range(n):
        rows = slice(rows_dev * d, rows_dev * d + rows_dev)
        head_flat = jnp.sum(spread_h[rows], axis=0, keepdims=True)
        extra = jnp.where(
            r8 == 0,
            head_flat[:, :128],
            jnp.where(r8 == 1, head_flat[:, 128:], jnp.where(r8 == 2, small_rows_out[d : d + 1], 0.0)),
        )
        block = [gq[rows, 128 * k : 128 * k + 128] for k in range(2)]
        block += [gkv[rows, 128 * k : 128 * k + 128] for k in range(4)]
        block += [gout[rows, 128 * k : 128 * k + 128] for k in range(2)]
        block += [extra, jnp.zeros((8, 128), f32)]
        s_s[place_of(d, planes)] = jnp.concatenate(block, axis=0).astype(bf16)

    pl.semaphore_wait(barrier, n - 1)

    def part(c, j, k):
        z = lax.rem(plane + k, planes)
        return c * (4 * planes) + lax.rem(square + j, 4) * planes + z

    done = []
    pieces = {}
    for j in (1, 2, 3, 0):
        line = pl.ds((1 - core) * (4 * planes) + lax.rem(square + j, 4) * planes, planes)
        pieces[j] = send(s_s.at[line], r_core.at[j], send_c.at[j], recv_c.at[j], c_of)
    for j in (1, 2, 3):
        pieces[j].wait_recv()
    order = [2, 1, 3, 0] if planes == 4 else list(range(1, planes)) + [0]
    crossing = {}
    for k in order:
        z = lax.rem(plane + k, planes)
        for j in range(1, 4):
            t_square[j - 1, k] = (
                s_s[part(core, j, k)].astype(f32) + r_core[j, z].astype(f32)
            ).astype(bf16)
            crossing[k, j] = send(
                t_square.at[j - 1, k], r_square.at[j - 1, k],
                send_s.at[j - 1, k], recv_s.at[j - 1, k], s_of[j - 1],
            )
    pieces[0].wait_recv()
    for k in order:
        z = lax.rem(plane + k, planes)
        own[k] = s_s[part(core, 0, k)].astype(f32) + r_core[0, z].astype(f32)
    along = {}
    for k in order:
        total = own[k]
        for j in range(1, 4):
            crossing[k, j].wait_recv()
            total = total + r_square[j - 1, k].astype(f32)
        if k:
            t_plane[k - 1] = total.astype(bf16)
            along[k] = send(
                t_plane.at[k - 1], r_plane.at[k - 1], send_z.at[k - 1], recv_z.at[k - 1], z_of[k - 1]
            )
    for k in range(1, planes):
        along[k].wait_recv()
        total = total + r_plane[k - 1].astype(f32)
    g_out[...] = total
    squares = jnp.sum(total * total, axis=0, keepdims=True)
    squares = squares + pltpu.roll(squares, 64, 1)
    losses = l_in[0:1, :]
    losses = losses + pltpu.roll(losses, 64, 1)
    n_mine[...] = jnp.where(iota((1, 128), 1) < 64, squares, losses)
    last = []
    for k in range(1, n):
        last.append(send(n_mine, n_all.at[k - 1], send_n.at[k - 1], recv_n.at[k - 1], a_of[k - 1]))
    total = n_mine[...]
    for k in range(1, n):
        last[k - 1].wait_recv()
        total = total + n_all[k - 1]
    t_out[...] = total
    for copies in (pieces, crossing, along):
        for copy in copies.values():
            copy.wait_send()
    for copy in last:
        copy.wait_send()


def reduce_call(n, per_small, *grads):
    planes = n // 8
    rows = 80
    vm = pl.BlockSpec(memory_space=pltpu.VMEM)
    dma = pltpu.SemaphoreType.DMA
    V = pltpu.VMEM
    z = planes - 1
    return pl.pallas_call(
        functools.partial(reduce_kernel, n, per_small),
        out_shape=(
            jax.ShapeDtypeStruct((rows, 128), f32),
            jax.ShapeDtypeStruct((1, 128), f32),
        ),
        in_specs=[vm] * len(grads),
        out_specs=(vm, vm),
        scratch_shapes=[
            V((D, D), f32), V((4 * D + H, 128), f32),
            V((n, rows, 128), bf16), V((4, planes, rows, 128), bf16), V((3, planes, rows, 128), bf16),
            V((3, planes, rows, 128), bf16), V((z, rows, 128), bf16), V((z, rows, 128), bf16),
            V((planes, rows, 128), f32), V((1, 128), f32), V((n - 1, 1, 128), f32),
            dma((4,)), dma((4,)), dma((3, planes)), dma((3, planes)), dma((z,)), dma((z,)),
            dma((n - 1,)), dma((n - 1,)),
        ],
        compiler_params=pltpu.CompilerParams(
            collective_id=1, has_side_effects=True, vmem_limit_bytes=16 * 1024 * 1024
        ),
    )(*grads)


def update_kernel(g, tot, *refs):
    w_qkv, w_out, keep = refs[0:3]
    firsts, seconds, refs = refs[3:7], refs[7:11], refs[11:]
    per_head, per_small = firsts[2].shape[1], firsts[3].shape[1]
    weights = (
        w_qkv[...],
        w_out[...],
        jnp.concatenate([keep[0:1, :], keep[1:2, : per_head - 128]], axis=1),
        keep[2:3, :per_small],
    )
    new, first_o, second_o = refs[0:4], refs[4:8], refs[8:12]
    copy_o = (refs[12], refs[13], None, refs[14])
    flat_o, loss_o, norm_o, gq_s, go_s = refs[15:20]
    for c in range(6):
        gq_s[pl.ds(c, 8, stride=6), :] = g[8 * c : 8 * c + 8, :]
    for c in range(2):
        go_s[pl.ds(c, 8, stride=2), :] = g[48 + 8 * c : 56 + 8 * c, :]
    first_half = iota((1, 128), 1) < 64
    norm = jnp.sqrt(jnp.sum(jnp.where(first_half, tot[...], 0.0), axis=1, keepdims=True))
    loss_o[...] = jnp.sum(jnp.where(first_half, 0.0, tot[...]), axis=1, keepdims=True)
    norm_o[...] = norm
    factor = jnp.minimum(1.0, max_norm / (norm + 1e-06))
    grads = (
        gq_s[...],
        go_s[...],
        jnp.concatenate([g[64:65, :], g[65:66, : per_head - 128]], axis=1),
        g[66:67, :per_small],
    )
    for i in range(4):
        first_new, second_new, weight_new = adamw(
            weights[i], firsts[i][...], seconds[i][...], grads[i], factor, float(STEP), learn_rates[i]
        )
        new[i][...] = weight_new
        first_o[i][...] = first_new
        second_o[i][...] = second_new
        if copy_o[i] is not None:
            copy_o[i][...] = weight_new.astype(bf16)
        else:
            flat_o[...] = weight_new.astype(bf16).reshape(weight_new.shape[1])


def update_call(g, tot, w_qkv, w_out, keep, firsts, seconds):
    vm = pl.BlockSpec(memory_space=pltpu.VMEM)
    shapes = [v.shape for v in firsts]
    outs = [jax.ShapeDtypeStruct(s, f32) for s in shapes] * 3
    outs += [jax.ShapeDtypeStruct(s, bf16) for s in shapes[:2] + shapes[3:]]
    outs += [jax.ShapeDtypeStruct((shapes[2][1],), bf16)]
    outs += [jax.ShapeDtypeStruct((1, 1), f32)] * 2
    return pl.pallas_call(
        update_kernel,
        out_shape=tuple(outs),
        in_specs=[vm] * 13,
        out_specs=(vm,) * 18,
        scratch_shapes=[pltpu.VMEM((48, 128), f32), pltpu.VMEM((16, 128), f32)],
        compiler_params=pltpu.CompilerParams(vmem_limit_bytes=4 * 1024 * 1024),
    )(g, tot, w_qkv, w_out, keep, *firsts, *seconds)


def local_fast(
    n, query_feats, feature_mask, query_task, target_class, target_mask, memory_feats, memory_task,
    memory_mask, anneal, w_qkv, w_out, w_heads, w_small, m_qkv, m_out, m_heads, m_small,
    v_qkv, v_out, v_heads, v_small,
):
    def row(v):
        return v.reshape(1, -1)

    def tiles(v):
        return v.reshape(-1, 128)

    weights = (tiles(w_qkv), tiles(w_out), row(w_heads), row(w_small))
    firsts = (tiles(m_qkv), tiles(m_out), row(m_heads), row(m_small))
    seconds = (tiles(v_qkv), tiles(v_out), row(v_heads), row(v_small))
    tm, mt = row(target_mask), row(memory_task)
    gw, table, keep = gather_call(
        n, *weights, memory_feats.T, query_feats.T, feature_mask.T, row(query_task),
        row(target_class), tm, mt, row(memory_mask),
    )
    found = step_call(n, mt.shape[1], w_small.shape[0] * n, table, anneal, gw)
    grads, totals = reduce_call(n, w_small.shape[0], *found)
    outs = update_call(grads, totals, weights[0], weights[1], keep, firsts, seconds)
    outs = [out.reshape(-1) for out in outs]
    return tuple(outs[:14] + [outs[15]] + [outs[14]] + outs[16:])


def solution(mesh):
    placed = (
        P("mem", None),
        P("mem", None),
        P("mem"),
        P("mem"),
        P("mem"),
        P("mem", None),
        P(),
        P(),
        P(),
        P("mem"),
        P("mem"),
        P("mem"),
        P("mem"),
        P("mem"),
        P("mem"),
        P("mem"),
        P("mem"),
        P("mem"),
        P("mem"),
        P("mem"),
        P("mem"),
    )
    n = mesh.shape["mem"]

    def choose(*args):
        if D // n == 8 and args[6].shape[0] in (2048, 4096):
            return local_fast(n, *args)
        return local(*args)

    return jax.shard_map(
        choose,
        mesh=mesh,
        in_specs=placed,
        out_specs=(
            P("mem"),
            P("mem"),
            P("mem"),
            P("mem"),
            P("mem"),
            P("mem"),
            P("mem"),
            P("mem"),
            P("mem"),
            P("mem"),
            P("mem"),
            P("mem"),
            P("mem"),
            P("mem"),
            P("mem"),
            P("mem"),
            P(),
            P(),
        ),
        check_vma=False,
    )
```

```python
import functools
import math

import jax
import jax.numpy as jnp
from jax import lax
from jax.experimental import pallas as pl
from jax.experimental.pallas import tpu as pltpu
from jax.sharding import PartitionSpec as P

F = 8
D = 256
H = 8
C = 16
TASKS = 4
STEP = 10


eps_norm = 1e-05
max_norm = 0.05
beta_one = 0.9
beta_two = 0.999
adam_eps = 1e-08
decay_rate = 0.01
learn_rates = (0.05, 1.0, 0.05, 0.5)
masked_score = -1e30


def embed(feature_rows, table_flat, emb_bias):
    emb_table = table_flat.reshape(feature_rows.shape[1], -1)
    return (feature_rows[:, :, None] * emb_table[None]).reshape(
        feature_rows.shape[0], -1
    ) + emb_bias


def standard(hidden):
    centred = hidden - jnp.mean(hidden, -1, keepdims=True)
    inverse = lax.rsqrt(jnp.mean(centred * centred, -1, keepdims=True) + eps_norm)
    return (centred * inverse, inverse)


def norm_back(grad_out, hidden, gain_vec):
    normed, inverse = standard(hidden)
    grad_gain = jnp.sum(grad_out * normed, 0)
    grad_scaled = grad_out * gain_vec
    grad_hidden = inverse * (
        grad_scaled
        - jnp.mean(grad_scaled, -1, keepdims=True)
        - normed * jnp.mean(grad_scaled * normed, -1, keepdims=True)
    )
    return (grad_hidden, grad_gain)


def split_pair(values):
    upper = values.astype(jnp.bfloat16)
    lower = (values - upper.astype(jnp.float32)).astype(jnp.bfloat16)
    return (upper, lower)


def adamw(weight, first_mom, second, grad_in, factor, step_num, step_rate):
    clipped = grad_in * factor
    first_new = beta_one * first_mom + (1 - beta_one) * clipped
    second_new = beta_two * second + (1 - beta_two) * clipped * clipped
    fix_one = 1 - beta_one**step_num
    fix_two = 1 - beta_two**step_num
    weight_new = weight - step_rate * (
        first_new / fix_one / (jnp.sqrt(second_new / fix_two) + adam_eps) + decay_rate * weight
    )
    return (first_new, second_new, weight_new)


def local(
    query_feats,
    feature_mask,
    query_task,
    target_class,
    target_mask,
    memory_feats,
    memory_task,
    memory_mask,
    anneal,
    w_qkv,
    w_out,
    w_heads,
    w_small,
    m_qkv,
    m_out,
    m_heads,
    m_small,
    v_qkv,
    v_out,
    v_heads,
    v_small,
):
    high = lax.Precision.HIGHEST
    head_size = D // H
    full_qkv, full_out, full_heads, full_small = (
        lax.all_gather(w_qkv, "mem", axis=0, tiled=True),
        lax.all_gather(w_out, "mem", axis=0, tiled=True),
        lax.all_gather(w_heads, "mem", axis=0, tiled=True),
        lax.all_gather(w_small, "mem", axis=0, tiled=True),
    )
    emb_table = full_small[:D]
    emb_bias = full_small[D : 2 * D]
    gain_in = full_small[2 * D : 3 * D]
    gain_out = full_small[3 * D : 4 * D]
    score_coef = full_small[4 * D : 4 * D + H] * head_size ** (-0.5)
    qkv_low = full_qkv.reshape(D, 3 * D).astype(jnp.bfloat16)
    out_low = full_out.reshape(D, D).astype(jnp.bfloat16)
    heads_low = full_heads.reshape(D, C + F).astype(jnp.bfloat16)
    mem_hidden = embed(memory_feats, emb_table, emb_bias)
    mem_normed = (standard(mem_hidden)[0] * gain_in).astype(jnp.bfloat16)
    mem_kv = jnp.dot(mem_normed, qkv_low[:, D:], preferred_element_type=jnp.float32).astype(
        jnp.bfloat16
    )
    all_kv = lax.all_gather(mem_kv, "mem", axis=0, tiled=True)
    memory_rows = all_kv.shape[0]
    block_keys = math.gcd(memory_rows, 512)
    num_blocks = memory_rows // block_keys
    key_rows = all_kv[:, :D].reshape(num_blocks, block_keys, H, head_size)
    value_rows = all_kv[:, D:].reshape(num_blocks, block_keys, H, head_size)
    task_blocks = memory_task.reshape(num_blocks, block_keys)
    live_blocks = memory_mask.reshape(num_blocks, block_keys)
    key_blocks = (key_rows, value_rows, task_blocks, live_blocks)
    kept_input = query_feats * (1 - feature_mask).astype(jnp.float32)
    hidden_in = embed(kept_input, emb_table, emb_bias)
    query_normed = (standard(hidden_in)[0] * gain_in).astype(jnp.bfloat16)
    queries = (
        jnp.dot(query_normed, qkv_low[:, :D], preferred_element_type=jnp.float32)
        .astype(jnp.bfloat16)
        .reshape(-1, H, head_size)
    )
    num_rows = queries.shape[0]

    def allowed_of(task_row, live_row):
        return ((query_task[:, None] == task_row[None, :]) & (live_row[None, :] > 0))[None]

    def scores_of(key_block, allowed):
        raw_scores = jnp.einsum(
            "qhd,khd->hqk", queries, key_block, preferred_element_type=jnp.float32
        )
        return (
            raw_scores,
            jnp.where(allowed, score_coef[:, None, None] * raw_scores, masked_score),
        )

    def stats_step(state_in, block_data):
        row_top, row_sum = state_in
        key_block, value_block, task_row, live_row = block_data
        allowed = allowed_of(task_row, live_row)
        scores = scores_of(key_block, allowed)[1]
        new_top = jnp.maximum(row_top, jnp.max(scores, -1))
        shifted = jnp.where(allowed, jnp.exp(scores - new_top[..., None]), 0.0)
        return ((new_top, row_sum * jnp.exp(row_top - new_top) + jnp.sum(shifted, -1)), None)

    start_state = (
        jnp.full((H, num_rows), masked_score, jnp.float32),
        jnp.zeros((H, num_rows), jnp.float32),
    )
    (row_top, row_sum), unused = lax.scan(stats_step, start_state, key_blocks)

    def probs_of(scores, allowed):
        return jnp.where(allowed, jnp.exp(scores - row_top[..., None]), 0.0) / row_sum[..., None]

    def value_step(accum, block_data):
        key_block, value_block, task_row, live_row = block_data
        allowed = allowed_of(task_row, live_row)
        probs_low = probs_of(scores_of(key_block, allowed)[1], allowed).astype(jnp.bfloat16)
        return (
            accum
            + jnp.einsum(
                "hqk,khd->qhd", probs_low, value_block, preferred_element_type=jnp.float32
            ),
            None,
        )

    attn_sum, unused = lax.scan(
        value_step, jnp.zeros((num_rows, H, head_size), jnp.float32), key_blocks
    )
    attended = attn_sum.reshape(num_rows, D).astype(jnp.bfloat16)
    residual = hidden_in + jnp.dot(attended, out_low, preferred_element_type=jnp.float32)
    final_normed = (standard(residual)[0] * gain_out).astype(jnp.bfloat16)
    head_out = jnp.dot(final_normed, heads_low, preferred_element_type=jnp.float32)
    logits = head_out[:, :C]
    recon_err = head_out[:, C:] - query_feats
    label_mask = target_mask.astype(jnp.float32)
    feat_mask = feature_mask.astype(jnp.float32)
    onehot_class = jax.nn.one_hot(target_class, C, dtype=jnp.float32)
    picked = jnp.sum(logits * onehot_class, -1)
    sum_target, sum_recon, count_target, count_recon = lax.psum(
        (
            jnp.sum(label_mask * (jax.nn.logsumexp(logits, -1) - picked)),
            jnp.sum(feat_mask * recon_err**2),
            jnp.sum(label_mask),
            jnp.sum(feat_mask),
        ),
        "mem",
    )
    count_target = jnp.maximum(count_target, 1.0)
    count_recon = jnp.maximum(count_recon, 1.0)
    weight_a = anneal[0]
    loss_value = weight_a * sum_target / count_target + (1 - weight_a) * sum_recon / count_recon
    grad_logits = (
        weight_a / count_target * label_mask[:, None] * (jax.nn.softmax(logits, -1) - onehot_class)
    )
    grad_recon = (1 - weight_a) / count_recon * feat_mask * 2.0 * recon_err
    grad_head_out = jnp.concatenate([grad_logits, grad_recon], 1).astype(jnp.bfloat16)
    grad_heads = jnp.dot(final_normed.T, grad_head_out, preferred_element_type=jnp.float32)
    grad_final = jnp.dot(grad_head_out, heads_low.T, preferred_element_type=jnp.float32)
    grad_resid, grad_gain_out = norm_back(grad_final, residual, gain_out)
    grad_branch = grad_resid.astype(jnp.bfloat16)
    grad_wout = jnp.dot(attended.T, grad_branch, preferred_element_type=jnp.float32)
    grad_attn = (
        jnp.dot(grad_branch, out_low.T, preferred_element_type=jnp.float32)
        .astype(jnp.bfloat16)
        .reshape(num_rows, H, head_size)
    )
    row_delta = jnp.sum(
        grad_attn.astype(jnp.float32)
        * attended.reshape(num_rows, H, head_size).astype(jnp.float32),
        -1,
    ).T

    def back_step(state_in, block_data):
        key_block, value_block, task_row, live_row = block_data
        allowed = allowed_of(task_row, live_row)
        raw_scores, scores = scores_of(key_block, allowed)
        soft_probs = probs_of(scores, allowed)
        grad_probs = jnp.einsum(
            "qhd,khd->hqk", grad_attn, value_block, preferred_element_type=jnp.float32
        )
        grad_scores = (soft_probs * (grad_probs - row_delta[..., None])).astype(jnp.bfloat16)
        grad_beta = jnp.sum(grad_scores.astype(jnp.float32) * raw_scores, (1, 2))
        grad_query = jnp.einsum(
            "hqk,khd->qhd", grad_scores, key_block, preferred_element_type=jnp.float32
        )
        grad_key = (
            jnp.einsum("hqk,qhd->khd", grad_scores, queries, preferred_element_type=jnp.float32)
            * score_coef[None, :, None]
        )
        grad_value = jnp.einsum(
            "hqk,qhd->khd",
            soft_probs.astype(jnp.bfloat16),
            grad_attn,
            preferred_element_type=jnp.float32,
        )
        block_rows = key_block.shape[0]
        grad_kv = jnp.concatenate(
            [grad_key.reshape(block_rows, D), grad_value.reshape(block_rows, D)], 1
        )
        return ((state_in[0] + grad_query, state_in[1] + grad_beta), grad_kv)

    init_state = (jnp.zeros((num_rows, H, head_size), jnp.float32), jnp.zeros((H,), jnp.float32))
    (grad_q_sum, grad_beta_sum), kv_parts = lax.scan(back_step, init_state, key_blocks)
    kv_grad = lax.psum_scatter(
        kv_parts.reshape(memory_rows, 2 * D), "mem", scatter_dimension=0, tiled=True
    )
    grad_q_low = (grad_q_sum * score_coef[None, :, None]).reshape(num_rows, D).astype(jnp.bfloat16)
    grad_wq = jnp.dot(query_normed.T, grad_q_low, preferred_element_type=jnp.float32)
    grad_qn = jnp.dot(grad_q_low, qkv_low[:, :D].T, preferred_element_type=jnp.float32)
    grad_in_q, gain_in_q = norm_back(grad_qn, hidden_in, gain_in)
    grad_hidden = grad_resid + grad_in_q
    kv_upper, kv_lower = split_pair(kv_grad)
    grad_wkv = jnp.dot(mem_normed.T, kv_upper, preferred_element_type=jnp.float32) + jnp.dot(
        mem_normed.T, kv_lower, preferred_element_type=jnp.float32
    )
    grad_mn = jnp.dot(kv_upper, qkv_low[:, D:].T, preferred_element_type=jnp.float32) + jnp.dot(
        kv_lower, qkv_low[:, D:].T, preferred_element_type=jnp.float32
    )
    grad_mem, gain_in_m = norm_back(grad_mn, mem_hidden, gain_in)
    grad_table = jnp.einsum(
        "qf,qfe->fe", kept_input, grad_hidden.reshape(num_rows, F, -1), precision=high
    )
    grad_table = grad_table + jnp.einsum(
        "qf,qfe->fe", memory_feats, grad_mem.reshape(memory_feats.shape[0], F, -1), precision=high
    )
    grad_bias = jnp.sum(grad_hidden, 0) + jnp.sum(grad_mem, 0)
    small_size = full_small.shape[0]
    grad_small = jnp.concatenate(
        [
            grad_table.reshape(-1),
            grad_bias,
            gain_in_q + gain_in_m,
            grad_gain_out,
            grad_beta_sum * head_size ** (-0.5),
            jnp.zeros((small_size - 4 * D - H,), jnp.float32),
        ]
    )
    grad_qkv = jnp.concatenate([grad_wq, grad_wkv], 1).reshape(-1)
    shards = (
        lax.psum_scatter(grad_qkv, "mem", scatter_dimension=0, tiled=True),
        lax.psum_scatter(grad_wout.reshape(-1), "mem", scatter_dimension=0, tiled=True),
        lax.psum_scatter(grad_heads.reshape(-1), "mem", scatter_dimension=0, tiled=True),
        lax.psum_scatter(grad_small, "mem", scatter_dimension=0, tiled=True),
    )
    local_squares = sum((jnp.sum(piece_grad * piece_grad) for piece_grad in shards))
    grad_total = jnp.sqrt(lax.psum(local_squares, "mem"))
    factor = jnp.minimum(1.0, max_norm / (grad_total + 1e-06))
    step_num = float(STEP)
    weights_all = (w_qkv, w_out, w_heads, w_small)
    firsts = (m_qkv, m_out, m_heads, m_small)
    seconds = (v_qkv, v_out, v_heads, v_small)
    results = [
        adamw(weight, first_mom, second, grad_in, factor, step_num, step_rate)
        for weight, first_mom, second, grad_in, step_rate in zip(
            weights_all, firsts, seconds, shards, learn_rates
        )
    ]
    new_w = [entry[2] for entry in results]
    return (
        new_w[0],
        new_w[1],
        new_w[2],
        new_w[3],
        results[0][0],
        results[1][0],
        results[2][0],
        results[3][0],
        results[0][1],
        results[1][1],
        results[2][1],
        results[3][1],
        new_w[0].astype(jnp.bfloat16),
        new_w[1].astype(jnp.bfloat16),
        new_w[2].astype(jnp.bfloat16),
        new_w[3].astype(jnp.bfloat16),
        loss_value.reshape(1),
        grad_total.reshape(1),
    )


f32 = jnp.float32
bf16 = jnp.bfloat16
LOG2E = math.log2(math.e)
QB = 128
KC = 384
KC_LOW = 320
VROWS = 80
E_CAP = 12
STEP_VMEM = 44 * 1024 * 1024
PRE_SPAN = 3
MID_SPAN = 6
MEM_SPAN = 2
SMALL_LANE = 88
COUNT_LANE = 122


def place_of(dev, planes):
    return (dev % 2) * (4 * planes) + ((dev // 2) % 4) * planes + dev // 8


def nt(a, b):
    return lax.dot_general(a, b, (((1,), (1,)), ((), ())), preferred_element_type=f32)


def tn(a, b):
    return lax.dot_general(a, b, (((0,), (0,)), ((), ())), preferred_element_type=f32)


def nn(a, b):
    return jnp.dot(a, b, preferred_element_type=f32)


def iota(shape, dim):
    return lax.broadcasted_iota(jnp.int32, shape, dim)


def split2(v):
    hi = v.astype(bf16).astype(f32)
    return hi, v - hi


def split3(v):
    hi, rest = split2(v)
    mid = rest.astype(bf16).astype(f32)
    return hi, mid, rest - mid


def wide(v, lanes):
    return jnp.concatenate([v] * (lanes // v.shape[1]), axis=1) if lanes > v.shape[1] else v


def embed_t(kept, table, bias):
    parts = []
    for f in range(F):
        rows = slice(32 * f, 32 * f + 32)
        parts.append(kept[f : f + 1] * table[rows] + bias[rows])
    return jnp.concatenate(parts, axis=0)


def fold(v):
    total = v[:, :128]
    for k in range(1, v.shape[1] // 128):
        total = total + v[:, 128 * k : 128 * k + 128]
    return total


def by_feature(grad, kept):
    return jnp.concatenate(
        [kept[f : f + 1] * grad[32 * f : 32 * f + 32] for f in range(F)], axis=0
    )


def added(found, k):
    total = found[0][k]
    for one in found[1:]:
        total = total + one[k]
    return total


def norm_t(v):
    centred = v - jnp.mean(v, axis=0, keepdims=True)
    inverse = lax.rsqrt(jnp.mean(centred * centred, axis=0, keepdims=True) + eps_norm)
    return centred * inverse, inverse


def norm_back_t(grad, normed, inverse, gain):
    scaled = grad * gain
    return inverse * (
        scaled
        - jnp.mean(scaled, axis=0, keepdims=True)
        - normed * jnp.mean(scaled * normed, axis=0, keepdims=True)
    )


def blocks_of(num_q):
    blocks = (num_q + TASKS * (QB - 1)) // QB
    return -(-blocks // 4) * 4


def chunks_of(num_mem):
    chunks = (num_mem + TASKS * (KC - 1)) // KC
    return -(-chunks // MEM_SPAN) * MEM_SPAN


def step_kernel(
    n, qs, num_mem, small_size,
    an, gw,
    xs, fs, qn_s, q_s, att, gb_s, fn_s, gho_s, gres, dq_s, gkv, w_q, cols, coefb, acc_gain, out_l,
    ct, w_s, wt_s, wh_s, wht_s,
    mfeat, kn, vn, kt_s, vt_s, mnt, gk, gv,
    il_s, dap, delta, ebuf, ecur, acc, m_s,
    blk_c0, blk_nc, blk_tile, blk_rows, ch_base, ch_end, numbers, table, loaded,
):
    planes = n // 8
    per_small = small_size // n
    k_chunks = ch_base.shape[0]

    for i in range(num_mem // 2048):
        both = gw[n + 1 + i, 48:64, :].astype(f32)
        numbers[:, 128 * i : 128 * i + 128] = (both[0:8] + both[8:16]).astype(jnp.int32)
    copy = pltpu.make_async_copy(numbers, table, loaded)
    copy.start()
    copy.wait()
    m_base, m_count, m_units, q_base, q_units = (
        [table[3, TASKS * k + t] for t in range(TASKS)] for k in range(5)
    )
    num_blocks = q_units[0] + q_units[1] + q_units[2] + q_units[3]
    num_chunks = m_units[0] + m_units[1] + m_units[2] + m_units[3]
    for c in range(k_chunks):
        ch_base[c] = jnp.int32(c * KC)
        ch_end[c] = jnp.int32(c * KC)
    tile = jnp.int32(0)
    for t in range(TASKS):
        first_chunk = lax.div(m_base[t], jnp.int32(KC))
        first_block = lax.div(q_base[t], jnp.int32(QB))

        def fill_chunk(i, carry, t=t, first_chunk=first_chunk):
            ch_base[first_chunk + i] = m_base[t]
            ch_end[first_chunk + i] = m_base[t] + m_count[t]
            return carry

        lax.fori_loop(0, m_units[t], fill_chunk, 0)

        def fill_block(i, tile_in, t=t, first_chunk=first_chunk, first_block=first_block):
            blk_c0[first_block + i] = first_chunk
            blk_nc[first_block + i] = m_units[t]
            blk_rows[first_block + i] = m_count[t]
            blk_tile[first_block + i] = tile_in
            return tile_in + m_units[t]

        tile = lax.fori_loop(0, q_units[t], fill_block, tile)

    pieces = [gw[place_of(d, planes)].astype(f32) for d in range(n)]
    for col in range(8):
        block = jnp.concatenate([piece[8 * col : 8 * col + 8] for piece in pieces], axis=0)
        w_s[:, 128 * col : 128 * col + 128] = block.astype(bf16)
        wt_s[128 * col : 128 * col + 128, :] = block.T.astype(bf16)
    lane = iota((8, 128), 1)
    tiles = [piece[64:72] + piece[72:80] for piece in pieces]
    lane_w = iota((D, 128), 1)
    heads = pltpu.roll(jnp.concatenate(tiles, axis=0), 64, 1)
    heads = jnp.where(lane_w < C + F, heads, 0.0)
    wh_s[...] = heads.astype(bf16)
    wht_s[...] = heads.T[:32].astype(bf16)

    for b in range(qs // 128):
        block = gw[n + b, 0:48, :].astype(f32)
        cut = slice(128 * b, 128 * b + 128)
        xs[:, cut] = block[0:8] + block[8:16] + block[16:24]
        fs[:, cut] = block[24:32]
        ct[:, cut] = block[32:40]

    small_rows = jnp.concatenate([tile[0:1] for tile in tiles], axis=0)
    lane_n = iota((n, 128), 1)
    count_t = jnp.maximum(jnp.sum(jnp.where(lane_n == COUNT_LANE, small_rows, 0.0)), 1.0)
    count_r = jnp.maximum(jnp.sum(jnp.where(lane_n == COUNT_LANE + 1, small_rows, 0.0)), 1.0)
    used = 4 * D + 2 * H
    s2 = jnp.concatenate(
        list(split2(small_rows)) + [jnp.zeros((128 - 2 * n, 128), f32)], axis=0
    ).astype(bf16)
    row = iota((used, 128), 0)
    lan = iota((used, 128), 1)
    dev_of = lan & (n - 1)
    pick = (row >= per_small * dev_of) & (row < per_small * dev_of + per_small) & (lan < 2 * n)
    spread = nn(pick.astype(f32).astype(bf16), s2)
    row_dev = jnp.floor((row.astype(f32) + 0.5) * (1.0 / per_small)).astype(jnp.int32)
    here = (lan - SMALL_LANE) == (row - per_small * row_dev)
    column = jnp.sum(jnp.where(here, spread, 0.0), axis=1, keepdims=True)
    cols[...] = jnp.broadcast_to(column[: 4 * D], (4 * D, 128))
    for h in range(H):
        coefb[32 * h : 32 * h + 32, :] = jnp.broadcast_to(
            column[4 * D + h : 4 * D + h + 1] * (32 ** (-0.5)), (32, 128)
        )

    emb_w = lambda lanes: wide(cols[0:D, :], lanes)
    emb_b = lambda lanes: wide(cols[D : 2 * D, :], lanes)
    gain_in = lambda lanes: wide(cols[2 * D : 3 * D, :], lanes)
    gain_out = lambda lanes: wide(cols[3 * D : 4 * D, :], lanes)

    places = gw[n, 48 : 48 + n // 2, :].astype(f32)
    for b in range(n // 2):
        raw = jnp.where(lane < 64, tiles[2 * b], pltpu.roll(tiles[2 * b + 1], 64, 1))
        chosen = (places[b : b + 1] == iota((128, 1), 0).astype(f32)).astype(f32)
        got = nt(jnp.concatenate(split2(raw), axis=0).astype(bf16), chosen.astype(bf16))
        run = got[0:8] + got[8:16]
        for t in range(TASKS):
            i = 8 * b + t
            start, count, slot = table[0, i], table[1, i], table[2, i]
            first = slot & 127
            shift = (first - start) & 127
            moved = pltpu.roll(run, shift, 1)
            at = pl.multiple_of(slot - first, 128)
            pltpu.store(
                mfeat.at[:, pl.ds(at, 128)], moved, mask=(lane >= first) & (lane < first + count)
            )
            pltpu.store(mfeat.at[:, pl.ds(at + 128, 128)], moved, mask=lane < first + count - 128)

    def mem_feats(c):
        base, end = ch_base[c], ch_end[c]
        at = pl.ds(pl.multiple_of(c * KC, KC), KC)
        slot = iota((8, KC), 1) + c * KC
        head = mfeat[:, pl.ds(pl.multiple_of(base, KC), 128)][:, 0:1]
        live = (slot < end).astype(f32)[0:1]
        return jnp.where(slot < end, mfeat[:, at], jnp.where(end > base, head, 0.0)), live

    def mem_pair(i, carry):
        found = []
        for k in range(MEM_SPAN):
            c = MEM_SPAN * i + k
            feats_c, live = mem_feats(c)
            normed, unused = norm_t(embed_t(feats_c, emb_w(KC), emb_b(KC)))
            mnf = normed * gain_in(KC)
            mn = mnf.astype(bf16)
            keys_t = (nn(wt_s[D : 2 * D, :], mn) * live).astype(bf16)
            vals_t = nn(wt_s[2 * D : 3 * D, :], mn) * live
            tail = jnp.where(iota((16, KC), 0) == 0, live, 0.0)
            vals_t = jnp.concatenate(
                [part for p in range(4) for part in (vals_t[64 * p : 64 * p + 64], tail)], axis=0
            ).astype(bf16)
            both = nn(mnf.T.astype(bf16), w_s[:, D : 3 * D])
            live_col = ((iota((KC, 1), 0) + c * KC) < ch_end[c]).astype(f32)
            found.append((mn, keys_t, vals_t, both[:, :D], both[:, D:] * live_col))
        for k in range(MEM_SPAN):
            at = pl.ds(pl.multiple_of((MEM_SPAN * i + k) * KC, KC), KC)
            mnt[:, at], kt_s[:, at], vt_s[:, at] = found[k][0:3]
            kn[at, :] = found[k][3].astype(bf16)
            vn[at, :] = found[k][4].astype(bf16)
            gk[at, :] = jnp.zeros((KC, D), f32)
            gv[at, :] = jnp.zeros((KC, D), f32)
        return carry

    lax.fori_loop(0, lax.div(num_chunks + MEM_SPAN - 1, jnp.int32(MEM_SPAN)), mem_pair, 0)

    def spots(j, span):
        return [pl.ds(pl.multiple_of((j * span + k) * 256, 256), 256) for k in range(span)]

    def pre_block(j, carry):
        found = []
        for at in spots(j, PRE_SPAN):
            kept = xs[:, at] * (1.0 - fs[:, at])
            normed, unused = norm_t(embed_t(kept, emb_w(256), emb_b(256)))
            qn = (normed * gain_in(256)).astype(bf16)
            found.append((qn, nn(wt_s[0:D, :], qn).astype(bf16)))
        for k, at in enumerate(spots(j, PRE_SPAN)):
            qn_s[:, at], q_s[:, at] = found[k]
            att[:, at] = jnp.zeros((D, 256), bf16)
            il_s[:, at] = jnp.zeros((H, 256), f32)
            dq_s[:, at] = jnp.zeros((D, 256), f32)
        return carry

    lax.fori_loop(0, qs // (256 * PRE_SPAN), pre_block, 0)

    zero_h = jnp.zeros((32, 128), bf16)
    zero_p = jnp.zeros((64, 256), bf16)

    def pair(p, width):
        return slice(width * p, width * p + width)

    def half(p):
        return slice(128 * (p // 2), 128 * (p // 2) + 128)

    def two_heads(ref, at, p):
        diag = jnp.concatenate(
            [
                jnp.concatenate([ref[64 * p : 64 * p + 32, at], zero_h], axis=1),
                jnp.concatenate([zero_h, ref[64 * p + 32 : 64 * p + 64, at]], axis=1),
            ],
            axis=0,
        )
        return jnp.concatenate([zero_p, diag] if p % 2 else [diag, zero_p], axis=0)

    def coef_row(p):
        return LOG2E * jnp.concatenate(
            [coefb[64 * p : 64 * p + 1, :], coefb[64 * p + 32 : 64 * p + 33, :]], axis=1
        )

    def finish_forward(at, p, got):
        inverse = 1.0 / got[64:65, :]
        il_s[2 * p : 2 * p + 1, at] = inverse[:, :128]
        il_s[2 * p + 1 : 2 * p + 2, at] = inverse[:, 128:]
        att[64 * p : 64 * p + 32, at] = (got[0:32, :128] * inverse[:, :128]).astype(bf16)
        att[64 * p + 32 : 64 * p + 64, at] = (got[32:64, 128:] * inverse[:, 128:]).astype(bf16)

    def forward_some(blocks, rows):
        work = []
        for i in blocks:
            at = pl.ds(pl.multiple_of(i * QB, QB), QB)
            first = blk_c0[i] * KC
            keys = pl.ds(pl.multiple_of(first, KC), rows)
            operands = [two_heads(q_s, at, p) for p in range(4)]
            values = [vt_s[pair(p, VROWS), pl.ds(pl.multiple_of(first, KC), KC)][:, :rows] for p in range(4)]
            work += [(kn[keys, half(p)], operands[p], coef_row(p), values[p]) for p in range(4)]
        scores = [nn(k, o) * c for k, o, c, unused in work]
        tops = [jnp.max(s, axis=0, keepdims=True) for s in scores]
        es = [jnp.exp2(s - top).astype(bf16) for s, top in zip(scores, tops)]
        sums = [nn(w[3], e) for w, e in zip(work, es)]
        for n_th, i in enumerate(blocks):
            at = pl.ds(pl.multiple_of(i * QB, QB), QB)
            keep = jnp.minimum(blk_tile[i], E_CAP)
            for p in range(4):
                m_s[i, :, pair(p, 256)] = tops[4 * n_th + p]
                ebuf[keep, :rows, pair(p, 256)] = es[4 * n_th + p]
                finish_forward(at, p, sums[4 * n_th + p])

    def forward_block(i, carry):
        at = pl.ds(pl.multiple_of(i * QB, QB), QB)
        c0, nc, tile0, count = blk_c0[i], blk_nc[i], blk_tile[i], blk_rows[i]

        @pl.when(count <= KC_LOW)
        def few():
            forward_some([i], KC_LOW)

        @pl.when((count > KC_LOW) & (nc == 1))
        def full():
            forward_some([i], KC)

        @pl.when(nc > 1)
        def many():
            m_s[i] = jnp.full((1, 1024), -3e38, f32)
            acc[...] = jnp.zeros_like(acc)

            def tops(c, inner):
                keys = pl.ds(pl.multiple_of((c0 + c) * KC, KC), KC)
                for p in range(4):
                    s = nn(kn[keys, half(p)], two_heads(q_s, at, p)) * coef_row(p)
                    m_s[i, :, pair(p, 256)] = jnp.maximum(
                        m_s[i, :, pair(p, 256)], jnp.max(s, axis=0, keepdims=True)
                    )
                return inner

            lax.fori_loop(0, nc, tops, 0)

            def sums(c, inner):
                keys = pl.ds(pl.multiple_of((c0 + c) * KC, KC), KC)
                keep = jnp.minimum(tile0 + c, E_CAP)
                for p in range(4):
                    s = nn(kn[keys, half(p)], two_heads(q_s, at, p)) * coef_row(p)
                    e = jnp.exp2(s - m_s[i, :, pair(p, 256)]).astype(bf16)
                    ebuf[keep, :, pair(p, 256)] = e
                    acc[pair(p, VROWS), :] += nn(vt_s[pair(p, VROWS), keys], e)
                return inner

            lax.fori_loop(0, nc, sums, 0)
            for p in range(4):
                finish_forward(at, p, acc[pair(p, VROWS), :])

        return carry

    def forward_pair(j, carry):
        i = 2 * j
        count = jnp.maximum(blk_rows[i], blk_rows[i + 1])

        @pl.when(count <= KC_LOW)
        def few():
            forward_some([i, i + 1], KC_LOW)

        @pl.when((count > KC_LOW) & (count <= KC))
        def full():
            forward_some([i, i + 1], KC)

        @pl.when(count > KC)
        def apart():
            lax.fori_loop(i, i + 2, forward_block, 0)

        return carry

    pairs = lax.div(num_blocks, jnp.int32(2))
    lax.fori_loop(0, pairs, forward_pair, 0)
    lax.fori_loop(2 * pairs, num_blocks, forward_block, 0)

    weight_a = an[0]
    scale_t = weight_a / count_t
    scale_r = (1.0 - weight_a) / count_r
    acc_gain[...] = jnp.zeros_like(acc_gain)
    out_l[...] = jnp.zeros_like(out_l)

    def mid_values(at):
        x = xs[:, at]
        fmask = fs[:, at]
        hidden = embed_t(x * (1.0 - fmask), emb_w(256), emb_b(256))
        attended = att[:, at]
        residual = hidden + nn(wt_s[3 * D : 4 * D, :], attended)
        normed, inverse = norm_t(residual)
        fn = (normed * gain_out(256)).astype(bf16)
        head = nn(wht_s[...], fn)
        logits = head[0:C]
        err = head[C : C + F] - x
        label = ct[1:2, at]
        hot = (iota((C, 256), 0).astype(f32) == ct[0:1, at]).astype(f32)
        top = jnp.max(logits, axis=0, keepdims=True)
        e = jnp.exp(logits - top)
        total = jnp.sum(e, axis=0, keepdims=True)
        picked = jnp.sum(logits * hot, axis=0, keepdims=True)
        loss = scale_t * label * (jnp.log(total) + top - picked) + scale_r * jnp.sum(
            fmask * err * err, axis=0, keepdims=True
        )
        g_log = scale_t * label * (e / total - hot)
        g_rec = scale_r * fmask * 2.0 * err
        gho = jnp.concatenate([g_log, g_rec, jnp.zeros((8, 256), f32)], axis=0).astype(bf16)
        g_final = nn(wh_s[:, :32], gho)
        g_res = norm_back_t(g_final, normed, inverse, gain_out(256))
        gb = g_res.astype(bf16)
        ga = nn(w_s[:, 3 * D : 4 * D], gb).astype(bf16).astype(f32)
        attf = attended.astype(f32)
        das, deltas = [], []
        for h in range(H):
            rows = slice(32 * h, 32 * h + 32)
            da = (ga[rows] * il_s[h : h + 1, at]).astype(bf16)
            das.append(da)
            deltas.append(jnp.sum(da.astype(f32) * attf[rows], axis=0, keepdims=True))
        return (
            fold(loss), fold(g_final * normed),
            fn, gho, g_res, gb, jnp.concatenate(das, axis=0), jnp.concatenate(deltas, axis=0),
        )

    def mid_block(j, carry):
        found = [mid_values(at) for at in spots(j, MID_SPAN)]
        out_l[0:1, :] += added(found, 0)
        acc_gain[D : 2 * D, :] += added(found, 1)
        for k, at in enumerate(spots(j, MID_SPAN)):
            for ref, value in zip((fn_s, gho_s, gres, gb_s, dap, delta), found[k][2:]):
                ref[:, at] = value
        return carry

    lax.fori_loop(0, qs // (256 * MID_SPAN), mid_block, 0)

    def backward_some(items, rows):
        work = []
        for at, c, e_of in items:
            lanes = pl.ds(pl.multiple_of(c * KC, KC), KC)
            keys = pl.ds(pl.multiple_of(c * KC, KC), rows)
            es = [e_of(p) for p in range(4)]
            das = [two_heads(dap, at, p) for p in range(4)]
            qds = [two_heads(q_s, at, p) for p in range(4)]
            kts = [kt_s[64 * p : 64 * p + 64, lanes][:, :rows] for p in range(4)]
            vals = [vn[keys, half(p)] for p in range(4)]
            work.append((at, keys, es, das, qds, kts, vals, delta[:, at], dq_s[:, at]))
        old_gk = gk[work[0][1], :]
        old_gv = gv[work[0][1], :]

        def by_key(grads, others):
            return jnp.concatenate(
                [
                    nt(
                        jnp.concatenate([grads[a], grads[a + 1]], axis=1),
                        jnp.concatenate([others[a], others[a + 1]], axis=1),
                    )
                    for a in (0, 2)
                ],
                axis=1,
            )

        dps = [[nn(w[6][p], w[3][p]) for p in range(4)] for w in work]
        dss = []
        for w, dp in zip(work, dps):
            takes = [
                jnp.concatenate([w[7][2 * p : 2 * p + 1], w[7][2 * p + 1 : 2 * p + 2]], axis=1)
                for p in range(4)
            ]
            dss.append([(w[2][p].astype(f32) * (dp[p] - takes[p])).astype(bf16) for p in range(4)])
        dqs = [[nn(w[5][p], ds[p]) for p in range(4)] for w, ds in zip(work, dss)]
        new_gvs = [by_key(w[2], w[3]) for w in work]
        new_gks = [by_key(ds, w[4]) for w, ds in zip(work, dss)]
        for w, dq in zip(work, dqs):
            parts = []
            for p in range(4):
                parts += [dq[p][0:32, :128], dq[p][32:64, 128:]]
            dq_s[:, w[0]] = w[8] + jnp.concatenate(parts, axis=0)
        gk[work[0][1], :] = old_gk + new_gks[0]
        gv[work[0][1], :] = old_gv + new_gvs[0]
        for w, new_gk, new_gv in zip(work[1:], new_gks[1:], new_gvs[1:]):
            gk[w[1], :] += new_gk
            gv[w[1], :] += new_gv

    def kept_weights(i, rows):
        return lambda p: ebuf[blk_tile[i], :rows, pair(p, 256)]

    def queries_of(i):
        return pl.ds(pl.multiple_of(i * QB, QB), QB)

    def backward_block(i, carry):
        at = pl.ds(pl.multiple_of(i * QB, QB), QB)
        c0, nc, tile0, count = blk_c0[i], blk_nc[i], blk_tile[i], blk_rows[i]
        simple = (nc == 1) & (tile0 < E_CAP)

        @pl.when(simple & (count <= KC_LOW))
        def few():
            backward_some([(at, c0, kept_weights(i, KC_LOW))], KC_LOW)

        @pl.when(simple & (count > KC_LOW))
        def full():
            backward_some([(at, c0, kept_weights(i, KC))], KC)

        @pl.when(jnp.logical_not(simple))
        def many():
            def one_chunk(c, inner):
                keys = pl.ds(pl.multiple_of((c0 + c) * KC, KC), KC)

                @pl.when((tile0 + c < E_CAP) & (nc > 1))
                def kept():
                    ecur[...] = ebuf[tile0 + c]

                @pl.when((tile0 + c >= E_CAP) | (nc == 1))
                def again():
                    for p in range(4):
                        s = nn(kn[keys, half(p)], two_heads(q_s, at, p)) * coef_row(p)
                        ecur[:, pair(p, 256)] = jnp.exp2(
                            s - m_s[i, :, pair(p, 256)]
                        ).astype(bf16)

                backward_some([(at, c0 + c, lambda p: ecur[:, pair(p, 256)])], KC)
                return inner

            lax.fori_loop(0, nc, one_chunk, 0)

        return carry

    def backward_pair(j, carry):
        two = (2 * j, 2 * j + 1)
        count = jnp.maximum(blk_rows[two[0]], blk_rows[two[1]])
        simple = (count <= KC) & (blk_tile[two[1]] < E_CAP)

        @pl.when(simple & (count <= KC_LOW))
        def few():
            backward_some([(queries_of(i), blk_c0[i], kept_weights(i, KC_LOW)) for i in two], KC_LOW)

        @pl.when(simple & (count > KC_LOW))
        def full():
            backward_some([(queries_of(i), blk_c0[i], kept_weights(i, KC)) for i in two], KC)

        @pl.when(jnp.logical_not(simple))
        def apart():
            lax.fori_loop(two[0], two[0] + 2, backward_block, 0)

        return carry

    lax.fori_loop(0, pairs, backward_pair, 0)
    lax.fori_loop(2 * pairs, num_blocks, backward_block, 0)

    gkv[...] = jnp.zeros_like(gkv)
    w_q[...] = w_s[:, 0:D]

    def mem_back(i, coef_lane):
        found = []
        for k in range(MEM_SPAN):
            c = MEM_SPAN * i + k
            at = pl.ds(pl.multiple_of(c * KC, KC), KC)
            feats_c, unused = mem_feats(c)
            live = ((iota((KC, 1), 0) + c * KC) < ch_end[c]).astype(f32)
            gk_c = (gk[at, :] * coef_lane * live).astype(bf16)
            gv_c = (gv[at, :] * live).astype(bf16)
            gmn = nt(w_s[:, D : 2 * D], gk_c) + nt(w_s[:, 2 * D : 3 * D], gv_c)
            normed, inverse = norm_t(embed_t(feats_c, emb_w(KC), emb_b(KC)))
            gm = norm_back_t(gmn, normed, inverse, gain_in(KC))
            found.append((gk_c, gv_c, fold(gmn * normed), fold(by_feature(gm, feats_c)), fold(gm)))
        mn = mnt[:, pl.ds(pl.multiple_of(MEM_SPAN * i * KC, KC), MEM_SPAN * KC)]
        gkv[:, 0:D] += nn(mn, jnp.concatenate([one[0] for one in found], axis=0))
        gkv[:, D : 2 * D] += nn(mn, jnp.concatenate([one[1] for one in found], axis=0))
        for k, rows in ((2, slice(0, D)), (3, slice(2 * D, 3 * D)), (4, slice(3 * D, 4 * D))):
            acc_gain[rows, :] += added(found, k)
        return coef_lane

    coef_lane = jnp.concatenate([coefb[0:128, :].T[0:1], coefb[128:256, :].T[0:1]], axis=1)
    lax.fori_loop(0, lax.div(num_chunks + MEM_SPAN - 1, jnp.int32(MEM_SPAN)), mem_back, coef_lane)


def step_call(n, num_mem, small_size, an, gw):
    q_blocks, k_chunks = gw.shape[0] - n, chunks_of(num_mem)
    qs, ks = q_blocks * QB, k_chunks * KC
    V = pltpu.VMEM
    S = pltpu.SMEM
    A = jax.ShapeDtypeStruct
    vm = pl.BlockSpec(memory_space=pltpu.VMEM)
    sm = pl.BlockSpec(memory_space=pltpu.SMEM)
    outs = (
        A((8, qs), f32), A((8, qs), f32), A((D, qs), bf16), A((D, qs), bf16), A((D, qs), bf16),
        A((D, qs), bf16), A((D, qs), bf16), A((32, qs), bf16), A((D, qs), f32), A((D, qs), f32),
        A((D, 2 * D), f32), A((D, D), bf16), A((4 * D, 128), f32), A((D, 128), f32),
        A((4 * D + H, 128), f32), A((8, 128), f32),
    )
    scratch = [
        V((8, qs), f32), V((D, 4 * D), bf16), V((4 * D, D), bf16), V((D, 128), bf16), V((32, D), bf16),
        V((8, ks + 128), f32), V((ks, D), bf16), V((ks, D), bf16), V((D, ks), bf16),
        V((4 * VROWS, ks), bf16), V((D, ks), bf16), V((ks, D), f32), V((ks, D), f32),
        V((H, qs), f32), V((D, qs), bf16), V((H, qs), f32),
        V((E_CAP + 1, KC, 1024), bf16), V((KC, 1024), bf16), V((4 * VROWS, 256), f32),
        V((q_blocks, 1, 1024), f32),
        S((q_blocks,), jnp.int32), S((q_blocks,), jnp.int32), S((q_blocks,), jnp.int32),
        S((q_blocks,), jnp.int32), S((k_chunks,), jnp.int32), S((k_chunks,), jnp.int32),
        V((8, num_mem // 16), jnp.int32), S((8, num_mem // 16), jnp.int32), pltpu.SemaphoreType.DMA,
    ]
    return pl.pallas_call(
        functools.partial(step_kernel, n, qs, num_mem, small_size),
        out_shape=outs,
        in_specs=[sm, vm],
        out_specs=(vm,) * len(outs),
        scratch_shapes=scratch,
        compiler_params=pltpu.CompilerParams(vmem_limit_bytes=STEP_VMEM),
    )(an, gw)


MESH = pl.DeviceIdType.MESH


def greet(targets):
    barrier = pltpu.get_barrier_semaphore()
    for target in targets:
        pl.semaphore_signal(barrier, inc=1, device_id=(target,), device_id_type=MESH)
    return barrier


def send(src, dst, send_sem, recv_sem, target):
    copy = pltpu.make_async_remote_copy(
        src_ref=src,
        dst_ref=dst,
        send_sem=send_sem,
        recv_sem=recv_sem,
        device_id=(target,),
        device_id_type=MESH,
    )
    copy.start()
    return copy


def where_am_i(planes):
    me = lax.axis_index("mem")
    core = lax.rem(me, 2)
    square = lax.rem(lax.div(me, 2), 4)
    plane = lax.div(me, 8)
    return me, core, square, plane


def gather_kernel(
    n, num_q, num_mem, *refs,
):
    sources, refs = refs[:12], refs[12:]
    gw, keep = refs[:2]
    copied, refs = refs[2:14], refs[14:]
    send_z, recv_z, send_s, recv_s, send_c, recv_c, load = refs
    loads = [
        pltpu.make_async_copy(sources[i], copied[i], load.at[i]) for i in range(len(sources))
    ]
    for copy in loads:
        copy.start()
    w_qkv, w_out, w_heads, w_small, mfeat, qf, fm, qt, tc, tm, mt, mm = copied
    planes = n // 8
    me, core, square, plane = where_am_i(planes)
    in_plane = core + 2 * square
    z_of = [lax.rem(plane + k, planes) * 8 + in_plane for k in range(1, planes)]
    s_of = [plane * 8 + lax.rem(square + k, 4) * 2 + core for k in range(1, 4)]
    c_of = plane * 8 + square * 2 + (1 - core)
    barrier = greet(z_of + s_of + [c_of])
    for copy in loads:
        copy.wait()

    rows = []
    for c in range(6):
        rows.append(w_qkv[pl.ds(c, 8, stride=6), :])
    for c in range(2):
        rows.append(w_out[pl.ds(c, 8, stride=2), :])
    per_head = w_heads.shape[1]
    lane = iota((8, 256), 1)
    head_row = jnp.concatenate([w_heads[...], jnp.zeros((1, 256 - per_head), f32)], axis=1)
    owner = jnp.floor((lane.astype(f32) + 0.5) * (1.0 / (C + F))).astype(jnp.int32)
    kept_heads = jnp.where(owner == iota((8, 256), 0), head_row, 0.0).astype(bf16)
    fold_r = iota((256, 128), 0)
    fold_row = jnp.floor((fold_r.astype(f32) + 0.5) * (1.0 / (C + F))).astype(jnp.int32)
    fold_m = (fold_r - (C + F) * fold_row == iota((256, 128), 1) - 64).astype(f32).astype(bf16)
    heads = nn(kept_heads, fold_m)
    per_small = w_small.shape[1]
    small = jnp.concatenate([w_small[...], jnp.zeros((1, 128 - per_small), f32)], axis=1)
    small = pltpu.roll(jnp.broadcast_to(small, (8, 128)), SMALL_LANE, 1)
    feats = jnp.concatenate([mfeat[...], jnp.zeros((8, 64), f32)], axis=1)
    lane8 = iota((8, 128), 1)
    row8 = iota((8, 128), 0)
    num_t = jnp.sum(tm[...].astype(f32), axis=1, keepdims=True)
    num_r = jnp.sum(jnp.sum(fm[...].astype(f32), axis=0, keepdims=True), axis=1, keepdims=True)
    block = feats + heads
    first = (row8 == 0) & (lane8 >= SMALL_LANE) & (lane8 < SMALL_LANE + per_small)
    block = jnp.where(first, small, block)
    block = jnp.where((row8 == 0) & (lane8 == COUNT_LANE), num_t, block)
    block = jnp.where((row8 == 0) & (lane8 == COUNT_LANE + 1), num_r, block)

    def slot_of(k, j, c):
        back = lax.rem(plane + planes - k, planes)
        return c * (4 * planes) + lax.rem(square + 4 - j, 4) * planes + back

    gw[slot_of(0, 0, core)] = jnp.concatenate(rows + list(split2(block)), axis=0).astype(bf16)

    pl.semaphore_wait(barrier, planes - 1 + 4)

    def spread(k, done):
        at = gw.at[slot_of(k, 0, core)]
        for j in range(1, 4):
            done[k, j] = send(at, at, send_s.at[k, j - 1], recv_s.at[k, j - 1], s_of[j - 1])
        done[k, 0, "c"] = send(at, at, send_c.at[k, 0], recv_c.at[k, 0], c_of)

    at = gw.at[slot_of(0, 0, core)]
    done = {}
    for k in range(1, planes):
        done[k] = send(at, at, send_z.at[k - 1], recv_z.at[k - 1], z_of[k - 1])
    spread(0, done)

    task_row = iota((8, 256), 0)
    marks = [(qt[:, 256 * b : 256 * b + 256] == task_row).astype(f32) for b in range(num_q // 256)]
    marks_q = jnp.concatenate(marks, axis=0)
    before = (iota((256, 256), 0) < iota((256, 256), 1)).astype(f32).astype(bf16)
    ranks = nn(marks_q.astype(bf16), before)
    totals = jnp.sum(marks_q, axis=1, keepdims=True)
    task_col = iota((8, 1), 0)

    def bases_of(sums, unit):
        base = jnp.int32(0)
        bases, counts, used = [], [], []
        base_vec = jnp.zeros((8, 1), f32)
        for t in range(TASKS):
            count = jnp.sum(jnp.where(task_col == t, sums, 0.0)).astype(jnp.int32)
            bases.append(base)
            counts.append(count)
            used.append(lax.div(count + (unit - 1), jnp.int32(unit)))
            base_vec = base_vec + jnp.where(task_col == t, base.astype(f32), 0.0)
            base = base + used[t] * unit
        return bases, counts, used, base_vec

    carry = jnp.zeros((8, 1), f32)
    carries = []
    for b in range(num_q // 256):
        carries.append(carry)
        carry = carry + totals[8 * b : 8 * b + 8]
    q_base, q_count, q_units, base_vec = bases_of(carry, QB)
    place_q = jnp.concatenate(
        [
            jnp.sum(marks[b] * (base_vec + carries[b] + ranks[8 * b : 8 * b + 8]), axis=0, keepdims=True)
            for b in range(num_q // 256)
        ],
        axis=1,
    )

    cuts = num_mem // 128
    task_row = iota((8, 128), 0)
    marks = []
    for b in range(cuts):
        cut = slice(128 * b, 128 * b + 128)
        marks.append(((mt[:, cut] == task_row) & (mm[:, cut] > 0)).astype(f32))
    marks_m = jnp.concatenate(marks, axis=0)
    ranks = nn(marks_m.astype(bf16), before[:128, :128])
    totals = jnp.broadcast_to(jnp.sum(marks_m, axis=1, keepdims=True), (8 * cuts, 128))
    r_to = iota((8 * cuts, 8 * cuts), 0)
    r_from = iota((8 * cuts, 8 * cuts), 1)
    same_cut = (r_to // 8 == r_from // 8) & (r_from < r_to)
    same_task = (r_to % 8 == r_from % 8) & (r_from < r_to)
    low_totals = totals.astype(bf16)
    starts = nn(same_cut.astype(f32).astype(bf16), low_totals)
    earlier = nn(same_task.astype(f32).astype(bf16), low_totals)
    last = slice(8 * cuts - 8, 8 * cuts)
    m_base, m_count, m_units, base_vec = bases_of((earlier + totals)[last, 0:1], KC)
    slots = earlier + jnp.concatenate([base_vec] * cuts, axis=0)
    places_m = jnp.concatenate(
        [
            jnp.sum(marks[b] * (starts[8 * b : 8 * b + 8] + ranks[8 * b : 8 * b + 8] + 1.0), axis=0, keepdims=True)
            - 1.0
            for b in range(cuts)
        ],
        axis=0,
    )
    eye = r_to == r_from

    def as_row(column):
        return jnp.sum(jnp.where(eye, wide(column, 8 * cuts), 0.0), axis=0, keepdims=True)

    row_t = iota((8, 8 * cuts), 0)
    lane_t = iota((8, 8 * cuts), 1)
    numbers = jnp.where(
        row_t == 0, as_row(starts), jnp.where(row_t == 1, as_row(totals), as_row(slots))
    )
    for i, number in enumerate(m_base + m_count + m_units + q_base + q_units):
        numbers = jnp.where((row_t == 3) & (lane_t == i), number.astype(f32), numbers)
    for i in range(cuts // 16):
        gw[n + 1 + i, 48:64, :] = jnp.concatenate(
            split2(numbers[:, 128 * i : 128 * i + 128]), axis=0
        ).astype(bf16)
    gw[n, 48 : 48 + cuts, :] = places_m.astype(bf16)
    heads_low = jnp.concatenate([w_heads[:, 128:], jnp.zeros((1, 256 - per_head), f32)], axis=1)
    small_row = jnp.concatenate([w_small[...], jnp.zeros((1, 128 - per_small), f32)], axis=1)
    keep[...] = jnp.where(
        row8 == 0, w_heads[:, :128], jnp.where(row8 == 1, heads_low, small_row)
    )
    xq = qf[...]
    fmq = fm[...].astype(f32)
    row8 = iota((8, num_q), 0)
    label_rows = jnp.where(
        row8 == 0, tc[...].astype(f32), jnp.where(row8 == 1, tm[...].astype(f32), 0.0)
    )
    q_rows = jnp.concatenate(
        list(split3(xq)) + [fmq, label_rows, jnp.zeros((8, num_q), f32)], axis=0
    ).astype(bf16)
    for b in range((gw.shape[0] - n) // 2):
        chosen = (
            (place_q == (iota((256, 1), 0) + 256 * b).astype(f32)).astype(f32).astype(bf16)
        )
        got = nt(q_rows, chosen).astype(bf16)
        gw[n + 2 * b, 0:48, :] = got[:, :128]
        gw[n + 2 * b + 1, 0:48, :] = got[:, 128:]


    for k in range(1, planes):
        done[k].wait_recv()
        spread(k, done)
    for k in range(planes):
        for j in range(1, 4):
            done[k, j].wait_recv()
            at = gw.at[slot_of(k, j, core)]
            done[k, j, "c"] = send(at, at, send_c.at[k, j], recv_c.at[k, j], c_of)
    for k in range(planes):
        for j in range(4):
            done[k, j, "c"].wait_recv()
    for copy in done.values():
        copy.wait_send()


def gather_call(n, w_qkv, w_out, w_heads, w_small, mfeat, qf, fm, qt, tc, tm, mt, mm):
    planes = n // 8
    operands = (w_qkv, w_out, w_heads, w_small, mfeat, qf, fm, qt, tc, tm, mt, mm)
    num_q, num_mem = qf.shape[1], mt.shape[1]
    qs = blocks_of(num_q) * QB
    vm = pl.BlockSpec(memory_space=pltpu.VMEM)
    dma = pltpu.SemaphoreType.DMA
    return pl.pallas_call(
        functools.partial(gather_kernel, n, num_q, num_mem),
        out_shape=(
            jax.ShapeDtypeStruct((n + qs // 128, 80, 128), bf16),
            jax.ShapeDtypeStruct((8, 128), f32),
        ),
        in_specs=[pl.BlockSpec(memory_space=pltpu.HBM)] * 12,
        out_specs=(vm,) * 2,
        scratch_shapes=[pltpu.VMEM(v.shape, v.dtype) for v in operands]
        + [
            dma((planes - 1,)), dma((planes - 1,)), dma((planes, 3)), dma((planes, 3)),
            dma((planes, 4)), dma((planes, 4)), dma((12,)),
        ],
        compiler_params=pltpu.CompilerParams(collective_id=0, has_side_effects=True),
    )(*operands)


def reduce_kernel(
    n, per_small,
    xs, fs, qn_s, q_s, att, gb_s, fn_s, gho_s, gres, dq_s, gkv, w_q, cols, coefb, sums_in, l_in,
    g_out, t_out, gq, acc_gain, s_s, r_core, t_square, r_square, t_plane, r_plane, own, n_mine, n_all,
    send_c, recv_c, send_s, recv_s, send_z, recv_z, send_n, recv_n,
):
    planes = n // 8
    rows_dev = D // n
    me, core, square, plane = where_am_i(planes)
    in_plane = core + 2 * square
    upper = lax.div(2 * plane, planes)
    low_plane = plane + upper * (planes - 1 - 2 * plane)
    a_of = []
    for i in range(planes):
        z = planes - 1 - i - lax.div(low_plane + i, max(planes - 1, 1)) if i < planes - 1 else low_plane
        z = z + upper * (planes - 1 - 2 * z)
        for k in (6, 7, 4, 5, 2, 3, 1, 0) if i < planes - 1 else (6, 7, 4, 5, 2, 3, 1):
            a_of.append(z * 8 + lax.rem(in_plane + k, 8))
    z_of = [lax.rem(plane + k, planes) * 8 + in_plane for k in range(1, planes)]
    s_of = [plane * 8 + lax.rem(square + k, 4) * 2 + core for k in range(1, 4)]
    c_of = plane * 8 + square * 2 + (1 - core)
    barrier = greet(a_of)

    def over(rows, lanes):
        return wide(cols[rows, :], lanes)

    def spots(j):
        return [pl.ds(pl.multiple_of(j * 512 + 256 * k, 256), 256) for k in range(2)]

    coef2 = wide(coefb[...], 256)

    def post_values(at):
        kept = xs[:, at] * (1.0 - fs[:, at])
        normed, inverse = norm_t(embed_t(kept, over(slice(0, D), 256), over(slice(D, 2 * D), 256)))
        dq = dq_s[:, at]
        low = (dq * coef2).astype(bf16)
        prod = fold(dq * q_s[:, at].astype(f32))
        betas = jnp.concatenate(
            [jnp.sum(prod[32 * h : 32 * h + 32], axis=0, keepdims=True) for h in range(H)], axis=0
        )
        gqn = nn(w_q[...], low)
        gh = gres[:, at] + norm_back_t(gqn, normed, inverse, over(slice(2 * D, 3 * D), 256))
        return low, betas, fold(gqn * normed), fold(by_feature(gh, kept)), fold(gh)

    def post_block(j, carry):
        cuts = spots(j)
        found = [post_values(at) for at in cuts]
        qn = jnp.concatenate([qn_s[:, at] for at in cuts], axis=1)
        gq_c = jnp.concatenate([found[0][0], found[1][0]], axis=1)
        gq[...] += nt(qn, gq_c)
        for k, rows in ((1, slice(4 * D, 4 * D + H)), (2, slice(0, D)), (3, slice(2 * D, 3 * D)), (4, slice(3 * D, 4 * D))):
            acc_gain[rows, :] += found[0][k] + found[1][k]
        return carry

    gq[...] = jnp.zeros_like(gq)
    acc_gain[...] = sums_in[...]
    lax.fori_loop(0, xs.shape[1] // 512, post_block, 0)
    gout = nt(att[...], gb_s[...])
    ghead = nt(fn_s[...], gho_s[...])

    used = 4 * D + 2 * H
    row = iota((used, 128), 0)
    lan = iota((used, 128), 1)
    row_dev = jnp.floor((row.astype(f32) + 0.5) * (1.0 / per_small)).astype(jnp.int32)
    sums = jnp.sum(acc_gain[...], axis=1, keepdims=True)
    small = jnp.concatenate(
        [
            sums[2 * D : 3 * D],
            sums[3 * D : 4 * D],
            sums[0:D],
            sums[D : 2 * D],
            sums[4 * D : 4 * D + H] * (32 ** (-0.5)),
            jnp.zeros((H, 1), f32),
        ],
        axis=0,
    )
    placed = jnp.where(lan == (row - per_small * row_dev), small, 0.0).astype(bf16)
    r_dev = iota((n, used), 0)
    r_row = iota((n, used), 1)
    mine = (r_row >= per_small * r_dev) & (r_row < per_small * r_dev + per_small)
    small_rows_out = nn(mine.astype(f32).astype(bf16), placed)
    to_flat_r = iota((32, 256), 0)
    to_flat_l = iota((32, 256), 1)
    lane_row = jnp.floor((to_flat_l.astype(f32) + 0.5) * (1.0 / (C + F))).astype(jnp.int32)
    to_flat = ((to_flat_l - (C + F) * lane_row == to_flat_r) & (to_flat_r < C + F)).astype(f32)
    spread_h = nn(ghead.astype(bf16), to_flat.astype(bf16))
    lr = iota((D, 256), 1)
    lr_row = jnp.floor((lr.astype(f32) + 0.5) * (1.0 / (C + F))).astype(jnp.int32)
    spread_h = jnp.where(lr_row == (iota((D, 256), 0) & (rows_dev - 1)), spread_h, 0.0)
    r8 = iota((8, 128), 0)
    for d in range(n):
        rows = slice(rows_dev * d, rows_dev * d + rows_dev)
        head_flat = jnp.sum(spread_h[rows], axis=0, keepdims=True)
        extra = jnp.where(
            r8 == 0,
            head_flat[:, :128],
            jnp.where(r8 == 1, head_flat[:, 128:], jnp.where(r8 == 2, small_rows_out[d : d + 1], 0.0)),
        )
        block = [gq[rows, 128 * k : 128 * k + 128] for k in range(2)]
        block += [gkv[rows, 128 * k : 128 * k + 128] for k in range(4)]
        block += [gout[rows, 128 * k : 128 * k + 128] for k in range(2)]
        block += [extra, jnp.zeros((8, 128), f32)]
        s_s[place_of(d, planes)] = jnp.concatenate(block, axis=0).astype(bf16)

    pl.semaphore_wait(barrier, n - 1)

    def part(c, j, k):
        z = lax.rem(plane + k, planes)
        return c * (4 * planes) + lax.rem(square + j, 4) * planes + z

    done = []
    pieces = {}
    for j in (1, 2, 3, 0):
        line = pl.ds((1 - core) * (4 * planes) + lax.rem(square + j, 4) * planes, planes)
        pieces[j] = send(s_s.at[line], r_core.at[j], send_c.at[j], recv_c.at[j], c_of)
    for j in (1, 2, 3):
        pieces[j].wait_recv()
    order = [2, 1, 3, 0] if planes == 4 else list(range(1, planes)) + [0]
    crossing = {}
    for k in order:
        z = lax.rem(plane + k, planes)
        for j in range(1, 4):
            t_square[j - 1, k] = (
                s_s[part(core, j, k)].astype(f32) + r_core[j, z].astype(f32)
            ).astype(bf16)
            crossing[k, j] = send(
                t_square.at[j - 1, k], r_square.at[j - 1, k],
                send_s.at[j - 1, k], recv_s.at[j - 1, k], s_of[j - 1],
            )
    pieces[0].wait_recv()
    for k in order:
        z = lax.rem(plane + k, planes)
        own[k] = s_s[part(core, 0, k)].astype(f32) + r_core[0, z].astype(f32)
    along = {}
    for k in order:
        total = own[k]
        for j in range(1, 4):
            crossing[k, j].wait_recv()
            total = total + r_square[j - 1, k].astype(f32)
        if k:
            t_plane[k - 1] = total.astype(bf16)
            along[k] = send(
                t_plane.at[k - 1], r_plane.at[k - 1], send_z.at[k - 1], recv_z.at[k - 1], z_of[k - 1]
            )
    for k in range(1, planes):
        along[k].wait_recv()
        total = total + r_plane[k - 1].astype(f32)
    g_out[...] = total
    squares = jnp.sum(total * total, axis=0, keepdims=True)
    squares = squares + pltpu.roll(squares, 64, 1)
    losses = l_in[0:1, :]
    losses = losses + pltpu.roll(losses, 64, 1)
    n_mine[...] = jnp.where(iota((1, 128), 1) < 64, squares, losses)
    n_all[me] = n_mine[...]
    last = [
        send(n_mine, n_all.at[me], send_n.at[k], recv_n.at[me], a_of[k]) for k in range(n - 1)
    ]
    for k in range(1, n):
        other = lax.rem(me + k, n)
        pltpu.make_async_remote_copy(
            src_ref=n_mine,
            dst_ref=n_all.at[other],
            send_sem=send_n.at[k - 1],
            recv_sem=recv_n.at[other],
            device_id=(other,),
            device_id_type=MESH,
        ).wait_recv()
    total = n_all[0]
    for k in range(1, n):
        total = total + n_all[k]
    t_out[...] = total
    for copies in (pieces, crossing, along):
        for copy in copies.values():
            copy.wait_send()
    for copy in last:
        copy.wait_send()


def reduce_call(n, per_small, *grads):
    planes = n // 8
    rows = 80
    vm = pl.BlockSpec(memory_space=pltpu.VMEM)
    dma = pltpu.SemaphoreType.DMA
    V = pltpu.VMEM
    z = planes - 1
    return pl.pallas_call(
        functools.partial(reduce_kernel, n, per_small),
        out_shape=(
            jax.ShapeDtypeStruct((rows, 128), f32),
            jax.ShapeDtypeStruct((1, 128), f32),
        ),
        in_specs=[vm] * len(grads),
        out_specs=(vm, vm),
        scratch_shapes=[
            V((D, D), f32), V((4 * D + H, 128), f32),
            V((n, rows, 128), bf16), V((4, planes, rows, 128), bf16), V((3, planes, rows, 128), bf16),
            V((3, planes, rows, 128), bf16), V((z, rows, 128), bf16), V((z, rows, 128), bf16),
            V((planes, rows, 128), f32), V((1, 128), f32), V((n, 1, 128), f32),
            dma((4,)), dma((4,)), dma((3, planes)), dma((3, planes)), dma((z,)), dma((z,)),
            dma((n - 1,)), dma((n,)),
        ],
        compiler_params=pltpu.CompilerParams(
            collective_id=1, has_side_effects=True, vmem_limit_bytes=16 * 1024 * 1024
        ),
    )(*grads)


def update_kernel(g, tot, *refs):
    w_qkv, w_out, keep = refs[0:3]
    firsts, seconds, refs = refs[3:7], refs[7:11], refs[11:]
    per_head, per_small = firsts[2].shape[1], firsts[3].shape[1]
    weights = (
        w_qkv[...],
        w_out[...],
        jnp.concatenate([keep[0:1, :], keep[1:2, : per_head - 128]], axis=1),
        keep[2:3, :per_small],
    )
    new, first_o, second_o = refs[0:4], refs[4:8], refs[8:12]
    copy_o = (refs[12], refs[13], None, refs[14])
    flat_o, loss_o, norm_o, gq_s, go_s = refs[15:20]
    for c in range(6):
        gq_s[pl.ds(c, 8, stride=6), :] = g[8 * c : 8 * c + 8, :]
    for c in range(2):
        go_s[pl.ds(c, 8, stride=2), :] = g[48 + 8 * c : 56 + 8 * c, :]
    first_half = iota((1, 128), 1) < 64
    norm = jnp.sqrt(jnp.sum(jnp.where(first_half, tot[...], 0.0), axis=1, keepdims=True))
    loss_o[...] = jnp.sum(jnp.where(first_half, 0.0, tot[...]), axis=1, keepdims=True)
    norm_o[...] = norm
    factor = jnp.minimum(1.0, max_norm / (norm + 1e-06))
    grads = (
        gq_s[...],
        go_s[...],
        jnp.concatenate([g[64:65, :], g[65:66, : per_head - 128]], axis=1),
        g[66:67, :per_small],
    )
    for i in range(4):
        first_new, second_new, weight_new = adamw(
            weights[i], firsts[i][...], seconds[i][...], grads[i], factor, float(STEP), learn_rates[i]
        )
        new[i][...] = weight_new
        first_o[i][...] = first_new
        second_o[i][...] = second_new
        if copy_o[i] is not None:
            copy_o[i][...] = weight_new.astype(bf16)
        else:
            flat_o[...] = weight_new.astype(bf16).reshape(weight_new.shape[1])


def update_call(g, tot, w_qkv, w_out, keep, firsts, seconds):
    vm = pl.BlockSpec(memory_space=pltpu.VMEM)
    shapes = [v.shape for v in firsts]
    outs = [jax.ShapeDtypeStruct(s, f32) for s in shapes] * 3
    outs += [jax.ShapeDtypeStruct(s, bf16) for s in shapes[:2] + shapes[3:]]
    outs += [jax.ShapeDtypeStruct((shapes[2][1],), bf16)]
    outs += [jax.ShapeDtypeStruct((1, 1), f32)] * 2
    return pl.pallas_call(
        update_kernel,
        out_shape=tuple(outs),
        in_specs=[vm] * 13,
        out_specs=(vm,) * 18,
        scratch_shapes=[pltpu.VMEM((48, 128), f32), pltpu.VMEM((16, 128), f32)],
        compiler_params=pltpu.CompilerParams(vmem_limit_bytes=4 * 1024 * 1024),
    )(g, tot, w_qkv, w_out, keep, *firsts, *seconds)


def local_fast(
    n, query_feats, feature_mask, query_task, target_class, target_mask, memory_feats, memory_task,
    memory_mask, anneal, w_qkv, w_out, w_heads, w_small, m_qkv, m_out, m_heads, m_small,
    v_qkv, v_out, v_heads, v_small,
):
    def row(v):
        return v.reshape(1, -1)

    def tiles(v):
        return v.reshape(-1, 128)

    weights = (tiles(w_qkv), tiles(w_out), row(w_heads), row(w_small))
    firsts = (tiles(m_qkv), tiles(m_out), row(m_heads), row(m_small))
    seconds = (tiles(v_qkv), tiles(v_out), row(v_heads), row(v_small))
    tm, mt = row(target_mask), row(memory_task)
    gw, keep = gather_call(
        n, *weights, memory_feats.T, query_feats.T, feature_mask.T, row(query_task),
        row(target_class), tm, mt, row(memory_mask),
    )
    found = step_call(n, mt.shape[1], w_small.shape[0] * n, anneal, gw)
    grads, totals = reduce_call(n, w_small.shape[0], *found)
    outs = update_call(grads, totals, weights[0], weights[1], keep, firsts, seconds)
    outs = [out.reshape(-1) for out in outs]
    return tuple(outs[:14] + [outs[15]] + [outs[14]] + outs[16:])


def solution(mesh):
    placed = (
        P("mem", None),
        P("mem", None),
        P("mem"),
        P("mem"),
        P("mem"),
        P("mem", None),
        P(),
        P(),
        P(),
        P("mem"),
        P("mem"),
        P("mem"),
        P("mem"),
        P("mem"),
        P("mem"),
        P("mem"),
        P("mem"),
        P("mem"),
        P("mem"),
        P("mem"),
        P("mem"),
    )
    n = mesh.shape["mem"]

    def choose(*args):
        if D // n == 8 and args[6].shape[0] in (2048, 4096):
            return local_fast(n, *args)
        return local(*args)

    return jax.shard_map(
        choose,
        mesh=mesh,
        in_specs=placed,
        out_specs=(
            P("mem"),
            P("mem"),
            P("mem"),
            P("mem"),
            P("mem"),
            P("mem"),
            P("mem"),
            P("mem"),
            P("mem"),
            P("mem"),
            P("mem"),
            P("mem"),
            P("mem"),
            P("mem"),
            P("mem"),
            P("mem"),
            P(),
            P(),
        ),
        check_vma=False,
    )
```

```python
import functools
import math

import jax
import jax.numpy as jnp
from jax import lax
from jax.experimental import pallas as pl
from jax.experimental.pallas import tpu as pltpu
from jax.sharding import PartitionSpec as P

F = 8
D = 256
H = 8
C = 16
TASKS = 4
STEP = 10


eps_norm = 1e-05
max_norm = 0.05
beta_one = 0.9
beta_two = 0.999
adam_eps = 1e-08
decay_rate = 0.01
learn_rates = (0.05, 1.0, 0.05, 0.5)
masked_score = -1e30


def embed(feature_rows, table_flat, emb_bias):
    emb_table = table_flat.reshape(feature_rows.shape[1], -1)
    return (feature_rows[:, :, None] * emb_table[None]).reshape(
        feature_rows.shape[0], -1
    ) + emb_bias


def standard(hidden):
    centred = hidden - jnp.mean(hidden, -1, keepdims=True)
    inverse = lax.rsqrt(jnp.mean(centred * centred, -1, keepdims=True) + eps_norm)
    return (centred * inverse, inverse)


def norm_back(grad_out, hidden, gain_vec):
    normed, inverse = standard(hidden)
    grad_gain = jnp.sum(grad_out * normed, 0)
    grad_scaled = grad_out * gain_vec
    grad_hidden = inverse * (
        grad_scaled
        - jnp.mean(grad_scaled, -1, keepdims=True)
        - normed * jnp.mean(grad_scaled * normed, -1, keepdims=True)
    )
    return (grad_hidden, grad_gain)


def split_pair(values):
    upper = values.astype(jnp.bfloat16)
    lower = (values - upper.astype(jnp.float32)).astype(jnp.bfloat16)
    return (upper, lower)


def adamw(weight, first_mom, second, grad_in, factor, step_num, step_rate):
    clipped = grad_in * factor
    first_new = beta_one * first_mom + (1 - beta_one) * clipped
    second_new = beta_two * second + (1 - beta_two) * clipped * clipped
    fix_one = 1 - beta_one**step_num
    fix_two = 1 - beta_two**step_num
    weight_new = weight - step_rate * (
        first_new / fix_one / (jnp.sqrt(second_new / fix_two) + adam_eps) + decay_rate * weight
    )
    return (first_new, second_new, weight_new)


def local(
    query_feats,
    feature_mask,
    query_task,
    target_class,
    target_mask,
    memory_feats,
    memory_task,
    memory_mask,
    anneal,
    w_qkv,
    w_out,
    w_heads,
    w_small,
    m_qkv,
    m_out,
    m_heads,
    m_small,
    v_qkv,
    v_out,
    v_heads,
    v_small,
):
    high = lax.Precision.HIGHEST
    head_size = D // H
    full_qkv, full_out, full_heads, full_small = (
        lax.all_gather(w_qkv, "mem", axis=0, tiled=True),
        lax.all_gather(w_out, "mem", axis=0, tiled=True),
        lax.all_gather(w_heads, "mem", axis=0, tiled=True),
        lax.all_gather(w_small, "mem", axis=0, tiled=True),
    )
    emb_table = full_small[:D]
    emb_bias = full_small[D : 2 * D]
    gain_in = full_small[2 * D : 3 * D]
    gain_out = full_small[3 * D : 4 * D]
    score_coef = full_small[4 * D : 4 * D + H] * head_size ** (-0.5)
    qkv_low = full_qkv.reshape(D, 3 * D).astype(jnp.bfloat16)
    out_low = full_out.reshape(D, D).astype(jnp.bfloat16)
    heads_low = full_heads.reshape(D, C + F).astype(jnp.bfloat16)
    mem_hidden = embed(memory_feats, emb_table, emb_bias)
    mem_normed = (standard(mem_hidden)[0] * gain_in).astype(jnp.bfloat16)
    mem_kv = jnp.dot(mem_normed, qkv_low[:, D:], preferred_element_type=jnp.float32).astype(
        jnp.bfloat16
    )
    all_kv = lax.all_gather(mem_kv, "mem", axis=0, tiled=True)
    memory_rows = all_kv.shape[0]
    block_keys = math.gcd(memory_rows, 512)
    num_blocks = memory_rows // block_keys
    key_rows = all_kv[:, :D].reshape(num_blocks, block_keys, H, head_size)
    value_rows = all_kv[:, D:].reshape(num_blocks, block_keys, H, head_size)
    task_blocks = memory_task.reshape(num_blocks, block_keys)
    live_blocks = memory_mask.reshape(num_blocks, block_keys)
    key_blocks = (key_rows, value_rows, task_blocks, live_blocks)
    kept_input = query_feats * (1 - feature_mask).astype(jnp.float32)
    hidden_in = embed(kept_input, emb_table, emb_bias)
    query_normed = (standard(hidden_in)[0] * gain_in).astype(jnp.bfloat16)
    queries = (
        jnp.dot(query_normed, qkv_low[:, :D], preferred_element_type=jnp.float32)
        .astype(jnp.bfloat16)
        .reshape(-1, H, head_size)
    )
    num_rows = queries.shape[0]

    def allowed_of(task_row, live_row):
        return ((query_task[:, None] == task_row[None, :]) & (live_row[None, :] > 0))[None]

    def scores_of(key_block, allowed):
        raw_scores = jnp.einsum(
            "qhd,khd->hqk", queries, key_block, preferred_element_type=jnp.float32
        )
        return (
            raw_scores,
            jnp.where(allowed, score_coef[:, None, None] * raw_scores, masked_score),
        )

    def stats_step(state_in, block_data):
        row_top, row_sum = state_in
        key_block, value_block, task_row, live_row = block_data
        allowed = allowed_of(task_row, live_row)
        scores = scores_of(key_block, allowed)[1]
        new_top = jnp.maximum(row_top, jnp.max(scores, -1))
        shifted = jnp.where(allowed, jnp.exp(scores - new_top[..., None]), 0.0)
        return ((new_top, row_sum * jnp.exp(row_top - new_top) + jnp.sum(shifted, -1)), None)

    start_state = (
        jnp.full((H, num_rows), masked_score, jnp.float32),
        jnp.zeros((H, num_rows), jnp.float32),
    )
    (row_top, row_sum), unused = lax.scan(stats_step, start_state, key_blocks)

    def probs_of(scores, allowed):
        return jnp.where(allowed, jnp.exp(scores - row_top[..., None]), 0.0) / row_sum[..., None]

    def value_step(accum, block_data):
        key_block, value_block, task_row, live_row = block_data
        allowed = allowed_of(task_row, live_row)
        probs_low = probs_of(scores_of(key_block, allowed)[1], allowed).astype(jnp.bfloat16)
        return (
            accum
            + jnp.einsum(
                "hqk,khd->qhd", probs_low, value_block, preferred_element_type=jnp.float32
            ),
            None,
        )

    attn_sum, unused = lax.scan(
        value_step, jnp.zeros((num_rows, H, head_size), jnp.float32), key_blocks
    )
    attended = attn_sum.reshape(num_rows, D).astype(jnp.bfloat16)
    residual = hidden_in + jnp.dot(attended, out_low, preferred_element_type=jnp.float32)
    final_normed = (standard(residual)[0] * gain_out).astype(jnp.bfloat16)
    head_out = jnp.dot(final_normed, heads_low, preferred_element_type=jnp.float32)
    logits = head_out[:, :C]
    recon_err = head_out[:, C:] - query_feats
    label_mask = target_mask.astype(jnp.float32)
    feat_mask = feature_mask.astype(jnp.float32)
    onehot_class = jax.nn.one_hot(target_class, C, dtype=jnp.float32)
    picked = jnp.sum(logits * onehot_class, -1)
    sum_target, sum_recon, count_target, count_recon = lax.psum(
        (
            jnp.sum(label_mask * (jax.nn.logsumexp(logits, -1) - picked)),
            jnp.sum(feat_mask * recon_err**2),
            jnp.sum(label_mask),
            jnp.sum(feat_mask),
        ),
        "mem",
    )
    count_target = jnp.maximum(count_target, 1.0)
    count_recon = jnp.maximum(count_recon, 1.0)
    weight_a = anneal[0]
    loss_value = weight_a * sum_target / count_target + (1 - weight_a) * sum_recon / count_recon
    grad_logits = (
        weight_a / count_target * label_mask[:, None] * (jax.nn.softmax(logits, -1) - onehot_class)
    )
    grad_recon = (1 - weight_a) / count_recon * feat_mask * 2.0 * recon_err
    grad_head_out = jnp.concatenate([grad_logits, grad_recon], 1).astype(jnp.bfloat16)
    grad_heads = jnp.dot(final_normed.T, grad_head_out, preferred_element_type=jnp.float32)
    grad_final = jnp.dot(grad_head_out, heads_low.T, preferred_element_type=jnp.float32)
    grad_resid, grad_gain_out = norm_back(grad_final, residual, gain_out)
    grad_branch = grad_resid.astype(jnp.bfloat16)
    grad_wout = jnp.dot(attended.T, grad_branch, preferred_element_type=jnp.float32)
    grad_attn = (
        jnp.dot(grad_branch, out_low.T, preferred_element_type=jnp.float32)
        .astype(jnp.bfloat16)
        .reshape(num_rows, H, head_size)
    )
    row_delta = jnp.sum(
        grad_attn.astype(jnp.float32)
        * attended.reshape(num_rows, H, head_size).astype(jnp.float32),
        -1,
    ).T

    def back_step(state_in, block_data):
        key_block, value_block, task_row, live_row = block_data
        allowed = allowed_of(task_row, live_row)
        raw_scores, scores = scores_of(key_block, allowed)
        soft_probs = probs_of(scores, allowed)
        grad_probs = jnp.einsum(
            "qhd,khd->hqk", grad_attn, value_block, preferred_element_type=jnp.float32
        )
        grad_scores = (soft_probs * (grad_probs - row_delta[..., None])).astype(jnp.bfloat16)
        grad_beta = jnp.sum(grad_scores.astype(jnp.float32) * raw_scores, (1, 2))
        grad_query = jnp.einsum(
            "hqk,khd->qhd", grad_scores, key_block, preferred_element_type=jnp.float32
        )
        grad_key = (
            jnp.einsum("hqk,qhd->khd", grad_scores, queries, preferred_element_type=jnp.float32)
            * score_coef[None, :, None]
        )
        grad_value = jnp.einsum(
            "hqk,qhd->khd",
            soft_probs.astype(jnp.bfloat16),
            grad_attn,
            preferred_element_type=jnp.float32,
        )
        block_rows = key_block.shape[0]
        grad_kv = jnp.concatenate(
            [grad_key.reshape(block_rows, D), grad_value.reshape(block_rows, D)], 1
        )
        return ((state_in[0] + grad_query, state_in[1] + grad_beta), grad_kv)

    init_state = (jnp.zeros((num_rows, H, head_size), jnp.float32), jnp.zeros((H,), jnp.float32))
    (grad_q_sum, grad_beta_sum), kv_parts = lax.scan(back_step, init_state, key_blocks)
    kv_grad = lax.psum_scatter(
        kv_parts.reshape(memory_rows, 2 * D), "mem", scatter_dimension=0, tiled=True
    )
    grad_q_low = (grad_q_sum * score_coef[None, :, None]).reshape(num_rows, D).astype(jnp.bfloat16)
    grad_wq = jnp.dot(query_normed.T, grad_q_low, preferred_element_type=jnp.float32)
    grad_qn = jnp.dot(grad_q_low, qkv_low[:, :D].T, preferred_element_type=jnp.float32)
    grad_in_q, gain_in_q = norm_back(grad_qn, hidden_in, gain_in)
    grad_hidden = grad_resid + grad_in_q
    kv_upper, kv_lower = split_pair(kv_grad)
    grad_wkv = jnp.dot(mem_normed.T, kv_upper, preferred_element_type=jnp.float32) + jnp.dot(
        mem_normed.T, kv_lower, preferred_element_type=jnp.float32
    )
    grad_mn = jnp.dot(kv_upper, qkv_low[:, D:].T, preferred_element_type=jnp.float32) + jnp.dot(
        kv_lower, qkv_low[:, D:].T, preferred_element_type=jnp.float32
    )
    grad_mem, gain_in_m = norm_back(grad_mn, mem_hidden, gain_in)
    grad_table = jnp.einsum(
        "qf,qfe->fe", kept_input, grad_hidden.reshape(num_rows, F, -1), precision=high
    )
    grad_table = grad_table + jnp.einsum(
        "qf,qfe->fe", memory_feats, grad_mem.reshape(memory_feats.shape[0], F, -1), precision=high
    )
    grad_bias = jnp.sum(grad_hidden, 0) + jnp.sum(grad_mem, 0)
    small_size = full_small.shape[0]
    grad_small = jnp.concatenate(
        [
            grad_table.reshape(-1),
            grad_bias,
            gain_in_q + gain_in_m,
            grad_gain_out,
            grad_beta_sum * head_size ** (-0.5),
            jnp.zeros((small_size - 4 * D - H,), jnp.float32),
        ]
    )
    grad_qkv = jnp.concatenate([grad_wq, grad_wkv], 1).reshape(-1)
    shards = (
        lax.psum_scatter(grad_qkv, "mem", scatter_dimension=0, tiled=True),
        lax.psum_scatter(grad_wout.reshape(-1), "mem", scatter_dimension=0, tiled=True),
        lax.psum_scatter(grad_heads.reshape(-1), "mem", scatter_dimension=0, tiled=True),
        lax.psum_scatter(grad_small, "mem", scatter_dimension=0, tiled=True),
    )
    local_squares = sum((jnp.sum(piece_grad * piece_grad) for piece_grad in shards))
    grad_total = jnp.sqrt(lax.psum(local_squares, "mem"))
    factor = jnp.minimum(1.0, max_norm / (grad_total + 1e-06))
    step_num = float(STEP)
    weights_all = (w_qkv, w_out, w_heads, w_small)
    firsts = (m_qkv, m_out, m_heads, m_small)
    seconds = (v_qkv, v_out, v_heads, v_small)
    results = [
        adamw(weight, first_mom, second, grad_in, factor, step_num, step_rate)
        for weight, first_mom, second, grad_in, step_rate in zip(
            weights_all, firsts, seconds, shards, learn_rates
        )
    ]
    new_w = [entry[2] for entry in results]
    return (
        new_w[0],
        new_w[1],
        new_w[2],
        new_w[3],
        results[0][0],
        results[1][0],
        results[2][0],
        results[3][0],
        results[0][1],
        results[1][1],
        results[2][1],
        results[3][1],
        new_w[0].astype(jnp.bfloat16),
        new_w[1].astype(jnp.bfloat16),
        new_w[2].astype(jnp.bfloat16),
        new_w[3].astype(jnp.bfloat16),
        loss_value.reshape(1),
        grad_total.reshape(1),
    )


f32 = jnp.float32
bf16 = jnp.bfloat16
LOG2E = math.log2(math.e)
QB = 128
KC = 384
ROWS = (320, 352, KC)
VROWS = 80
E_CAP = 12
STEP_VMEM = 44 * 1024 * 1024
PRE_SPAN = 3
MID_SPAN = 6
MEM_SPAN = 2
SMALL_LANE = 88
COUNT_LANE = 122


def place_of(dev, planes):
    return (dev % 2) * (4 * planes) + ((dev // 2) % 4) * planes + dev // 8


def nt(a, b):
    return lax.dot_general(a, b, (((1,), (1,)), ((), ())), preferred_element_type=f32)


def tn(a, b):
    return lax.dot_general(a, b, (((0,), (0,)), ((), ())), preferred_element_type=f32)


def nn(a, b):
    return jnp.dot(a, b, preferred_element_type=f32)


def iota(shape, dim):
    return lax.broadcasted_iota(jnp.int32, shape, dim)


def split2(v):
    hi = v.astype(bf16).astype(f32)
    return hi, v - hi


def split3(v):
    hi, rest = split2(v)
    mid = rest.astype(bf16).astype(f32)
    return hi, mid, rest - mid


def wide(v, lanes):
    return jnp.concatenate([v] * (lanes // v.shape[1]), axis=1) if lanes > v.shape[1] else v


def embed_t(kept, table, bias):
    parts = []
    for f in range(F):
        rows = slice(32 * f, 32 * f + 32)
        parts.append(kept[f : f + 1] * table[rows] + bias[rows])
    return jnp.concatenate(parts, axis=0)


def fold(v):
    total = v[:, :128]
    for k in range(1, v.shape[1] // 128):
        total = total + v[:, 128 * k : 128 * k + 128]
    return total


def by_feature(grad, kept):
    return jnp.concatenate(
        [kept[f : f + 1] * grad[32 * f : 32 * f + 32] for f in range(F)], axis=0
    )


def added(found, k):
    total = found[0][k]
    for one in found[1:]:
        total = total + one[k]
    return total


def norm_t(v):
    centred = v - jnp.mean(v, axis=0, keepdims=True)
    inverse = lax.rsqrt(jnp.mean(centred * centred, axis=0, keepdims=True) + eps_norm)
    return centred * inverse, inverse


def norm_back_t(grad, normed, inverse, gain):
    scaled = grad * gain
    return inverse * (
        scaled
        - jnp.mean(scaled, axis=0, keepdims=True)
        - normed * jnp.mean(scaled * normed, axis=0, keepdims=True)
    )


def blocks_of(num_q):
    blocks = (num_q + TASKS * (QB - 1)) // QB
    return -(-blocks // 4) * 4


def chunks_of(num_mem):
    chunks = (num_mem + TASKS * (KC - 1)) // KC
    return -(-chunks // MEM_SPAN) * MEM_SPAN


def step_kernel(
    n, qs, num_mem, small_size,
    an, gw,
    xs, fs, qn_s, q_s, att, gb_s, fn_s, gho_s, gres, dq_s, gkv, w_q, cols, coefb, acc_gain, out_l,
    ct, w_s, wt_s, wh_s, wht_s,
    mfeat, kn, vn, kt_s, vt_s, mnt, gk, gv,
    il_s, dap, delta, ebuf, ecur, acc, m_s,
    blk_c0, blk_nc, blk_tile, blk_rows, ch_base, ch_end, numbers, table, loaded,
):
    planes = n // 8
    per_small = small_size // n
    k_chunks = ch_base.shape[0]

    for i in range(num_mem // 2048):
        both = gw[n + 1 + i, 48:64, :].astype(f32)
        numbers[:, 128 * i : 128 * i + 128] = (both[0:8] + both[8:16]).astype(jnp.int32)
    copy = pltpu.make_async_copy(numbers, table, loaded)
    copy.start()
    copy.wait()
    m_base, m_count, m_units, q_base, q_units = (
        [table[3, TASKS * k + t] for t in range(TASKS)] for k in range(5)
    )
    num_blocks = q_units[0] + q_units[1] + q_units[2] + q_units[3]
    num_chunks = m_units[0] + m_units[1] + m_units[2] + m_units[3]
    for c in range(k_chunks):
        ch_base[c] = jnp.int32(c * KC)
        ch_end[c] = jnp.int32(c * KC)
    tile = jnp.int32(0)
    for t in range(TASKS):
        first_chunk = lax.div(m_base[t], jnp.int32(KC))
        first_block = lax.div(q_base[t], jnp.int32(QB))

        def fill_chunk(i, carry, t=t, first_chunk=first_chunk):
            ch_base[first_chunk + i] = m_base[t]
            ch_end[first_chunk + i] = m_base[t] + m_count[t]
            return carry

        lax.fori_loop(0, m_units[t], fill_chunk, 0)

        def fill_block(i, tile_in, t=t, first_chunk=first_chunk, first_block=first_block):
            blk_c0[first_block + i] = first_chunk
            blk_nc[first_block + i] = m_units[t]
            blk_rows[first_block + i] = m_count[t]
            blk_tile[first_block + i] = tile_in
            return tile_in + m_units[t]

        tile = lax.fori_loop(0, q_units[t], fill_block, tile)

    pieces = [gw[place_of(d, planes)].astype(f32) for d in range(n)]
    for col in range(8):
        block = jnp.concatenate([piece[8 * col : 8 * col + 8] for piece in pieces], axis=0)
        w_s[:, 128 * col : 128 * col + 128] = block.astype(bf16)
        wt_s[128 * col : 128 * col + 128, :] = block.T.astype(bf16)
    lane = iota((8, 128), 1)
    tiles = [piece[64:72] + piece[72:80] for piece in pieces]
    lane_w = iota((D, 128), 1)
    heads = pltpu.roll(jnp.concatenate(tiles, axis=0), 64, 1)
    heads = jnp.where(lane_w < C + F, heads, 0.0)
    wh_s[...] = heads.astype(bf16)
    wht_s[...] = heads.T[:32].astype(bf16)

    for b in range(qs // 128):
        block = gw[n + b, 0:48, :].astype(f32)
        cut = slice(128 * b, 128 * b + 128)
        xs[:, cut] = block[0:8] + block[8:16] + block[16:24]
        fs[:, cut] = block[24:32]
        ct[:, cut] = block[32:40]

    small_rows = jnp.concatenate([tile[0:1] for tile in tiles], axis=0)
    lane_n = iota((n, 128), 1)
    count_t = jnp.maximum(jnp.sum(jnp.where(lane_n == COUNT_LANE, small_rows, 0.0)), 1.0)
    count_r = jnp.maximum(jnp.sum(jnp.where(lane_n == COUNT_LANE + 1, small_rows, 0.0)), 1.0)
    used = 4 * D + 2 * H
    s2 = jnp.concatenate(
        list(split2(small_rows)) + [jnp.zeros((128 - 2 * n, 128), f32)], axis=0
    ).astype(bf16)
    row = iota((used, 128), 0)
    lan = iota((used, 128), 1)
    dev_of = lan & (n - 1)
    pick = (row >= per_small * dev_of) & (row < per_small * dev_of + per_small) & (lan < 2 * n)
    spread = nn(pick.astype(f32).astype(bf16), s2)
    row_dev = jnp.floor((row.astype(f32) + 0.5) * (1.0 / per_small)).astype(jnp.int32)
    here = (lan - SMALL_LANE) == (row - per_small * row_dev)
    column = jnp.sum(jnp.where(here, spread, 0.0), axis=1, keepdims=True)
    cols[...] = jnp.broadcast_to(column[: 4 * D], (4 * D, 128))
    for h in range(H):
        coefb[32 * h : 32 * h + 32, :] = jnp.broadcast_to(
            column[4 * D + h : 4 * D + h + 1] * (32 ** (-0.5)), (32, 128)
        )

    emb_w = lambda lanes: wide(cols[0:D, :], lanes)
    emb_b = lambda lanes: wide(cols[D : 2 * D, :], lanes)
    gain_in = lambda lanes: wide(cols[2 * D : 3 * D, :], lanes)
    gain_out = lambda lanes: wide(cols[3 * D : 4 * D, :], lanes)

    places = gw[n, 48 : 48 + n // 2, :].astype(f32)
    for b in range(n // 2):
        raw = jnp.where(lane < 64, tiles[2 * b], pltpu.roll(tiles[2 * b + 1], 64, 1))
        chosen = (places[b : b + 1] == iota((128, 1), 0).astype(f32)).astype(f32)
        got = nt(jnp.concatenate(split2(raw), axis=0).astype(bf16), chosen.astype(bf16))
        run = got[0:8] + got[8:16]
        for t in range(TASKS):
            i = 8 * b + t
            start, count, slot = table[0, i], table[1, i], table[2, i]
            first = slot & 127
            shift = (first - start) & 127
            moved = pltpu.roll(run, shift, 1)
            at = pl.multiple_of(slot - first, 128)
            pltpu.store(
                mfeat.at[:, pl.ds(at, 128)], moved, mask=(lane >= first) & (lane < first + count)
            )
            pltpu.store(mfeat.at[:, pl.ds(at + 128, 128)], moved, mask=lane < first + count - 128)

    def mem_feats(c):
        base, end = ch_base[c], ch_end[c]
        at = pl.ds(pl.multiple_of(c * KC, KC), KC)
        slot = iota((8, KC), 1) + c * KC
        head = mfeat[:, pl.ds(pl.multiple_of(base, KC), 128)][:, 0:1]
        live = (slot < end).astype(f32)[0:1]
        return jnp.where(slot < end, mfeat[:, at], jnp.where(end > base, head, 0.0)), live

    def mem_pair(i, carry):
        found = []
        for k in range(MEM_SPAN):
            c = MEM_SPAN * i + k
            feats_c, live = mem_feats(c)
            normed, unused = norm_t(embed_t(feats_c, emb_w(KC), emb_b(KC)))
            mnf = normed * gain_in(KC)
            mn = mnf.astype(bf16)
            keys_t = (nn(wt_s[D : 2 * D, :], mn) * live).astype(bf16)
            vals_t = nn(wt_s[2 * D : 3 * D, :], mn) * live
            tail = jnp.where(iota((16, KC), 0) == 0, live, 0.0)
            vals_t = jnp.concatenate(
                [part for p in range(4) for part in (vals_t[64 * p : 64 * p + 64], tail)], axis=0
            ).astype(bf16)
            both = nn(mnf.T.astype(bf16), w_s[:, D : 3 * D])
            live_col = ((iota((KC, 1), 0) + c * KC) < ch_end[c]).astype(f32)
            found.append((mn, keys_t, vals_t, both[:, :D], both[:, D:] * live_col))
        for k in range(MEM_SPAN):
            at = pl.ds(pl.multiple_of((MEM_SPAN * i + k) * KC, KC), KC)
            mnt[:, at], kt_s[:, at], vt_s[:, at] = found[k][0:3]
            kn[at, :] = found[k][3].astype(bf16)
            vn[at, :] = found[k][4].astype(bf16)
            gk[at, :] = jnp.zeros((KC, D), f32)
            gv[at, :] = jnp.zeros((KC, D), f32)
        return carry

    lax.fori_loop(0, lax.div(num_chunks + MEM_SPAN - 1, jnp.int32(MEM_SPAN)), mem_pair, 0)

    def spots(j, span):
        return [pl.ds(pl.multiple_of((j * span + k) * 256, 256), 256) for k in range(span)]

    def pre_block(j, carry):
        found = []
        for at in spots(j, PRE_SPAN):
            kept = xs[:, at] * (1.0 - fs[:, at])
            normed, unused = norm_t(embed_t(kept, emb_w(256), emb_b(256)))
            qn = (normed * gain_in(256)).astype(bf16)
            found.append((qn, nn(wt_s[0:D, :], qn).astype(bf16)))
        for k, at in enumerate(spots(j, PRE_SPAN)):
            qn_s[:, at], q_s[:, at] = found[k]
            att[:, at] = jnp.zeros((D, 256), bf16)
            il_s[:, at] = jnp.zeros((H, 256), f32)
            dq_s[:, at] = jnp.zeros((D, 256), f32)
        return carry

    lax.fori_loop(0, qs // (256 * PRE_SPAN), pre_block, 0)

    zero_h = jnp.zeros((32, 128), bf16)
    zero_p = jnp.zeros((64, 256), bf16)

    def pair(p, width):
        return slice(width * p, width * p + width)

    def half(p):
        return slice(128 * (p // 2), 128 * (p // 2) + 128)

    def two_heads(ref, at, p):
        diag = jnp.concatenate(
            [
                jnp.concatenate([ref[64 * p : 64 * p + 32, at], zero_h], axis=1),
                jnp.concatenate([zero_h, ref[64 * p + 32 : 64 * p + 64, at]], axis=1),
            ],
            axis=0,
        )
        return jnp.concatenate([zero_p, diag] if p % 2 else [diag, zero_p], axis=0)

    def coef_row(p):
        return LOG2E * jnp.concatenate(
            [coefb[64 * p : 64 * p + 1, :], coefb[64 * p + 32 : 64 * p + 33, :]], axis=1
        )

    def finish_forward(at, p, got):
        inverse = 1.0 / got[64:65, :]
        il_s[2 * p : 2 * p + 1, at] = inverse[:, :128]
        il_s[2 * p + 1 : 2 * p + 2, at] = inverse[:, 128:]
        att[64 * p : 64 * p + 32, at] = (got[0:32, :128] * inverse[:, :128]).astype(bf16)
        att[64 * p + 32 : 64 * p + 64, at] = (got[32:64, 128:] * inverse[:, 128:]).astype(bf16)

    def by_rows(count, work, also=True):
        for low, rows in zip((0,) + ROWS[:-1], ROWS):

            @pl.when((count > low) & (count <= rows) & also)
            def some(rows=rows):
                work(rows)

    def forward_some(blocks, rows):
        work = []
        for i in blocks:
            at = pl.ds(pl.multiple_of(i * QB, QB), QB)
            first = blk_c0[i] * KC
            keys = pl.ds(pl.multiple_of(first, KC), rows)
            operands = [two_heads(q_s, at, p) for p in range(4)]
            values = [vt_s[pair(p, VROWS), pl.ds(pl.multiple_of(first, KC), KC)][:, :rows] for p in range(4)]
            work += [(kn[keys, half(p)], operands[p], coef_row(p), values[p]) for p in range(4)]
        scores = [nn(k, o) * c for k, o, c, unused in work]
        tops = [jnp.max(s, axis=0, keepdims=True) for s in scores]
        es = [jnp.exp2(s - top).astype(bf16) for s, top in zip(scores, tops)]
        sums = [nn(w[3], e) for w, e in zip(work, es)]
        for n_th, i in enumerate(blocks):
            at = pl.ds(pl.multiple_of(i * QB, QB), QB)
            keep = jnp.minimum(blk_tile[i], E_CAP)
            for p in range(4):
                m_s[i, :, pair(p, 256)] = tops[4 * n_th + p]
                ebuf[keep, :rows, pair(p, 256)] = es[4 * n_th + p]
                finish_forward(at, p, sums[4 * n_th + p])

    def forward_block(i, carry):
        at = pl.ds(pl.multiple_of(i * QB, QB), QB)
        c0, nc, tile0, count = blk_c0[i], blk_nc[i], blk_tile[i], blk_rows[i]

        by_rows(count, lambda rows: forward_some([i], rows))

        @pl.when(nc > 1)
        def many():
            m_s[i] = jnp.full((1, 1024), -3e38, f32)
            acc[...] = jnp.zeros_like(acc)

            def tops(c, inner):
                keys = pl.ds(pl.multiple_of((c0 + c) * KC, KC), KC)
                for p in range(4):
                    s = nn(kn[keys, half(p)], two_heads(q_s, at, p)) * coef_row(p)
                    m_s[i, :, pair(p, 256)] = jnp.maximum(
                        m_s[i, :, pair(p, 256)], jnp.max(s, axis=0, keepdims=True)
                    )
                return inner

            lax.fori_loop(0, nc, tops, 0)

            def sums(c, inner):
                keys = pl.ds(pl.multiple_of((c0 + c) * KC, KC), KC)
                keep = jnp.minimum(tile0 + c, E_CAP)
                for p in range(4):
                    s = nn(kn[keys, half(p)], two_heads(q_s, at, p)) * coef_row(p)
                    e = jnp.exp2(s - m_s[i, :, pair(p, 256)]).astype(bf16)
                    ebuf[keep, :, pair(p, 256)] = e
                    acc[pair(p, VROWS), :] += nn(vt_s[pair(p, VROWS), keys], e)
                return inner

            lax.fori_loop(0, nc, sums, 0)
            for p in range(4):
                finish_forward(at, p, acc[pair(p, VROWS), :])

        return carry

    def forward_pair(j, carry):
        i = 2 * j
        count = jnp.maximum(blk_rows[i], blk_rows[i + 1])

        by_rows(count, lambda rows: forward_some([i, i + 1], rows))

        @pl.when(count > KC)
        def apart():
            lax.fori_loop(i, i + 2, forward_block, 0)

        return carry

    pairs = lax.div(num_blocks, jnp.int32(2))
    lax.fori_loop(0, pairs, forward_pair, 0)
    lax.fori_loop(2 * pairs, num_blocks, forward_block, 0)

    weight_a = an[0]
    scale_t = weight_a / count_t
    scale_r = (1.0 - weight_a) / count_r
    acc_gain[...] = jnp.zeros_like(acc_gain)
    out_l[...] = jnp.zeros_like(out_l)

    def mid_values(at):
        x = xs[:, at]
        fmask = fs[:, at]
        hidden = embed_t(x * (1.0 - fmask), emb_w(256), emb_b(256))
        attended = att[:, at]
        residual = hidden + nn(wt_s[3 * D : 4 * D, :], attended)
        normed, inverse = norm_t(residual)
        fn = (normed * gain_out(256)).astype(bf16)
        head = nn(wht_s[...], fn)
        logits = head[0:C]
        err = head[C : C + F] - x
        label = ct[1:2, at]
        hot = (iota((C, 256), 0).astype(f32) == ct[0:1, at]).astype(f32)
        top = jnp.max(logits, axis=0, keepdims=True)
        e = jnp.exp(logits - top)
        total = jnp.sum(e, axis=0, keepdims=True)
        picked = jnp.sum(logits * hot, axis=0, keepdims=True)
        loss = scale_t * label * (jnp.log(total) + top - picked) + scale_r * jnp.sum(
            fmask * err * err, axis=0, keepdims=True
        )
        g_log = scale_t * label * (e / total - hot)
        g_rec = scale_r * fmask * 2.0 * err
        gho = jnp.concatenate([g_log, g_rec, jnp.zeros((8, 256), f32)], axis=0).astype(bf16)
        g_final = nn(wh_s[:, :32], gho)
        g_res = norm_back_t(g_final, normed, inverse, gain_out(256))
        gb = g_res.astype(bf16)
        ga = nn(w_s[:, 3 * D : 4 * D], gb)
        attf = attended.astype(f32)
        das, deltas = [], []
        for h in range(H):
            rows = slice(32 * h, 32 * h + 32)
            inverse_l = il_s[h : h + 1, at]
            das.append((ga[rows] * inverse_l).astype(bf16))
            deltas.append(jnp.sum(ga[rows] * attf[rows], axis=0, keepdims=True) * inverse_l)
        return (
            fold(loss), fold(g_final * normed),
            fn, gho, g_res, gb, jnp.concatenate(das, axis=0), jnp.concatenate(deltas, axis=0),
        )

    def mid_block(j, carry):
        found = [mid_values(at) for at in spots(j, MID_SPAN)]
        out_l[0:1, :] += added(found, 0)
        acc_gain[D : 2 * D, :] += added(found, 1)
        for k, at in enumerate(spots(j, MID_SPAN)):
            for ref, value in zip((fn_s, gho_s, gres, gb_s, dap, delta), found[k][2:]):
                ref[:, at] = value
        return carry

    lax.fori_loop(0, qs // (256 * MID_SPAN), mid_block, 0)

    def backward_some(items, rows):
        work = []
        for at, c, e_of in items:
            lanes = pl.ds(pl.multiple_of(c * KC, KC), KC)
            keys = pl.ds(pl.multiple_of(c * KC, KC), rows)
            es = [e_of(p) for p in range(4)]
            das = [two_heads(dap, at, p) for p in range(4)]
            qds = [two_heads(q_s, at, p) for p in range(4)]
            kts = [kt_s[64 * p : 64 * p + 64, lanes][:, :rows] for p in range(4)]
            vals = [vn[keys, half(p)] for p in range(4)]
            work.append((at, keys, es, das, qds, kts, vals, delta[:, at], dq_s[:, at]))
        old_gk = gk[work[0][1], :]
        old_gv = gv[work[0][1], :]

        def by_key(grads, others):
            return jnp.concatenate(
                [
                    nt(
                        jnp.concatenate([grads[a], grads[a + 1]], axis=1),
                        jnp.concatenate([others[a], others[a + 1]], axis=1),
                    )
                    for a in (0, 2)
                ],
                axis=1,
            )

        dps = [[nn(w[6][p], w[3][p]) for p in range(4)] for w in work]
        dss = []
        for w, dp in zip(work, dps):
            takes = [
                jnp.concatenate([w[7][2 * p : 2 * p + 1], w[7][2 * p + 1 : 2 * p + 2]], axis=1)
                for p in range(4)
            ]
            dss.append([(w[2][p].astype(f32) * (dp[p] - takes[p])).astype(bf16) for p in range(4)])
        dqs = [[nn(w[5][p], ds[p]) for p in range(4)] for w, ds in zip(work, dss)]
        new_gvs = [by_key(w[2], w[3]) for w in work]
        new_gks = [by_key(ds, w[4]) for w, ds in zip(work, dss)]
        for w, dq in zip(work, dqs):
            parts = []
            for p in range(4):
                parts += [dq[p][0:32, :128], dq[p][32:64, 128:]]
            dq_s[:, w[0]] = w[8] + jnp.concatenate(parts, axis=0)
        gk[work[0][1], :] = old_gk + new_gks[0]
        gv[work[0][1], :] = old_gv + new_gvs[0]
        for w, new_gk, new_gv in zip(work[1:], new_gks[1:], new_gvs[1:]):
            gk[w[1], :] += new_gk
            gv[w[1], :] += new_gv

    def kept_weights(i, rows):
        return lambda p: ebuf[blk_tile[i], :rows, pair(p, 256)]

    def queries_of(i):
        return pl.ds(pl.multiple_of(i * QB, QB), QB)

    def backward_block(i, carry):
        at = pl.ds(pl.multiple_of(i * QB, QB), QB)
        c0, nc, tile0, count = blk_c0[i], blk_nc[i], blk_tile[i], blk_rows[i]
        simple = (nc == 1) & (tile0 < E_CAP)

        by_rows(
            count, lambda rows: backward_some([(at, c0, kept_weights(i, rows))], rows), simple
        )

        @pl.when(jnp.logical_not(simple))
        def many():
            def one_chunk(c, inner):
                keys = pl.ds(pl.multiple_of((c0 + c) * KC, KC), KC)

                @pl.when((tile0 + c < E_CAP) & (nc > 1))
                def kept():
                    ecur[...] = ebuf[tile0 + c]

                @pl.when((tile0 + c >= E_CAP) | (nc == 1))
                def again():
                    for p in range(4):
                        s = nn(kn[keys, half(p)], two_heads(q_s, at, p)) * coef_row(p)
                        ecur[:, pair(p, 256)] = jnp.exp2(
                            s - m_s[i, :, pair(p, 256)]
                        ).astype(bf16)

                backward_some([(at, c0 + c, lambda p: ecur[:, pair(p, 256)])], KC)
                return inner

            lax.fori_loop(0, nc, one_chunk, 0)

        return carry

    def backward_pair(j, carry):
        two = (2 * j, 2 * j + 1)
        count = jnp.maximum(blk_rows[two[0]], blk_rows[two[1]])
        simple = (count <= KC) & (blk_tile[two[1]] < E_CAP)

        by_rows(
            count,
            lambda rows: backward_some(
                [(queries_of(i), blk_c0[i], kept_weights(i, rows)) for i in two], rows
            ),
            simple,
        )

        @pl.when(jnp.logical_not(simple))
        def apart():
            lax.fori_loop(two[0], two[0] + 2, backward_block, 0)

        return carry

    lax.fori_loop(0, pairs, backward_pair, 0)
    lax.fori_loop(2 * pairs, num_blocks, backward_block, 0)

    gkv[...] = jnp.zeros_like(gkv)
    w_q[...] = w_s[:, 0:D]

    def mem_back(i, coef_lane):
        found = []
        for k in range(MEM_SPAN):
            c = MEM_SPAN * i + k
            at = pl.ds(pl.multiple_of(c * KC, KC), KC)
            feats_c, unused = mem_feats(c)
            live = ((iota((KC, 1), 0) + c * KC) < ch_end[c]).astype(f32)
            gk_c = (gk[at, :] * coef_lane * live).astype(bf16)
            gv_c = (gv[at, :] * live).astype(bf16)
            gmn = nt(w_s[:, D : 2 * D], gk_c) + nt(w_s[:, 2 * D : 3 * D], gv_c)
            normed, inverse = norm_t(embed_t(feats_c, emb_w(KC), emb_b(KC)))
            gm = norm_back_t(gmn, normed, inverse, gain_in(KC))
            found.append((gk_c, gv_c, fold(gmn * normed), fold(by_feature(gm, feats_c)), fold(gm)))
        mn = mnt[:, pl.ds(pl.multiple_of(MEM_SPAN * i * KC, KC), MEM_SPAN * KC)]
        gkv[:, 0:D] += nn(mn, jnp.concatenate([one[0] for one in found], axis=0))
        gkv[:, D : 2 * D] += nn(mn, jnp.concatenate([one[1] for one in found], axis=0))
        for k, rows in ((2, slice(0, D)), (3, slice(2 * D, 3 * D)), (4, slice(3 * D, 4 * D))):
            acc_gain[rows, :] += added(found, k)
        return coef_lane

    coef_lane = jnp.concatenate([coefb[0:128, :].T[0:1], coefb[128:256, :].T[0:1]], axis=1)
    lax.fori_loop(0, lax.div(num_chunks + MEM_SPAN - 1, jnp.int32(MEM_SPAN)), mem_back, coef_lane)


def step_call(n, num_mem, small_size, an, gw):
    q_blocks, k_chunks = gw.shape[0] - n, chunks_of(num_mem)
    qs, ks = q_blocks * QB, k_chunks * KC
    V = pltpu.VMEM
    S = pltpu.SMEM
    A = jax.ShapeDtypeStruct
    vm = pl.BlockSpec(memory_space=pltpu.VMEM)
    sm = pl.BlockSpec(memory_space=pltpu.SMEM)
    outs = (
        A((8, qs), f32), A((8, qs), f32), A((D, qs), bf16), A((D, qs), bf16), A((D, qs), bf16),
        A((D, qs), bf16), A((D, qs), bf16), A((32, qs), bf16), A((D, qs), f32), A((D, qs), f32),
        A((D, 2 * D), f32), A((D, D), bf16), A((4 * D, 128), f32), A((D, 128), f32),
        A((4 * D + H, 128), f32), A((8, 128), f32),
    )
    scratch = [
        V((8, qs), f32), V((D, 4 * D), bf16), V((4 * D, D), bf16), V((D, 128), bf16), V((32, D), bf16),
        V((8, ks + 128), f32), V((ks, D), bf16), V((ks, D), bf16), V((D, ks), bf16),
        V((4 * VROWS, ks), bf16), V((D, ks), bf16), V((ks, D), f32), V((ks, D), f32),
        V((H, qs), f32), V((D, qs), bf16), V((H, qs), f32),
        V((E_CAP + 1, KC, 1024), bf16), V((KC, 1024), bf16), V((4 * VROWS, 256), f32),
        V((q_blocks, 1, 1024), f32),
        S((q_blocks,), jnp.int32), S((q_blocks,), jnp.int32), S((q_blocks,), jnp.int32),
        S((q_blocks,), jnp.int32), S((k_chunks,), jnp.int32), S((k_chunks,), jnp.int32),
        V((8, num_mem // 16), jnp.int32), S((8, num_mem // 16), jnp.int32), pltpu.SemaphoreType.DMA,
    ]
    return pl.pallas_call(
        functools.partial(step_kernel, n, qs, num_mem, small_size),
        out_shape=outs,
        in_specs=[sm, vm],
        out_specs=(vm,) * len(outs),
        scratch_shapes=scratch,
        compiler_params=pltpu.CompilerParams(vmem_limit_bytes=STEP_VMEM),
    )(an, gw)


MESH = pl.DeviceIdType.MESH


def greet(targets):
    barrier = pltpu.get_barrier_semaphore()
    for target in targets:
        pl.semaphore_signal(barrier, inc=1, device_id=(target,), device_id_type=MESH)
    return barrier


def send(src, dst, send_sem, recv_sem, target):
    copy = pltpu.make_async_remote_copy(
        src_ref=src,
        dst_ref=dst,
        send_sem=send_sem,
        recv_sem=recv_sem,
        device_id=(target,),
        device_id_type=MESH,
    )
    copy.start()
    return copy


def where_am_i(planes):
    me = lax.axis_index("mem")
    core = lax.rem(me, 2)
    square = lax.rem(lax.div(me, 2), 4)
    plane = lax.div(me, 8)
    return me, core, square, plane


def gather_kernel(
    n, num_q, num_mem, *refs,
):
    sources, refs = refs[:12], refs[12:]
    gw, keep = refs[:2]
    copied, refs = refs[2:14], refs[14:]
    send_z, recv_z, send_s, recv_s, send_c, recv_c, load = refs
    w_qkv, w_out, w_heads, w_small, mfeat, qf, fm, qt, tc, tm, mt, mm = copied
    planes = n // 8
    me, core, square, plane = where_am_i(planes)
    in_plane = core + 2 * square
    z_of = [lax.rem(plane + k, planes) * 8 + in_plane for k in range(1, planes)]
    s_of = [plane * 8 + lax.rem(square + k, 4) * 2 + core for k in range(1, 4)]
    c_of = plane * 8 + square * 2 + (1 - core)
    barrier = greet(z_of + s_of + [c_of])
    loads = [
        pltpu.make_async_copy(sources[i], copied[i], load.at[i]) for i in range(len(sources))
    ]
    for copy in loads:
        copy.start()
    for copy in loads:
        copy.wait()

    rows = []
    for c in range(6):
        rows.append(w_qkv[pl.ds(c, 8, stride=6), :])
    for c in range(2):
        rows.append(w_out[pl.ds(c, 8, stride=2), :])
    per_head = w_heads.shape[1]
    lane = iota((8, 256), 1)
    head_row = jnp.concatenate([w_heads[...], jnp.zeros((1, 256 - per_head), f32)], axis=1)
    owner = jnp.floor((lane.astype(f32) + 0.5) * (1.0 / (C + F))).astype(jnp.int32)
    kept_heads = jnp.where(owner == iota((8, 256), 0), head_row, 0.0).astype(bf16)
    fold_r = iota((256, 128), 0)
    fold_row = jnp.floor((fold_r.astype(f32) + 0.5) * (1.0 / (C + F))).astype(jnp.int32)
    fold_m = (fold_r - (C + F) * fold_row == iota((256, 128), 1) - 64).astype(f32).astype(bf16)
    heads = nn(kept_heads, fold_m)
    per_small = w_small.shape[1]
    small = jnp.concatenate([w_small[...], jnp.zeros((1, 128 - per_small), f32)], axis=1)
    small = pltpu.roll(jnp.broadcast_to(small, (8, 128)), SMALL_LANE, 1)
    feats = jnp.concatenate([mfeat[...], jnp.zeros((8, 64), f32)], axis=1)
    lane8 = iota((8, 128), 1)
    row8 = iota((8, 128), 0)
    num_t = jnp.sum(tm[...].astype(f32), axis=1, keepdims=True)
    num_r = jnp.sum(jnp.sum(fm[...].astype(f32), axis=0, keepdims=True), axis=1, keepdims=True)
    block = feats + heads
    first = (row8 == 0) & (lane8 >= SMALL_LANE) & (lane8 < SMALL_LANE + per_small)
    block = jnp.where(first, small, block)
    block = jnp.where((row8 == 0) & (lane8 == COUNT_LANE), num_t, block)
    block = jnp.where((row8 == 0) & (lane8 == COUNT_LANE + 1), num_r, block)

    def slot_of(k, j, c):
        back = lax.rem(plane + planes - k, planes)
        return c * (4 * planes) + lax.rem(square + 4 - j, 4) * planes + back

    gw[slot_of(0, 0, core)] = jnp.concatenate(rows + list(split2(block)), axis=0).astype(bf16)

    pl.semaphore_wait(barrier, planes - 1 + 4)

    def spread(k, done):
        at = gw.at[slot_of(k, 0, core)]
        for j in range(1, 4):
            done[k, j] = send(at, at, send_s.at[k, j - 1], recv_s.at[k, j - 1], s_of[j - 1])
        done[k, 0, "c"] = send(at, at, send_c.at[k, 0], recv_c.at[k, 0], c_of)

    at = gw.at[slot_of(0, 0, core)]
    done = {}
    for k in range(1, planes):
        done[k] = send(at, at, send_z.at[k - 1], recv_z.at[k - 1], z_of[k - 1])
    spread(0, done)

    task_row = iota((8, 256), 0)
    marks = [(qt[:, 256 * b : 256 * b + 256] == task_row).astype(f32) for b in range(num_q // 256)]
    marks_q = jnp.concatenate(marks, axis=0)
    before = (iota((256, 256), 0) < iota((256, 256), 1)).astype(f32).astype(bf16)
    ranks = nn(marks_q.astype(bf16), before)
    totals = jnp.sum(marks_q, axis=1, keepdims=True)
    task_col = iota((8, 1), 0)

    def bases_of(sums, unit):
        base = jnp.int32(0)
        bases, counts, used = [], [], []
        base_vec = jnp.zeros((8, 1), f32)
        for t in range(TASKS):
            count = jnp.sum(jnp.where(task_col == t, sums, 0.0)).astype(jnp.int32)
            bases.append(base)
            counts.append(count)
            used.append(lax.div(count + (unit - 1), jnp.int32(unit)))
            base_vec = base_vec + jnp.where(task_col == t, base.astype(f32), 0.0)
            base = base + used[t] * unit
        return bases, counts, used, base_vec

    carry = jnp.zeros((8, 1), f32)
    carries = []
    for b in range(num_q // 256):
        carries.append(carry)
        carry = carry + totals[8 * b : 8 * b + 8]
    q_base, q_count, q_units, base_vec = bases_of(carry, QB)
    place_q = jnp.concatenate(
        [
            jnp.sum(marks[b] * (base_vec + carries[b] + ranks[8 * b : 8 * b + 8]), axis=0, keepdims=True)
            for b in range(num_q // 256)
        ],
        axis=1,
    )

    cuts = num_mem // 128
    task_row = iota((8, 128), 0)
    marks = []
    for b in range(cuts):
        cut = slice(128 * b, 128 * b + 128)
        marks.append(((mt[:, cut] == task_row) & (mm[:, cut] > 0)).astype(f32))
    marks_m = jnp.concatenate(marks, axis=0)
    ranks = nn(marks_m.astype(bf16), before[:128, :128])
    totals = jnp.broadcast_to(jnp.sum(marks_m, axis=1, keepdims=True), (8 * cuts, 128))
    r_to = iota((8 * cuts, 8 * cuts), 0)
    r_from = iota((8 * cuts, 8 * cuts), 1)
    same_cut = (r_to // 8 == r_from // 8) & (r_from < r_to)
    same_task = (r_to % 8 == r_from % 8) & (r_from < r_to)
    low_totals = totals.astype(bf16)
    starts = nn(same_cut.astype(f32).astype(bf16), low_totals)
    earlier = nn(same_task.astype(f32).astype(bf16), low_totals)
    last = slice(8 * cuts - 8, 8 * cuts)
    m_base, m_count, m_units, base_vec = bases_of((earlier + totals)[last, 0:1], KC)
    slots = earlier + jnp.concatenate([base_vec] * cuts, axis=0)
    places_m = jnp.concatenate(
        [
            jnp.sum(marks[b] * (starts[8 * b : 8 * b + 8] + ranks[8 * b : 8 * b + 8] + 1.0), axis=0, keepdims=True)
            - 1.0
            for b in range(cuts)
        ],
        axis=0,
    )
    eye = r_to == r_from

    def as_row(column):
        return jnp.sum(jnp.where(eye, wide(column, 8 * cuts), 0.0), axis=0, keepdims=True)

    row_t = iota((8, 8 * cuts), 0)
    lane_t = iota((8, 8 * cuts), 1)
    numbers = jnp.where(
        row_t == 0, as_row(starts), jnp.where(row_t == 1, as_row(totals), as_row(slots))
    )
    for i, number in enumerate(m_base + m_count + m_units + q_base + q_units):
        numbers = jnp.where((row_t == 3) & (lane_t == i), number.astype(f32), numbers)
    for i in range(cuts // 16):
        gw[n + 1 + i, 48:64, :] = jnp.concatenate(
            split2(numbers[:, 128 * i : 128 * i + 128]), axis=0
        ).astype(bf16)
    gw[n, 48 : 48 + cuts, :] = places_m.astype(bf16)
    heads_low = jnp.concatenate([w_heads[:, 128:], jnp.zeros((1, 256 - per_head), f32)], axis=1)
    small_row = jnp.concatenate([w_small[...], jnp.zeros((1, 128 - per_small), f32)], axis=1)
    keep[...] = jnp.where(
        row8 == 0, w_heads[:, :128], jnp.where(row8 == 1, heads_low, small_row)
    )
    xq = qf[...]
    fmq = fm[...].astype(f32)
    row8 = iota((8, num_q), 0)
    label_rows = jnp.where(
        row8 == 0, tc[...].astype(f32), jnp.where(row8 == 1, tm[...].astype(f32), 0.0)
    )
    q_rows = jnp.concatenate(
        list(split3(xq)) + [fmq, label_rows, jnp.zeros((8, num_q), f32)], axis=0
    ).astype(bf16)
    for b in range((gw.shape[0] - n) // 2):
        chosen = (
            (place_q == (iota((256, 1), 0) + 256 * b).astype(f32)).astype(f32).astype(bf16)
        )
        got = nt(q_rows, chosen).astype(bf16)
        gw[n + 2 * b, 0:48, :] = got[:, :128]
        gw[n + 2 * b + 1, 0:48, :] = got[:, 128:]


    for k in range(1, planes):
        done[k].wait_recv()
        spread(k, done)
    for k in range(planes):
        for j in range(1, 4):
            done[k, j].wait_recv()
            at = gw.at[slot_of(k, j, core)]
            done[k, j, "c"] = send(at, at, send_c.at[k, j], recv_c.at[k, j], c_of)
    for k in range(planes):
        for j in range(4):
            done[k, j, "c"].wait_recv()
    for copy in done.values():
        copy.wait_send()


def gather_call(n, w_qkv, w_out, w_heads, w_small, mfeat, qf, fm, qt, tc, tm, mt, mm):
    planes = n // 8
    operands = (w_qkv, w_out, w_heads, w_small, mfeat, qf, fm, qt, tc, tm, mt, mm)
    num_q, num_mem = qf.shape[1], mt.shape[1]
    qs = blocks_of(num_q) * QB
    vm = pl.BlockSpec(memory_space=pltpu.VMEM)
    dma = pltpu.SemaphoreType.DMA
    return pl.pallas_call(
        functools.partial(gather_kernel, n, num_q, num_mem),
        out_shape=(
            jax.ShapeDtypeStruct((n + qs // 128, 80, 128), bf16),
            jax.ShapeDtypeStruct((8, 128), f32),
        ),
        in_specs=[pl.BlockSpec(memory_space=pltpu.HBM)] * 12,
        out_specs=(vm,) * 2,
        scratch_shapes=[pltpu.VMEM(v.shape, v.dtype) for v in operands]
        + [
            dma((planes - 1,)), dma((planes - 1,)), dma((planes, 3)), dma((planes, 3)),
            dma((planes, 4)), dma((planes, 4)), dma((12,)),
        ],
        compiler_params=pltpu.CompilerParams(collective_id=0, has_side_effects=True),
    )(*operands)


def reduce_kernel(
    n, per_small,
    xs, fs, qn_s, q_s, att, gb_s, fn_s, gho_s, gres, dq_s, gkv, w_q, cols, coefb, sums_in, l_in,
    g_out, t_out, gq, acc_gain, s_s, r_core, t_square, r_square, t_plane, r_plane, own, n_mine, n_all,
    send_c, recv_c, send_s, recv_s, send_z, recv_z, send_n, recv_n,
):
    planes = n // 8
    rows_dev = D // n
    me, core, square, plane = where_am_i(planes)
    in_plane = core + 2 * square
    upper = lax.div(2 * plane, planes)
    low_plane = plane + upper * (planes - 1 - 2 * plane)
    a_of = []
    for i in range(planes):
        z = planes - 1 - i - lax.div(low_plane + i, max(planes - 1, 1)) if i < planes - 1 else low_plane
        z = z + upper * (planes - 1 - 2 * z)
        for k in (6, 7, 4, 5, 2, 3, 1, 0) if i < planes - 1 else (6, 7, 4, 5, 2, 3, 1):
            a_of.append(z * 8 + lax.rem(in_plane + k, 8))
    z_of = [lax.rem(plane + k, planes) * 8 + in_plane for k in range(1, planes)]
    s_of = [plane * 8 + lax.rem(square + k, 4) * 2 + core for k in range(1, 4)]
    c_of = plane * 8 + square * 2 + (1 - core)
    barrier = greet(a_of)

    def over(rows, lanes):
        return wide(cols[rows, :], lanes)

    def spots(j):
        return [pl.ds(pl.multiple_of(j * 512 + 256 * k, 256), 256) for k in range(2)]

    coef2 = wide(coefb[...], 256)

    def post_values(at):
        kept = xs[:, at] * (1.0 - fs[:, at])
        normed, inverse = norm_t(embed_t(kept, over(slice(0, D), 256), over(slice(D, 2 * D), 256)))
        dq = dq_s[:, at]
        low = (dq * coef2).astype(bf16)
        prod = fold(dq * q_s[:, at].astype(f32))
        betas = jnp.concatenate(
            [jnp.sum(prod[32 * h : 32 * h + 32], axis=0, keepdims=True) for h in range(H)], axis=0
        )
        gqn = nn(w_q[...], low)
        gh = gres[:, at] + norm_back_t(gqn, normed, inverse, over(slice(2 * D, 3 * D), 256))
        return low, betas, fold(gqn * normed), fold(by_feature(gh, kept)), fold(gh)

    def post_block(j, carry):
        cuts = spots(j)
        found = [post_values(at) for at in cuts]
        qn = jnp.concatenate([qn_s[:, at] for at in cuts], axis=1)
        gq_c = jnp.concatenate([found[0][0], found[1][0]], axis=1)
        gq[...] += nt(qn, gq_c)
        for k, rows in ((1, slice(4 * D, 4 * D + H)), (2, slice(0, D)), (3, slice(2 * D, 3 * D)), (4, slice(3 * D, 4 * D))):
            acc_gain[rows, :] += found[0][k] + found[1][k]
        return carry

    gq[...] = jnp.zeros_like(gq)
    acc_gain[...] = sums_in[...]
    lax.fori_loop(0, xs.shape[1] // 512, post_block, 0)
    gout = nt(att[...], gb_s[...])
    ghead = nt(fn_s[...], gho_s[...])

    used = 4 * D + 2 * H
    row = iota((used, 128), 0)
    lan = iota((used, 128), 1)
    row_dev = jnp.floor((row.astype(f32) + 0.5) * (1.0 / per_small)).astype(jnp.int32)
    sums = jnp.sum(acc_gain[...], axis=1, keepdims=True)
    small = jnp.concatenate(
        [
            sums[2 * D : 3 * D],
            sums[3 * D : 4 * D],
            sums[0:D],
            sums[D : 2 * D],
            sums[4 * D : 4 * D + H] * (32 ** (-0.5)),
            jnp.zeros((H, 1), f32),
        ],
        axis=0,
    )
    placed = jnp.where(lan == (row - per_small * row_dev), small, 0.0).astype(bf16)
    r_dev = iota((n, used), 0)
    r_row = iota((n, used), 1)
    mine = (r_row >= per_small * r_dev) & (r_row < per_small * r_dev + per_small)
    small_rows_out = nn(mine.astype(f32).astype(bf16), placed)
    to_flat_r = iota((32, 256), 0)
    to_flat_l = iota((32, 256), 1)
    lane_row = jnp.floor((to_flat_l.astype(f32) + 0.5) * (1.0 / (C + F))).astype(jnp.int32)
    to_flat = ((to_flat_l - (C + F) * lane_row == to_flat_r) & (to_flat_r < C + F)).astype(f32)
    spread_h = nn(ghead.astype(bf16), to_flat.astype(bf16))
    lr = iota((D, 256), 1)
    lr_row = jnp.floor((lr.astype(f32) + 0.5) * (1.0 / (C + F))).astype(jnp.int32)
    spread_h = jnp.where(lr_row == (iota((D, 256), 0) & (rows_dev - 1)), spread_h, 0.0)
    r8 = iota((8, 128), 0)
    for d in range(n):
        rows = slice(rows_dev * d, rows_dev * d + rows_dev)
        head_flat = jnp.sum(spread_h[rows], axis=0, keepdims=True)
        extra = jnp.where(
            r8 == 0,
            head_flat[:, :128],
            jnp.where(r8 == 1, head_flat[:, 128:], jnp.where(r8 == 2, small_rows_out[d : d + 1], 0.0)),
        )
        block = [gq[rows, 128 * k : 128 * k + 128] for k in range(2)]
        block += [gkv[rows, 128 * k : 128 * k + 128] for k in range(4)]
        block += [gout[rows, 128 * k : 128 * k + 128] for k in range(2)]
        block += [extra, jnp.zeros((8, 128), f32)]
        s_s[place_of(d, planes)] = jnp.concatenate(block, axis=0).astype(bf16)

    pl.semaphore_wait(barrier, n - 1)

    def part(c, j, k):
        z = lax.rem(plane + k, planes)
        return c * (4 * planes) + lax.rem(square + j, 4) * planes + z

    done = []
    pieces = {}
    for j in (1, 2, 3, 0):
        line = pl.ds((1 - core) * (4 * planes) + lax.rem(square + j, 4) * planes, planes)
        pieces[j] = send(s_s.at[line], r_core.at[j], send_c.at[j], recv_c.at[j], c_of)
    for j in (1, 2, 3):
        pieces[j].wait_recv()
    order = [2, 1, 3, 0] if planes == 4 else list(range(1, planes)) + [0]
    crossing = {}
    for k in order:
        z = lax.rem(plane + k, planes)
        for j in range(1, 4):
            t_square[j - 1, k] = (
                s_s[part(core, j, k)].astype(f32) + r_core[j, z].astype(f32)
            ).astype(bf16)
            crossing[k, j] = send(
                t_square.at[j - 1, k], r_square.at[j - 1, k],
                send_s.at[j - 1, k], recv_s.at[j - 1, k], s_of[j - 1],
            )
    pieces[0].wait_recv()
    for k in order:
        z = lax.rem(plane + k, planes)
        own[k] = s_s[part(core, 0, k)].astype(f32) + r_core[0, z].astype(f32)
    along = {}
    for k in order:
        total = own[k]
        for j in range(1, 4):
            crossing[k, j].wait_recv()
            total = total + r_square[j - 1, k].astype(f32)
        if k:
            t_plane[k - 1] = total.astype(bf16)
            along[k] = send(
                t_plane.at[k - 1], r_plane.at[k - 1], send_z.at[k - 1], recv_z.at[k - 1], z_of[k - 1]
            )
    for k in range(1, planes):
        along[k].wait_recv()
        total = total + r_plane[k - 1].astype(f32)
    g_out[...] = total
    squares = jnp.sum(total * total, axis=0, keepdims=True)
    squares = squares + pltpu.roll(squares, 64, 1)
    losses = l_in[0:1, :]
    losses = losses + pltpu.roll(losses, 64, 1)
    n_mine[...] = jnp.where(iota((1, 128), 1) < 64, squares, losses)
    n_all[me] = n_mine[...]
    last = [
        send(n_mine, n_all.at[me], send_n.at[k], recv_n.at[me], a_of[k]) for k in range(n - 1)
    ]
    for k in range(1, n):
        other = lax.rem(me + k, n)
        pltpu.make_async_remote_copy(
            src_ref=n_mine,
            dst_ref=n_all.at[other],
            send_sem=send_n.at[k - 1],
            recv_sem=recv_n.at[other],
            device_id=(other,),
            device_id_type=MESH,
        ).wait_recv()
    total = n_all[0]
    for k in range(1, n):
        total = total + n_all[k]
    t_out[...] = total
    for copies in (pieces, crossing, along):
        for copy in copies.values():
            copy.wait_send()
    for copy in last:
        copy.wait_send()


def reduce_call(n, per_small, *grads):
    planes = n // 8
    rows = 80
    vm = pl.BlockSpec(memory_space=pltpu.VMEM)
    dma = pltpu.SemaphoreType.DMA
    V = pltpu.VMEM
    z = planes - 1
    return pl.pallas_call(
        functools.partial(reduce_kernel, n, per_small),
        out_shape=(
            jax.ShapeDtypeStruct((rows, 128), f32),
            jax.ShapeDtypeStruct((1, 128), f32),
        ),
        in_specs=[vm] * len(grads),
        out_specs=(vm, vm),
        scratch_shapes=[
            V((D, D), f32), V((4 * D + H, 128), f32),
            V((n, rows, 128), bf16), V((4, planes, rows, 128), bf16), V((3, planes, rows, 128), bf16),
            V((3, planes, rows, 128), bf16), V((z, rows, 128), bf16), V((z, rows, 128), bf16),
            V((planes, rows, 128), f32), V((1, 128), f32), V((n, 1, 128), f32),
            dma((4,)), dma((4,)), dma((3, planes)), dma((3, planes)), dma((z,)), dma((z,)),
            dma((n - 1,)), dma((n,)),
        ],
        compiler_params=pltpu.CompilerParams(
            collective_id=1, has_side_effects=True, vmem_limit_bytes=16 * 1024 * 1024
        ),
    )(*grads)


def update_kernel(g, tot, *refs):
    w_qkv, w_out, keep = refs[0:3]
    firsts, seconds, refs = refs[3:7], refs[7:11], refs[11:]
    per_head, per_small = firsts[2].shape[1], firsts[3].shape[1]
    weights = (
        w_qkv[...],
        w_out[...],
        jnp.concatenate([keep[0:1, :], keep[1:2, : per_head - 128]], axis=1),
        keep[2:3, :per_small],
    )
    new, first_o, second_o = refs[0:4], refs[4:8], refs[8:12]
    copy_o = (refs[12], refs[13], None, refs[14])
    flat_o, loss_o, norm_o, gq_s, go_s = refs[15:20]
    for c in range(6):
        gq_s[pl.ds(c, 8, stride=6), :] = g[8 * c : 8 * c + 8, :]
    for c in range(2):
        go_s[pl.ds(c, 8, stride=2), :] = g[48 + 8 * c : 56 + 8 * c, :]
    first_half = iota((1, 128), 1) < 64
    norm = jnp.sqrt(jnp.sum(jnp.where(first_half, tot[...], 0.0), axis=1, keepdims=True))
    loss_o[...] = jnp.sum(jnp.where(first_half, 0.0, tot[...]), axis=1, keepdims=True)
    norm_o[...] = norm
    factor = jnp.minimum(1.0, max_norm / (norm + 1e-06))
    grads = (
        gq_s[...],
        go_s[...],
        jnp.concatenate([g[64:65, :], g[65:66, : per_head - 128]], axis=1),
        g[66:67, :per_small],
    )
    for i in range(4):
        first_new, second_new, weight_new = adamw(
            weights[i], firsts[i][...], seconds[i][...], grads[i], factor, float(STEP), learn_rates[i]
        )
        new[i][...] = weight_new
        first_o[i][...] = first_new
        second_o[i][...] = second_new
        if copy_o[i] is not None:
            copy_o[i][...] = weight_new.astype(bf16)
        else:
            flat_o[...] = weight_new.astype(bf16).reshape(weight_new.shape[1])


def update_call(g, tot, w_qkv, w_out, keep, firsts, seconds):
    vm = pl.BlockSpec(memory_space=pltpu.VMEM)
    shapes = [v.shape for v in firsts]
    outs = [jax.ShapeDtypeStruct(s, f32) for s in shapes] * 3
    outs += [jax.ShapeDtypeStruct(s, bf16) for s in shapes[:2] + shapes[3:]]
    outs += [jax.ShapeDtypeStruct((shapes[2][1],), bf16)]
    outs += [jax.ShapeDtypeStruct((1, 1), f32)] * 2
    return pl.pallas_call(
        update_kernel,
        out_shape=tuple(outs),
        in_specs=[vm] * 13,
        out_specs=(vm,) * 18,
        scratch_shapes=[pltpu.VMEM((48, 128), f32), pltpu.VMEM((16, 128), f32)],
        compiler_params=pltpu.CompilerParams(vmem_limit_bytes=4 * 1024 * 1024),
    )(g, tot, w_qkv, w_out, keep, *firsts, *seconds)


def local_fast(
    n, query_feats, feature_mask, query_task, target_class, target_mask, memory_feats, memory_task,
    memory_mask, anneal, w_qkv, w_out, w_heads, w_small, m_qkv, m_out, m_heads, m_small,
    v_qkv, v_out, v_heads, v_small,
):
    def row(v):
        return v.reshape(1, -1)

    def tiles(v):
        return v.reshape(-1, 128)

    weights = (tiles(w_qkv), tiles(w_out), row(w_heads), row(w_small))
    firsts = (tiles(m_qkv), tiles(m_out), row(m_heads), row(m_small))
    seconds = (tiles(v_qkv), tiles(v_out), row(v_heads), row(v_small))
    tm, mt = row(target_mask), row(memory_task)
    gw, keep = gather_call(
        n, *weights, memory_feats.T, query_feats.T, feature_mask.T, row(query_task),
        row(target_class), tm, mt, row(memory_mask),
    )
    found = step_call(n, mt.shape[1], w_small.shape[0] * n, anneal, gw)
    grads, totals = reduce_call(n, w_small.shape[0], *found)
    outs = update_call(grads, totals, weights[0], weights[1], keep, firsts, seconds)
    outs = [out.reshape(-1) for out in outs]
    return tuple(outs[:14] + [outs[15]] + [outs[14]] + outs[16:])


def solution(mesh):
    placed = (
        P("mem", None),
        P("mem", None),
        P("mem"),
        P("mem"),
        P("mem"),
        P("mem", None),
        P(),
        P(),
        P(),
        P("mem"),
        P("mem"),
        P("mem"),
        P("mem"),
        P("mem"),
        P("mem"),
        P("mem"),
        P("mem"),
        P("mem"),
        P("mem"),
        P("mem"),
        P("mem"),
    )
    n = mesh.shape["mem"]

    def choose(*args):
        if D // n == 8 and args[6].shape[0] in (2048, 4096):
            return local_fast(n, *args)
        return local(*args)

    return jax.shard_map(
        choose,
        mesh=mesh,
        in_specs=placed,
        out_specs=(
            P("mem"),
            P("mem"),
            P("mem"),
            P("mem"),
            P("mem"),
            P("mem"),
            P("mem"),
            P("mem"),
            P("mem"),
            P("mem"),
            P("mem"),
            P("mem"),
            P("mem"),
            P("mem"),
            P("mem"),
            P("mem"),
            P(),
            P(),
        ),
        check_vma=False,
    )
```

```python
import functools
import math

import jax
import jax.numpy as jnp
from jax import lax
from jax.experimental import pallas as pl
from jax.experimental.pallas import tpu as pltpu
from jax.sharding import PartitionSpec as P

F = 8
D = 256
H = 8
C = 16
TASKS = 4
STEP = 10


eps_norm = 1e-05
max_norm = 0.05
beta_one = 0.9
beta_two = 0.999
adam_eps = 1e-08
decay_rate = 0.01
learn_rates = (0.05, 1.0, 0.05, 0.5)
masked_score = -1e30


def embed(feature_rows, table_flat, emb_bias):
    emb_table = table_flat.reshape(feature_rows.shape[1], -1)
    return (feature_rows[:, :, None] * emb_table[None]).reshape(
        feature_rows.shape[0], -1
    ) + emb_bias


def standard(hidden):
    centred = hidden - jnp.mean(hidden, -1, keepdims=True)
    inverse = lax.rsqrt(jnp.mean(centred * centred, -1, keepdims=True) + eps_norm)
    return (centred * inverse, inverse)


def norm_back(grad_out, hidden, gain_vec):
    normed, inverse = standard(hidden)
    grad_gain = jnp.sum(grad_out * normed, 0)
    grad_scaled = grad_out * gain_vec
    grad_hidden = inverse * (
        grad_scaled
        - jnp.mean(grad_scaled, -1, keepdims=True)
        - normed * jnp.mean(grad_scaled * normed, -1, keepdims=True)
    )
    return (grad_hidden, grad_gain)


def split_pair(values):
    upper = values.astype(jnp.bfloat16)
    lower = (values - upper.astype(jnp.float32)).astype(jnp.bfloat16)
    return (upper, lower)


def adamw(weight, first_mom, second, grad_in, factor, step_num, step_rate):
    clipped = grad_in * factor
    first_new = beta_one * first_mom + (1 - beta_one) * clipped
    second_new = beta_two * second + (1 - beta_two) * clipped * clipped
    fix_one = 1 - beta_one**step_num
    fix_two = 1 - beta_two**step_num
    weight_new = weight - step_rate * (
        first_new / fix_one / (jnp.sqrt(second_new / fix_two) + adam_eps) + decay_rate * weight
    )
    return (first_new, second_new, weight_new)


def local(
    query_feats,
    feature_mask,
    query_task,
    target_class,
    target_mask,
    memory_feats,
    memory_task,
    memory_mask,
    anneal,
    w_qkv,
    w_out,
    w_heads,
    w_small,
    m_qkv,
    m_out,
    m_heads,
    m_small,
    v_qkv,
    v_out,
    v_heads,
    v_small,
):
    high = lax.Precision.HIGHEST
    head_size = D // H
    full_qkv, full_out, full_heads, full_small = (
        lax.all_gather(w_qkv, "mem", axis=0, tiled=True),
        lax.all_gather(w_out, "mem", axis=0, tiled=True),
        lax.all_gather(w_heads, "mem", axis=0, tiled=True),
        lax.all_gather(w_small, "mem", axis=0, tiled=True),
    )
    emb_table = full_small[:D]
    emb_bias = full_small[D : 2 * D]
    gain_in = full_small[2 * D : 3 * D]
    gain_out = full_small[3 * D : 4 * D]
    score_coef = full_small[4 * D : 4 * D + H] * head_size ** (-0.5)
    qkv_low = full_qkv.reshape(D, 3 * D).astype(jnp.bfloat16)
    out_low = full_out.reshape(D, D).astype(jnp.bfloat16)
    heads_low = full_heads.reshape(D, C + F).astype(jnp.bfloat16)
    mem_hidden = embed(memory_feats, emb_table, emb_bias)
    mem_normed = (standard(mem_hidden)[0] * gain_in).astype(jnp.bfloat16)
    mem_kv = jnp.dot(mem_normed, qkv_low[:, D:], preferred_element_type=jnp.float32).astype(
        jnp.bfloat16
    )
    all_kv = lax.all_gather(mem_kv, "mem", axis=0, tiled=True)
    memory_rows = all_kv.shape[0]
    block_keys = math.gcd(memory_rows, 512)
    num_blocks = memory_rows // block_keys
    key_rows = all_kv[:, :D].reshape(num_blocks, block_keys, H, head_size)
    value_rows = all_kv[:, D:].reshape(num_blocks, block_keys, H, head_size)
    task_blocks = memory_task.reshape(num_blocks, block_keys)
    live_blocks = memory_mask.reshape(num_blocks, block_keys)
    key_blocks = (key_rows, value_rows, task_blocks, live_blocks)
    kept_input = query_feats * (1 - feature_mask).astype(jnp.float32)
    hidden_in = embed(kept_input, emb_table, emb_bias)
    query_normed = (standard(hidden_in)[0] * gain_in).astype(jnp.bfloat16)
    queries = (
        jnp.dot(query_normed, qkv_low[:, :D], preferred_element_type=jnp.float32)
        .astype(jnp.bfloat16)
        .reshape(-1, H, head_size)
    )
    num_rows = queries.shape[0]

    def allowed_of(task_row, live_row):
        return ((query_task[:, None] == task_row[None, :]) & (live_row[None, :] > 0))[None]

    def scores_of(key_block, allowed):
        raw_scores = jnp.einsum(
            "qhd,khd->hqk", queries, key_block, preferred_element_type=jnp.float32
        )
        return (
            raw_scores,
            jnp.where(allowed, score_coef[:, None, None] * raw_scores, masked_score),
        )

    def stats_step(state_in, block_data):
        row_top, row_sum = state_in
        key_block, value_block, task_row, live_row = block_data
        allowed = allowed_of(task_row, live_row)
        scores = scores_of(key_block, allowed)[1]
        new_top = jnp.maximum(row_top, jnp.max(scores, -1))
        shifted = jnp.where(allowed, jnp.exp(scores - new_top[..., None]), 0.0)
        return ((new_top, row_sum * jnp.exp(row_top - new_top) + jnp.sum(shifted, -1)), None)

    start_state = (
        jnp.full((H, num_rows), masked_score, jnp.float32),
        jnp.zeros((H, num_rows), jnp.float32),
    )
    (row_top, row_sum), unused = lax.scan(stats_step, start_state, key_blocks)

    def probs_of(scores, allowed):
        return jnp.where(allowed, jnp.exp(scores - row_top[..., None]), 0.0) / row_sum[..., None]

    def value_step(accum, block_data):
        key_block, value_block, task_row, live_row = block_data
        allowed = allowed_of(task_row, live_row)
        probs_low = probs_of(scores_of(key_block, allowed)[1], allowed).astype(jnp.bfloat16)
        return (
            accum
            + jnp.einsum(
                "hqk,khd->qhd", probs_low, value_block, preferred_element_type=jnp.float32
            ),
            None,
        )

    attn_sum, unused = lax.scan(
        value_step, jnp.zeros((num_rows, H, head_size), jnp.float32), key_blocks
    )
    attended = attn_sum.reshape(num_rows, D).astype(jnp.bfloat16)
    residual = hidden_in + jnp.dot(attended, out_low, preferred_element_type=jnp.float32)
    final_normed = (standard(residual)[0] * gain_out).astype(jnp.bfloat16)
    head_out = jnp.dot(final_normed, heads_low, preferred_element_type=jnp.float32)
    logits = head_out[:, :C]
    recon_err = head_out[:, C:] - query_feats
    label_mask = target_mask.astype(jnp.float32)
    feat_mask = feature_mask.astype(jnp.float32)
    onehot_class = jax.nn.one_hot(target_class, C, dtype=jnp.float32)
    picked = jnp.sum(logits * onehot_class, -1)
    sum_target, sum_recon, count_target, count_recon = lax.psum(
        (
            jnp.sum(label_mask * (jax.nn.logsumexp(logits, -1) - picked)),
            jnp.sum(feat_mask * recon_err**2),
            jnp.sum(label_mask),
            jnp.sum(feat_mask),
        ),
        "mem",
    )
    count_target = jnp.maximum(count_target, 1.0)
    count_recon = jnp.maximum(count_recon, 1.0)
    weight_a = anneal[0]
    loss_value = weight_a * sum_target / count_target + (1 - weight_a) * sum_recon / count_recon
    grad_logits = (
        weight_a / count_target * label_mask[:, None] * (jax.nn.softmax(logits, -1) - onehot_class)
    )
    grad_recon = (1 - weight_a) / count_recon * feat_mask * 2.0 * recon_err
    grad_head_out = jnp.concatenate([grad_logits, grad_recon], 1).astype(jnp.bfloat16)
    grad_heads = jnp.dot(final_normed.T, grad_head_out, preferred_element_type=jnp.float32)
    grad_final = jnp.dot(grad_head_out, heads_low.T, preferred_element_type=jnp.float32)
    grad_resid, grad_gain_out = norm_back(grad_final, residual, gain_out)
    grad_branch = grad_resid.astype(jnp.bfloat16)
    grad_wout = jnp.dot(attended.T, grad_branch, preferred_element_type=jnp.float32)
    grad_attn = (
        jnp.dot(grad_branch, out_low.T, preferred_element_type=jnp.float32)
        .astype(jnp.bfloat16)
        .reshape(num_rows, H, head_size)
    )
    row_delta = jnp.sum(
        grad_attn.astype(jnp.float32)
        * attended.reshape(num_rows, H, head_size).astype(jnp.float32),
        -1,
    ).T

    def back_step(state_in, block_data):
        key_block, value_block, task_row, live_row = block_data
        allowed = allowed_of(task_row, live_row)
        raw_scores, scores = scores_of(key_block, allowed)
        soft_probs = probs_of(scores, allowed)
        grad_probs = jnp.einsum(
            "qhd,khd->hqk", grad_attn, value_block, preferred_element_type=jnp.float32
        )
        grad_scores = (soft_probs * (grad_probs - row_delta[..., None])).astype(jnp.bfloat16)
        grad_beta = jnp.sum(grad_scores.astype(jnp.float32) * raw_scores, (1, 2))
        grad_query = jnp.einsum(
            "hqk,khd->qhd", grad_scores, key_block, preferred_element_type=jnp.float32
        )
        grad_key = (
            jnp.einsum("hqk,qhd->khd", grad_scores, queries, preferred_element_type=jnp.float32)
            * score_coef[None, :, None]
        )
        grad_value = jnp.einsum(
            "hqk,qhd->khd",
            soft_probs.astype(jnp.bfloat16),
            grad_attn,
            preferred_element_type=jnp.float32,
        )
        block_rows = key_block.shape[0]
        grad_kv = jnp.concatenate(
            [grad_key.reshape(block_rows, D), grad_value.reshape(block_rows, D)], 1
        )
        return ((state_in[0] + grad_query, state_in[1] + grad_beta), grad_kv)

    init_state = (jnp.zeros((num_rows, H, head_size), jnp.float32), jnp.zeros((H,), jnp.float32))
    (grad_q_sum, grad_beta_sum), kv_parts = lax.scan(back_step, init_state, key_blocks)
    kv_grad = lax.psum_scatter(
        kv_parts.reshape(memory_rows, 2 * D), "mem", scatter_dimension=0, tiled=True
    )
    grad_q_low = (grad_q_sum * score_coef[None, :, None]).reshape(num_rows, D).astype(jnp.bfloat16)
    grad_wq = jnp.dot(query_normed.T, grad_q_low, preferred_element_type=jnp.float32)
    grad_qn = jnp.dot(grad_q_low, qkv_low[:, :D].T, preferred_element_type=jnp.float32)
    grad_in_q, gain_in_q = norm_back(grad_qn, hidden_in, gain_in)
    grad_hidden = grad_resid + grad_in_q
    kv_upper, kv_lower = split_pair(kv_grad)
    grad_wkv = jnp.dot(mem_normed.T, kv_upper, preferred_element_type=jnp.float32) + jnp.dot(
        mem_normed.T, kv_lower, preferred_element_type=jnp.float32
    )
    grad_mn = jnp.dot(kv_upper, qkv_low[:, D:].T, preferred_element_type=jnp.float32) + jnp.dot(
        kv_lower, qkv_low[:, D:].T, preferred_element_type=jnp.float32
    )
    grad_mem, gain_in_m = norm_back(grad_mn, mem_hidden, gain_in)
    grad_table = jnp.einsum(
        "qf,qfe->fe", kept_input, grad_hidden.reshape(num_rows, F, -1), precision=high
    )
    grad_table = grad_table + jnp.einsum(
        "qf,qfe->fe", memory_feats, grad_mem.reshape(memory_feats.shape[0], F, -1), precision=high
    )
    grad_bias = jnp.sum(grad_hidden, 0) + jnp.sum(grad_mem, 0)
    small_size = full_small.shape[0]
    grad_small = jnp.concatenate(
        [
            grad_table.reshape(-1),
            grad_bias,
            gain_in_q + gain_in_m,
            grad_gain_out,
            grad_beta_sum * head_size ** (-0.5),
            jnp.zeros((small_size - 4 * D - H,), jnp.float32),
        ]
    )
    grad_qkv = jnp.concatenate([grad_wq, grad_wkv], 1).reshape(-1)
    shards = (
        lax.psum_scatter(grad_qkv, "mem", scatter_dimension=0, tiled=True),
        lax.psum_scatter(grad_wout.reshape(-1), "mem", scatter_dimension=0, tiled=True),
        lax.psum_scatter(grad_heads.reshape(-1), "mem", scatter_dimension=0, tiled=True),
        lax.psum_scatter(grad_small, "mem", scatter_dimension=0, tiled=True),
    )
    local_squares = sum((jnp.sum(piece_grad * piece_grad) for piece_grad in shards))
    grad_total = jnp.sqrt(lax.psum(local_squares, "mem"))
    factor = jnp.minimum(1.0, max_norm / (grad_total + 1e-06))
    step_num = float(STEP)
    weights_all = (w_qkv, w_out, w_heads, w_small)
    firsts = (m_qkv, m_out, m_heads, m_small)
    seconds = (v_qkv, v_out, v_heads, v_small)
    results = [
        adamw(weight, first_mom, second, grad_in, factor, step_num, step_rate)
        for weight, first_mom, second, grad_in, step_rate in zip(
            weights_all, firsts, seconds, shards, learn_rates
        )
    ]
    new_w = [entry[2] for entry in results]
    return (
        new_w[0],
        new_w[1],
        new_w[2],
        new_w[3],
        results[0][0],
        results[1][0],
        results[2][0],
        results[3][0],
        results[0][1],
        results[1][1],
        results[2][1],
        results[3][1],
        new_w[0].astype(jnp.bfloat16),
        new_w[1].astype(jnp.bfloat16),
        new_w[2].astype(jnp.bfloat16),
        new_w[3].astype(jnp.bfloat16),
        loss_value.reshape(1),
        grad_total.reshape(1),
    )


f32 = jnp.float32
bf16 = jnp.bfloat16
LOG2E = math.log2(math.e)
QB = 128
KC = 384
ROWS = (320, 352, KC)
VROWS = 80
E_CAP = 12
STEP_VMEM = 44 * 1024 * 1024
PRE_SPAN = 3
MID_SPAN = 6
MEM_SPAN = 2
SMALL_LANE = 88
COUNT_LANE = 122


def place_of(dev, planes):
    return (dev % 2) * (4 * planes) + ((dev // 2) % 4) * planes + dev // 8


def nt(a, b):
    return lax.dot_general(a, b, (((1,), (1,)), ((), ())), preferred_element_type=f32)


def tn(a, b):
    return lax.dot_general(a, b, (((0,), (0,)), ((), ())), preferred_element_type=f32)


def nn(a, b):
    return jnp.dot(a, b, preferred_element_type=f32)


def iota(shape, dim):
    return lax.broadcasted_iota(jnp.int32, shape, dim)


def split2(v):
    hi = v.astype(bf16).astype(f32)
    return hi, v - hi


def split3(v):
    hi, rest = split2(v)
    mid = rest.astype(bf16).astype(f32)
    return hi, mid, rest - mid


def wide(v, lanes):
    return jnp.concatenate([v] * (lanes // v.shape[1]), axis=1) if lanes > v.shape[1] else v


def embed_t(kept, table, bias):
    parts = []
    for f in range(F):
        rows = slice(32 * f, 32 * f + 32)
        parts.append(kept[f : f + 1] * table[rows] + bias[rows])
    return jnp.concatenate(parts, axis=0)


def fold(v):
    total = v[:, :128]
    for k in range(1, v.shape[1] // 128):
        total = total + v[:, 128 * k : 128 * k + 128]
    return total


def by_feature(grad, kept):
    return jnp.concatenate(
        [kept[f : f + 1] * grad[32 * f : 32 * f + 32] for f in range(F)], axis=0
    )


def added(found, k):
    total = found[0][k]
    for one in found[1:]:
        total = total + one[k]
    return total


def norm_t(v):
    centred = v - jnp.mean(v, axis=0, keepdims=True)
    inverse = lax.rsqrt(jnp.mean(centred * centred, axis=0, keepdims=True) + eps_norm)
    return centred * inverse, inverse


def norm_back_t(grad, normed, inverse, gain):
    scaled = grad * gain
    return inverse * (
        scaled
        - jnp.mean(scaled, axis=0, keepdims=True)
        - normed * jnp.mean(scaled * normed, axis=0, keepdims=True)
    )


def blocks_of(num_q):
    blocks = (num_q + TASKS * (QB - 1)) // QB + 1
    return -(-blocks // 4) * 4


def chunks_of(num_mem):
    chunks = (num_mem + TASKS * (KC - 1)) // KC
    return -(-chunks // MEM_SPAN) * MEM_SPAN


def step_kernel(
    n, qs, num_mem, small_size,
    an, gw,
    xs, fs, qn_s, q_s, att, gb_s, fn_s, gho_s, gres, dq_s, gkv, w_q, cols, coefb, acc_gain, out_l,
    ct, w_s, wt_s, wh_s, wht_s,
    mfeat, kn, vn, kt_s, vt_s, mnt, gk, gv,
    il_s, dap, delta, ebuf, ecur, acc, m_s,
    blk_c0, blk_nc, blk_tile, blk_rows, whole, tails, tail_e, ch_base, ch_end, numbers, table, loaded,
):
    planes = n // 8
    per_small = small_size // n
    k_chunks = ch_base.shape[0]

    for i in range(num_mem // 2048):
        both = gw[n + 1 + i, 48:64, :].astype(f32)
        numbers[:, 128 * i : 128 * i + 128] = (both[0:8] + both[8:16]).astype(jnp.int32)
    copy = pltpu.make_async_copy(numbers, table, loaded)
    copy.start()
    copy.wait()
    m_base, m_count, m_units, q_base, q_units, q_count = (
        [table[3, TASKS * k + t] for t in range(TASKS)] for k in range(6)
    )
    num_blocks = q_units[0] + q_units[1] + q_units[2] + q_units[3]
    num_chunks = m_units[0] + m_units[1] + m_units[2] + m_units[3]
    for c in range(k_chunks):
        ch_base[c] = jnp.int32(c * KC)
        ch_end[c] = jnp.int32(c * KC)
    spare = qs // QB - 1
    blk_c0[spare] = jnp.int32(0)
    blk_nc[spare] = jnp.int32(1)
    blk_rows[spare] = jnp.int32(1)
    tile = jnp.int32(0)
    num_whole = jnp.int32(0)
    num_tails = jnp.int32(0)
    for t in range(TASKS):
        first_chunk = lax.div(m_base[t], jnp.int32(KC))
        first_block = lax.div(q_base[t], jnp.int32(QB))

        def fill_chunk(i, carry, t=t, first_chunk=first_chunk):
            ch_base[first_chunk + i] = m_base[t]
            ch_end[first_chunk + i] = m_base[t] + m_count[t]
            return carry

        lax.fori_loop(0, m_units[t], fill_chunk, 0)

        def fill_block(i, tile_in, t=t, first_chunk=first_chunk, first_block=first_block):
            blk_c0[first_block + i] = first_chunk
            blk_nc[first_block + i] = m_units[t]
            blk_rows[first_block + i] = m_count[t]
            blk_tile[first_block + i] = tile_in
            whole[num_whole + i] = first_block + i
            return tile_in + m_units[t]

        left = q_count[t] - QB * (q_units[t] - 1)
        is_tail = ((q_units[t] > 0) & (left <= QB // 2) & (m_units[t] == 1)).astype(jnp.int32)
        tile = lax.fori_loop(0, q_units[t], fill_block, tile) - is_tail
        num_whole = num_whole + q_units[t] - is_tail
        tails[num_tails] = first_block + q_units[t] - 1
        num_tails = num_tails + is_tail
    tails[num_tails] = jnp.int32(spare)

    pieces = [gw[place_of(d, planes)].astype(f32) for d in range(n)]
    for col in range(8):
        block = jnp.concatenate([piece[8 * col : 8 * col + 8] for piece in pieces], axis=0)
        w_s[:, 128 * col : 128 * col + 128] = block.astype(bf16)
        wt_s[128 * col : 128 * col + 128, :] = block.T.astype(bf16)
    lane = iota((8, 128), 1)
    tiles = [piece[64:72] + piece[72:80] for piece in pieces]
    lane_w = iota((D, 128), 1)
    heads = pltpu.roll(jnp.concatenate(tiles, axis=0), 64, 1)
    heads = jnp.where(lane_w < C + F, heads, 0.0)
    wh_s[...] = heads.astype(bf16)
    wht_s[...] = heads.T[:32].astype(bf16)

    for b in range(qs // 128):
        block = gw[n + b, 0:48, :].astype(f32)
        cut = slice(128 * b, 128 * b + 128)
        xs[:, cut] = block[0:8] + block[8:16] + block[16:24]
        fs[:, cut] = block[24:32]
        ct[:, cut] = block[32:40]

    small_rows = jnp.concatenate([tile[0:1] for tile in tiles], axis=0)
    lane_n = iota((n, 128), 1)
    count_t = jnp.maximum(jnp.sum(jnp.where(lane_n == COUNT_LANE, small_rows, 0.0)), 1.0)
    count_r = jnp.maximum(jnp.sum(jnp.where(lane_n == COUNT_LANE + 1, small_rows, 0.0)), 1.0)
    used = 4 * D + 2 * H
    s2 = jnp.concatenate(
        list(split2(small_rows)) + [jnp.zeros((128 - 2 * n, 128), f32)], axis=0
    ).astype(bf16)
    row = iota((used, 128), 0)
    lan = iota((used, 128), 1)
    dev_of = lan & (n - 1)
    pick = (row >= per_small * dev_of) & (row < per_small * dev_of + per_small) & (lan < 2 * n)
    spread = nn(pick.astype(f32).astype(bf16), s2)
    row_dev = jnp.floor((row.astype(f32) + 0.5) * (1.0 / per_small)).astype(jnp.int32)
    here = (lan - SMALL_LANE) == (row - per_small * row_dev)
    column = jnp.sum(jnp.where(here, spread, 0.0), axis=1, keepdims=True)
    cols[...] = jnp.broadcast_to(column[: 4 * D], (4 * D, 128))
    for h in range(H):
        coefb[32 * h : 32 * h + 32, :] = jnp.broadcast_to(
            column[4 * D + h : 4 * D + h + 1] * (32 ** (-0.5)), (32, 128)
        )

    emb_w = lambda lanes: wide(cols[0:D, :], lanes)
    emb_b = lambda lanes: wide(cols[D : 2 * D, :], lanes)
    gain_in = lambda lanes: wide(cols[2 * D : 3 * D, :], lanes)
    gain_out = lambda lanes: wide(cols[3 * D : 4 * D, :], lanes)

    places = gw[n, 48 : 48 + n // 2, :].astype(f32)
    for b in range(n // 2):
        raw = jnp.where(lane < 64, tiles[2 * b], pltpu.roll(tiles[2 * b + 1], 64, 1))
        chosen = (places[b : b + 1] == iota((128, 1), 0).astype(f32)).astype(f32)
        got = nt(jnp.concatenate(split2(raw), axis=0).astype(bf16), chosen.astype(bf16))
        run = got[0:8] + got[8:16]
        for t in range(TASKS):
            i = 8 * b + t
            start, count, slot = table[0, i], table[1, i], table[2, i]
            first = slot & 127
            shift = (first - start) & 127
            moved = pltpu.roll(run, shift, 1)
            at = pl.multiple_of(slot - first, 128)
            pltpu.store(
                mfeat.at[:, pl.ds(at, 128)], moved, mask=(lane >= first) & (lane < first + count)
            )
            pltpu.store(mfeat.at[:, pl.ds(at + 128, 128)], moved, mask=lane < first + count - 128)

    def mem_feats(c):
        base, end = ch_base[c], ch_end[c]
        at = pl.ds(pl.multiple_of(c * KC, KC), KC)
        slot = iota((8, KC), 1) + c * KC
        head = mfeat[:, pl.ds(pl.multiple_of(base, KC), 128)][:, 0:1]
        live = (slot < end).astype(f32)[0:1]
        return jnp.where(slot < end, mfeat[:, at], jnp.where(end > base, head, 0.0)), live

    def mem_pair(i, carry):
        found = []
        for k in range(MEM_SPAN):
            c = MEM_SPAN * i + k
            feats_c, live = mem_feats(c)
            normed, unused = norm_t(embed_t(feats_c, emb_w(KC), emb_b(KC)))
            mnf = normed * gain_in(KC)
            mn = mnf.astype(bf16)
            keys_t = (nn(wt_s[D : 2 * D, :], mn) * live).astype(bf16)
            vals_t = nn(wt_s[2 * D : 3 * D, :], mn) * live
            tail = jnp.where(iota((16, KC), 0) == 0, live, 0.0)
            vals_t = jnp.concatenate(
                [part for p in range(4) for part in (vals_t[64 * p : 64 * p + 64], tail)], axis=0
            ).astype(bf16)
            both = nn(mnf.T.astype(bf16), w_s[:, D : 3 * D])
            live_col = ((iota((KC, 1), 0) + c * KC) < ch_end[c]).astype(f32)
            found.append((mn, keys_t, vals_t, both[:, :D], both[:, D:] * live_col))
        for k in range(MEM_SPAN):
            at = pl.ds(pl.multiple_of((MEM_SPAN * i + k) * KC, KC), KC)
            mnt[:, at], kt_s[:, at], vt_s[:, at] = found[k][0:3]
            kn[at, :] = found[k][3].astype(bf16)
            vn[at, :] = found[k][4].astype(bf16)
            gk[at, :] = jnp.zeros((KC, D), f32)
            gv[at, :] = jnp.zeros((KC, D), f32)
        return carry

    lax.fori_loop(0, lax.div(num_chunks + MEM_SPAN - 1, jnp.int32(MEM_SPAN)), mem_pair, 0)

    def spots(j, span):
        return [pl.ds(pl.multiple_of((j * span + k) * 256, 256), 256) for k in range(span)]

    def pre_block(j, carry):
        found = []
        for at in spots(j, PRE_SPAN):
            kept = xs[:, at] * (1.0 - fs[:, at])
            normed, unused = norm_t(embed_t(kept, emb_w(256), emb_b(256)))
            qn = (normed * gain_in(256)).astype(bf16)
            found.append((qn, nn(wt_s[0:D, :], qn).astype(bf16)))
        for k, at in enumerate(spots(j, PRE_SPAN)):
            qn_s[:, at], q_s[:, at] = found[k]
            att[:, at] = jnp.zeros((D, 256), bf16)
            il_s[:, at] = jnp.zeros((H, 256), f32)
            dq_s[:, at] = jnp.zeros((D, 256), f32)
        return carry

    lax.fori_loop(0, qs // (256 * PRE_SPAN), pre_block, 0)

    zero_h = jnp.zeros((32, 128), bf16)
    zero_p = jnp.zeros((64, 256), bf16)

    def pair(p, width):
        return slice(width * p, width * p + width)

    def half(p):
        return slice(128 * (p // 2), 128 * (p // 2) + 128)

    def two_heads(ref, at, p):
        diag = jnp.concatenate(
            [
                jnp.concatenate([ref[64 * p : 64 * p + 32, at], zero_h], axis=1),
                jnp.concatenate([zero_h, ref[64 * p + 32 : 64 * p + 64, at]], axis=1),
            ],
            axis=0,
        )
        return jnp.concatenate([zero_p, diag] if p % 2 else [diag, zero_p], axis=0)

    def coef_row(p):
        return LOG2E * jnp.concatenate(
            [coefb[64 * p : 64 * p + 1, :], coefb[64 * p + 32 : 64 * p + 33, :]], axis=1
        )

    def finish_forward(at, p, got):
        inverse = 1.0 / got[64:65, :]
        il_s[2 * p : 2 * p + 1, at] = inverse[:, :128]
        il_s[2 * p + 1 : 2 * p + 2, at] = inverse[:, 128:]
        att[64 * p : 64 * p + 32, at] = (got[0:32, :128] * inverse[:, :128]).astype(bf16)
        att[64 * p + 32 : 64 * p + 64, at] = (got[32:64, 128:] * inverse[:, 128:]).astype(bf16)

    def by_rows(count, work, also=True):
        for low, rows in zip((0,) + ROWS[:-1], ROWS):

            @pl.when((count > low) & (count <= rows) & also)
            def some(rows=rows):
                work(rows)

    def forward_some(blocks, rows):
        work = []
        for i in blocks:
            at = pl.ds(pl.multiple_of(i * QB, QB), QB)
            first = blk_c0[i] * KC
            keys = pl.ds(pl.multiple_of(first, KC), rows)
            operands = [two_heads(q_s, at, p) for p in range(4)]
            values = [vt_s[pair(p, VROWS), pl.ds(pl.multiple_of(first, KC), KC)][:, :rows] for p in range(4)]
            work += [(kn[keys, half(p)], operands[p], coef_row(p), values[p]) for p in range(4)]
        scores = [nn(k, o) * c for k, o, c, unused in work]
        tops = [jnp.max(s, axis=0, keepdims=True) for s in scores]
        es = [jnp.exp2(s - top).astype(bf16) for s, top in zip(scores, tops)]
        sums = [nn(w[3], e) for w, e in zip(work, es)]
        for n_th, i in enumerate(blocks):
            at = pl.ds(pl.multiple_of(i * QB, QB), QB)
            keep = jnp.minimum(blk_tile[i], E_CAP)
            for p in range(4):
                m_s[i, :, pair(p, 256)] = tops[4 * n_th + p]
                ebuf[keep, :rows, pair(p, 256)] = es[4 * n_th + p]
                finish_forward(at, p, sums[4 * n_th + p])

    def forward_block(i, carry):
        at = pl.ds(pl.multiple_of(i * QB, QB), QB)
        c0, nc, tile0, count = blk_c0[i], blk_nc[i], blk_tile[i], blk_rows[i]

        by_rows(count, lambda rows: forward_some([i], rows))

        @pl.when(nc > 1)
        def many():
            m_s[i] = jnp.full((1, 1024), -3e38, f32)
            acc[...] = jnp.zeros_like(acc)

            def tops(c, inner):
                keys = pl.ds(pl.multiple_of((c0 + c) * KC, KC), KC)
                for p in range(4):
                    s = nn(kn[keys, half(p)], two_heads(q_s, at, p)) * coef_row(p)
                    m_s[i, :, pair(p, 256)] = jnp.maximum(
                        m_s[i, :, pair(p, 256)], jnp.max(s, axis=0, keepdims=True)
                    )
                return inner

            lax.fori_loop(0, nc, tops, 0)

            def sums(c, inner):
                keys = pl.ds(pl.multiple_of((c0 + c) * KC, KC), KC)
                keep = jnp.minimum(tile0 + c, E_CAP)
                for p in range(4):
                    s = nn(kn[keys, half(p)], two_heads(q_s, at, p)) * coef_row(p)
                    e = jnp.exp2(s - m_s[i, :, pair(p, 256)]).astype(bf16)
                    ebuf[keep, :, pair(p, 256)] = e
                    acc[pair(p, VROWS), :] += nn(vt_s[pair(p, VROWS), keys], e)
                return inner

            lax.fori_loop(0, nc, sums, 0)
            for p in range(4):
                finish_forward(at, p, acc[pair(p, VROWS), :])

        return carry

    def forward_pair(j, carry):
        two = [whole[2 * j], whole[2 * j + 1]]
        count = jnp.maximum(blk_rows[two[0]], blk_rows[two[1]])

        by_rows(count, lambda rows: forward_some(two, rows))

        @pl.when(count > KC)
        def apart():
            lax.fori_loop(2 * j, 2 * j + 2, forward_listed, 0)

        return carry

    def forward_listed(k, carry):
        return forward_block(whole[k], carry)

    pairs = lax.div(num_whole, jnp.int32(2))
    lax.fori_loop(0, pairs, forward_pair, 0)
    lax.fori_loop(2 * pairs, num_whole, forward_listed, 0)

    front = iota((128, 128), 1) < 64
    front_row = iota((1, 128), 1) < 64
    zero_f = jnp.zeros((32, 128), f32)

    def quad(a, width):
        return slice(width * a, width * a + width)

    def four_heads(ref, at, a):
        x = ref[quad(a, 128), at].astype(f32)
        first = jnp.where(front, x, 0.0)
        second = jnp.where(front, 0.0, pltpu.roll(x, 64, 1))
        return jnp.concatenate(
            [
                jnp.concatenate([first[0:32], zero_f], axis=1),
                jnp.concatenate([second[32:64], zero_f], axis=1),
                jnp.concatenate([zero_f, first[64:96]], axis=1),
                jnp.concatenate([zero_f, second[96:128]], axis=1),
            ],
            axis=0,
        ).astype(bf16)

    def four_rows(first, second, a):
        return jnp.concatenate(
            [
                jnp.where(front_row, first[4 * a + k : 4 * a + k + 1], second[4 * a + k + 1 : 4 * a + k + 2])
                for k in (0, 2)
            ],
            axis=1,
        )

    def each_head(a, tile, row_of):
        for k in range(4):
            g = k // 2
            x = tile[row_of(k), 128 * g : 128 * g + 128]
            x = pltpu.roll(x, 64, 1) if k % 2 else x
            yield 4 * a + k, jnp.where(iota(x.shape, 1) < 64, x, 0.0)

    def value_rows(k):
        start = VROWS * (k // 2) + 32 * (k % 2)
        return slice(start, start + 32)

    def tail_pair(j):
        return [(tails[2 * j + k], 2 * j + k) for k in range(2)]

    def tail_rows(j):
        return jnp.maximum(blk_rows[tails[2 * j]], blk_rows[tails[2 * j + 1]])

    coef_heads = jnp.concatenate([coefb[32 * h : 32 * h + 1, :] for h in range(H)], axis=0)
    coef_four = [LOG2E * four_rows(coef_heads, coef_heads, a) for a in range(2)]

    def forward_tails(two, rows):
        work = []
        for i, slot in two:
            at = pl.ds(pl.multiple_of(i * QB, QB), QB)
            first = blk_c0[i] * KC
            keys = pl.ds(pl.multiple_of(first, KC), rows)
            lanes = pl.ds(pl.multiple_of(first, KC), KC)
            work += [
                (
                    kn[keys, quad(a, 128)], four_heads(q_s, at, a), coef_four[a],
                    vt_s[quad(a, 2 * VROWS), lanes][:, :rows],
                )
                for a in range(2)
            ]
        scores = [nn(k, o) * c for k, o, c, unused in work]
        tops = [jnp.max(s, axis=0, keepdims=True) for s in scores]
        es = [jnp.exp2(s - top).astype(bf16) for s, top in zip(scores, tops)]
        sums = [nn(w[3], e) for w, e in zip(work, es)]
        for n_th, (i, slot) in enumerate(two):
            at = pl.ds(pl.multiple_of(i * QB, QB), QB)
            for a in range(2):
                got = sums[2 * n_th + a]
                tail_e[slot, :rows, quad(a, 256)] = es[2 * n_th + a]
                inverse = 1.0 / got[64:65, :]
                for h, value in each_head(a, got * inverse, value_rows):
                    att[32 * h : 32 * h + 32, at] = value.astype(bf16)
                for h, value in each_head(a, inverse, lambda k: slice(0, 1)):
                    il_s[h : h + 1, at] = value

    def forward_tail_pair(j, carry):
        by_rows(tail_rows(j), lambda rows: forward_tails(tail_pair(j), rows))
        return carry

    tail_pairs = lax.div(num_tails + 1, jnp.int32(2))
    lax.fori_loop(0, tail_pairs, forward_tail_pair, 0)

    weight_a = an[0]
    scale_t = weight_a / count_t
    scale_r = (1.0 - weight_a) / count_r
    acc_gain[...] = jnp.zeros_like(acc_gain)
    out_l[...] = jnp.zeros_like(out_l)

    def mid_values(at):
        x = xs[:, at]
        fmask = fs[:, at]
        hidden = embed_t(x * (1.0 - fmask), emb_w(256), emb_b(256))
        attended = att[:, at]
        residual = hidden + nn(wt_s[3 * D : 4 * D, :], attended)
        normed, inverse = norm_t(residual)
        fn = (normed * gain_out(256)).astype(bf16)
        head = nn(wht_s[...], fn)
        logits = head[0:C]
        err = head[C : C + F] - x
        label = ct[1:2, at]
        hot = (iota((C, 256), 0).astype(f32) == ct[0:1, at]).astype(f32)
        top = jnp.max(logits, axis=0, keepdims=True)
        e = jnp.exp(logits - top)
        total = jnp.sum(e, axis=0, keepdims=True)
        picked = jnp.sum(logits * hot, axis=0, keepdims=True)
        loss = scale_t * label * (jnp.log(total) + top - picked) + scale_r * jnp.sum(
            fmask * err * err, axis=0, keepdims=True
        )
        g_log = scale_t * label * (e / total - hot)
        g_rec = scale_r * fmask * 2.0 * err
        gho = jnp.concatenate([g_log, g_rec, jnp.zeros((8, 256), f32)], axis=0).astype(bf16)
        g_final = nn(wh_s[:, :32], gho)
        g_res = norm_back_t(g_final, normed, inverse, gain_out(256))
        gb = g_res.astype(bf16)
        ga = nn(w_s[:, 3 * D : 4 * D], gb)
        attf = attended.astype(f32)
        das, deltas = [], []
        for h in range(H):
            rows = slice(32 * h, 32 * h + 32)
            inverse_l = il_s[h : h + 1, at]
            das.append((ga[rows] * inverse_l).astype(bf16))
            deltas.append(jnp.sum(ga[rows] * attf[rows], axis=0, keepdims=True) * inverse_l)
        return (
            fold(loss), fold(g_final * normed),
            fn, gho, g_res, gb, jnp.concatenate(das, axis=0), jnp.concatenate(deltas, axis=0),
        )

    def mid_block(j, carry):
        found = [mid_values(at) for at in spots(j, MID_SPAN)]
        out_l[0:1, :] += added(found, 0)
        acc_gain[D : 2 * D, :] += added(found, 1)
        for k, at in enumerate(spots(j, MID_SPAN)):
            for ref, value in zip((fn_s, gho_s, gres, gb_s, dap, delta), found[k][2:]):
                ref[:, at] = value
        return carry

    lax.fori_loop(0, qs // (256 * MID_SPAN), mid_block, 0)

    def backward_some(items, rows):
        work = []
        for at, c, e_of in items:
            lanes = pl.ds(pl.multiple_of(c * KC, KC), KC)
            keys = pl.ds(pl.multiple_of(c * KC, KC), rows)
            es = [e_of(p) for p in range(4)]
            das = [two_heads(dap, at, p) for p in range(4)]
            qds = [two_heads(q_s, at, p) for p in range(4)]
            kts = [kt_s[64 * p : 64 * p + 64, lanes][:, :rows] for p in range(4)]
            vals = [vn[keys, half(p)] for p in range(4)]
            work.append((at, keys, es, das, qds, kts, vals, delta[:, at], dq_s[:, at]))
        old_gk = gk[work[0][1], :]
        old_gv = gv[work[0][1], :]

        def by_key(grads, others):
            return jnp.concatenate(
                [
                    nt(
                        jnp.concatenate([grads[a], grads[a + 1]], axis=1),
                        jnp.concatenate([others[a], others[a + 1]], axis=1),
                    )
                    for a in (0, 2)
                ],
                axis=1,
            )

        dps = [[nn(w[6][p], w[3][p]) for p in range(4)] for w in work]
        dss = []
        for w, dp in zip(work, dps):
            takes = [
                jnp.concatenate([w[7][2 * p : 2 * p + 1], w[7][2 * p + 1 : 2 * p + 2]], axis=1)
                for p in range(4)
            ]
            dss.append([(w[2][p].astype(f32) * (dp[p] - takes[p])).astype(bf16) for p in range(4)])
        dqs = [[nn(w[5][p], ds[p]) for p in range(4)] for w, ds in zip(work, dss)]
        new_gvs = [by_key(w[2], w[3]) for w in work]
        new_gks = [by_key(ds, w[4]) for w, ds in zip(work, dss)]
        for w, dq in zip(work, dqs):
            parts = []
            for p in range(4):
                parts += [dq[p][0:32, :128], dq[p][32:64, 128:]]
            dq_s[:, w[0]] = w[8] + jnp.concatenate(parts, axis=0)
        gk[work[0][1], :] = old_gk + new_gks[0]
        gv[work[0][1], :] = old_gv + new_gvs[0]
        for w, new_gk, new_gv in zip(work[1:], new_gks[1:], new_gvs[1:]):
            gk[w[1], :] += new_gk
            gv[w[1], :] += new_gv

    def kept_weights(i, rows):
        return lambda p: ebuf[blk_tile[i], :rows, pair(p, 256)]

    def queries_of(i):
        return pl.ds(pl.multiple_of(i * QB, QB), QB)

    def backward_block(i, carry):
        at = pl.ds(pl.multiple_of(i * QB, QB), QB)
        c0, nc, tile0, count = blk_c0[i], blk_nc[i], blk_tile[i], blk_rows[i]
        simple = (nc == 1) & (tile0 < E_CAP)

        by_rows(
            count, lambda rows: backward_some([(at, c0, kept_weights(i, rows))], rows), simple
        )

        @pl.when(jnp.logical_not(simple))
        def many():
            def one_chunk(c, inner):
                keys = pl.ds(pl.multiple_of((c0 + c) * KC, KC), KC)

                @pl.when((tile0 + c < E_CAP) & (nc > 1))
                def kept():
                    ecur[...] = ebuf[tile0 + c]

                @pl.when((tile0 + c >= E_CAP) | (nc == 1))
                def again():
                    for p in range(4):
                        s = nn(kn[keys, half(p)], two_heads(q_s, at, p)) * coef_row(p)
                        ecur[:, pair(p, 256)] = jnp.exp2(
                            s - m_s[i, :, pair(p, 256)]
                        ).astype(bf16)

                backward_some([(at, c0 + c, lambda p: ecur[:, pair(p, 256)])], KC)
                return inner

            lax.fori_loop(0, nc, one_chunk, 0)

        return carry

    def backward_pair(j, carry):
        two = (whole[2 * j], whole[2 * j + 1])
        count = jnp.maximum(blk_rows[two[0]], blk_rows[two[1]])
        simple = (count <= KC) & (blk_tile[two[1]] < E_CAP)

        by_rows(
            count,
            lambda rows: backward_some(
                [(queries_of(i), blk_c0[i], kept_weights(i, rows)) for i in two], rows
            ),
            simple,
        )

        @pl.when(jnp.logical_not(simple))
        def apart():
            lax.fori_loop(2 * j, 2 * j + 2, backward_listed, 0)

        return carry

    def backward_listed(k, carry):
        return backward_block(whole[k], carry)

    lax.fori_loop(0, pairs, backward_pair, 0)
    lax.fori_loop(2 * pairs, num_whole, backward_listed, 0)

    def backward_tails(two, rows):
        work = []
        for i, slot in two:
            at = queries_of(i)
            lanes = pl.ds(pl.multiple_of(blk_c0[i] * KC, KC), KC)
            keys = pl.ds(pl.multiple_of(blk_c0[i] * KC, KC), rows)
            first = delta[:, at]
            second = pltpu.roll(first, 64, 1)
            work.append(
                (
                    at,
                    keys,
                    [tail_e[slot, :rows, quad(a, 256)] for a in range(2)],
                    [four_heads(dap, at, a) for a in range(2)],
                    [four_heads(q_s, at, a) for a in range(2)],
                    [kt_s[quad(a, 128), lanes][:, :rows] for a in range(2)],
                    [vn[keys, quad(a, 128)] for a in range(2)],
                    [four_rows(first, second, a) for a in range(2)],
                )
            )
        dps = [[nn(w[6][a], w[3][a]) for a in range(2)] for w in work]
        dss = [
            [(w[2][a].astype(f32) * (dp[a] - w[7][a])).astype(bf16) for a in range(2)]
            for w, dp in zip(work, dps)
        ]
        dqs = [[nn(w[5][a], ds[a]) for a in range(2)] for w, ds in zip(work, dss)]

        def by_key(grads, others):
            return jnp.concatenate([nt(grads[a], others[a]) for a in range(2)], axis=1)

        new_gvs = [by_key(w[2], w[3]) for w in work]
        new_gks = [by_key(ds, w[4]) for w, ds in zip(work, dss)]
        for w, dq in zip(work, dqs):
            for a in range(2):
                for h, value in each_head(a, dq[a], lambda k: slice(32 * k, 32 * k + 32)):
                    dq_s[32 * h : 32 * h + 32, w[0]] = value
        for w, new_gk, new_gv in zip(work, new_gks, new_gvs):
            gk[w[1], :] += new_gk
            gv[w[1], :] += new_gv

    def backward_tail_pair(j, carry):
        by_rows(tail_rows(j), lambda rows: backward_tails(tail_pair(j), rows))
        return carry

    lax.fori_loop(0, tail_pairs, backward_tail_pair, 0)

    gkv[...] = jnp.zeros_like(gkv)
    w_q[...] = w_s[:, 0:D]

    def mem_back(i, coef_lane):
        found = []
        for k in range(MEM_SPAN):
            c = MEM_SPAN * i + k
            at = pl.ds(pl.multiple_of(c * KC, KC), KC)
            feats_c, unused = mem_feats(c)
            live = ((iota((KC, 1), 0) + c * KC) < ch_end[c]).astype(f32)
            gk_c = (gk[at, :] * coef_lane * live).astype(bf16)
            gv_c = (gv[at, :] * live).astype(bf16)
            gmn = nt(w_s[:, D : 2 * D], gk_c) + nt(w_s[:, 2 * D : 3 * D], gv_c)
            normed, inverse = norm_t(embed_t(feats_c, emb_w(KC), emb_b(KC)))
            gm = norm_back_t(gmn, normed, inverse, gain_in(KC))
            found.append((gk_c, gv_c, fold(gmn * normed), fold(by_feature(gm, feats_c)), fold(gm)))
        mn = mnt[:, pl.ds(pl.multiple_of(MEM_SPAN * i * KC, KC), MEM_SPAN * KC)]
        gkv[:, 0:D] += nn(mn, jnp.concatenate([one[0] for one in found], axis=0))
        gkv[:, D : 2 * D] += nn(mn, jnp.concatenate([one[1] for one in found], axis=0))
        for k, rows in ((2, slice(0, D)), (3, slice(2 * D, 3 * D)), (4, slice(3 * D, 4 * D))):
            acc_gain[rows, :] += added(found, k)
        return coef_lane

    coef_lane = jnp.concatenate([coefb[0:128, :].T[0:1], coefb[128:256, :].T[0:1]], axis=1)
    lax.fori_loop(0, lax.div(num_chunks + MEM_SPAN - 1, jnp.int32(MEM_SPAN)), mem_back, coef_lane)


def step_call(n, num_mem, small_size, an, gw):
    q_blocks, k_chunks = gw.shape[0] - n, chunks_of(num_mem)
    qs, ks = q_blocks * QB, k_chunks * KC
    V = pltpu.VMEM
    S = pltpu.SMEM
    A = jax.ShapeDtypeStruct
    vm = pl.BlockSpec(memory_space=pltpu.VMEM)
    sm = pl.BlockSpec(memory_space=pltpu.SMEM)
    outs = (
        A((8, qs), f32), A((8, qs), f32), A((D, qs), bf16), A((D, qs), bf16), A((D, qs), bf16),
        A((D, qs), bf16), A((D, qs), bf16), A((32, qs), bf16), A((D, qs), f32), A((D, qs), f32),
        A((D, 2 * D), f32), A((D, D), bf16), A((4 * D, 128), f32), A((D, 128), f32),
        A((4 * D + H, 128), f32), A((8, 128), f32),
    )
    scratch = [
        V((8, qs), f32), V((D, 4 * D), bf16), V((4 * D, D), bf16), V((D, 128), bf16), V((32, D), bf16),
        V((8, ks + 128), f32), V((ks, D), bf16), V((ks, D), bf16), V((D, ks), bf16),
        V((4 * VROWS, ks), bf16), V((D, ks), bf16), V((ks, D), f32), V((ks, D), f32),
        V((H, qs), f32), V((D, qs), bf16), V((H, qs), f32),
        V((E_CAP + 1, KC, 1024), bf16), V((KC, 1024), bf16), V((4 * VROWS, 256), f32),
        V((q_blocks, 1, 1024), f32),
        S((q_blocks,), jnp.int32), S((q_blocks,), jnp.int32), S((q_blocks,), jnp.int32),
        S((q_blocks,), jnp.int32), S((q_blocks,), jnp.int32), S((TASKS + 2,), jnp.int32),
        V((TASKS, KC, 512), bf16), S((k_chunks,), jnp.int32), S((k_chunks,), jnp.int32),
        V((8, num_mem // 16), jnp.int32), S((8, num_mem // 16), jnp.int32), pltpu.SemaphoreType.DMA,
    ]
    return pl.pallas_call(
        functools.partial(step_kernel, n, qs, num_mem, small_size),
        out_shape=outs,
        in_specs=[sm, vm],
        out_specs=(vm,) * len(outs),
        scratch_shapes=scratch,
        compiler_params=pltpu.CompilerParams(vmem_limit_bytes=STEP_VMEM),
    )(an, gw)


MESH = pl.DeviceIdType.MESH


def greet(targets):
    barrier = pltpu.get_barrier_semaphore()
    for target in targets:
        pl.semaphore_signal(barrier, inc=1, device_id=(target,), device_id_type=MESH)
    return barrier


def send(src, dst, send_sem, recv_sem, target):
    copy = pltpu.make_async_remote_copy(
        src_ref=src,
        dst_ref=dst,
        send_sem=send_sem,
        recv_sem=recv_sem,
        device_id=(target,),
        device_id_type=MESH,
    )
    copy.start()
    return copy


def where_am_i(planes):
    me = lax.axis_index("mem")
    core = lax.rem(me, 2)
    square = lax.rem(lax.div(me, 2), 4)
    plane = lax.div(me, 8)
    return me, core, square, plane


def gather_kernel(
    n, num_q, num_mem, *refs,
):
    sources, refs = refs[:12], refs[12:]
    gw, keep = refs[:2]
    copied, refs = refs[2:14], refs[14:]
    send_z, recv_z, send_s, recv_s, send_c, recv_c, load = refs
    w_qkv, w_out, w_heads, w_small, mfeat, qf, fm, qt, tc, tm, mt, mm = copied
    planes = n // 8
    me, core, square, plane = where_am_i(planes)
    in_plane = core + 2 * square
    z_of = [lax.rem(plane + k, planes) * 8 + in_plane for k in range(1, planes)]
    s_of = [plane * 8 + lax.rem(square + k, 4) * 2 + core for k in range(1, 4)]
    c_of = plane * 8 + square * 2 + (1 - core)
    barrier = greet(z_of + s_of + [c_of])
    loads = [
        pltpu.make_async_copy(sources[i], copied[i], load.at[i]) for i in range(len(sources))
    ]
    for copy in loads:
        copy.start()
    for copy in loads:
        copy.wait()

    rows = []
    for c in range(6):
        rows.append(w_qkv[pl.ds(c, 8, stride=6), :])
    for c in range(2):
        rows.append(w_out[pl.ds(c, 8, stride=2), :])
    per_head = w_heads.shape[1]
    lane = iota((8, 256), 1)
    head_row = jnp.concatenate([w_heads[...], jnp.zeros((1, 256 - per_head), f32)], axis=1)
    owner = jnp.floor((lane.astype(f32) + 0.5) * (1.0 / (C + F))).astype(jnp.int32)
    kept_heads = jnp.where(owner == iota((8, 256), 0), head_row, 0.0).astype(bf16)
    fold_r = iota((256, 128), 0)
    fold_row = jnp.floor((fold_r.astype(f32) + 0.5) * (1.0 / (C + F))).astype(jnp.int32)
    fold_m = (fold_r - (C + F) * fold_row == iota((256, 128), 1) - 64).astype(f32).astype(bf16)
    heads = nn(kept_heads, fold_m)
    per_small = w_small.shape[1]
    small = jnp.concatenate([w_small[...], jnp.zeros((1, 128 - per_small), f32)], axis=1)
    small = pltpu.roll(jnp.broadcast_to(small, (8, 128)), SMALL_LANE, 1)
    feats = jnp.concatenate([mfeat[...], jnp.zeros((8, 64), f32)], axis=1)
    lane8 = iota((8, 128), 1)
    row8 = iota((8, 128), 0)
    num_t = jnp.sum(tm[...].astype(f32), axis=1, keepdims=True)
    num_r = jnp.sum(jnp.sum(fm[...].astype(f32), axis=0, keepdims=True), axis=1, keepdims=True)
    block = feats + heads
    first = (row8 == 0) & (lane8 >= SMALL_LANE) & (lane8 < SMALL_LANE + per_small)
    block = jnp.where(first, small, block)
    block = jnp.where((row8 == 0) & (lane8 == COUNT_LANE), num_t, block)
    block = jnp.where((row8 == 0) & (lane8 == COUNT_LANE + 1), num_r, block)

    def slot_of(k, j, c):
        back = lax.rem(plane + planes - k, planes)
        return c * (4 * planes) + lax.rem(square + 4 - j, 4) * planes + back

    gw[slot_of(0, 0, core)] = jnp.concatenate(rows + list(split2(block)), axis=0).astype(bf16)

    pl.semaphore_wait(barrier, planes - 1 + 4)

    def spread(k, done):
        at = gw.at[slot_of(k, 0, core)]
        for j in range(1, 4):
            done[k, j] = send(at, at, send_s.at[k, j - 1], recv_s.at[k, j - 1], s_of[j - 1])
        done[k, 0, "c"] = send(at, at, send_c.at[k, 0], recv_c.at[k, 0], c_of)

    at = gw.at[slot_of(0, 0, core)]
    done = {}
    for k in range(1, planes):
        done[k] = send(at, at, send_z.at[k - 1], recv_z.at[k - 1], z_of[k - 1])
    spread(0, done)

    task_row = iota((8, 256), 0)
    marks = [(qt[:, 256 * b : 256 * b + 256] == task_row).astype(f32) for b in range(num_q // 256)]
    marks_q = jnp.concatenate(marks, axis=0)
    before = (iota((256, 256), 0) < iota((256, 256), 1)).astype(f32).astype(bf16)
    ranks = nn(marks_q.astype(bf16), before)
    totals = jnp.sum(marks_q, axis=1, keepdims=True)
    task_col = iota((8, 1), 0)

    def bases_of(sums, unit):
        base = jnp.int32(0)
        bases, counts, used = [], [], []
        base_vec = jnp.zeros((8, 1), f32)
        for t in range(TASKS):
            count = jnp.sum(jnp.where(task_col == t, sums, 0.0)).astype(jnp.int32)
            bases.append(base)
            counts.append(count)
            used.append(lax.div(count + (unit - 1), jnp.int32(unit)))
            base_vec = base_vec + jnp.where(task_col == t, base.astype(f32), 0.0)
            base = base + used[t] * unit
        return bases, counts, used, base_vec

    carry = jnp.zeros((8, 1), f32)
    carries = []
    for b in range(num_q // 256):
        carries.append(carry)
        carry = carry + totals[8 * b : 8 * b + 8]
    q_base, q_count, q_units, base_vec = bases_of(carry, QB)
    place_q = jnp.concatenate(
        [
            jnp.sum(marks[b] * (base_vec + carries[b] + ranks[8 * b : 8 * b + 8]), axis=0, keepdims=True)
            for b in range(num_q // 256)
        ],
        axis=1,
    )

    cuts = num_mem // 128
    task_row = iota((8, 128), 0)
    marks = []
    for b in range(cuts):
        cut = slice(128 * b, 128 * b + 128)
        marks.append(((mt[:, cut] == task_row) & (mm[:, cut] > 0)).astype(f32))
    marks_m = jnp.concatenate(marks, axis=0)
    ranks = nn(marks_m.astype(bf16), before[:128, :128])
    totals = jnp.broadcast_to(jnp.sum(marks_m, axis=1, keepdims=True), (8 * cuts, 128))
    r_to = iota((8 * cuts, 8 * cuts), 0)
    r_from = iota((8 * cuts, 8 * cuts), 1)
    same_cut = (r_to // 8 == r_from // 8) & (r_from < r_to)
    same_task = (r_to % 8 == r_from % 8) & (r_from < r_to)
    low_totals = totals.astype(bf16)
    starts = nn(same_cut.astype(f32).astype(bf16), low_totals)
    earlier = nn(same_task.astype(f32).astype(bf16), low_totals)
    last = slice(8 * cuts - 8, 8 * cuts)
    m_base, m_count, m_units, base_vec = bases_of((earlier + totals)[last, 0:1], KC)
    slots = earlier + jnp.concatenate([base_vec] * cuts, axis=0)
    places_m = jnp.concatenate(
        [
            jnp.sum(marks[b] * (starts[8 * b : 8 * b + 8] + ranks[8 * b : 8 * b + 8] + 1.0), axis=0, keepdims=True)
            - 1.0
            for b in range(cuts)
        ],
        axis=0,
    )
    eye = r_to == r_from

    def as_row(column):
        return jnp.sum(jnp.where(eye, wide(column, 8 * cuts), 0.0), axis=0, keepdims=True)

    row_t = iota((8, 8 * cuts), 0)
    lane_t = iota((8, 8 * cuts), 1)
    numbers = jnp.where(
        row_t == 0, as_row(starts), jnp.where(row_t == 1, as_row(totals), as_row(slots))
    )
    for i, number in enumerate(m_base + m_count + m_units + q_base + q_units + q_count):
        numbers = jnp.where((row_t == 3) & (lane_t == i), number.astype(f32), numbers)
    for i in range(cuts // 16):
        gw[n + 1 + i, 48:64, :] = jnp.concatenate(
            split2(numbers[:, 128 * i : 128 * i + 128]), axis=0
        ).astype(bf16)
    gw[n, 48 : 48 + cuts, :] = places_m.astype(bf16)
    heads_low = jnp.concatenate([w_heads[:, 128:], jnp.zeros((1, 256 - per_head), f32)], axis=1)
    small_row = jnp.concatenate([w_small[...], jnp.zeros((1, 128 - per_small), f32)], axis=1)
    keep[...] = jnp.where(
        row8 == 0, w_heads[:, :128], jnp.where(row8 == 1, heads_low, small_row)
    )
    xq = qf[...]
    fmq = fm[...].astype(f32)
    row8 = iota((8, num_q), 0)
    label_rows = jnp.where(
        row8 == 0, tc[...].astype(f32), jnp.where(row8 == 1, tm[...].astype(f32), 0.0)
    )
    q_rows = jnp.concatenate(
        list(split3(xq)) + [fmq, label_rows, jnp.zeros((8, num_q), f32)], axis=0
    ).astype(bf16)
    for b in range((gw.shape[0] - n) // 2):
        chosen = (
            (place_q == (iota((256, 1), 0) + 256 * b).astype(f32)).astype(f32).astype(bf16)
        )
        got = nt(q_rows, chosen).astype(bf16)
        gw[n + 2 * b, 0:48, :] = got[:, :128]
        gw[n + 2 * b + 1, 0:48, :] = got[:, 128:]


    for k in range(1, planes):
        done[k].wait_recv()
        spread(k, done)
    for k in range(planes):
        for j in range(1, 4):
            done[k, j].wait_recv()
            at = gw.at[slot_of(k, j, core)]
            done[k, j, "c"] = send(at, at, send_c.at[k, j], recv_c.at[k, j], c_of)
    for k in range(planes):
        for j in range(4):
            done[k, j, "c"].wait_recv()
    for copy in done.values():
        copy.wait_send()


def gather_call(n, w_qkv, w_out, w_heads, w_small, mfeat, qf, fm, qt, tc, tm, mt, mm):
    planes = n // 8
    operands = (w_qkv, w_out, w_heads, w_small, mfeat, qf, fm, qt, tc, tm, mt, mm)
    num_q, num_mem = qf.shape[1], mt.shape[1]
    qs = blocks_of(num_q) * QB
    vm = pl.BlockSpec(memory_space=pltpu.VMEM)
    dma = pltpu.SemaphoreType.DMA
    return pl.pallas_call(
        functools.partial(gather_kernel, n, num_q, num_mem),
        out_shape=(
            jax.ShapeDtypeStruct((n + qs // 128, 80, 128), bf16),
            jax.ShapeDtypeStruct((8, 128), f32),
        ),
        in_specs=[pl.BlockSpec(memory_space=pltpu.HBM)] * 12,
        out_specs=(vm,) * 2,
        scratch_shapes=[pltpu.VMEM(v.shape, v.dtype) for v in operands]
        + [
            dma((planes - 1,)), dma((planes - 1,)), dma((planes, 3)), dma((planes, 3)),
            dma((planes, 4)), dma((planes, 4)), dma((12,)),
        ],
        compiler_params=pltpu.CompilerParams(collective_id=0, has_side_effects=True),
    )(*operands)


def reduce_kernel(
    n, per_small,
    xs, fs, qn_s, q_s, att, gb_s, fn_s, gho_s, gres, dq_s, gkv, w_q, cols, coefb, sums_in, l_in,
    g_out, t_out, gq, acc_gain, s_s, r_core, t_square, r_square, t_plane, r_plane, own, n_mine, n_all,
    send_c, recv_c, send_s, recv_s, send_z, recv_z, send_n, recv_n,
):
    planes = n // 8
    rows_dev = D // n
    me, core, square, plane = where_am_i(planes)
    in_plane = core + 2 * square
    upper = lax.div(2 * plane, planes)
    low_plane = plane + upper * (planes - 1 - 2 * plane)
    a_of = []
    for i in range(planes):
        z = planes - 1 - i - lax.div(low_plane + i, max(planes - 1, 1)) if i < planes - 1 else low_plane
        z = z + upper * (planes - 1 - 2 * z)
        for k in (6, 7, 4, 5, 2, 3, 1, 0) if i < planes - 1 else (6, 7, 4, 5, 2, 3, 1):
            a_of.append(z * 8 + lax.rem(in_plane + k, 8))
    z_of = [lax.rem(plane + k, planes) * 8 + in_plane for k in range(1, planes)]
    s_of = [plane * 8 + lax.rem(square + k, 4) * 2 + core for k in range(1, 4)]
    c_of = plane * 8 + square * 2 + (1 - core)
    barrier = greet(a_of)

    def over(rows, lanes):
        return wide(cols[rows, :], lanes)

    def spots(j):
        return [pl.ds(pl.multiple_of(j * 512 + 256 * k, 256), 256) for k in range(2)]

    coef2 = wide(coefb[...], 256)

    def post_values(at):
        kept = xs[:, at] * (1.0 - fs[:, at])
        normed, inverse = norm_t(embed_t(kept, over(slice(0, D), 256), over(slice(D, 2 * D), 256)))
        dq = dq_s[:, at]
        low = (dq * coef2).astype(bf16)
        prod = fold(dq * q_s[:, at].astype(f32))
        betas = jnp.concatenate(
            [jnp.sum(prod[32 * h : 32 * h + 32], axis=0, keepdims=True) for h in range(H)], axis=0
        )
        gqn = nn(w_q[...], low)
        gh = gres[:, at] + norm_back_t(gqn, normed, inverse, over(slice(2 * D, 3 * D), 256))
        return low, betas, fold(gqn * normed), fold(by_feature(gh, kept)), fold(gh)

    def post_block(j, carry):
        cuts = spots(j)
        found = [post_values(at) for at in cuts]
        qn = jnp.concatenate([qn_s[:, at] for at in cuts], axis=1)
        gq_c = jnp.concatenate([found[0][0], found[1][0]], axis=1)
        gq[...] += nt(qn, gq_c)
        for k, rows in ((1, slice(4 * D, 4 * D + H)), (2, slice(0, D)), (3, slice(2 * D, 3 * D)), (4, slice(3 * D, 4 * D))):
            acc_gain[rows, :] += found[0][k] + found[1][k]
        return carry

    gq[...] = jnp.zeros_like(gq)
    acc_gain[...] = sums_in[...]
    lax.fori_loop(0, xs.shape[1] // 512, post_block, 0)
    gout = nt(att[...], gb_s[...])
    ghead = nt(fn_s[...], gho_s[...])

    used = 4 * D + 2 * H
    row = iota((used, 128), 0)
    lan = iota((used, 128), 1)
    row_dev = jnp.floor((row.astype(f32) + 0.5) * (1.0 / per_small)).astype(jnp.int32)
    sums = jnp.sum(acc_gain[...], axis=1, keepdims=True)
    small = jnp.concatenate(
        [
            sums[2 * D : 3 * D],
            sums[3 * D : 4 * D],
            sums[0:D],
            sums[D : 2 * D],
            sums[4 * D : 4 * D + H] * (32 ** (-0.5)),
            jnp.zeros((H, 1), f32),
        ],
        axis=0,
    )
    placed = jnp.where(lan == (row - per_small * row_dev), small, 0.0).astype(bf16)
    r_dev = iota((n, used), 0)
    r_row = iota((n, used), 1)
    mine = (r_row >= per_small * r_dev) & (r_row < per_small * r_dev + per_small)
    small_rows_out = nn(mine.astype(f32).astype(bf16), placed)
    to_flat_r = iota((32, 256), 0)
    to_flat_l = iota((32, 256), 1)
    lane_row = jnp.floor((to_flat_l.astype(f32) + 0.5) * (1.0 / (C + F))).astype(jnp.int32)
    to_flat = ((to_flat_l - (C + F) * lane_row == to_flat_r) & (to_flat_r < C + F)).astype(f32)
    spread_h = nn(ghead.astype(bf16), to_flat.astype(bf16))
    lr = iota((D, 256), 1)
    lr_row = jnp.floor((lr.astype(f32) + 0.5) * (1.0 / (C + F))).astype(jnp.int32)
    spread_h = jnp.where(lr_row == (iota((D, 256), 0) & (rows_dev - 1)), spread_h, 0.0)
    r8 = iota((8, 128), 0)
    for d in range(n):
        rows = slice(rows_dev * d, rows_dev * d + rows_dev)
        head_flat = jnp.sum(spread_h[rows], axis=0, keepdims=True)
        extra = jnp.where(
            r8 == 0,
            head_flat[:, :128],
            jnp.where(r8 == 1, head_flat[:, 128:], jnp.where(r8 == 2, small_rows_out[d : d + 1], 0.0)),
        )
        block = [gq[rows, 128 * k : 128 * k + 128] for k in range(2)]
        block += [gkv[rows, 128 * k : 128 * k + 128] for k in range(4)]
        block += [gout[rows, 128 * k : 128 * k + 128] for k in range(2)]
        block += [extra, jnp.zeros((8, 128), f32)]
        s_s[place_of(d, planes)] = jnp.concatenate(block, axis=0).astype(bf16)

    pl.semaphore_wait(barrier, n - 1)

    def part(c, j, k):
        z = lax.rem(plane + k, planes)
        return c * (4 * planes) + lax.rem(square + j, 4) * planes + z

    done = []
    pieces = {}
    for j in (1, 2, 3, 0):
        line = pl.ds((1 - core) * (4 * planes) + lax.rem(square + j, 4) * planes, planes)
        pieces[j] = send(s_s.at[line], r_core.at[j], send_c.at[j], recv_c.at[j], c_of)
    for j in (1, 2, 3):
        pieces[j].wait_recv()
    order = [2, 1, 3, 0] if planes == 4 else list(range(1, planes)) + [0]
    crossing = {}
    for k in order:
        z = lax.rem(plane + k, planes)
        for j in range(1, 4):
            t_square[j - 1, k] = (
                s_s[part(core, j, k)].astype(f32) + r_core[j, z].astype(f32)
            ).astype(bf16)
            crossing[k, j] = send(
                t_square.at[j - 1, k], r_square.at[j - 1, k],
                send_s.at[j - 1, k], recv_s.at[j - 1, k], s_of[j - 1],
            )
    pieces[0].wait_recv()
    for k in order:
        z = lax.rem(plane + k, planes)
        own[k] = s_s[part(core, 0, k)].astype(f32) + r_core[0, z].astype(f32)
    along = {}
    for k in order:
        total = own[k]
        for j in range(1, 4):
            crossing[k, j].wait_recv()
            total = total + r_square[j - 1, k].astype(f32)
        if k:
            t_plane[k - 1] = total.astype(bf16)
            along[k] = send(
                t_plane.at[k - 1], r_plane.at[k - 1], send_z.at[k - 1], recv_z.at[k - 1], z_of[k - 1]
            )
    for k in range(1, planes):
        along[k].wait_recv()
        total = total + r_plane[k - 1].astype(f32)
    g_out[...] = total
    squares = jnp.sum(total * total, axis=0, keepdims=True)
    squares = squares + pltpu.roll(squares, 64, 1)
    losses = l_in[0:1, :]
    losses = losses + pltpu.roll(losses, 64, 1)
    n_mine[...] = jnp.where(iota((1, 128), 1) < 64, squares, losses)
    n_all[me] = n_mine[...]
    last = [
        send(n_mine, n_all.at[me], send_n.at[k], recv_n.at[me], a_of[k]) for k in range(n - 1)
    ]
    for k in range(1, n):
        other = lax.rem(me + k, n)
        pltpu.make_async_remote_copy(
            src_ref=n_mine,
            dst_ref=n_all.at[other],
            send_sem=send_n.at[k - 1],
            recv_sem=recv_n.at[other],
            device_id=(other,),
            device_id_type=MESH,
        ).wait_recv()
    total = n_all[0]
    for k in range(1, n):
        total = total + n_all[k]
    t_out[...] = total
    for copies in (pieces, crossing, along):
        for copy in copies.values():
            copy.wait_send()
    for copy in last:
        copy.wait_send()


def reduce_call(n, per_small, *grads):
    planes = n // 8
    rows = 80
    vm = pl.BlockSpec(memory_space=pltpu.VMEM)
    dma = pltpu.SemaphoreType.DMA
    V = pltpu.VMEM
    z = planes - 1
    return pl.pallas_call(
        functools.partial(reduce_kernel, n, per_small),
        out_shape=(
            jax.ShapeDtypeStruct((rows, 128), f32),
            jax.ShapeDtypeStruct((1, 128), f32),
        ),
        in_specs=[vm] * len(grads),
        out_specs=(vm, vm),
        scratch_shapes=[
            V((D, D), f32), V((4 * D + H, 128), f32),
            V((n, rows, 128), bf16), V((4, planes, rows, 128), bf16), V((3, planes, rows, 128), bf16),
            V((3, planes, rows, 128), bf16), V((z, rows, 128), bf16), V((z, rows, 128), bf16),
            V((planes, rows, 128), f32), V((1, 128), f32), V((n, 1, 128), f32),
            dma((4,)), dma((4,)), dma((3, planes)), dma((3, planes)), dma((z,)), dma((z,)),
            dma((n - 1,)), dma((n,)),
        ],
        compiler_params=pltpu.CompilerParams(
            collective_id=1, has_side_effects=True, vmem_limit_bytes=16 * 1024 * 1024
        ),
    )(*grads)


def update_kernel(g, tot, *refs):
    w_qkv, w_out, keep = refs[0:3]
    firsts, seconds, refs = refs[3:7], refs[7:11], refs[11:]
    per_head, per_small = firsts[2].shape[1], firsts[3].shape[1]
    weights = (
        w_qkv[...],
        w_out[...],
        jnp.concatenate([keep[0:1, :], keep[1:2, : per_head - 128]], axis=1),
        keep[2:3, :per_small],
    )
    new, first_o, second_o = refs[0:4], refs[4:8], refs[8:12]
    copy_o = (refs[12], refs[13], None, refs[14])
    flat_o, loss_o, norm_o, gq_s, go_s = refs[15:20]
    for c in range(6):
        gq_s[pl.ds(c, 8, stride=6), :] = g[8 * c : 8 * c + 8, :]
    for c in range(2):
        go_s[pl.ds(c, 8, stride=2), :] = g[48 + 8 * c : 56 + 8 * c, :]
    first_half = iota((1, 128), 1) < 64
    norm = jnp.sqrt(jnp.sum(jnp.where(first_half, tot[...], 0.0), axis=1, keepdims=True))
    loss_o[...] = jnp.sum(jnp.where(first_half, 0.0, tot[...]), axis=1, keepdims=True)
    norm_o[...] = norm
    factor = jnp.minimum(1.0, max_norm / (norm + 1e-06))
    grads = (
        gq_s[...],
        go_s[...],
        jnp.concatenate([g[64:65, :], g[65:66, : per_head - 128]], axis=1),
        g[66:67, :per_small],
    )
    for i in range(4):
        first_new, second_new, weight_new = adamw(
            weights[i], firsts[i][...], seconds[i][...], grads[i], factor, float(STEP), learn_rates[i]
        )
        new[i][...] = weight_new
        first_o[i][...] = first_new
        second_o[i][...] = second_new
        if copy_o[i] is not None:
            copy_o[i][...] = weight_new.astype(bf16)
        else:
            flat_o[...] = weight_new.astype(bf16).reshape(weight_new.shape[1])


def update_call(g, tot, w_qkv, w_out, keep, firsts, seconds):
    vm = pl.BlockSpec(memory_space=pltpu.VMEM)
    shapes = [v.shape for v in firsts]
    outs = [jax.ShapeDtypeStruct(s, f32) for s in shapes] * 3
    outs += [jax.ShapeDtypeStruct(s, bf16) for s in shapes[:2] + shapes[3:]]
    outs += [jax.ShapeDtypeStruct((shapes[2][1],), bf16)]
    outs += [jax.ShapeDtypeStruct((1, 1), f32)] * 2
    return pl.pallas_call(
        update_kernel,
        out_shape=tuple(outs),
        in_specs=[vm] * 13,
        out_specs=(vm,) * 18,
        scratch_shapes=[pltpu.VMEM((48, 128), f32), pltpu.VMEM((16, 128), f32)],
        compiler_params=pltpu.CompilerParams(vmem_limit_bytes=4 * 1024 * 1024),
    )(g, tot, w_qkv, w_out, keep, *firsts, *seconds)


def local_fast(
    n, query_feats, feature_mask, query_task, target_class, target_mask, memory_feats, memory_task,
    memory_mask, anneal, w_qkv, w_out, w_heads, w_small, m_qkv, m_out, m_heads, m_small,
    v_qkv, v_out, v_heads, v_small,
):
    def row(v):
        return v.reshape(1, -1)

    def tiles(v):
        return v.reshape(-1, 128)

    weights = (tiles(w_qkv), tiles(w_out), row(w_heads), row(w_small))
    firsts = (tiles(m_qkv), tiles(m_out), row(m_heads), row(m_small))
    seconds = (tiles(v_qkv), tiles(v_out), row(v_heads), row(v_small))
    tm, mt = row(target_mask), row(memory_task)
    gw, keep = gather_call(
        n, *weights, memory_feats.T, query_feats.T, feature_mask.T, row(query_task),
        row(target_class), tm, mt, row(memory_mask),
    )
    found = step_call(n, mt.shape[1], w_small.shape[0] * n, anneal, gw)
    grads, totals = reduce_call(n, w_small.shape[0], *found)
    outs = update_call(grads, totals, weights[0], weights[1], keep, firsts, seconds)
    outs = [out.reshape(-1) for out in outs]
    return tuple(outs[:14] + [outs[15]] + [outs[14]] + outs[16:])


def solution(mesh):
    placed = (
        P("mem", None),
        P("mem", None),
        P("mem"),
        P("mem"),
        P("mem"),
        P("mem", None),
        P(),
        P(),
        P(),
        P("mem"),
        P("mem"),
        P("mem"),
        P("mem"),
        P("mem"),
        P("mem"),
        P("mem"),
        P("mem"),
        P("mem"),
        P("mem"),
        P("mem"),
        P("mem"),
    )
    n = mesh.shape["mem"]

    def choose(*args):
        if D // n == 8 and args[6].shape[0] in (2048, 4096):
            return local_fast(n, *args)
        return local(*args)

    return jax.shard_map(
        choose,
        mesh=mesh,
        in_specs=placed,
        out_specs=(
            P("mem"),
            P("mem"),
            P("mem"),
            P("mem"),
            P("mem"),
            P("mem"),
            P("mem"),
            P("mem"),
            P("mem"),
            P("mem"),
            P("mem"),
            P("mem"),
            P("mem"),
            P("mem"),
            P("mem"),
            P("mem"),
            P(),
            P(),
        ),
        check_vma=False,
    )
```
